32 devices in a mesh: dp: 16 (over z, y, core), group: 2 (over x).
Axes of the slice: x: 2, y: 2, z: 4, core: 2. Of those that a mesh axis runs over, the one named last changes fastest.
Arguments:
- tokens: bfloat16 [28224, 256], P('dp'), may hold values from -6 to 6
- cotangent: bfloat16 [28224, 256], P('dp'), may hold values from -6 to 6
- image_ids: int32 [16, 42, 42], P('dp'), may hold values from 0 to 63, as said below
- qkv_weight: float32 [2, 256, 768], P(None, None, 'group'), may hold values from -0.375 to 0.375
- proj_weight: float32 [2, 256, 256], P(None, 'group'), may hold values from -1 to 1
- up_weight: float32 [2, 256, 1024], P(None, None, 'group'), may hold values from -0.375 to 0.375
- down_weight: float32 [2, 1024, 256], P(None, 'group'), may hold values from -0.1875 to 0.1875
- shared_vectors: float32 [2, 1536], replicated
- group_vectors: float32 [2, 2, 2048], P(None, 'group'), may hold values from -3 to 3
- qkv_moment: float32 [2, 256, 768], P(None, 'dp', 'group'), may hold values from -320 to 320
- proj_moment: float32 [2, 256, 256], P(None, 'group', 'dp'), may hold values from -320 to 320
- up_moment: float32 [2, 256, 1024], P(None, 'dp', 'group'), may hold values from -320 to 320
- down_moment: float32 [2, 1024, 256], P(None, 'group', 'dp'), may hold values from -320 to 320
- shared_moment: float32 [2, 1536], P(None, 'dp'), may hold values from -512 to 512
- group_moment: float32 [2, 2, 2048], P(None, 'group', 'dp'), may hold values from -512 to 512
Outputs:
- outputs: bfloat16 [28224, 256], P('dp')
- input_grad: float32 [28224, 256], P('dp')
- qkv_momentum: float32 [2, 256, 768], P(None, 'dp', 'group')
- qkv_master: float32 [2, 256, 768], P(None, 'dp', 'group')
- proj_momentum: float32 [2, 256, 256], P(None, 'group', 'dp')
- proj_master: float32 [2, 256, 256], P(None, 'group', 'dp')
- up_momentum: float32 [2, 256, 1024], P(None, 'dp', 'group')
- up_master: float32 [2, 256, 1024], P(None, 'dp', 'group')
- down_momentum: float32 [2, 1024, 256], P(None, 'group', 'dp')
- down_master: float32 [2, 1024, 256], P(None, 'group', 'dp')
- shared_momentum: float32 [2, 1536], P(None, 'dp')
- shared_master: float32 [2, 1536], P(None, 'dp')
- group_momentum: float32 [2, 2, 2048], P(None, 'group', 'dp')
- group_master: float32 [2, 2, 2048], P(None, 'group', 'dp')
The draws below stay inside these ranges and needn't reach their ends.
Inputs may be any that keep to these rules, and one draw needn't show every extreme that they name: `image_ids`: each canvas is cut into rectangles, one per image: its rows fall into bands and each band into pieces side by side. All tokens of one rectangle hold one number and different rectangles of a canvas hold different numbers; the bottom right rectangle of every canvas holds 63.
All inputs are finite; a program needn't handle non-finite values.
Results may differ from the reference program's by a relative error of at most 0.03.
Values may be sent and summed in bfloat16 or wider, within the bound.
No kernel may reach another device: no remote copies, remote signals or barrier semaphores. Data moves between devices by JAX's collectives and lax.ppermute only.
A program may use at most 192 MiB of HBM per device.

```python
import math
import jax
import jax.numpy as jnp
from jax import lax

D = 256
FF = 1024
HEADS = 8
STRIPE = 7
SIDE = 42
LAYERS = 2
NS_STEPS = 5
CANVASES = 16
TOKENS = 28224
SHARED_VEC = 1536
GROUP_VEC = 2048


def draw_image_ids(key, part):
    key = jax.random.fold_in(key, 7)
    first, second = jax.random.split(key)
    lowest = max(2, SIDE // 8)
    upper = SIDE // 2 + 1
    heights = jax.random.randint(first, (CANVASES, 8), lowest, upper)
    widths = jax.random.randint(second, (CANVASES, 8, 8), lowest, upper)
    places = jnp.arange(SIDE)
    tops = jnp.cumsum(heights, axis=-1)
    band = jnp.minimum(jnp.sum((places[None, :, None] >= tops[:, None, :]).astype(jnp.int32), axis=-1), 7)
    rights = jnp.cumsum(widths, axis=-1)
    picker = (band[:, :, None] == jnp.arange(8)[None, None, :]).astype(jnp.int32)
    row_rights = jnp.sum(picker[:, :, :, None] * rights[:, None, :, :], axis=2)
    piece = jnp.minimum(jnp.sum((places[None, None, :, None] >= row_rights[:, :, None, :]).astype(jnp.int32), axis=-1), 7)
    numbers = (band[:, :, None] * 8 + piece).astype(jnp.int32)
    corner = numbers[:, SIDE - 1, SIDE - 1]
    return jnp.where(numbers == corner[:, None, None], 63, numbers).astype(jnp.int32)


def draw_shared_vectors(key, part):
    key = jax.random.fold_in(key, 5)
    first, second = jax.random.split(key)
    slot = jnp.arange(6 * D) // D
    is_gain = (slot == 0) | (slot == 3)
    gains = jax.random.uniform(first, (LAYERS, 6 * D), jnp.float32, 0.5, 1.5)
    shifts = 0.3 * jax.random.normal(second, (LAYERS, 6 * D), jnp.float32)
    return jnp.where(is_gain[None, :], gains, shifts)


def steps_of(own_key, dims, pieces, smallest, largest):
    level, own = 1.0, jax.random.fold_in(own_key, 6)
    for dim, shards_of in pieces:
        steps = jnp.exp(jax.random.uniform(jax.random.fold_in(own, dim), (shards_of,), jnp.float32, smallest / len(pieces), largest / len(pieces)))
        level = level * jnp.repeat(steps, dims[dim] // shards_of).reshape([-1 if axis == dim else 1 for axis in range(len(dims))])
    return level


def gaussian(own_key, shape, scale, reach, cuts=(), held_as=jnp.bfloat16):
    factor_of = steps_of(own_key, shape, cuts, -0.22, 0.18) if cuts else 1.0
    drawn = jax.random.normal(own_key, shape, jnp.float32) * scale * factor_of
    return jnp.minimum(jnp.maximum(drawn, -reach), reach).astype(held_as)


def setup_inputs(seed: int = 0) -> dict:
    keys = jax.random.split(jax.random.key(seed), 16)
    tokens = gaussian(keys[0], (TOKENS, D), 1.0, 6.0, ((0, 16),))
    cotangent = gaussian(keys[1], (TOKENS, D), 1.0, 6.0, ((0, 16),))
    image_ids = draw_image_ids(jax.random.fold_in(keys[15], 71), 0)
    qkv_weight = gaussian(keys[3], (LAYERS, D, 3 * D), D ** -0.5, 0.375, ((2, 2),), jnp.float32)
    proj_weight = gaussian(keys[4], (LAYERS, D, D), (D // 8) ** -0.5, 1.0, ((1, 2),), jnp.float32)
    up_weight = gaussian(keys[5], (LAYERS, D, FF), D ** -0.5, 0.375, ((2, 2),), jnp.float32)
    down_weight = gaussian(keys[6], (LAYERS, FF, D), FF ** -0.5, 0.1875, ((1, 2),), jnp.float32)
    shared_vectors = draw_shared_vectors(jax.random.fold_in(keys[15], 71), 0)
    group_vectors = gaussian(keys[8], (LAYERS, 2, GROUP_VEC), 0.2, 3.0, ((1, 2),), jnp.float32)
    qkv_moment = gaussian(keys[9], (LAYERS, D, 3 * D), (0.3 * TOKENS ** 0.5), 320.0, ((1, 16), (2, 2)), jnp.float32)
    proj_moment = gaussian(keys[10], (LAYERS, D, D), (0.3 * TOKENS ** 0.5), 320.0, ((1, 2), (2, 16)), jnp.float32)
    up_moment = gaussian(keys[11], (LAYERS, D, FF), (0.3 * TOKENS ** 0.5), 320.0, ((1, 16), (2, 2)), jnp.float32)
    down_moment = gaussian(keys[12], (LAYERS, FF, D), (0.3 * TOKENS ** 0.5), 320.0, ((1, 2), (2, 16)), jnp.float32)
    shared_moment = gaussian(keys[13], (LAYERS, SHARED_VEC), (0.5 * TOKENS ** 0.5), 512.0, ((1, 16),), jnp.float32)
    group_moment = gaussian(keys[14], (LAYERS, 2, GROUP_VEC), (0.5 * TOKENS ** 0.5), 512.0, ((1, 2), (2, 16)), jnp.float32)
    return {"tokens": tokens, "cotangent": cotangent, "image_ids": image_ids, "qkv_weight": qkv_weight, "proj_weight": proj_weight, "up_weight": up_weight, "down_weight": down_weight, "shared_vectors": shared_vectors, "group_vectors": group_vectors, "qkv_moment": qkv_moment, "proj_moment": proj_moment, "up_moment": up_moment, "down_moment": down_moment, "shared_moment": shared_moment, "group_moment": group_moment}


@jax.custom_vjp
def low(v):
    return lax.optimization_barrier(v.astype(jnp.bfloat16)).astype(jnp.float32)

@jax.custom_vjp
def low_back(v):
    return v

def low_keep(v):
    return (low(v), None)

def low_pass(kept, grad):
    return (grad,)

def back_keep(v):
    return (v, None)

def back_low(kept, grad):
    return (low(grad),)
low.defvjp(low_keep, low_pass)
low_back.defvjp(back_keep, back_low)
epsilon = 1e-05
highest = lax.Precision.HIGHEST
coeff_first = 3.4445
coeff_second = -4.775
coeff_third = 2.0315
momentum_decay = 0.95
matrix_rate = 0.25
weight_decay = 0.1
vector_rate = 0.001
match_scale = 0.2
masked_score = -1e+30

def norm_rows(rows, gain, shift):
    mean = lax.optimization_barrier(jnp.mean(rows, axis=-1, keepdims=True))
    centred = rows - mean
    spread = lax.optimization_barrier(jnp.mean(centred * centred, axis=-1, keepdims=True))
    return centred * lax.rsqrt(spread + epsilon) * gain + shift

def position_term(values, ids, kernel, shift):
    side = values.shape[-2]
    padded = jnp.pad(values, ((0, 0), (1, 1), (1, 1), (0, 0)))
    padded_ids = jnp.pad(ids, ((0, 0), (1, 1), (1, 1)), constant_values=-1)
    band = jnp.arange(side) // STRIPE
    padded_band = jnp.pad(band, 1, constant_values=-1)
    total = jnp.zeros_like(values) + shift
    for tap in range(9):
        row_step = tap // 3
        col_step = tap % 3
        moved = padded[:, row_step:row_step + side, col_step:col_step + side]
        moved_ids = padded_ids[:, row_step:row_step + side, col_step:col_step + side]
        same_band = padded_band[row_step:row_step + side] == band
        valid = (moved_ids == ids) & same_band[None, :, None]
        total = total + jnp.where(valid[..., None], moved * kernel[tap], 0.0)
    return total

def newton(matrix):
    tall = matrix.shape[0] > matrix.shape[1]
    work = matrix.T if tall else matrix
    work = work / (jnp.sqrt(jnp.sum(work * work)) + 1e-07)
    for step in range(NS_STEPS):
        gram = jnp.dot(work, work.T, precision=highest)
        blend = coeff_second * gram + coeff_third * jnp.dot(gram, gram, precision=highest)
        work = coeff_first * work + jnp.dot(blend, work, precision=highest)
    return work.T if tall else work

def stripe_attention(block):
    query, keys_part, values_part, ids = block
    scale = (D // HEADS) ** (-0.5)
    scores = low_back(jnp.einsum('qhe,khe->hqk', query, keys_part, precision=highest) * scale)
    same = ids[:, None] == ids[None, :]
    scores = jnp.where(same[None], scores, masked_score)
    weights = low(jax.nn.softmax(scores, axis=-1))
    return jnp.einsum('hqk,khe->qhe', weights, values_part, precision=highest)

def head_outputs(query, keys_part, values_part, ids, kernel, shift, flip):
    channels = D // 2
    heads_local = HEADS // 2
    head_size = D // HEADS
    grids = [part.reshape(SIDE, SIDE, channels) for part in (query, keys_part, values_part)]
    id_grid = ids
    if flip:
        grids = [jnp.swapaxes(grid, 0, 1) for grid in grids]
        id_grid = ids.T
    stripes = [grid.reshape(SIDE // STRIPE, STRIPE * SIDE, heads_local, head_size) for grid in grids]
    id_stripes = id_grid.reshape(SIDE // STRIPE, STRIPE * SIDE)
    attended = lax.map(jax.checkpoint(stripe_attention), (stripes[0], stripes[1], stripes[2], id_stripes))
    total = attended.reshape(SIDE, SIDE, channels)
    total = total + position_term(grids[2][None], id_grid[None], kernel, shift)[0]
    if flip:
        total = jnp.swapaxes(total, 0, 1)
    return total.reshape(SIDE * SIDE, channels)

def layer_block(stream, ids, qkv_w, proj_w, up_w, down_w, shared, groups):
    channels = D // 2
    half_hidden = FF // 2
    gain_first = shared[0:D]
    shift_first = shared[D:2 * D]
    proj_bias = shared[2 * D:3 * D]
    gain_second = shared[3 * D:4 * D]
    shift_second = shared[4 * D:5 * D]
    down_bias = shared[5 * D:6 * D]
    inputs = low(norm_rows(stream, gain_first, shift_first))
    branch_sum = jnp.zeros_like(stream)
    for group in range(2):
        vector = groups[group]
        bias_query = vector[0:channels]
        bias_value = vector[channels:2 * channels]
        position_shift = vector[2 * channels:3 * channels]
        position_kernel = vector[3 * channels:12 * channels].reshape(9, channels)
        weight = low(qkv_w[:, group * 3 * channels:(group + 1) * 3 * channels])
        mixed = jnp.dot(low_back(inputs), weight, precision=highest)
        query = low(low_back(mixed[:, :channels] + bias_query))
        keys_part = low(low_back(mixed[:, channels:2 * channels]))
        values_part = low(low_back(mixed[:, 2 * channels:] + bias_value))
        heads = head_outputs(query, keys_part, values_part, ids, position_kernel, position_shift, group == 1)
        heads = low(low_back(heads))
        rows = low(proj_w[group * channels:(group + 1) * channels])
        branch_sum = branch_sum + low(jnp.dot(heads, rows, precision=highest))
    middle = stream + low_back(branch_sum + proj_bias)
    inputs_second = low(norm_rows(middle, gain_second, shift_second))
    feed_sum = jnp.zeros_like(stream)
    for group in range(2):
        up_bias = groups[group][12 * channels:]
        columns = low(up_w[:, group * half_hidden:(group + 1) * half_hidden])
        hidden = low_back(jnp.dot(low_back(inputs_second), columns, precision=highest) + up_bias)
        active = low(jax.nn.gelu(hidden, approximate=False))
        rows = low(down_w[group * half_hidden:(group + 1) * half_hidden])
        feed_sum = feed_sum + low(jnp.dot(active, rows, precision=highest))
    return middle + low_back(feed_sum + down_bias)

def forward_all(params, rows, ids):
    qkv_all, proj_all, up_all, down_all, shared_all, group_all = params
    stream = rows
    for layer in range(LAYERS):
        stream = layer_block(stream, ids, qkv_all[layer], proj_all[layer], up_all[layer], down_all[layer], shared_all[layer], group_all[layer])
    return stream

def muon_matrix(weight_all, grad_all, moment_all, axis, piece):
    moments = []
    masters = []
    for layer in range(LAYERS):
        moment_parts = []
        master_parts = []
        for group in range(2):
            weight = lax.slice_in_dim(weight_all[layer], group * piece, (group + 1) * piece, axis=axis)
            grad = lax.slice_in_dim(grad_all[layer], group * piece, (group + 1) * piece, axis=axis)
            moment = lax.slice_in_dim(moment_all[layer], group * piece, (group + 1) * piece, axis=axis)
            moment_new = momentum_decay * moment + grad
            ortho = newton(grad + momentum_decay * moment_new)
            step_size = matrix_rate * match_scale * math.sqrt(max(weight.shape))
            moment_parts.append(moment_new)
            master_parts.append(weight * (1.0 - matrix_rate * weight_decay) - step_size * ortho)
        moments.append(jnp.concatenate(moment_parts, axis=axis))
        masters.append(jnp.concatenate(master_parts, axis=axis))
    return (jnp.stack(moments), jnp.stack(masters))

def reference(tokens, cotangent, image_ids, qkv_weight, proj_weight, up_weight, down_weight, shared_vectors, group_vectors, qkv_moment, proj_moment, up_moment, down_moment, shared_moment, group_moment):
    params = (qkv_weight, proj_weight, up_weight, down_weight, shared_vectors, group_vectors)
    rows_all = tokens.astype(jnp.float32).reshape(CANVASES, SIDE * SIDE, D)
    backs_all = cotangent.astype(jnp.float32).reshape(CANVASES, SIDE * SIDE, D)

    def one_canvas(carry, item):
        rows, back, ids = item

        def network(weights, inputs):
            return forward_all(weights, inputs, ids)
        output, pull = jax.vjp(network, params, rows)
        grads, grad_rows = pull(back)
        return (jax.tree.map(jnp.add, carry, grads), (output.astype(jnp.bfloat16), grad_rows))
    start = jax.tree.map(jnp.zeros_like, params)
    grads, (outputs, grad_rows) = lax.scan(one_canvas, start, (rows_all, backs_all, image_ids))
    grad_qkv, grad_proj, grad_up, grad_down, grad_shared, grad_group = grads
    channels = D // 2
    half_hidden = FF // 2
    qkv_momentum, qkv_master = muon_matrix(qkv_weight, grad_qkv, qkv_moment, 1, 3 * channels)
    proj_momentum, proj_master = muon_matrix(proj_weight, grad_proj, proj_moment, 0, channels)
    up_momentum, up_master = muon_matrix(up_weight, grad_up, up_moment, 1, half_hidden)
    down_momentum, down_master = muon_matrix(down_weight, grad_down, down_moment, 0, half_hidden)
    shared_momentum = momentum_decay * shared_moment + grad_shared
    shared_master = shared_vectors - vector_rate * shared_momentum
    group_momentum = momentum_decay * group_moment + grad_group
    group_master = group_vectors - vector_rate * group_momentum
    return (outputs.reshape(TOKENS, D), grad_rows.reshape(TOKENS, D), qkv_momentum, qkv_master, proj_momentum, proj_master, up_momentum, up_master, down_momentum, down_master, shared_momentum, shared_master, group_momentum, group_master)
```

```python
import functools
import math

import jax
import jax.numpy as jnp
from jax import lax
from jax.experimental import pallas as pl
from jax.experimental.pallas import tpu as pltpu
from jax.sharding import PartitionSpec as P

HEADS = 8
STRIPE = 7
LAYERS = 2
NS_STEPS = 5

epsilon = 1e-05
coeff_first = 3.4445
coeff_second = -4.775
coeff_third = 2.0315
momentum_decay = 0.95
matrix_rate = 0.25
weight_decay = 0.1
vector_rate = 0.001
match_scale = 0.2
masked_score = -1e30

f32 = jnp.float32
bf16 = jnp.bfloat16
LOG2E = 1.4426950408889634
VMEM_LIMIT = 62 * 1024 * 1024

SIDE = 42
NS = 6
SLOT = 8
ROWS = SIDE * SLOT
KEYS = 384
WIDTH = 256
CH = 128
HALF = 512
HL = 4
HEAD = 32


def dot(a, b):
    return jnp.dot(a, b, preferred_element_type=f32)


def dot_t(a, b):
    return lax.dot_general(a, b, (((1,), (1,)), ((), ())), preferred_element_type=f32)


def dot_rows(a, b):
    return lax.dot_general(a, b, (((0,), (0,)), ((), ())), preferred_element_type=f32)


def lane_head():
    return lax.broadcasted_iota(jnp.int32, (1, CH), 1) // HEAD


def stripe_of(ref, g, s):
    if g == 0:
        block = ref[pl.ds(STRIPE * s, STRIPE)]
    else:
        block = ref[:, pl.ds(s, 1)]
    return block.reshape(ROWS, block.shape[-1])


def put_stripe(ref, g, s, value):
    if g == 0:
        ref[pl.ds(STRIPE * s, STRIPE)] = value.reshape(STRIPE, NS, SLOT, value.shape[-1])
    else:
        ref[:, pl.ds(s, 1)] = value.reshape(SIDE, 1, SLOT, value.shape[-1])


def normed(rows):
    mean = jnp.mean(rows, axis=-1, keepdims=True)
    centred = rows - mean
    spread = jnp.mean(centred * centred, axis=-1, keepdims=True)
    rstd = lax.rsqrt(spread + epsilon)
    return centred * rstd, rstd


def norm_back(grad, hat, rstd, gain):
    scaled = grad * gain
    first = jnp.mean(scaled, axis=-1, keepdims=True)
    second = jnp.mean(scaled * hat, axis=-1, keepdims=True)
    return rstd * (scaled - first - hat * second)


def tile_sum(rows):
    return jnp.sum(rows.reshape(-1, SLOT, rows.shape[-1]), axis=0)


def gelu_parts(x):
    z = jnp.abs(x)
    bell = jnp.exp2(x * x * (-0.5 * LOG2E))
    t = 1.0 / (1.0 + (0.3275911 * math.sqrt(0.5)) * z)
    poly = 0.5 * 1.061405429
    for coeff in (-1.453152027, 1.421413741, -0.284496736, 0.254829592):
        poly = poly * t + 0.5 * coeff
    tail = poly * t * bell
    phi = jnp.where(x >= 0.0, 1.0 - tail, tail)
    return x * phi, phi + x * bell * (1.0 / math.sqrt(2.0 * math.pi))


def fine_shifts(x, g):
    axis = x.ndim - 2
    one_up = pltpu.roll(x, SLOT - 1, axis)
    one_down = pltpu.roll(x, 1, axis)
    if g == 1:
        return one_up, one_down
    place = lax.broadcasted_iota(jnp.int32, (1, 1, SLOT, 1), 2)
    after = jnp.concatenate([x[:, 1:], x[:, :1]], axis=1)
    before = jnp.concatenate([x[:, -1:], x[:, :-1]], axis=1)
    up = jnp.where(place == STRIPE - 1, pltpu.roll(after, STRIPE - 1, axis), one_up)
    down = jnp.where(place == 0, pltpu.roll(before, 2, axis), one_down)
    return up, down


def coarse(x, step):
    if step == 0:
        return x
    zero = jnp.zeros_like(x[:1])
    if step > 0:
        return jnp.concatenate([x[1:], zero], axis=0)
    return jnp.concatenate([zero, x[:-1]], axis=0)


def masked_neighbours(x, ids, g):
    shape = (STRIPE, NS, SLOT, CH) if g == 0 else (SIDE, SLOT, CH)
    x = x.reshape(shape)
    up, down = fine_shifts(x, g)
    centre = ids[0].reshape(shape)
    around = {0: (x, centre), 1: (up, ids[1].reshape(shape)), -1: (down, ids[2].reshape(shape))}
    for row_step in (-1, 0, 1):
        for col_step in (-1, 0, 1):
            tap = 3 * (row_step + 1) + col_step + 1
            coarse_step, fine_step = (row_step, col_step) if g == 0 else (col_step, row_step)
            source, source_ids = around[fine_step]
            if coarse_step == 0 and fine_step == 0:
                yield tap, source.reshape(ROWS, CH)
                continue
            if coarse_step != 0:
                source = coarse(source, coarse_step)
                zero = jnp.full_like(source_ids[:1], -9.0)
                parts = [source_ids[1:], zero] if coarse_step > 0 else [zero, source_ids[:-1]]
                source_ids = jnp.concatenate(parts, axis=0)
            kept = jnp.where(source_ids == centre, source, 0.0)
            yield tap, kept.reshape(ROWS, CH)


def block_diagonal(x):
    head = lane_head()
    zero = jnp.zeros((KEYS - ROWS, CH), f32)
    parts = []
    for h in range(HL):
        parts += [jnp.where(head == h, x, 0.0), zero]
    return jnp.concatenate(parts, axis=0).astype(bf16)


def take_diagonal(x):
    head = lane_head()
    total = jnp.where(head == 0, x[0:ROWS], 0.0)
    for h in range(1, HL):
        total = jnp.where(head == h, x[h * KEYS : h * KEYS + ROWS], total)
    return total


def ids_of(idb, g, s):
    names = (0, 1, 2) if g == 0 else (0, 3, 4)
    return [stripe_of(idb.at[n], g, s) for n in names]


def fill_weights(own, wq, wqo, wp, wpo, gv, gvo, wq2, wp2, gv2, layer):
    other = 1 - own
    wq2[own] = wq[0]
    wq2[other] = wqo[0]
    wp2[own] = wp[0]
    wp2[other] = wpo[0]
    gv2[own] = gv[layer]
    gv2[other] = gvo[layer]


def forward_kernel(
    layer, own_ref, stream, wq, wqo, wp, wpo, wu, wuo, wd, wdo, sv, gv, gvo, idb, idrow,
    out, mid, qkv_s, e_s, rl_s, att_s, heads_s, active_s, dgelu_s, wq2, wp2, gv2,
):
    own = own_ref[0]
    fill_weights(own, wq, wqo, wp, wpo, gv, gvo, wq2, wp2, gv2, layer)

    def shared(index):
        return sv[layer : layer + 1, index * WIDTH : (index + 1) * WIDTH]

    for g in range(2):
        def stripe(s, carry, g=g):
            i = g * NS + s
            rows = stripe_of(stream, g, s)
            hat, _ = normed(rows)
            a1 = (hat * shared(0) + shared(1)).astype(bf16)
            mixed = dot(a1, wq2[g])
            vec = gv2[g]
            q = ((mixed[:, :CH] + vec[:, :CH]) * (HEAD ** -0.5 * LOG2E)).astype(bf16)
            k = mixed[:, CH : 2 * CH].astype(bf16)
            v = (mixed[:, 2 * CH :] + vec[:, CH : 2 * CH]).astype(bf16)
            qkv_s[i, :, 0:CH] = q
            qkv_s[i, :, CH : 2 * CH] = k
            qkv_s[i, :, 2 * CH :] = v
            ids = ids_of(idb, g, s)
            key_ids = idrow[i]
            bias = jnp.where(jnp.concatenate([ids[0]] * 3, axis=1) == key_ids, 0.0, masked_score)
            scores = dot_t(q, block_diagonal(k.astype(f32)))
            parts = []
            for h in range(HL):
                score = scores[:, h * KEYS : (h + 1) * KEYS] + bias
                top = jnp.max(score, axis=-1, keepdims=True)
                parts.append(jnp.exp2(score - top).astype(bf16))
            e = jnp.concatenate(parts, axis=1)
            e_s[i] = e
            vf = v.astype(f32)
            ones = block_diagonal(jnp.ones((ROWS, CH), f32))
            both = dot(e, jnp.concatenate([block_diagonal(vf), ones], axis=1))
            rl = 1.0 / both[:, CH:]
            att = both[:, :CH] * rl
            rl_s[i] = rl
            att_s[i] = att.astype(bf16)
            total = att + vec[:, 2 * CH : 3 * CH]
            for tap, near in masked_neighbours(vf, ids, g):
                total = total + near * vec[:, (3 + tap) * CH : (4 + tap) * CH]
            heads = total.astype(bf16)
            heads_s[i] = heads
            part = dot(heads, wp2[g]).astype(bf16).astype(f32)
            if g == 0:
                put_stripe(mid, g, s, part)
            else:
                put_stripe(mid, g, s, rows + (stripe_of(mid, g, s) + part + shared(2)))
            return carry

        lax.fori_loop(0, NS, stripe, 0)

    def block(s, carry):
        rows = stripe_of(mid, 0, s)
        hat, _ = normed(rows)
        a2 = (hat * shared(3) + shared(4)).astype(bf16)
        parts = []
        for slot, (up, down, vec) in enumerate(((wu, wd, gv), (wuo, wdo, gvo))):
            hidden = dot(a2, up[0]) + vec[layer][:, 12 * CH :]
            active, slope = gelu_parts(hidden)
            active = active.astype(bf16)
            if slot == 0:
                active_s[s] = active
            dgelu_s[slot, s] = slope.astype(bf16)
            parts.append(dot(active, down[0]).astype(bf16).astype(f32))
        put_stripe(out, 0, s, rows + ((parts[0] + parts[1]) + shared(5)))
        return carry

    lax.fori_loop(0, NS, block, 0)


def backward_kernel(
    layer, own_ref, grad, stream, mid, qkv_s, e_s, rl_s, att_s, heads_s, active_s, dgelu_s,
    wq, wqo, wp, wpo, wu, wuo, wd, wdo, sv, gv, gvo, idb,
    grad_in, big, svec, gvec,
    wq2, wp2, gv2, gmid, gb, da1, a1_own, dqkv_own, gb_own, a2_s, gh_s, gm_s, acc_s, acc_b1, acc_g,
):
    own = own_ref[0]
    fill_weights(own, wq, wqo, wp, wpo, gv, gvo, wq2, wp2, gv2, layer)
    acc_s[...] = jnp.zeros_like(acc_s)
    acc_b1[...] = jnp.zeros_like(acc_b1)
    acc_g[...] = jnp.zeros_like(acc_g)

    def shared(index):
        return sv[layer : layer + 1, index * WIDTH : (index + 1) * WIDTH]

    def block(s, carry):
        rows = stripe_of(grad, 0, s)
        gm = rows.astype(bf16)
        gm_s[s] = gm
        acc_s[5] += tile_sum(gm.astype(f32))
        hat, rstd = normed(stripe_of(mid, 0, s))
        a2_s[s] = (hat * shared(3) + shared(4)).astype(bf16)
        parts = []
        for slot, (up, down) in enumerate(((wu, wd), (wuo, wdo))):
            gh = (dot_t(gm, down[0]) * dgelu_s[slot, s].astype(f32)).astype(bf16)
            if slot == 0:
                gh_s[s] = gh
                acc_b1[...] += tile_sum(gh.astype(f32))
            parts.append(dot_t(gh, up[0]).astype(bf16).astype(f32))
        da2 = parts[0] + parts[1]
        acc_s[3] += tile_sum(da2 * hat)
        acc_s[4] += tile_sum(da2)
        new = rows + norm_back(da2, hat, rstd, shared(3))
        put_stripe(gmid, 0, s, new)
        low = new.astype(bf16).astype(f32)
        put_stripe(gb, 0, s, low)
        acc_s[2] += tile_sum(low)
        return carry

    lax.fori_loop(0, NS, block, 0)

    lanes = lax.broadcasted_iota(jnp.int32, (CH, CH), 1)
    rows_of = lax.broadcasted_iota(jnp.int32, (CH, CH), 0)
    gather = jnp.where((lanes % HEAD == rows_of // HEAD) & (lanes < 3 * HEAD), 1.0, 0.0).astype(bf16)
    gather = jnp.concatenate([gather, gather], axis=0)

    for g in range(2):
        def stripe(s, carry, g=g):
            i = g * NS + s
            hat, _ = normed(stripe_of(stream, g, s))
            a1 = (hat * shared(0) + shared(1)).astype(bf16)
            gbs = stripe_of(gb, g, s).astype(bf16)
            vec = gv2[g]
            d_out = dot_t(gbs, wp2[g]).astype(bf16).astype(f32)
            q = qkv_s[i, :, 0:CH]
            k = qkv_s[i, :, CH : 2 * CH]
            v = qkv_s[i, :, 2 * CH :]
            vf = v.astype(f32)
            scaled = (d_out * rl_s[i]).astype(bf16)
            prod = scaled.astype(f32) * att_s[i].astype(f32)
            prod_high = prod.astype(bf16)
            prod_low = (prod - prod_high.astype(f32)).astype(bf16)
            centre = dot(jnp.concatenate([prod_high, prod_low], axis=1), gather)
            first = centre.astype(bf16).astype(f32)
            rest = centre - first
            second = rest.astype(bf16).astype(f32)
            lane = lax.broadcasted_iota(jnp.int32, (1, CH), 1)
            pieces = jnp.where(lane < HEAD, first, jnp.where(lane < 2 * HEAD, second, rest - second))
            left = jnp.concatenate([scaled, (-pieces).astype(bf16)], axis=1)
            marks = []
            for h in range(HL):
                mark = jnp.where((lane % HEAD == h) & (lane < 3 * HEAD), 1.0, 0.0)
                marks.append(jnp.broadcast_to(mark, (KEYS, CH)))
            marks = jnp.concatenate(marks, axis=0).astype(bf16)
            right = jnp.concatenate([block_diagonal(vf), marks], axis=1)
            e = e_s[i]
            ds = (e.astype(f32) * dot_t(left, right)).astype(bf16)
            dq = (dot(ds, block_diagonal(k.astype(f32))) * HEAD ** -0.5).astype(bf16)
            dk = (take_diagonal(dot_rows(ds, q)) * (1.0 / LOG2E)).astype(bf16)
            dv = take_diagonal(dot_rows(e, scaled))
            ids = ids_of(idb, g, s)
            for tap, near in masked_neighbours(d_out, ids, g):
                mirror = 8 - tap
                dv = dv + near * vec[:, (3 + mirror) * CH : (4 + mirror) * CH]
                acc_g[g, 3 + mirror] += tile_sum(near * vf)
            dv = dv.astype(bf16)
            acc_g[g, 0] += tile_sum(dq.astype(f32))
            acc_g[g, 1] += tile_sum(dv.astype(f32))
            acc_g[g, 2] += tile_sum(d_out)
            dqkv = jnp.concatenate([dq, dk, dv], axis=1)
            part = dot_t(dqkv, wq2[g]).astype(bf16).astype(f32)
            if g == 0:
                put_stripe(da1, g, s, part)
            else:
                put_stripe(da1, g, s, stripe_of(da1, g, s) + part)

            @pl.when(own == g)
            def _():
                a1_own[s] = a1
                dqkv_own[s] = dqkv
                gb_own[s] = gbs

            return carry

        lax.fori_loop(0, NS, stripe, 0)

    def last(s, carry):
        hat, rstd = normed(stripe_of(stream, 0, s))
        da = stripe_of(da1, 0, s)
        acc_s[0] += tile_sum(da * hat)
        acc_s[1] += tile_sum(da)
        put_stripe(grad_in, 0, s, stripe_of(gmid, 0, s) + norm_back(da, hat, rstd, shared(0)))
        return carry

    lax.fori_loop(0, NS, last, 0)

    def flat(ref):
        return ref[...].reshape(NS * ROWS, ref.shape[-1])

    heads = heads_s[pl.ds(own * NS, NS)].reshape(NS * ROWS, CH)
    big[:, 0:384] = dot_rows(flat(a1_own), flat(dqkv_own)).astype(bf16)
    big[:, 384:512] = dot_rows(flat(gb_own), heads).astype(bf16)
    big[:, 512:1024] = dot_rows(flat(a2_s), flat(gh_s)).astype(bf16)
    big[:, 1024:1536] = dot_rows(flat(gm_s), flat(active_s)).astype(bf16)
    for index in range(6):
        svec[:, index * WIDTH : (index + 1) * WIDTH] = jnp.sum(acc_s[index], axis=0, keepdims=True)
    for index in range(12):
        gvec[:, index * CH : (index + 1) * CH] = jnp.sum(acc_g[own, index], axis=0, keepdims=True)
    gvec[:, 12 * CH :] = jnp.sum(acc_b1[...], axis=0, keepdims=True)


def sds(shape, dtype):
    return jax.ShapeDtypeStruct(shape, dtype)


CANVAS = (SIDE, NS, SLOT, WIDTH)
SAVED = [
    sds(CANVAS, f32),
    sds((2 * NS, ROWS, 3 * CH), bf16),
    sds((2 * NS, ROWS, HL * KEYS), bf16),
    sds((2 * NS, ROWS, CH), f32),
    sds((2 * NS, ROWS, CH), bf16),
    sds((2 * NS, ROWS, CH), bf16),
    sds((NS, ROWS, HALF), bf16),
    sds((2, NS, ROWS, HALF), bf16),
]
PAIR_SCRATCH = [
    pltpu.VMEM((2, WIDTH, 3 * CH), bf16),
    pltpu.VMEM((2, CH, WIDTH), bf16),
    pltpu.VMEM((2, 1, 16 * CH), f32),
]


def specs(n):
    return [pl.BlockSpec(memory_space=pltpu.SMEM)] + [pl.BlockSpec(memory_space=pltpu.VMEM)] * n


def run_forward(layer, own, args):
    return pl.pallas_call(
        functools.partial(forward_kernel, layer),
        out_shape=[sds(CANVAS, f32)] + SAVED,
        in_specs=specs(len(args)),
        out_specs=[pl.BlockSpec(memory_space=pltpu.VMEM)] * (1 + len(SAVED)),
        scratch_shapes=PAIR_SCRATCH,
        compiler_params=pltpu.CompilerParams(vmem_limit_bytes=VMEM_LIMIT),
        cost_estimate=pl.CostEstimate(flops=8 * 10**9, bytes_accessed=40 * 10**6, transcendentals=0),
        name=f"layer{layer}_forward",
    )(own, *args)


def run_backward(layer, own, args):
    return pl.pallas_call(
        functools.partial(backward_kernel, layer),
        out_shape=[
            sds(CANVAS, f32),
            sds((WIDTH, 12 * CH), bf16),
            sds((1, 6 * WIDTH), f32),
            sds((1, 16 * CH), f32),
        ],
        in_specs=specs(len(args)),
        out_specs=[pl.BlockSpec(memory_space=pltpu.VMEM)] * 4,
        scratch_shapes=PAIR_SCRATCH
        + [
            pltpu.VMEM(CANVAS, f32),
            pltpu.VMEM(CANVAS, f32),
            pltpu.VMEM(CANVAS, f32),
            pltpu.VMEM((NS, ROWS, WIDTH), bf16),
            pltpu.VMEM((NS, ROWS, 3 * CH), bf16),
            pltpu.VMEM((NS, ROWS, WIDTH), bf16),
            pltpu.VMEM((NS, ROWS, WIDTH), bf16),
            pltpu.VMEM((NS, ROWS, HALF), bf16),
            pltpu.VMEM((NS, ROWS, WIDTH), bf16),
            pltpu.VMEM((6, SLOT, WIDTH), f32),
            pltpu.VMEM((SLOT, HALF), f32),
            pltpu.VMEM((2, 12, SLOT, CH), f32),
        ],
        compiler_params=pltpu.CompilerParams(vmem_limit_bytes=VMEM_LIMIT),
        cost_estimate=pl.CostEstimate(flops=16 * 10**9, bytes_accessed=40 * 10**6, transcendentals=0),
        name=f"layer{layer}_backward",
    )(own, *args)


def split_dot(a, b, dims):
    a_high, b_high = a.astype(bf16), b.astype(bf16)
    a_low = (a - a_high.astype(f32)).astype(bf16)
    b_low = (b - b_high.astype(f32)).astype(bf16)

    def one(x, y):
        return lax.dot_general(x, y, (dims, ((), ())), preferred_element_type=f32)

    return one(a_high, b_high) + (one(a_high, b_low) + one(a_low, b_high))


def newton_kernel(spans, big, out):
    works = []
    for (start, stop), turned in spans:
        work = big[:, start:stop].astype(f32)
        if turned:
            work = work.T
        works.append(work / (jnp.sqrt(jnp.sum(work * work)) + 1e-07))
    for _ in range(NS_STEPS):
        grams = [split_dot(work, work, ((1,), (1,))) for work in works]
        blends = [
            coeff_second * gram + coeff_third * split_dot(gram, gram, ((1,), (0,))) for gram in grams
        ]
        works = [
            coeff_first * work + split_dot(blend, work, ((1,), (0,)))
            for work, blend in zip(works, blends)
        ]
    for ((start, stop), turned), work in zip(spans, works):
        out[:, start:stop] = work.T if turned else work


def run_newton(big, spans):
    return pl.pallas_call(
        functools.partial(newton_kernel, spans),
        out_shape=sds(big.shape, f32),
        in_specs=[pl.BlockSpec(memory_space=pltpu.VMEM)],
        out_specs=pl.BlockSpec(memory_space=pltpu.VMEM),
        compiler_params=pltpu.CompilerParams(vmem_limit_bytes=VMEM_LIMIT),
        cost_estimate=pl.CostEstimate(flops=7 * 10**9, bytes_accessed=3 * 10**6, transcendentals=0),
        name="newton",
    )(big)


def swap(x, axis, bit):
    n = lax.axis_size(axis)
    return lax.ppermute(x, axis, [(i, i ^ bit) for i in range(n)])


def scatter_sum(chunks):
    n = chunks.shape[0]
    me = lax.axis_index("dp")
    bit = 1
    while bit < n:
        halves = chunks.reshape((chunks.shape[0] // 2, 2) + chunks.shape[1:])
        side = (me // bit) % 2
        send = lax.dynamic_index_in_dim(halves, 1 - side, 1, False)
        keep = lax.dynamic_index_in_dim(halves, side, 1, False)
        got = swap(send, "dp", bit)
        bit *= 2
        total = keep.astype(f32) + got.astype(f32)
        chunks = total.astype(bf16) if bit < n else total
    return chunks[0]


def gather_rows(mine):
    n = lax.axis_size("dp")
    me = lax.axis_index("dp")
    held = mine[None]
    bit = n // 2
    while bit >= 1:
        side = (me // bit) % 2
        got = swap(held, "dp", bit)
        first = jnp.where(side == 0, held, got)
        second = jnp.where(side == 0, got, held)
        held = jnp.stack([first, second], axis=1).reshape((-1,) + mine.shape)
        bit //= 2
    return held.reshape((-1,) + mine.shape[1:])


def padded(rows):
    grid = rows.astype(f32).reshape(SIDE, NS, STRIPE, WIDTH)
    return jnp.pad(grid, ((0, 0), (0, 0), (0, 1), (0, 0)))


def unpadded(grid):
    return grid[:, :, :STRIPE].reshape(SIDE * SIDE, WIDTH)


def local(
    tokens, cotangent, image_ids, qkv_weight, proj_weight, up_weight, down_weight, shared_vectors, group_vectors,
    qkv_moment, proj_moment, up_moment, down_moment, shared_moment, group_moment,
):
    own = lax.axis_index("group").astype(jnp.int32).reshape(1)
    devices = lax.axis_size("dp")
    index = lax.axis_index("dp")

    masters = (qkv_weight, proj_weight, up_weight, down_weight)
    weights = []
    for layer in range(LAYERS):
        pairs = []
        for master in masters:
            mine = master[layer : layer + 1].astype(bf16)
            pairs += [mine, swap(mine, "group", 1)]
        weights.append(pairs)
    other_vectors = swap(group_vectors, "group", 1)

    ids = image_ids[0].astype(f32)
    edge = jnp.full((SIDE, 1), -3.0, f32)
    right = jnp.concatenate([ids[:, 1:], edge], axis=1)
    left = jnp.concatenate([edge, ids[:, :-1]], axis=1)
    column = jnp.arange(SIDE) % STRIPE
    inner_right = jnp.where(column == STRIPE - 1, -3.0, right)
    inner_left = jnp.where(column == 0, -3.0, left)

    def cells(grid, fill):
        grid = grid.reshape(SIDE, NS, STRIPE)
        return jnp.pad(grid, ((0, 0), (0, 0), (0, 1)), constant_values=fill)

    centre = cells(ids, -1.0)
    grids = jnp.stack([centre] + [cells(grid, -3.0) for grid in (right, left, inner_right, inner_left)])
    idb = jnp.broadcast_to(grids[..., None], grids.shape + (CH,))
    rows_h = centre.reshape(NS, ROWS)
    rows_v = jnp.swapaxes(centre, 0, 1).reshape(NS, ROWS)
    idrow = jnp.concatenate([rows_h, rows_v], axis=0)
    idrow = jnp.pad(idrow, ((0, 0), (0, KEYS - ROWS)), constant_values=-5.0)[:, None, :]

    vectors = (shared_vectors, group_vectors, other_vectors)
    stream = padded(tokens)
    grad = padded(cotangent)
    streams, saved = [stream], []
    for layer in range(LAYERS):
        result = run_forward(layer, own, (streams[-1], *weights[layer], *vectors, idb, idrow))
        streams.append(result[0])
        saved.append(result[1:])
    outputs = unpadded(streams[-1]).astype(bf16)
    bigs, svecs, gvecs = [None] * LAYERS, [None] * LAYERS, [None] * LAYERS
    for layer in reversed(range(LAYERS)):
        grad, bigs[layer], svecs[layer], gvecs[layer] = run_backward(
            layer, own, (grad, streams[layer], *saved[layer], *weights[layer], *vectors, idb)
        )
    input_grad = unpadded(grad)

    rows_each = WIDTH // devices
    length_shared = shared_moment.shape[1]
    length_group = group_moment.shape[2]
    out = [[] for _ in range(12)]
    for layer in range(LAYERS):
        pack = jnp.concatenate(
            [svecs[layer].reshape(devices, length_shared), gvecs[layer].reshape(devices, length_group)], axis=1
        ).astype(bf16)
        width = 2 * CH
        pack = jnp.pad(pack, ((0, 0), (0, width - pack.shape[1])))[:, None, :]
        pack = jnp.pad(pack, ((0, 0), (0, rows_each - 1), (0, 0)))
        chunks = jnp.concatenate([bigs[layer].reshape(devices, rows_each, 12 * CH), pack], axis=2)
        total = scatter_sum(chunks)
        matrix = total[:, : 12 * CH]
        moment = jnp.concatenate(
            [qkv_moment[layer], proj_moment[layer].T, up_moment[layer], down_moment[layer].T], axis=1
        )
        moment_new = momentum_decay * moment + matrix
        whole = gather_rows((matrix + momentum_decay * moment_new).astype(bf16))
        ortho = run_newton(
            whole,
            (((0, 384), False), ((384, 512), True), ((512, 1024), False), ((1024, 1536), False)),
        )
        own_rows = lax.dynamic_slice_in_dim(ortho, index * rows_each, rows_each, 0)
        spans = ((0, 384, False), (384, 512, True), (512, 1024, False), (1024, 1536, True))
        for which, (start, stop, turned) in enumerate(spans):
            fresh = moment_new[:, start:stop]
            step = own_rows[:, start:stop]
            master = masters[which][layer]
            if turned:
                fresh, step = fresh.T, step.T
            old = lax.dynamic_slice_in_dim(master, index * rows_each, rows_each, 1 if turned else 0)
            size = matrix_rate * match_scale * math.sqrt(max(master.shape))
            out[2 * which].append(fresh)
            out[2 * which + 1].append(old * (1.0 - matrix_rate * weight_decay) - size * step)
        grad_shared = total[0, 12 * CH : 12 * CH + length_shared]
        grad_group = total[0, 12 * CH + length_shared : 12 * CH + length_shared + length_group][None]
        moment_shared = momentum_decay * shared_moment[layer] + grad_shared
        moment_group = momentum_decay * group_moment[layer] + grad_group
        old_shared = lax.dynamic_slice_in_dim(shared_vectors[layer], index * length_shared, length_shared, 0)
        old_group = lax.dynamic_slice_in_dim(group_vectors[layer], index * length_group, length_group, 1)
        out[8].append(moment_shared)
        out[9].append(old_shared - vector_rate * moment_shared)
        out[10].append(moment_group)
        out[11].append(old_group - vector_rate * moment_group)
    return (outputs, input_grad, *[jnp.stack(parts) for parts in out])


def solution(mesh):
    return jax.shard_map(
        local,
        mesh=mesh,
        in_specs=(
            P("dp", None),
            P("dp", None),
            P("dp", None, None),
            P(None, None, "group"),
            P(None, "group", None),
            P(None, None, "group"),
            P(None, "group", None),
            P(),
            P(None, "group", None),
            P(None, "dp", "group"),
            P(None, "group", "dp"),
            P(None, "dp", "group"),
            P(None, "group", "dp"),
            P(None, "dp"),
            P(None, "group", "dp"),
        ),
        out_specs=(
            P("dp", None),
            P("dp", None),
            P(None, "dp", "group"),
            P(None, "dp", "group"),
            P(None, "group", "dp"),
            P(None, "group", "dp"),
            P(None, "dp", "group"),
            P(None, "dp", "group"),
            P(None, "group", "dp"),
            P(None, "group", "dp"),
            P(None, "dp"),
            P(None, "dp"),
            P(None, "group", "dp"),
            P(None, "group", "dp"),
        ),
        check_vma=False,
    )
```

```python
import functools
import math

import jax
import jax.numpy as jnp
from jax import lax
from jax.experimental import pallas as pl
from jax.experimental.pallas import tpu as pltpu
from jax.sharding import PartitionSpec as P

HEADS = 8
STRIPE = 7
LAYERS = 2
NS_STEPS = 5

epsilon = 1e-05
coeff_first = 3.4445
coeff_second = -4.775
coeff_third = 2.0315
momentum_decay = 0.95
matrix_rate = 0.25
weight_decay = 0.1
vector_rate = 0.001
match_scale = 0.2
masked_score = -1e30

f32 = jnp.float32
bf16 = jnp.bfloat16
LOG2E = 1.4426950408889634
MIB = 1024 * 1024
SMALL, LARGE = 32, 62

SIDE = 42
NS = 6
GANG = 3
SLOT = 8
ROWS = SIDE * SLOT
KEPT = 208
TOKENS = 320
KEYS = 5 * 256
WIDTH = 256
CH = 128
HALF = 512
HL = 4
HEAD = 32


def dot(a, b):
    return jnp.dot(a, b, preferred_element_type=f32)


def dot_t(a, b):
    return lax.dot_general(a, b, (((1,), (1,)), ((), ())), preferred_element_type=f32)


def dot_rows(a, b):
    return lax.dot_general(a, b, (((0,), (0,)), ((), ())), preferred_element_type=f32)


def lane_head():
    return lax.broadcasted_iota(jnp.int32, (1, CH), 1) // HEAD


def stripe_of(ref, g, s):
    if g == 0:
        block = ref[pl.ds(STRIPE * s, STRIPE)]
    else:
        block = ref[:, pl.ds(s, 1)]
    return block.reshape(ROWS, block.shape[-1])


def put_stripe(ref, g, s, value):
    if g == 0:
        ref[pl.ds(STRIPE * s, STRIPE)] = value.reshape(STRIPE, NS, SLOT, value.shape[-1])
    else:
        ref[:, pl.ds(s, 1)] = value.reshape(SIDE, 1, SLOT, value.shape[-1])


def normed(rows):
    mean = jnp.mean(rows, axis=-1, keepdims=True)
    centred = rows - mean
    spread = jnp.mean(centred * centred, axis=-1, keepdims=True)
    rstd = lax.rsqrt(spread + epsilon)
    return centred * rstd, rstd


def norm_back(grad, hat, rstd, gain):
    scaled = grad * gain
    first = jnp.mean(scaled, axis=-1, keepdims=True)
    second = jnp.mean(scaled * hat, axis=-1, keepdims=True)
    return rstd * (scaled - first - hat * second)


def tile_sum(rows):
    return jnp.sum(rows.reshape(-1, SLOT, rows.shape[-1]), axis=0)


def gelu_parts(x):
    z = jnp.abs(x)
    bell = jnp.exp2(x * x * (-0.5 * LOG2E))
    t = 1.0 / (1.0 + (0.3275911 * math.sqrt(0.5)) * z)
    poly = 0.5 * 1.061405429
    for coeff in (-1.453152027, 1.421413741, -0.284496736, 0.254829592):
        poly = poly * t + 0.5 * coeff
    tail = poly * t * bell
    phi = jnp.where(x >= 0.0, 1.0 - tail, tail)
    return x * phi, phi + x * bell * (1.0 / math.sqrt(2.0 * math.pi))


def places(ndim):
    shape = (1,) * (ndim - 2) + (SLOT, 1)
    return lax.broadcasted_iota(jnp.int32, shape, ndim - 2)


def fine_shifts(x, g, edge):
    axis = x.ndim - 2
    place = places(x.ndim)
    up = pltpu.roll(x, SLOT - 1, axis)
    down = pltpu.roll(x, 1, axis)
    if g == 0:
        end = x[:, :1] if edge is None else jnp.full_like(x[:, :1], edge)
        after = jnp.concatenate([x[:, 1:], end], axis=1)
        before = jnp.concatenate([end, x[:, :-1]], axis=1)
        up = jnp.where(place == STRIPE - 1, pltpu.roll(after, STRIPE - 1, axis), up)
        down = jnp.where(place == 0, pltpu.roll(before, 2, axis), down)
        if edge is not None:
            up = jnp.where(place == STRIPE, edge, up)
            down = jnp.where(place == STRIPE, edge, down)
    elif edge is not None:
        up = jnp.where(place >= STRIPE - 1, edge, up)
        down = jnp.where((place == 0) | (place == STRIPE), edge, down)
    return up, down


def coarse(x, step, fill):
    if step == 0:
        return x
    end = jnp.full_like(x[:1], fill)
    if step > 0:
        return jnp.concatenate([x[1:], end], axis=0)
    return jnp.concatenate([end, x[:-1]], axis=0)


def masked_neighbours(x, ids, g):
    shape = (STRIPE, NS, SLOT, CH) if g == 0 else (SIDE, SLOT, CH)
    x = x.reshape(shape)
    centre = ids.reshape(shape)
    up, down = fine_shifts(x, g, None)
    up_ids, down_ids = fine_shifts(centre, g, -3.0)
    around = {0: (x, centre), 1: (up, up_ids), -1: (down, down_ids)}
    for row_step in (-1, 0, 1):
        for col_step in (-1, 0, 1):
            tap = 3 * (row_step + 1) + col_step + 1
            coarse_step, fine_step = (row_step, col_step) if g == 0 else (col_step, row_step)
            source, source_ids = around[fine_step]
            if coarse_step == 0 and fine_step == 0:
                yield tap, source.reshape(ROWS, CH)
                continue
            source = coarse(source, coarse_step, 0.0)
            source_ids = coarse(source_ids, coarse_step, -9.0)
            yield tap, jnp.where(source_ids == centre, source, 0.0).reshape(ROWS, CH)


def compact(x):
    width = x.shape[1]
    tiles = x[KEPT:].reshape(2, SLOT, SLOT, width)
    place = lax.broadcasted_iota(jnp.int32, (1, SLOT, 1), 1)
    parts = []
    for j in range(STRIPE):
        first, second = tiles[:, j], pltpu.roll(tiles[:, j + 1], STRIPE - j, 1)
        if j:
            first = pltpu.roll(first, SLOT - j, 1)
        parts.append(jnp.where(place < STRIPE - j, first, second))
    return jnp.concatenate([x[:KEPT], jnp.stack(parts, axis=1).reshape(TOKENS - KEPT, width)], axis=0)


def expand(x):
    width = x.shape[1]
    tiles = x[KEPT:].reshape(2, STRIPE, SLOT, width)
    place = lax.broadcasted_iota(jnp.int32, (1, SLOT, 1), 1)
    parts = [tiles[:, 0]]
    for t in range(1, STRIPE):
        both = pltpu.roll(tiles[:, t - 1], t, 1), pltpu.roll(tiles[:, t], t, 1)
        parts.append(jnp.where(place < t, *both))
    parts.append(pltpu.roll(tiles[:, STRIPE - 1], STRIPE, 1))
    parts = [jnp.where(place < STRIPE, part, 0.0) for part in parts]
    return jnp.concatenate([x[:KEPT], jnp.stack(parts, axis=1).reshape(ROWS - KEPT, width)], axis=0)


WIDE, TAIL, PAIR = 256, 64, 640


def by_heads(pieces):
    parts = []
    for h in range(0, HL, 2):
        (first, last), (other_first, other_last) = pieces(h), pieces(h + 1)
        parts += [first, last, other_last, other_first]
    return jnp.concatenate(parts, axis=0)


def block_diagonal(x):
    head = lane_head()

    def pieces(h):
        own = x * jnp.where(head == h, 1.0, 0.0).astype(bf16)
        return own[:WIDE], own[WIDE:]

    return by_heads(pieces)


def lane_marks(pick):
    lane = lax.broadcasted_iota(jnp.int32, (1, CH), 1)

    def pieces(h):
        mark = jnp.where(pick(lane, h), 1.0, 0.0).astype(bf16)
        return jnp.broadcast_to(mark, (WIDE, CH)), jnp.broadcast_to(mark, (TAIL, CH))

    return by_heads(pieces)


def gather_heads(x):
    rows = []
    for h in range(HL):
        own = x[h * HEAD : (h + 1) * HEAD, (h // 2) * PAIR : (h // 2 + 1) * PAIR]
        if h % 2 == 0:
            rows.append(own[:, 0 : WIDE + CH])
        else:
            last = pltpu.roll(own[:, WIDE : WIDE + CH], TAIL, 1)
            rows.append(jnp.concatenate([own[:, WIDE + CH :], last], axis=1))
    return jnp.concatenate(rows, axis=0).T[0:TOKENS]


def masked_softmax(scores, bias):
    left = lax.broadcasted_iota(jnp.int32, (1, CH), 1) < TAIL
    parts = []
    for h in range(0, HL, 2):
        own = [scores[:, (h // 2) * PAIR + n * CH : (h // 2) * PAIR + (n + 1) * CH] for n in range(5)]
        own = [x + bias[n] for x, n in zip(own, (0, 1, 2, 0, 1))]
        lowest = jnp.finfo(f32).min
        top = jnp.maximum(jnp.maximum(own[0], own[1]), jnp.where(left, own[2], lowest))
        other = jnp.maximum(jnp.maximum(own[3], own[4]), jnp.where(left, lowest, own[2]))
        top = jnp.max(top, axis=-1, keepdims=True)
        other = jnp.max(other, axis=-1, keepdims=True)
        tops = (top, top, jnp.where(left, top, other), other, other)
        parts += [jnp.exp2(x - y).astype(bf16) for x, y in zip(own, tops)]
    return jnp.concatenate(parts, axis=1)


def spread_ids(ids_t, idc):
    for r in range(SIDE):
        column = jnp.broadcast_to(ids_t[:, r : r + 1], (NS * SLOT, CH))
        idc[r] = column.reshape(NS, SLOT, CH)


def spread_rows(source, target):
    place = lax.broadcasted_iota(jnp.int32, (SLOT, 1), 0)
    for r in range(SIDE):
        for column in range(NS):
            tile = source[pl.ds(SIDE * r + STRIPE * column, SLOT)]
            target[r, column] = jnp.where(place < STRIPE, tile, 0.0)


def pack_rows(source, target):
    for r in range(SIDE):
        for column in range(NS):
            start = SIDE * r + STRIPE * column
            if start + SLOT <= SIDE * SIDE:
                target[pl.ds(start, SLOT)] = source[r, column]
            else:
                target[pl.ds(start, STRIPE)] = source[r, column, 0:STRIPE]


def attend(g, rows, ids, weights, vec, gain, shift):
    hat, _ = normed(rows)
    a1 = (hat * gain + shift).astype(bf16)
    mixed = dot(a1, weights)
    value = mixed[:, 2 * CH :] + vec[:, CH : 2 * CH]
    query = (mixed[:, :CH] + vec[:, :CH]) * (HEAD ** -0.5 * LOG2E)
    qkv = compact(jnp.concatenate([query, mixed[:, CH : 2 * CH], value], axis=1)).astype(bf16)
    q, k, v = qkv[:, :CH], qkv[:, CH : 2 * CH], qkv[:, 2 * CH :]
    ids_c = compact(ids)
    key_ids = jnp.concatenate([ids_c, jnp.full((3 * CH - TOKENS, CH), -5.0, f32)], axis=0).T[0:1]
    left = lax.broadcasted_iota(jnp.int32, (1, CH), 1) < TAIL
    last = key_ids[:, 2 * CH :]
    last = jnp.where(left, last, pltpu.roll(last, TAIL, 1))
    bias = [
        jnp.where(ids_c == part, 0.0, masked_score) for part in (key_ids[:, :CH], key_ids[:, CH : 2 * CH], last)
    ]
    e = masked_softmax(dot_t(q, block_diagonal(k)), bias)
    ones = lane_marks(lambda lane, h: lane // HEAD == h)
    both = dot(e, jnp.concatenate([block_diagonal(v), ones], axis=1))
    rl = 1.0 / both[:, CH:]
    att = both[:, :CH] * rl
    total = expand(att) + vec[:, 2 * CH : 3 * CH]
    for tap, near in masked_neighbours(value.astype(bf16).astype(f32), ids, g):
        total = total + near * vec[:, (3 + tap) * CH : (4 + tap) * CH]
    return a1, qkv, e, rl, att.astype(bf16), total.astype(bf16)


def attend_back(g, gbs, ids, weights, proj, vec, qkv, e, rl, att, add):
    d_out = dot_t(gbs, proj).astype(bf16).astype(f32)
    q, k, v = qkv[:, 0:CH], qkv[:, CH : 2 * CH], qkv[:, 2 * CH :]
    scaled = (compact(d_out) * rl).astype(bf16)
    prod = scaled.astype(f32) * att.astype(f32)
    prod_high = prod.astype(bf16)
    prod_low = (prod - prod_high.astype(f32)).astype(bf16)
    lanes = lax.broadcasted_iota(jnp.int32, (CH, CH), 1)
    rows_of = lax.broadcasted_iota(jnp.int32, (CH, CH), 0)
    gather = jnp.where((lanes % HEAD == rows_of // HEAD) & (lanes < 3 * HEAD), 1.0, 0.0).astype(bf16)
    centre = dot(
        jnp.concatenate([prod_high, prod_low], axis=1), jnp.concatenate([gather, gather], axis=0)
    )
    first = centre.astype(bf16).astype(f32)
    rest = centre - first
    second = rest.astype(bf16).astype(f32)
    lane = lax.broadcasted_iota(jnp.int32, (1, CH), 1)
    pieces = jnp.where(lane < HEAD, first, jnp.where(lane < 2 * HEAD, second, rest - second))
    left = jnp.concatenate([scaled, (-pieces).astype(bf16)], axis=1)
    marks = lane_marks(lambda lane, h: (lane % HEAD == h) & (lane < 3 * HEAD))
    right = jnp.concatenate([block_diagonal(v), marks], axis=1)
    ds = (e.astype(f32) * dot_t(left, right)).astype(bf16)
    dq = dot(ds, block_diagonal(k)) * HEAD ** -0.5
    dk = gather_heads(dot_rows(q, ds)) * (1.0 / LOG2E)
    dv = gather_heads(dot_rows(scaled, e))
    grads = expand(jnp.concatenate([dq, dk, dv], axis=1))
    vf = expand(v.astype(f32))
    dv = grads[:, 2 * CH :]
    for tap, near in masked_neighbours(d_out, ids, g):
        mirror = 8 - tap
        dv = dv + near * vec[:, (3 + mirror) * CH : (4 + mirror) * CH]
        if add is not None:
            add(3 + mirror, tile_sum(near * vf))
    dq, dk, dv = grads[:, :CH].astype(bf16), grads[:, CH : 2 * CH].astype(bf16), dv.astype(bf16)
    if add is not None:
        add(0, tile_sum(dq.astype(f32)))
        add(1, tile_sum(dv.astype(f32)))
        add(2, tile_sum(d_out))
    dqkv = jnp.concatenate([dq, dk, dv], axis=1)
    return dqkv, dot_t(dqkv, weights).astype(bf16).astype(f32)


def qkv_of(buffer):
    return buffer[:, 0 : 3 * CH]


def proj_of(buffer):
    return jnp.concatenate([buffer[0:CH, 3 * CH : 4 * CH], buffer[CH : 2 * CH, 3 * CH : 4 * CH]], axis=1)


def up_of(buffer, start):
    return buffer[:, start : start + HALF]


def down_of(buffer, start):
    return jnp.concatenate(
        [buffer[:, start + HALF : start + HALF + WIDTH], buffer[:, start + HALF + WIDTH : start + 2 * HALF]], axis=0
    )


def assemble(whole, near, far, core):
    half = WIDTH // 2
    whole[pl.ds(core * half, half)] = near[...]
    whole[pl.ds((1 - core) * half, half)] = far[...]


def shared_of(sv, layer, index):
    return sv[layer : layer + 1, index * WIDTH : (index + 1) * WIDTH]


def mlp_forward(rows, sv, layer, pairs):
    hat, _ = normed(rows)
    a2 = (hat * shared_of(sv, layer, 3) + shared_of(sv, layer, 4)).astype(bf16)
    parts, kept, slopes = [], [], []
    for up, down, bias in pairs:
        active, slope = gelu_parts(dot(a2, up) + bias)
        active = active.astype(bf16)
        kept.append(active)
        slopes.append(slope.astype(bf16))
        parts.append(dot(active, down).astype(bf16).astype(f32))
    return rows + ((parts[0] + parts[1]) + shared_of(sv, layer, 5)), kept[0], slopes


def mlp_backward(rows, mid, slopes, sv, layer, pairs):
    gm = rows.astype(bf16)
    hat, rstd = normed(mid)
    a2 = (hat * shared_of(sv, layer, 3) + shared_of(sv, layer, 4)).astype(bf16)
    parts, hidden = [], []
    for (up, down, _), slope in zip(pairs, slopes):
        gh = (dot_t(gm, down) * slope.astype(f32)).astype(bf16)
        hidden.append(gh)
        parts.append(dot_t(gh, up).astype(bf16).astype(f32))
    da2 = parts[0] + parts[1]
    new = rows + norm_back(da2, hat, rstd, shared_of(sv, layer, 3))
    low = new.astype(bf16)
    sums = (
        tile_sum(low.astype(f32)), tile_sum(da2 * hat), tile_sum(da2), tile_sum(gm.astype(f32)),
        tile_sum(hidden[0].astype(f32)),
    )
    return new, low, gm, a2, hidden[0], sums


def one_row(tile):
    return jnp.sum(tile, axis=0, keepdims=True)


def pack_vectors(devices, shared_row, group_row):
    rows = WIDTH // devices
    wide = shared_row.shape[1] // devices
    own = group_row.shape[1] // devices
    lines = []
    for i in range(devices):
        pieces = []
        for piece in (shared_row[:, i * wide : (i + 1) * wide], group_row[:, i * own : (i + 1) * own]):
            pieces.append(piece)
            if piece.shape[1] < CH:
                pieces.append(jnp.zeros((1, CH - piece.shape[1]), f32))
        line = jnp.concatenate(pieces, axis=1)
        lines.append(jnp.concatenate([line, jnp.zeros((rows - 1, 2 * CH), f32)], axis=0))
    return jnp.concatenate(lines, axis=0)


def sds(shape, dtype):
    return jax.ShapeDtypeStruct(shape, dtype)


def hbm(shape, dtype):
    return pltpu.HBM(shape, dtype)


def chunk_shapes(devices):
    return [sds((devices // 2, WIDTH // devices, 3 * HALF + 2 * CH), bf16)] * 2


def put_chunks(send, keep, core, start, value):
    rows, width = send.shape[1], value.shape[1]
    for m in range(send.shape[0]):
        even = value[2 * m * rows : (2 * m + 1) * rows]
        odd = value[(2 * m + 1) * rows : (2 * m + 2) * rows]
        keep[m, :, start : start + width] = jnp.where(core == 0, even, odd).astype(bf16)
        send[m, :, start : start + width] = jnp.where(core == 0, odd, even).astype(bf16)


def vmem_spec():
    return pl.BlockSpec(memory_space=pltpu.VMEM)


def smem_spec():
    return pl.BlockSpec(memory_space=pltpu.SMEM)


def waits(arrays):
    return [pl.BlockSpec(memory_space=pl.ANY)] * len(arrays)


def kept(shape):
    return pl.BlockSpec(shape, lambda s: (0,) * len(shape))


def per_step(shape, first=0, count=1):
    return pl.BlockSpec((count,) + shape, lambda s: (s + first,) + (0,) * len(shape))


def cost(us):
    return pl.CostEstimate(flops=int(us * 1.1e9), bytes_accessed=10**6, transcendentals=0)


def params(mib):
    return pltpu.CompilerParams(vmem_limit_bytes=mib * MIB)


CANVAS = (SIDE, NS, SLOT, WIDTH)
CORE, GROUP, INDEX = 0, 1, 2


def prepare_first_kernel(qkv, proj, att):
    att[:, 0 : 3 * CH] = qkv[0].astype(bf16)
    att[0:CH, 3 * CH :] = proj[0, :, 0:CH].astype(bf16)
    att[CH:, 3 * CH :] = proj[0, :, CH:].astype(bf16)


def prepare_rest_kernel(place, qkv, proj, up, down, mlp0, att1, mlp1, send):
    half = WIDTH // 2
    att1[:, 0 : 3 * CH] = qkv[0].astype(bf16)
    att1[0:CH, 3 * CH :] = proj[0, :, 0:CH].astype(bf16)
    att1[CH:, 3 * CH :] = proj[0, :, CH:].astype(bf16)
    for layer, mlp in enumerate((mlp0, mlp1)):
        mlp[:, 0:HALF] = up[layer].astype(bf16)
        mlp[:, HALF : HALF + WIDTH] = down[layer, 0:WIDTH].astype(bf16)
        mlp[:, HALF + WIDTH :] = down[layer, WIDTH:].astype(bf16)
    mine = pl.ds(place[CORE] * half, half)
    send[:, 0:HALF] = att1[mine]
    send[:, HALF:] = mlp1[mine]


def layer_spec(shape, layer):
    return pl.BlockSpec((1,) + shape[1:], lambda s: (layer, 0, 0))


def run_prepare(place, qkv, proj, up, down):
    half = WIDTH // 2
    att0 = pl.pallas_call(
        prepare_first_kernel,
        grid=(1,),
        out_shape=sds((WIDTH, HALF), bf16),
        in_specs=[layer_spec(qkv.shape, 0), layer_spec(proj.shape, 0)],
        out_specs=kept((WIDTH, HALF)),
        compiler_params=params(SMALL),
        cost_estimate=cost(1),
        name="prepare_first",
    )(qkv, proj)
    rest = pl.pallas_call(
        prepare_rest_kernel,
        grid=(1,),
        out_shape=[
            sds((WIDTH, 2 * HALF), bf16), sds((WIDTH, HALF), bf16), sds((WIDTH, 2 * HALF), bf16),
            sds((half, 3 * HALF), bf16),
        ],
        in_specs=[smem_spec(), layer_spec(qkv.shape, 1), layer_spec(proj.shape, 1), kept(up.shape), kept(down.shape)],
        out_specs=[
            kept((WIDTH, 2 * HALF)), kept((WIDTH, HALF)), kept((WIDTH, 2 * HALF)), kept((half, 3 * HALF)),
        ],
        compiler_params=params(SMALL),
        cost_estimate=cost(3),
        name="prepare_rest",
    )(place, qkv, proj, up, down)
    return att0, *rest


def attention_kernel(layer, mine, place, given, *refs):
    if mine:
        att_w, sv, gv, ids_t, part, qkv_o, e_o, rl_o, att_o, heads_o, a1_o, stream, idc, tall = refs
    else:
        stream = given
        att_w, sv, gv, ids_t, part, qkv_o, e_o, rl_o, att_o, idc = refs
    s = pl.program_id(0)

    @pl.when(s == 0)
    def _():
        spread_ids(ids_t, idc)
        if mine:
            tall[0 : SIDE * SIDE] = given[...].astype(f32)
            spread_rows(tall, stream)

    frame = place[GROUP] if mine else 1 - place[GROUP]
    for g in range(2):
        @pl.when(frame == g)
        def _(g=g):
            for n in range(GANG):
                row = GANG * s + n
                a1, qkv, e, rl, att, heads = attend(
                    g, stripe_of(stream, g, row), stripe_of(idc, g, row), qkv_of(att_w), gv[layer],
                    shared_of(sv, layer, 0), shared_of(sv, layer, 1),
                )
                qkv_o[n] = qkv
                e_o[n] = e
                rl_o[n] = rl
                att_o[n] = att
                part[n] = dot(heads, proj_of(att_w)).astype(bf16).astype(f32)
                if mine:
                    heads_o[n] = heads
                    a1_o[n] = a1


ATT_SAVED = [((TOKENS, 3 * CH), bf16), ((TOKENS, KEYS), bf16), ((TOKENS, CH), f32), ((TOKENS, CH), bf16)]


def run_attention(layer, mine, place, stream, weights, sv, gv, ids_t):
    outs = [((ROWS, WIDTH), f32)] + ATT_SAVED + ([((ROWS, CH), bf16), ((ROWS, WIDTH), bf16)] if mine else [])
    inputs = (stream, weights, sv, gv, ids_t)
    return pl.pallas_call(
        functools.partial(attention_kernel, layer, mine),
        grid=(NS // GANG,),
        out_shape=[(sds if n == 0 else hbm)((NS,) + shape, dtype) for n, (shape, dtype) in enumerate(outs)]
        + ([sds(CANVAS, f32)] if mine else []),
        in_specs=[smem_spec()] + [kept(x.shape) for x in inputs],
        out_specs=[per_step(shape, 0, GANG) for shape, _ in outs] + ([kept(CANVAS)] if mine else []),
        scratch_shapes=[pltpu.VMEM((SIDE, NS, SLOT, CH), f32)]
        + ([pltpu.VMEM((SIDE * SIDE + 4, WIDTH), f32)] if mine else []),
        compiler_params=params(SMALL),
        cost_estimate=cost(11),
        name=f"layer{layer}_attention_{'own' if mine else 'other'}",
    )(place, *inputs)


def in_frames(own, mine_h, mine_v, other_h, other_v):
    def turned(ref):
        return jnp.stack([ref[column] for column in range(NS)], axis=1).reshape(ROWS, WIDTH)

    mine = jnp.where(own == 0, mine_h[0], turned(mine_v))
    other = jnp.where(own == 0, turned(other_v), other_h[0])
    return mine + other


def frame_specs():
    flat = per_step((ROWS, WIDTH))
    tall = pl.BlockSpec((NS, STRIPE, SLOT, WIDTH), lambda s: (0, s, 0, 0))
    return [flat, tall, flat, tall]


def frame_views(mine, other):
    shape = (NS, SIDE, SLOT, WIDTH)
    return (mine, mine.reshape(shape), other, other.reshape(shape))


def canvas_block():
    return pl.BlockSpec((STRIPE, NS, SLOT, WIDTH), lambda s: (s, 0, 0, 0))


def feed_kernel(
    layer, place, stream, mine_h, mine_v, other_h, other_v, mlp_w, mlp_o, sv, gv, gvo,
    out, mid, active, slopes,
):
    both = in_frames(place[GROUP], mine_h, mine_v, other_h, other_v)
    rows = stream[...].reshape(ROWS, WIDTH) + (both + shared_of(sv, layer, 2))
    mid[...] = rows.reshape(STRIPE, NS, SLOT, WIDTH)
    pairs = [
        (up_of(w, 0), down_of(w, 0), v[layer][:, 12 * CH :]) for w, v in ((mlp_w, gv), (mlp_o, gvo))
    ]
    new, held, slope = mlp_forward(rows, sv, layer, pairs)
    out[...] = new.reshape(STRIPE, NS, SLOT, WIDTH)
    active[0] = held
    slopes[0, 0] = slope[0]
    slopes[0, 1] = slope[1]


def run_feed(layer, place, stream, mine, other, mlp_w, mlp_o, sv, gv, gvo):
    rest = (mlp_w, mlp_o, sv, gv, gvo)
    return pl.pallas_call(
        functools.partial(feed_kernel, layer),
        grid=(NS,),
        out_shape=[
            sds(CANVAS, f32), hbm(CANVAS, f32), hbm((NS, ROWS, HALF), bf16), hbm((NS, 2, ROWS, HALF), bf16)
        ],
        in_specs=[smem_spec(), canvas_block()] + frame_specs() + [kept(x.shape) for x in rest],
        out_specs=[canvas_block(), canvas_block(), per_step((ROWS, HALF)), per_step((2, ROWS, HALF))],
        compiler_params=params(SMALL),
        cost_estimate=cost(10),
        name=f"layer{layer}_feed_forward",
    )(place, stream, *frame_views(mine, other), *rest)


def last_layer_kernel(
    layer, devices, place, stream, cot, att_w, mlp_w, near, far, sv, gv, gvo, ids_t,
    out, grad_in, send, keep,
    whole, att2, gv2, idc, mid, gmid, gb, qkv_s, e_s, rl_s, att_s, heads_s, active_s, a1_s, dqkv_s, gb_s,
    a2_s, gh_s, gm_s, acc_s, acc_b1, acc_g, tall,
):
    own = place[GROUP]
    assemble(whole, near, far, place[CORE])
    att2[own] = att_w[...]
    att2[1 - own] = whole[:, 0:HALF]
    gv2[own] = gv[layer]
    gv2[1 - own] = gvo[layer]
    spread_ids(ids_t, idc)
    acc_s[...] = jnp.zeros_like(acc_s)
    acc_b1[...] = jnp.zeros_like(acc_b1)
    acc_g[...] = jnp.zeros_like(acc_g)

    for g in range(2):
        def gang(first, carry, g=g):
            for n in range(GANG):
                s = GANG * first + n
                i = g * NS + s
                rows = stripe_of(stream, g, s)
                a1, qkv, e, rl, att, heads = attend(
                    g, rows, stripe_of(idc, g, s), qkv_of(att2[g]), gv2[g],
                    shared_of(sv, layer, 0), shared_of(sv, layer, 1),
                )
                qkv_s[i] = qkv
                e_s[i] = e
                rl_s[i] = rl
                att_s[i] = att
                part = dot(heads, proj_of(att2[g])).astype(bf16).astype(f32)
                if g == 0:
                    put_stripe(mid, g, s, part)
                else:
                    put_stripe(mid, g, s, rows + ((stripe_of(mid, g, s) + part) + shared_of(sv, layer, 2)))
                a1_s[g, s] = a1
                heads_s[g, s] = heads
            return carry

        lax.fori_loop(0, NS // GANG, gang, 0)

    def pairs():
        return [
            (up_of(mlp_w, 0), down_of(mlp_w, 0), gv[layer][:, 12 * CH :]),
            (up_of(whole, HALF), down_of(whole, HALF), gvo[layer][:, 12 * CH :]),
        ]

    tall[0 : SIDE * SIDE] = cot[...].astype(f32)
    spread_rows(tall, gmid)

    def block(s, carry):
        rows = stripe_of(mid, 0, s)
        new, held, slope = mlp_forward(rows, sv, layer, pairs())
        put_stripe(grad_in, 0, s, new)
        active_s[s] = held
        grad = stripe_of(gmid, 0, s)
        new, low, gm, a2, gh, sums = mlp_backward(grad, rows, slope, sv, layer, pairs())
        put_stripe(gmid, 0, s, new)
        put_stripe(gb, 0, s, low.astype(f32))
        gm_s[s] = gm
        a2_s[s] = a2
        gh_s[s] = gh
        for index, value in zip((2, 3, 4, 5), sums):
            acc_s[index] += value
        acc_b1[...] += sums[4]
        return carry

    lax.fori_loop(0, NS, block, 0)
    pack_rows(grad_in, tall)
    out[...] = tall[0 : SIDE * SIDE].astype(bf16)

    for g in range(2):
        def gang(first, carry, g=g):
            def add(index, value):
                acc_g[g, index] += value

            for n in range(GANG):
                s = GANG * first + n
                i = g * NS + s
                gbs = stripe_of(gb, g, s).astype(bf16)
                dqkv, part = attend_back(
                    g, gbs, stripe_of(idc, g, s), qkv_of(att2[g]), proj_of(att2[g]), gv2[g], qkv_s[i], e_s[i],
                    rl_s[i], att_s[i], add,
                )
                if g == 0:
                    put_stripe(mid, g, s, part)
                else:
                    put_stripe(mid, g, s, stripe_of(mid, g, s) + part)
                dqkv_s[g, s] = dqkv
                gb_s[g, s] = gbs
            return carry

        lax.fori_loop(0, NS // GANG, gang, 0)

    def final(s, carry):
        hat, rstd = normed(stripe_of(stream, 0, s))
        da = stripe_of(mid, 0, s)
        acc_s[0] += tile_sum(da * hat)
        acc_s[1] += tile_sum(da)
        put_stripe(
            grad_in, 0, s, stripe_of(gmid, 0, s) + norm_back(da, hat, rstd, shared_of(sv, layer, 0))
        )
        return carry

    lax.fori_loop(0, NS, final, 0)

    def flat(ref):
        return ref[...].reshape(NS * ROWS, ref.shape[-1])

    core = place[CORE]
    put_chunks(send, keep, core, 0, dot_rows(flat(a1_s.at[own]), flat(dqkv_s.at[own])))
    put_chunks(send, keep, core, 3 * CH, dot_rows(flat(gb_s.at[own]), flat(heads_s.at[own])))
    put_chunks(send, keep, core, HALF, dot_rows(flat(a2_s), flat(gh_s)))
    put_chunks(send, keep, core, 2 * HALF, dot_rows(flat(gm_s), flat(active_s)))
    shared_row = jnp.concatenate([one_row(acc_s[index]) for index in range(6)], axis=1)
    group_row = jnp.concatenate([one_row(acc_g[own, index]) for index in range(12)] + [one_row(acc_b1[...])], axis=1)
    put_chunks(send, keep, core, 3 * HALF, pack_vectors(devices, shared_row, group_row))


def run_last_layer(layer, devices, place, args):
    return pl.pallas_call(
        functools.partial(last_layer_kernel, layer, devices),
        out_shape=[sds((SIDE * SIDE, WIDTH), bf16), sds(CANVAS, f32)] + chunk_shapes(devices),
        in_specs=[smem_spec()] + [vmem_spec()] * len(args),
        out_specs=[vmem_spec()] * 4,
        scratch_shapes=[
            pltpu.VMEM((WIDTH, 3 * HALF), bf16),
            pltpu.VMEM((2, WIDTH, HALF), bf16),
            pltpu.VMEM((2, 1, 16 * CH), f32),
            pltpu.VMEM((SIDE, NS, SLOT, CH), f32),
            pltpu.VMEM(CANVAS, f32),
            pltpu.VMEM(CANVAS, f32),
            pltpu.VMEM(CANVAS, f32),
            pltpu.VMEM((2 * NS, TOKENS, 3 * CH), bf16),
            pltpu.VMEM((2 * NS, TOKENS, KEYS), bf16),
            pltpu.VMEM((2 * NS, TOKENS, CH), f32),
            pltpu.VMEM((2 * NS, TOKENS, CH), bf16),
            pltpu.VMEM((2, NS, ROWS, CH), bf16),
            pltpu.VMEM((NS, ROWS, HALF), bf16),
            pltpu.VMEM((2, NS, ROWS, WIDTH), bf16),
            pltpu.VMEM((2, NS, ROWS, 3 * CH), bf16),
            pltpu.VMEM((2, NS, ROWS, WIDTH), bf16),
            pltpu.VMEM((NS, ROWS, WIDTH), bf16),
            pltpu.VMEM((NS, ROWS, HALF), bf16),
            pltpu.VMEM((NS, ROWS, WIDTH), bf16),
            pltpu.VMEM((6, SLOT, WIDTH), f32),
            pltpu.VMEM((SLOT, HALF), f32),
            pltpu.VMEM((2, 12, SLOT, CH), f32),
            pltpu.VMEM((SIDE * SIDE + 4, WIDTH), f32),
        ],
        compiler_params=params(LARGE),
        cost_estimate=cost(65),
        name=f"layer{layer}_forward_backward",
    )(place, *args)


def feed_back_kernel(
    layer, place, grad, mid, slopes, active, mlp_w, mlp_o, sv, gv, gvo, *refs,
):
    gmid, gb, big, rows_out, bias_out, a2_s, gh_s, gm_s, act_s, acc_s, acc_b1 = refs[-11:]
    s = pl.program_id(0)

    @pl.when(s == 0)
    def _():
        acc_s[...] = jnp.zeros_like(acc_s)
        acc_b1[...] = jnp.zeros_like(acc_b1)

    pairs = [
        (up_of(w, 0), down_of(w, 0), v[layer][:, 12 * CH :]) for w, v in ((mlp_w, gv), (mlp_o, gvo))
    ]
    new, low, gm, a2, gh, sums = mlp_backward(
        grad[...].reshape(ROWS, WIDTH), mid[...].reshape(ROWS, WIDTH), [slopes[0, 0], slopes[0, 1]], sv, layer, pairs
    )
    gmid[...] = new.reshape(STRIPE, NS, SLOT, WIDTH)
    gb[...] = low.astype(f32).reshape(STRIPE, NS, SLOT, WIDTH)
    gm_s[s] = gm
    a2_s[s] = a2
    gh_s[s] = gh
    act_s[s] = active[0]
    for index in range(4):
        acc_s[index] += sums[index]
    acc_b1[...] += sums[4]

    @pl.when(s == NS - 1)
    def _():
        def flat(ref):
            return ref[...].reshape(NS * ROWS, ref.shape[-1])

        big[:, 0:HALF] = dot_rows(flat(a2_s), flat(gh_s)).astype(bf16)
        big[:, HALF:] = dot_rows(flat(gm_s), flat(act_s)).astype(bf16)
        rows_out[...] = jnp.concatenate([one_row(acc_s[index]) for index in range(4)], axis=1)
        bias_out[...] = one_row(acc_b1[...])


def run_feed_back(layer, place, grad, mid, slopes, active, mlp_w, mlp_o, sv, gv, gvo, after):
    rest = (mlp_w, mlp_o, sv, gv, gvo)
    mid, slopes, active = (pltpu.with_memory_space_constraint(x, pltpu.HBM) for x in (mid, slopes, active))
    return pl.pallas_call(
        functools.partial(feed_back_kernel, layer),
        grid=(NS,),
        out_shape=[
            sds(CANVAS, f32), sds(CANVAS, f32), sds((WIDTH, 2 * HALF), bf16), sds((1, 4 * WIDTH), f32),
            sds((1, HALF), f32),
        ],
        in_specs=[smem_spec(), canvas_block(), canvas_block(), per_step((2, ROWS, HALF)), per_step((ROWS, HALF))]
        + [kept(x.shape) for x in rest]
        + waits(after),
        out_specs=[canvas_block(), canvas_block(), kept((WIDTH, 2 * HALF)), kept((1, 4 * WIDTH)), kept((1, HALF))],
        scratch_shapes=[
            pltpu.VMEM((NS, ROWS, WIDTH), bf16),
            pltpu.VMEM((NS, ROWS, HALF), bf16),
            pltpu.VMEM((NS, ROWS, WIDTH), bf16),
            pltpu.VMEM((NS, ROWS, HALF), bf16),
            pltpu.VMEM((4, SLOT, WIDTH), f32),
            pltpu.VMEM((SLOT, HALF), f32),
        ],
        compiler_params=params(SMALL),
        cost_estimate=cost(11),
        name=f"layer{layer}_feed_backward",
    )(place, grad, mid, slopes, active, *rest, *after)


def attention_back_kernel(layer, mine, devices, first, count, n_after, place, gb, qkv, e, rl, att, *refs):
    whole = first + count == NS
    if mine:
        att_w, sv, gv, ids_t, heads, a1 = refs[:6]
        idc, dqkv_s, gb_s, acc_g = refs[-4:]
        if whole:
            big_p, acc_p, big_m, rows_m, bias_m = refs[6:11]
            da, send, keep = refs[-7:-4]
        else:
            da, big, acc_o = refs[-7:-4]
    else:
        att_w, sv, gv, ids_t = refs[:4]
        da, idc = refs[-2:]
    step = pl.program_id(0)

    @pl.when(step == 0)
    def _():
        spread_ids(ids_t, idc)
        if mine and whole:
            acc_g[...] = acc_p[...]
        elif mine:
            acc_g[...] = jnp.zeros_like(acc_g)

    def add(index, value):
        acc_g[index] += value

    frame = place[GROUP] if mine else 1 - place[GROUP]
    for g in range(2):
        @pl.when(frame == g)
        def _(g=g):
            for n in range(GANG):
                place_in = GANG * step + n
                s = place_in + first
                gbs = stripe_of(gb, g, s).astype(bf16)
                dqkv, part = attend_back(
                    g, gbs, stripe_of(idc, g, s), qkv_of(att_w), proj_of(att_w), gv[layer], qkv[n], e[n], rl[n], att[n],
                    add if mine else None,
                )
                da[n] = part
                if mine:
                    dqkv_s[place_in] = dqkv
                    gb_s[place_in] = gbs

    if mine:
        @pl.when(step == count // GANG - 1)
        def _():
            def flat(ref):
                return ref[...].reshape(count * ROWS, ref.shape[-1])

            part = jnp.concatenate(
                [
                    dot_rows(flat(a1.at[pl.ds(first, count)]), flat(dqkv_s)),
                    dot_rows(flat(gb_s), flat(heads.at[pl.ds(first, count)])),
                ],
                axis=1,
            )
            if not whole:
                big[...] = part
                acc_o[...] = acc_g[...]
                return
            core = place[CORE]
            put_chunks(send, keep, core, 0, part + big_p[...])
            put_chunks(send, keep, core, HALF, big_m[...].astype(f32))
            shared_row = jnp.concatenate([jnp.zeros((1, 2 * WIDTH), f32), rows_m[...]], axis=1)
            group_row = jnp.concatenate([one_row(acc_g[index]) for index in range(12)] + [bias_m[...]], axis=1)
            put_chunks(send, keep, core, 3 * HALF, pack_vectors(devices, shared_row, group_row))


def run_attention_back(layer, mine, devices, first, count, place, gb, saved, weights, sv, gv, ids_t, extra, da, after):
    rest = (weights, sv, gv, ids_t, *extra)
    whole = first + count == NS
    last = (*after,) if da is None else (*after, da)
    outs = [sds((NS, ROWS, WIDTH), f32)]
    out_specs = [per_step((ROWS, WIDTH), first // GANG, GANG)]
    scratch = [pltpu.VMEM((SIDE, NS, SLOT, CH), f32)]
    if mine:
        if whole:
            outs += chunk_shapes(devices)
        else:
            outs += [sds((WIDTH, HALF), f32), sds((12, SLOT, CH), f32)]
        out_specs += [kept(x.shape) for x in outs[1:]]
        scratch += [
            pltpu.VMEM((count, ROWS, 3 * CH), bf16),
            pltpu.VMEM((count, ROWS, WIDTH), bf16),
            pltpu.VMEM((12, SLOT, CH), f32),
        ]
    inputs = (place, gb, *saved, *rest, *last)
    return pl.pallas_call(
        functools.partial(attention_back_kernel, layer, mine, devices, first, count, len(last)),
        grid=(count // GANG,),
        out_shape=outs,
        in_specs=[smem_spec(), kept(CANVAS)]
        + [per_step(shape, first // GANG, GANG) for shape, _ in ATT_SAVED]
        + [kept(x.shape) for x in rest]
        + waits(last),
        out_specs=out_specs,
        scratch_shapes=scratch,
        input_output_aliases={} if da is None else {len(inputs) - 1: 0},
        compiler_params=params(SMALL),
        cost_estimate=cost(2.2 * count),
        name=f"layer{layer}_attention_back_{'own' if mine else 'other'}_{first}",
    )(*inputs)


def norm_back_kernel(layer, place, stream, gmid, mine_h, mine_v, other_h, other_v, sv, *refs):
    out, sums, grad_in, acc = refs[-4:]
    s = pl.program_id(0)

    @pl.when(s == 0)
    def _():
        acc[...] = jnp.zeros_like(acc)

    da = in_frames(place[GROUP], mine_h, mine_v, other_h, other_v)
    hat, rstd = normed(stream[...].reshape(ROWS, WIDTH))
    acc[0] += tile_sum(da * hat)
    acc[1] += tile_sum(da)
    new = gmid[...].reshape(ROWS, WIDTH) + norm_back(da, hat, rstd, shared_of(sv, layer, 0))
    put_stripe(grad_in, 0, s, new)

    @pl.when(s == NS - 1)
    def _():
        pack_rows(grad_in, out)
        sums[...] = jnp.concatenate([one_row(acc[0]), one_row(acc[1])], axis=1)


def run_norm_back(layer, place, stream, gmid, mine, other, sv, after):
    return pl.pallas_call(
        functools.partial(norm_back_kernel, layer),
        grid=(NS,),
        out_shape=[sds((SIDE * SIDE, WIDTH), f32), sds((1, 2 * WIDTH), f32)],
        in_specs=[smem_spec(), canvas_block(), canvas_block()] + frame_specs() + [kept(sv.shape)] + waits(after),
        out_specs=[kept((SIDE * SIDE, WIDTH)), kept((1, 2 * WIDTH))],
        scratch_shapes=[pltpu.VMEM(CANVAS, f32), pltpu.VMEM((2, SLOT, WIDTH), f32)],
        compiler_params=params(SMALL),
        cost_estimate=cost(4),
        name=f"layer{layer}_norm_backward",
    )(place, stream, gmid, *frame_views(mine, other), sv, *after)


def halves_of(x):
    high = x.astype(bf16)
    return high, (x - high.astype(f32)).astype(bf16)


def split_dot(a, b, dims):
    (a_high, a_low), (b_high, b_low) = halves_of(a), halves_of(b)
    left = jnp.concatenate([a_high, a_high, a_low], axis=1)
    right = jnp.concatenate([b_high, b_low, b_high], axis=dims[1][0])
    return lax.dot_general(left, right, (dims, ((), ())), preferred_element_type=f32)


SPANS = ((0, 3 * CH), (3 * CH, HALF), (HALF, 2 * HALF), (2 * HALF, 3 * HALF))


def own_rows(ref, index, rows):
    if rows % SLOT == 0:
        return ref[pl.ds(pl.multiple_of(index * rows, SLOT), rows)]
    start = index * rows
    base = pl.multiple_of((start // SLOT) * SLOT, SLOT)
    return pltpu.roll(ref[pl.ds(base, SLOT)], SLOT - (start - base), 0)[0:rows]


def sums_width(rows):
    return max(CH, SLOT * CH // rows)


def sums_blocks(rows):
    per = sums_width(rows) // CH
    return [(b // per, 3 * HALF + (b % per) * CH) for b in range(SLOT)]


def read_sums(ref, rows):
    blocks = [ref[row : row + 1, lane : lane + CH].astype(f32) for row, lane in sums_blocks(rows)]
    return jnp.concatenate([blocks[n] + blocks[n + 4] for n in range(4)], axis=1)


def with_sums(matrix, sums):
    rows, width = matrix.shape[0], sums_width(matrix.shape[0])
    high, low = halves_of(sums)
    parts = [x[:, n * CH : (n + 1) * CH] for x in (high, low) for n in range(4)]
    per = width // CH
    lines = [jnp.concatenate(parts[n : n + per], axis=1) for n in range(0, SLOT, per)]
    if rows > len(lines):
        lines.append(jnp.zeros((rows - len(lines), width), bf16))
    beside = jnp.concatenate([x.astype(f32) for x in lines], axis=0).astype(bf16)
    return jnp.concatenate([matrix, beside], axis=1)


def momentum_kernel(layer, keep, got, qkv, proj, up, down, *refs):
    whole, fresh, vectors = refs[-3:]
    total = keep[0].astype(f32) + got[0].astype(f32)
    matrix = total[:, 0 : 3 * HALF]
    old = jnp.concatenate([qkv[layer], proj[layer], up[layer], down[layer]], axis=1)
    new = momentum_decay * old + matrix
    fresh[...] = new
    ahead = (matrix + momentum_decay * new).astype(bf16)
    whole[0] = ahead if layer else with_sums(ahead, refs[0][...])
    vectors[...] = total[0:1, 3 * HALF :]


def run_momentum(layer, keep, got, moments, sums=()):
    rows = keep.shape[1]
    width = 3 * HALF + (0 if layer else sums_width(rows))
    return pl.pallas_call(
        functools.partial(momentum_kernel, layer),
        out_shape=[sds((1, rows, width), bf16), sds((rows, 3 * HALF), f32), sds((1, 2 * CH), f32)],
        in_specs=[vmem_spec()] * (6 + len(sums)),
        out_specs=[vmem_spec()] * 3,
        compiler_params=params(SMALL),
        cost_estimate=cost(1),
        name=f"layer{layer}_momentum",
    )(keep, got, *moments, *sums)


def newton(works):
    works = [work / (jnp.sqrt(jnp.sum(work * work)) + 1e-07) for work in works]
    for _ in range(NS_STEPS):
        grams = [split_dot(work, work, ((1,), (1,))) for work in works]
        blends = [
            coeff_second * gram + coeff_third * split_dot(gram, gram, ((1,), (0,))) for gram in grams
        ]
        works = [
            coeff_first * work + split_dot(blend, work, ((1,), (0,)))
            for work, blend in zip(works, blends)
        ]
    return works


def new_rows(layer, place, rows, whole, masters, turned, rows_s):
    index = place[INDEX]
    works = []
    for which, (start, stop) in enumerate(SPANS):
        work = whole[:, start:stop].astype(f32)
        works.append(work.T if which == 1 else work)
    works = newton(works)
    for which, (work, master) in enumerate(zip(works, masters)):
        width = SPANS[which][1] - SPANS[which][0]
        rows_s[:, 0:width] = work.T if which == 1 else work
        step = own_rows(rows_s, index, rows)[:, 0:width]
        if which % 2 == 1:
            turned[:, 0:width] = master[layer].T
            old = own_rows(turned, index, rows)[:, 0:width]
        else:
            old = own_rows(master.at[layer], index, rows)
        size = matrix_rate * match_scale * math.sqrt(max(master.shape[1:]))
        yield which, old * (1.0 - matrix_rate * weight_decay) - size * step


def step_kernel(layer, place, whole, qkv, proj, up, down, *refs):
    out, turned, rows_s = refs[-3:]
    for which, new in new_rows(layer, place, out.shape[0], whole, (qkv, proj, up, down), turned, rows_s):
        out[:, SPANS[which][0] : SPANS[which][1]] = new


NEWTON_SCRATCH = [pltpu.VMEM((WIDTH, HALF), f32), pltpu.VMEM((WIDTH, HALF), f32)]


def run_step(layer, place, rows, whole, masters, after):
    return pl.pallas_call(
        functools.partial(step_kernel, layer),
        out_shape=sds((rows, 3 * HALF), f32),
        in_specs=[smem_spec()] + [vmem_spec()] * 5 + waits(after),
        out_specs=vmem_spec(),
        scratch_shapes=NEWTON_SCRATCH,
        compiler_params=params(SMALL),
        cost_estimate=cost(9),
        name=f"layer{layer}_newton",
    )(place, whole, *masters, *after)


def finish_kernel(place, whole, qkv, proj, up, down, fresh0, fresh1, step1, vectors0, vectors1, *refs):
    shared_m, group_m, shared_w, group_w = refs[0:4]
    outs = refs[4:-2]
    turned, rows_s = refs[-2:]
    for layer, fresh in enumerate((fresh0, fresh1)):
        for which, (start, stop) in enumerate(SPANS):
            outs[2 * which][layer] = fresh[:, start:stop]
    for which, (start, stop) in enumerate(SPANS):
        outs[2 * which + 1][1] = step1[:, start:stop]
    wide, own = shared_m.shape[1], group_m.shape[2]
    late = jnp.concatenate([read_sums(whole, fresh0.shape[0]), jnp.zeros((1, 4 * WIDTH), f32)], axis=1)
    late = jnp.broadcast_to(late, (SLOT, 6 * WIDTH))
    late = pltpu.roll(late, lax.rem(6 * WIDTH - place[INDEX] * wide, 6 * WIDTH), 1)[0:1, 0:wide]
    for layer, vectors in enumerate((vectors0, vectors1)):
        grad = vectors[:, 0:wide]
        if layer == 0:
            grad = grad + late
        new = momentum_decay * shared_m[layer : layer + 1, :] + grad
        outs[8][layer : layer + 1, :] = new
        outs[9][layer : layer + 1, :] = shared_w[layer : layer + 1, :] - vector_rate * new
        new = momentum_decay * group_m[layer] + vectors[:, CH : CH + own]
        outs[10][layer] = new
        outs[11][layer] = group_w[layer] - vector_rate * new
    for which, new in new_rows(0, place, fresh0.shape[0], whole, (qkv, proj, up, down), turned, rows_s):
        outs[2 * which + 1][0] = new


def run_finish(rows, place, *args):
    shapes = []
    for start, stop in SPANS:
        shapes += [sds((LAYERS, rows, stop - start), f32)] * 2
    shapes += [sds(args[10].shape, f32)] * 2 + [sds(args[11].shape, f32)] * 2
    return pl.pallas_call(
        finish_kernel,
        out_shape=shapes,
        in_specs=[smem_spec()] + [vmem_spec()] * len(args),
        out_specs=[vmem_spec()] * len(shapes),
        scratch_shapes=NEWTON_SCRATCH,
        compiler_params=params(SMALL),
        cost_estimate=cost(10),
        name="layer0_newton_finish",
    )(place, *args)


def combine_kernel(bit, place, keep, got, *refs):
    send, stay = refs[-2:]
    side = (place[INDEX] // bit) % 2
    for m in range(send.shape[0]):
        for out, n in ((stay, 2 * m + side), (send, 2 * m + 1 - side)):
            out[m] = (keep[n].astype(f32) + got[n].astype(f32)).astype(bf16)


def run_combine(bit, place, keep, got, after=()):
    shape = (keep.shape[0] // 2,) + keep.shape[1:]
    return pl.pallas_call(
        functools.partial(combine_kernel, bit),
        out_shape=[sds(shape, bf16)] * 2,
        in_specs=[smem_spec(), vmem_spec(), vmem_spec()] + waits(after),
        out_specs=[vmem_spec()] * 2,
        compiler_params=params(SMALL),
        cost_estimate=cost(1),
        name=f"combine_{bit}",
    )(place, keep, got, *after)


def join_kernel(bit, place, held, got, *refs):
    out = refs[-1]
    side = (place[INDEX] // bit) % 2
    for m in range(held.shape[0]):
        out[2 * m + side] = held[m]
        out[2 * m + 1 - side] = got[m]
    if held.shape[2] > 3 * HALF:
        out[0] = with_sums(out[0, :, 0 : 3 * HALF], read_sums(held.at[0], held.shape[1]) + read_sums(got.at[0], held.shape[1]))


def run_join(bit, place, held, got, after=()):
    return pl.pallas_call(
        functools.partial(join_kernel, bit),
        out_shape=sds((2 * held.shape[0],) + held.shape[1:], bf16),
        in_specs=[smem_spec(), vmem_spec(), vmem_spec()] + waits(after),
        out_specs=vmem_spec(),
        compiler_params=params(SMALL),
        cost_estimate=cost(1),
        name=f"join_{bit}",
    )(place, held, got, *after)


def swap(x, axis, bit):
    n = lax.axis_size(axis)
    return lax.ppermute(x, axis, [(i, i ^ bit) for i in range(n)])


def local(
    tokens, cotangent, image_ids, qkv_weight, proj_weight, up_weight, down_weight, shared_vectors, group_vectors,
    qkv_moment, proj_moment, up_moment, down_moment, shared_moment, group_moment,
):
    devices = lax.axis_size("dp")
    index = lax.axis_index("dp")
    place = jnp.stack([index % 2, lax.axis_index("group"), index]).astype(jnp.int32)
    masters = (qkv_weight, proj_weight, up_weight, down_weight)
    moments = (qkv_moment, jnp.swapaxes(proj_moment, 1, 2), up_moment, jnp.swapaxes(down_moment, 1, 2))
    rows = WIDTH // devices
    bits = [1 << n for n in range(devices.bit_length() - 1)]

    att0, mlp0, att1, mlp1, send = run_prepare(place, *masters)
    att0_o = swap(att0, "group", 1)
    gv, gvo = group_vectors, swap(group_vectors, "group", 1)
    mlp0_o = swap(mlp0, "group", 1)
    near = swap(send, "group", 1)
    far = swap(near, "dp", 1)
    sv = shared_vectors

    columns = jnp.swapaxes(image_ids[0].astype(f32), 0, 1).reshape(NS, STRIPE, SIDE)
    ids_t = jnp.pad(columns, ((0, 0), (0, 1), (0, 0)), constant_values=-1.0).reshape(NS * SLOT, SIDE)

    part_own, *rest_own, stream = run_attention(0, True, place, tokens, att0, sv, gv, ids_t)
    saved_own, own_kept = rest_own[:4], rest_own[4:]
    part_other, *saved_other = run_attention(0, False, place, stream, att0_o, sv, gvo, ids_t)
    middle, mid, active, slopes = run_feed(0, place, stream, part_own, part_other, mlp0, mlp0_o, sv, gv, gvo)
    outputs, grad, send1, keep1 = run_last_layer(
        1, devices, place, (middle, cotangent, att1, mlp1, near, far, sv, gv, gvo, ids_t)
    )

    def hop(x, bit):
        return swap(x, "dp", bit)

    top = bits[-1]
    send1, keep1 = run_combine(bits[1], place, keep1, hop(send1, bits[0]))
    got1 = hop(send1, bits[1])
    gmid, gb, big_m, rows_m, bias_m = run_feed_back(
        0, place, grad, mid, slopes, active, mlp0, mlp0_o, sv, gv, gvo, (keep1,)
    )

    def back(mine, first, extra, da, after):
        saved, weights, vec = (saved_own, att0, gv) if mine else (saved_other, att0_o, gvo)
        return run_attention_back(
            0, mine, devices, first, NS // 2, place, gb, saved, weights, sv, vec, ids_t, extra, da, after
        )

    send1, keep1 = run_combine(bits[2], place, keep1, got1, (rows_m,))
    got1 = hop(send1, bits[2])
    da_own, big_p, acc_p = back(True, 0, own_kept, None, (keep1,))
    for bit in bits[3:]:
        send1, keep1 = run_combine(bit, place, keep1, got1, (acc_p,))
        got1 = hop(send1, bit)
    da_own, send0, keep0 = back(True, NS // 2, (*own_kept, big_p, acc_p, big_m, rows_m, bias_m), da_own, (keep1,))
    held1, fresh1, vectors1 = run_momentum(1, keep1, got1, moments)
    got1 = hop(held1, top)
    send0, keep0 = run_combine(bits[1], place, keep0, hop(send0, bits[0]))
    got0 = hop(send0, bits[1])
    (da_other,) = back(False, 0, (), None, (keep0, held1))
    held1 = run_join(top, place, held1, got1, (da_other,))
    for bit in bits[-2:1:-1]:
        got1 = hop(held1, bit)
        if bit != bits[2]:
            held1 = run_join(bit, place, held1, got1)
    send0, keep0 = run_combine(bits[2], place, keep0, got0, (da_other,))
    got0 = hop(send0, bits[2])
    (da_other,) = back(False, NS // 2, (), da_other, (keep0, held1))
    held1 = run_join(bits[2], place, held1, got1, (da_other,))
    got1 = hop(held1, bits[1])
    for bit in bits[3:]:
        send0, keep0 = run_combine(bit, place, keep0, got0, (da_other,))
        got0 = hop(send0, bit)
    input_grad, norm_sums = run_norm_back(0, place, stream, gmid, da_own, da_other, sv, (keep0, held1))
    held0, fresh0, vectors0 = run_momentum(0, keep0, got0, moments, (norm_sums,))
    got0 = hop(held0, top)
    held1 = run_join(bits[1], place, held1, got1, (norm_sums,))
    held1 = run_join(bits[0], place, held1, hop(held1, bits[0]))
    step1 = run_step(1, place, rows, held1.reshape(WIDTH, 3 * HALF), masters, (held0,))
    held0 = run_join(top, place, held0, got0, (step1,))
    for bit in bits[-2::-1]:
        held0 = run_join(bit, place, held0, hop(held0, bit))
    whole0 = held0.reshape(WIDTH, held0.shape[2])

    length = shared_moment.shape[1]
    shared_w = lax.dynamic_slice_in_dim(shared_vectors, index * length, length, 1)
    length = group_moment.shape[2]
    group_w = lax.dynamic_slice_in_dim(group_vectors, index * length, length, 2)
    out = run_finish(
        rows, place, whole0, *masters, fresh0, fresh1, step1, vectors0, vectors1,
        shared_moment, group_moment, shared_w, group_w,
    )
    out = [jnp.swapaxes(x, 1, 2) if n in (2, 3, 6, 7) else x for n, x in enumerate(out)]
    return (outputs, input_grad, *out)


def solution(mesh):
    return jax.shard_map(
        local,
        mesh=mesh,
        in_specs=(
            P("dp", None),
            P("dp", None),
            P("dp", None, None),
            P(None, None, "group"),
            P(None, "group", None),
            P(None, None, "group"),
            P(None, "group", None),
            P(),
            P(None, "group", None),
            P(None, "dp", "group"),
            P(None, "group", "dp"),
            P(None, "dp", "group"),
            P(None, "group", "dp"),
            P(None, "dp"),
            P(None, "group", "dp"),
        ),
        out_specs=(
            P("dp", None),
            P("dp", None),
            P(None, "dp", "group"),
            P(None, "dp", "group"),
            P(None, "group", "dp"),
            P(None, "group", "dp"),
            P(None, "dp", "group"),
            P(None, "dp", "group"),
            P(None, "group", "dp"),
            P(None, "group", "dp"),
            P(None, "dp"),
            P(None, "dp"),
            P(None, "group", "dp"),
            P(None, "group", "dp"),
        ),
        check_vma=False,
    )
```

```python
import functools
import math

import jax
import jax.numpy as jnp
from jax import lax
from jax.experimental import pallas as pl
from jax.experimental.pallas import tpu as pltpu
from jax.sharding import PartitionSpec as P

HEADS = 8
STRIPE = 7
LAYERS = 2
NS_STEPS = 5

epsilon = 1e-05
coeff_first = 3.4445
coeff_second = -4.775
coeff_third = 2.0315
momentum_decay = 0.95
matrix_rate = 0.25
weight_decay = 0.1
vector_rate = 0.001
match_scale = 0.2
masked_score = -1e30

f32 = jnp.float32
bf16 = jnp.bfloat16
LOG2E = 1.4426950408889634
MIB = 1024 * 1024
SMALL, LARGE = 32, 62

SIDE = 42
NS = 6
GANG = 3
SLOT = 8
ROWS = SIDE * SLOT
KEPT = 208
TOKENS = 320
KEYS = 5 * 256
WIDTH = 256
CH = 128
HALF = 512
HL = 4
HEAD = 32


def dot(a, b):
    return jnp.dot(a, b, preferred_element_type=f32)


def dot_t(a, b):
    return lax.dot_general(a, b, (((1,), (1,)), ((), ())), preferred_element_type=f32)


def dot_rows(a, b):
    return lax.dot_general(a, b, (((0,), (0,)), ((), ())), preferred_element_type=f32)


def lane_head():
    return lax.broadcasted_iota(jnp.int32, (1, CH), 1) // HEAD


def stripe_of(ref, g, s):
    if g == 0:
        block = ref[pl.ds(STRIPE * s, STRIPE)]
    else:
        block = ref[:, pl.ds(s, 1)]
    return block.reshape(ROWS, block.shape[-1])


def put_stripe(ref, g, s, value):
    if g == 0:
        ref[pl.ds(STRIPE * s, STRIPE)] = value.reshape(STRIPE, NS, SLOT, value.shape[-1])
    else:
        ref[:, pl.ds(s, 1)] = value.reshape(SIDE, 1, SLOT, value.shape[-1])


def normed(rows):
    mean = jnp.mean(rows, axis=-1, keepdims=True)
    centred = rows - mean
    spread = jnp.mean(centred * centred, axis=-1, keepdims=True)
    rstd = lax.rsqrt(spread + epsilon)
    return centred * rstd, rstd


def norm_back(grad, hat, rstd, gain):
    scaled = grad * gain
    first = jnp.mean(scaled, axis=-1, keepdims=True)
    second = jnp.mean(scaled * hat, axis=-1, keepdims=True)
    return rstd * (scaled - first - hat * second)


def tile_sum(rows):
    return jnp.sum(rows.reshape(-1, SLOT, rows.shape[-1]), axis=0)


def gelu_parts(x):
    z = jnp.abs(x)
    bell = jnp.exp2(x * x * (-0.5 * LOG2E))
    t = 1.0 / (1.0 + (0.3275911 * math.sqrt(0.5)) * z)
    poly = 0.5 * 1.061405429
    for coeff in (-1.453152027, 1.421413741, -0.284496736, 0.254829592):
        poly = poly * t + 0.5 * coeff
    tail = poly * t * bell
    phi = jnp.where(x >= 0.0, 1.0 - tail, tail)
    return x * phi, phi + x * bell * (1.0 / math.sqrt(2.0 * math.pi))


def places(ndim):
    shape = (1,) * (ndim - 2) + (SLOT, 1)
    return lax.broadcasted_iota(jnp.int32, shape, ndim - 2)


def fine_shifts(x, g, edge):
    axis = x.ndim - 2
    place = places(x.ndim)
    up = pltpu.roll(x, SLOT - 1, axis)
    down = pltpu.roll(x, 1, axis)
    if g == 0:
        end = x[:, :1] if edge is None else jnp.full_like(x[:, :1], edge)
        after = jnp.concatenate([x[:, 1:], end], axis=1)
        before = jnp.concatenate([end, x[:, :-1]], axis=1)
        up = jnp.where(place == STRIPE - 1, pltpu.roll(after, STRIPE - 1, axis), up)
        down = jnp.where(place == 0, pltpu.roll(before, 2, axis), down)
        if edge is not None:
            up = jnp.where(place == STRIPE, edge, up)
            down = jnp.where(place == STRIPE, edge, down)
    elif edge is not None:
        up = jnp.where(place >= STRIPE - 1, edge, up)
        down = jnp.where((place == 0) | (place == STRIPE), edge, down)
    return up, down


def coarse(x, step, fill):
    if step == 0:
        return x
    end = jnp.full_like(x[:1], fill)
    if step > 0:
        return jnp.concatenate([x[1:], end], axis=0)
    return jnp.concatenate([end, x[:-1]], axis=0)


def masked_neighbours(x, ids, g):
    shape = (STRIPE, NS, SLOT, CH) if g == 0 else (SIDE, SLOT, CH)
    x = x.reshape(shape)
    centre = ids.reshape(shape)
    up, down = fine_shifts(x, g, None)
    up_ids, down_ids = fine_shifts(centre, g, -3.0)
    around = {0: (x, centre), 1: (up, up_ids), -1: (down, down_ids)}
    for row_step in (-1, 0, 1):
        for col_step in (-1, 0, 1):
            tap = 3 * (row_step + 1) + col_step + 1
            coarse_step, fine_step = (row_step, col_step) if g == 0 else (col_step, row_step)
            source, source_ids = around[fine_step]
            if coarse_step == 0 and fine_step == 0:
                yield tap, source.reshape(ROWS, CH)
                continue
            source = coarse(source, coarse_step, 0.0)
            source_ids = coarse(source_ids, coarse_step, -9.0)
            yield tap, jnp.where(source_ids == centre, source, 0.0).reshape(ROWS, CH)


def compact(x):
    width = x.shape[1]
    tiles = x[KEPT:].reshape(2, SLOT, SLOT, width)
    place = lax.broadcasted_iota(jnp.int32, (1, SLOT, 1), 1)
    parts = []
    for j in range(STRIPE):
        first, second = tiles[:, j], pltpu.roll(tiles[:, j + 1], STRIPE - j, 1)
        if j:
            first = pltpu.roll(first, SLOT - j, 1)
        parts.append(jnp.where(place < STRIPE - j, first, second))
    return jnp.concatenate([x[:KEPT], jnp.stack(parts, axis=1).reshape(TOKENS - KEPT, width)], axis=0)


def expand(x):
    width = x.shape[1]
    tiles = x[KEPT:].reshape(2, STRIPE, SLOT, width)
    place = lax.broadcasted_iota(jnp.int32, (1, SLOT, 1), 1)
    parts = [tiles[:, 0]]
    for t in range(1, STRIPE):
        both = pltpu.roll(tiles[:, t - 1], t, 1), pltpu.roll(tiles[:, t], t, 1)
        parts.append(jnp.where(place < t, *both))
    parts.append(pltpu.roll(tiles[:, STRIPE - 1], STRIPE, 1))
    parts = [jnp.where(place < STRIPE, part, 0.0) for part in parts]
    return jnp.concatenate([x[:KEPT], jnp.stack(parts, axis=1).reshape(ROWS - KEPT, width)], axis=0)


WIDE, TAIL, PAIR = 256, 64, 640


def by_heads(pieces):
    parts = []
    for h in range(0, HL, 2):
        (first, last), (other_first, other_last) = pieces(h), pieces(h + 1)
        parts += [first, last, other_last, other_first]
    return jnp.concatenate(parts, axis=0)


def block_diagonal(x):
    head = lane_head()

    def pieces(h):
        own = x * jnp.where(head == h, 1.0, 0.0).astype(bf16)
        return own[:WIDE], own[WIDE:]

    return by_heads(pieces)


def lane_marks(pick):
    lane = lax.broadcasted_iota(jnp.int32, (1, CH), 1)

    def pieces(h):
        mark = jnp.where(pick(lane, h), 1.0, 0.0).astype(bf16)
        return jnp.broadcast_to(mark, (WIDE, CH)), jnp.broadcast_to(mark, (TAIL, CH))

    return by_heads(pieces)


def gather_heads(x):
    rows = []
    for h in range(HL):
        own = x[h * HEAD : (h + 1) * HEAD, (h // 2) * PAIR : (h // 2 + 1) * PAIR]
        if h % 2 == 0:
            rows.append(own[:, 0 : WIDE + CH])
        else:
            last = pltpu.roll(own[:, WIDE : WIDE + CH], TAIL, 1)
            rows.append(jnp.concatenate([own[:, WIDE + CH :], last], axis=1))
    return jnp.concatenate(rows, axis=0).T[0:TOKENS]


def masked_softmax(scores, bias):
    left = lax.broadcasted_iota(jnp.int32, (1, CH), 1) < TAIL
    parts = []
    for h in range(0, HL, 2):
        own = [scores[:, (h // 2) * PAIR + n * CH : (h // 2) * PAIR + (n + 1) * CH] for n in range(5)]
        own = [x + bias[n] for x, n in zip(own, (0, 1, 2, 0, 1))]
        lowest = jnp.finfo(f32).min
        top = jnp.maximum(jnp.maximum(own[0], own[1]), jnp.where(left, own[2], lowest))
        other = jnp.maximum(jnp.maximum(own[3], own[4]), jnp.where(left, lowest, own[2]))
        top = jnp.max(top, axis=-1, keepdims=True)
        other = jnp.max(other, axis=-1, keepdims=True)
        tops = (top, top, jnp.where(left, top, other), other, other)
        parts += [jnp.exp2(x - y).astype(bf16) for x, y in zip(own, tops)]
    return jnp.concatenate(parts, axis=1)


def spread_ids(ids_t, idc):
    for r in range(SIDE):
        column = jnp.broadcast_to(ids_t[:, r : r + 1], (NS * SLOT, CH))
        idc[r] = column.reshape(NS, SLOT, CH)


def spread_rows(source, target):
    place = lax.broadcasted_iota(jnp.int32, (SLOT, 1), 0)
    for r in range(SIDE):
        for column in range(NS):
            tile = source[pl.ds(SIDE * r + STRIPE * column, SLOT)]
            target[r, column] = jnp.where(place < STRIPE, tile, 0.0)


def pack_rows(source, target):
    for r in range(SIDE):
        for column in range(NS):
            start = SIDE * r + STRIPE * column
            if start + SLOT <= SIDE * SIDE:
                target[pl.ds(start, SLOT)] = source[r, column]
            else:
                target[pl.ds(start, STRIPE)] = source[r, column, 0:STRIPE]


def attend(g, rows, ids, weights, vec, gain, shift):
    hat, _ = normed(rows)
    a1 = (hat * gain + shift).astype(bf16)
    mixed = dot(a1, weights)
    value = mixed[:, 2 * CH :] + vec[:, CH : 2 * CH]
    query = (mixed[:, :CH] + vec[:, :CH]) * (HEAD ** -0.5 * LOG2E)
    qkv = compact(jnp.concatenate([query, mixed[:, CH : 2 * CH], value], axis=1)).astype(bf16)
    q, k, v = qkv[:, :CH], qkv[:, CH : 2 * CH], qkv[:, 2 * CH :]
    ids_c = compact(ids)
    key_ids = jnp.concatenate([ids_c, jnp.full((3 * CH - TOKENS, CH), -5.0, f32)], axis=0).T[0:1]
    left = lax.broadcasted_iota(jnp.int32, (1, CH), 1) < TAIL
    last = key_ids[:, 2 * CH :]
    last = jnp.where(left, last, pltpu.roll(last, TAIL, 1))
    bias = [
        jnp.where(ids_c == part, 0.0, masked_score) for part in (key_ids[:, :CH], key_ids[:, CH : 2 * CH], last)
    ]
    e = masked_softmax(dot_t(q, block_diagonal(k)), bias)
    ones = lane_marks(lambda lane, h: lane // HEAD == h)
    both = dot(e, jnp.concatenate([block_diagonal(v), ones], axis=1))
    rl = 1.0 / both[:, CH:]
    att = both[:, :CH] * rl
    total = expand(att) + vec[:, 2 * CH : 3 * CH]
    for tap, near in masked_neighbours(value.astype(bf16).astype(f32), ids, g):
        total = total + near * vec[:, (3 + tap) * CH : (4 + tap) * CH]
    return a1, qkv, e, rl, att.astype(bf16), total.astype(bf16)


def attend_back(g, gbs, ids, weights, proj, vec, qkv, e, rl, att, add):
    d_out = dot_t(gbs, proj).astype(bf16).astype(f32)
    q, k, v = qkv[:, 0:CH], qkv[:, CH : 2 * CH], qkv[:, 2 * CH :]
    scaled = (compact(d_out) * rl).astype(bf16)
    prod = scaled.astype(f32) * att.astype(f32)
    prod_high = prod.astype(bf16)
    prod_low = (prod - prod_high.astype(f32)).astype(bf16)
    lanes = lax.broadcasted_iota(jnp.int32, (CH, CH), 1)
    rows_of = lax.broadcasted_iota(jnp.int32, (CH, CH), 0)
    gather = jnp.where((lanes % HEAD == rows_of // HEAD) & (lanes < 3 * HEAD), 1.0, 0.0).astype(bf16)
    centre = dot(
        jnp.concatenate([prod_high, prod_low], axis=1), jnp.concatenate([gather, gather], axis=0)
    )
    first = centre.astype(bf16).astype(f32)
    rest = centre - first
    second = rest.astype(bf16).astype(f32)
    lane = lax.broadcasted_iota(jnp.int32, (1, CH), 1)
    pieces = jnp.where(lane < HEAD, first, jnp.where(lane < 2 * HEAD, second, rest - second))
    left = jnp.concatenate([scaled, (-pieces).astype(bf16)], axis=1)
    marks = lane_marks(lambda lane, h: (lane % HEAD == h) & (lane < 3 * HEAD))
    right = jnp.concatenate([block_diagonal(v), marks], axis=1)
    ds = (e.astype(f32) * dot_t(left, right)).astype(bf16)
    dq = dot(ds, block_diagonal(k)) * HEAD ** -0.5
    dk = gather_heads(dot_rows(q, ds)) * (1.0 / LOG2E)
    dv = gather_heads(dot_rows(scaled, e))
    grads = expand(jnp.concatenate([dq, dk, dv], axis=1))
    vf = expand(v.astype(f32))
    dv = grads[:, 2 * CH :]
    for tap, near in masked_neighbours(d_out, ids, g):
        mirror = 8 - tap
        dv = dv + near * vec[:, (3 + mirror) * CH : (4 + mirror) * CH]
        if add is not None:
            add(3 + mirror, tile_sum(near * vf))
    dq, dk, dv = grads[:, :CH].astype(bf16), grads[:, CH : 2 * CH].astype(bf16), dv.astype(bf16)
    if add is not None:
        add(0, tile_sum(dq.astype(f32)))
        add(1, tile_sum(dv.astype(f32)))
        add(2, tile_sum(d_out))
    dqkv = jnp.concatenate([dq, dk, dv], axis=1)
    return dqkv, dot_t(dqkv, weights).astype(bf16).astype(f32)


def qkv_of(buffer):
    return buffer[:, 0 : 3 * CH]


def proj_of(buffer):
    return jnp.concatenate([buffer[0:CH, 3 * CH : 4 * CH], buffer[CH : 2 * CH, 3 * CH : 4 * CH]], axis=1)


def up_of(buffer, start):
    return buffer[:, start : start + HALF]


def down_of(buffer, start):
    return jnp.concatenate(
        [buffer[:, start + HALF : start + HALF + WIDTH], buffer[:, start + HALF + WIDTH : start + 2 * HALF]], axis=0
    )


def assemble(whole, near, far, core):
    half = WIDTH // 2
    whole[pl.ds(core * half, half)] = near[...]
    whole[pl.ds((1 - core) * half, half)] = far[...]


def shared_of(sv, layer, index):
    return sv[layer : layer + 1, index * WIDTH : (index + 1) * WIDTH]


def mlp_forward(rows, sv, layer, pairs):
    hat, _ = normed(rows)
    a2 = (hat * shared_of(sv, layer, 3) + shared_of(sv, layer, 4)).astype(bf16)
    parts, kept, slopes = [], [], []
    for up, down, bias in pairs:
        active, slope = gelu_parts(dot(a2, up) + bias)
        active = active.astype(bf16)
        kept.append(active)
        slopes.append(slope.astype(bf16))
        parts.append(dot(active, down).astype(bf16).astype(f32))
    return rows + ((parts[0] + parts[1]) + shared_of(sv, layer, 5)), kept[0], slopes


def mlp_backward(rows, mid, slopes, sv, layer, pairs):
    gm = rows.astype(bf16)
    hat, rstd = normed(mid)
    a2 = (hat * shared_of(sv, layer, 3) + shared_of(sv, layer, 4)).astype(bf16)
    parts, hidden = [], []
    for (up, down, _), slope in zip(pairs, slopes):
        gh = (dot_t(gm, down) * slope.astype(f32)).astype(bf16)
        hidden.append(gh)
        parts.append(dot_t(gh, up).astype(bf16).astype(f32))
    da2 = parts[0] + parts[1]
    new = rows + norm_back(da2, hat, rstd, shared_of(sv, layer, 3))
    low = new.astype(bf16)
    sums = (
        tile_sum(low.astype(f32)), tile_sum(da2 * hat), tile_sum(da2), tile_sum(gm.astype(f32)),
        tile_sum(hidden[0].astype(f32)),
    )
    return new, low, gm, a2, hidden[0], sums


def one_row(tile):
    return jnp.sum(tile, axis=0, keepdims=True)


def pack_vectors(devices, shared_row, group_row):
    rows = WIDTH // devices
    wide = shared_row.shape[1] // devices
    own = group_row.shape[1] // devices
    lines = []
    for i in range(devices):
        pieces = []
        for piece in (shared_row[:, i * wide : (i + 1) * wide], group_row[:, i * own : (i + 1) * own]):
            pieces.append(piece)
            if piece.shape[1] < CH:
                pieces.append(jnp.zeros((1, CH - piece.shape[1]), f32))
        line = jnp.concatenate(pieces, axis=1)
        lines.append(jnp.concatenate([line, jnp.zeros((rows - 1, 2 * CH), f32)], axis=0))
    return jnp.concatenate(lines, axis=0)


def sds(shape, dtype):
    return jax.ShapeDtypeStruct(shape, dtype)


def hbm(shape, dtype):
    return pltpu.HBM(shape, dtype)


def chunk_shapes(devices):
    return [sds((devices // 2, WIDTH // devices, 3 * HALF + 2 * CH), bf16)] * 2


def put_chunks(send, keep, core, start, value):
    rows, width = send.shape[1], value.shape[1]
    for m in range(send.shape[0]):
        even = value[2 * m * rows : (2 * m + 1) * rows]
        odd = value[(2 * m + 1) * rows : (2 * m + 2) * rows]
        keep[m, :, start : start + width] = jnp.where(core == 0, even, odd).astype(bf16)
        send[m, :, start : start + width] = jnp.where(core == 0, odd, even).astype(bf16)


def vmem_spec():
    return pl.BlockSpec(memory_space=pltpu.VMEM)


def smem_spec():
    return pl.BlockSpec(memory_space=pltpu.SMEM)


def waits(arrays):
    return [pl.BlockSpec(memory_space=pl.ANY)] * len(arrays)


def kept(shape):
    return pl.BlockSpec(shape, lambda s: (0,) * len(shape))


def per_step(shape, first=0, count=1):
    return pl.BlockSpec((count,) + shape, lambda s: (s + first,) + (0,) * len(shape))


def cost(us):
    return pl.CostEstimate(flops=int(us * 1.1e9), bytes_accessed=10**6, transcendentals=0)


def params(mib):
    return pltpu.CompilerParams(vmem_limit_bytes=mib * MIB)


CANVAS = (SIDE, NS, SLOT, WIDTH)
CORE, GROUP, INDEX = 0, 1, 2


def prepare_first_kernel(qkv, proj, att):
    att[:, 0 : 3 * CH] = qkv[0].astype(bf16)
    att[0:CH, 3 * CH :] = proj[0, :, 0:CH].astype(bf16)
    att[CH:, 3 * CH :] = proj[0, :, CH:].astype(bf16)


def prepare_rest_kernel(place, qkv, proj, up, down, mlp0, att1, mlp1, send):
    half = WIDTH // 2
    att1[:, 0 : 3 * CH] = qkv[0].astype(bf16)
    att1[0:CH, 3 * CH :] = proj[0, :, 0:CH].astype(bf16)
    att1[CH:, 3 * CH :] = proj[0, :, CH:].astype(bf16)
    for layer, mlp in enumerate((mlp0, mlp1)):
        mlp[:, 0:HALF] = up[layer].astype(bf16)
        mlp[:, HALF : HALF + WIDTH] = down[layer, 0:WIDTH].astype(bf16)
        mlp[:, HALF + WIDTH :] = down[layer, WIDTH:].astype(bf16)
    mine = pl.ds(place[CORE] * half, half)
    send[:, 0:HALF] = att1[mine]
    send[:, HALF:] = mlp1[mine]


def layer_spec(shape, layer):
    return pl.BlockSpec((1,) + shape[1:], lambda s: (layer, 0, 0))


def run_prepare(place, qkv, proj, up, down):
    half = WIDTH // 2
    qkv, proj, up, down = (pltpu.with_memory_space_constraint(x, pltpu.HBM) for x in (qkv, proj, up, down))
    att0 = pl.pallas_call(
        prepare_first_kernel,
        grid=(1,),
        out_shape=sds((WIDTH, HALF), bf16),
        in_specs=[layer_spec(qkv.shape, 0), layer_spec(proj.shape, 0)],
        out_specs=kept((WIDTH, HALF)),
        compiler_params=params(SMALL),
        cost_estimate=cost(1),
        name="prepare_first",
    )(qkv, proj)
    rest = pl.pallas_call(
        prepare_rest_kernel,
        grid=(1,),
        out_shape=[
            hbm((WIDTH, 2 * HALF), bf16), hbm((WIDTH, HALF), bf16), hbm((WIDTH, 2 * HALF), bf16),
            sds((half, 3 * HALF), bf16),
        ],
        in_specs=[smem_spec(), layer_spec(qkv.shape, 1), layer_spec(proj.shape, 1), kept(up.shape), kept(down.shape)],
        out_specs=[
            kept((WIDTH, 2 * HALF)), kept((WIDTH, HALF)), kept((WIDTH, 2 * HALF)), kept((half, 3 * HALF)),
        ],
        compiler_params=params(SMALL),
        cost_estimate=cost(3),
        name="prepare_rest",
    )(place, qkv, proj, up, down)
    return att0, *rest


def attention_kernel(layer, mine, place, given, *refs):
    if mine:
        att_w, sv, gv, ids_t, part, qkv_o, e_o, rl_o, att_o, heads_o, a1_o, stream, idc, tall = refs
    else:
        stream = given
        att_w, sv, gv, ids_t, part, qkv_o, e_o, rl_o, att_o, idc = refs
    s = pl.program_id(0)

    @pl.when(s == 0)
    def _():
        spread_ids(ids_t, idc)
        if mine:
            tall[0 : SIDE * SIDE] = given[...].astype(f32)
            spread_rows(tall, stream)

    frame = place[GROUP] if mine else 1 - place[GROUP]
    for g in range(2):
        @pl.when(frame == g)
        def _(g=g):
            for n in range(GANG):
                row = GANG * s + n
                a1, qkv, e, rl, att, heads = attend(
                    g, stripe_of(stream, g, row), stripe_of(idc, g, row), qkv_of(att_w), gv[layer],
                    shared_of(sv, layer, 0), shared_of(sv, layer, 1),
                )
                qkv_o[n] = qkv
                e_o[n] = e
                rl_o[n] = rl
                att_o[n] = att
                part[n] = dot(heads, proj_of(att_w)).astype(bf16).astype(f32)
                if mine:
                    heads_o[n] = heads
                    a1_o[n] = a1


ATT_SAVED = [((TOKENS, 3 * CH), bf16), ((TOKENS, KEYS), bf16), ((TOKENS, CH), f32), ((TOKENS, CH), bf16)]


def run_attention(layer, mine, place, stream, weights, sv, gv, ids_t):
    outs = [((ROWS, WIDTH), f32)] + ATT_SAVED + ([((ROWS, CH), bf16), ((ROWS, WIDTH), bf16)] if mine else [])
    inputs = (stream, weights, sv, gv, ids_t)
    return pl.pallas_call(
        functools.partial(attention_kernel, layer, mine),
        grid=(NS // GANG,),
        out_shape=[(sds if n == 0 else hbm)((NS,) + shape, dtype) for n, (shape, dtype) in enumerate(outs)]
        + ([sds(CANVAS, f32)] if mine else []),
        in_specs=[smem_spec()] + [kept(x.shape) for x in inputs],
        out_specs=[per_step(shape, 0, GANG) for shape, _ in outs] + ([kept(CANVAS)] if mine else []),
        scratch_shapes=[pltpu.VMEM((SIDE, NS, SLOT, CH), f32)]
        + ([pltpu.VMEM((SIDE * SIDE + 4, WIDTH), f32)] if mine else []),
        compiler_params=params(SMALL),
        cost_estimate=cost(11),
        name=f"layer{layer}_attention_{'own' if mine else 'other'}",
    )(place, *inputs)


def in_frames(own, mine_h, mine_v, other_h, other_v, n=0):
    def turned(ref):
        columns = [ref[column, pl.ds(STRIPE * n, STRIPE)] for column in range(NS)]
        return jnp.stack(columns, axis=1).reshape(ROWS, WIDTH)

    mine = jnp.where(own == 0, mine_h[n], turned(mine_v))
    other = jnp.where(own == 0, turned(other_v), other_h[n])
    return mine + other


def frame_specs(count=1):
    flat = per_step((ROWS, WIDTH), 0, count)
    tall = pl.BlockSpec((NS, STRIPE * count, SLOT, WIDTH), lambda s: (0, s, 0, 0))
    return [flat, tall, flat, tall]


def frame_views(mine, other):
    shape = (NS, SIDE, SLOT, WIDTH)
    return (mine, mine.reshape(shape), other, other.reshape(shape))


def canvas_block(count=1):
    return pl.BlockSpec((STRIPE * count, NS, SLOT, WIDTH), lambda s: (s, 0, 0, 0))


def feed_kernel(
    layer, place, stream, mine_h, mine_v, other_h, other_v, mlp_w, mlp_o, sv, gv, gvo,
    out, mid, active, slopes,
):
    pairs = [
        (up_of(w, 0), down_of(w, 0), v[layer][:, 12 * CH :]) for w, v in ((mlp_w, gv), (mlp_o, gvo))
    ]
    for n in range(2):
        both = in_frames(place[GROUP], mine_h, mine_v, other_h, other_v, n)
        rows = stripe_of(stream, 0, n) + (both + shared_of(sv, layer, 2))
        put_stripe(mid, 0, n, rows)
        new, held, slope = mlp_forward(rows, sv, layer, pairs)
        put_stripe(out, 0, n, new)
        active[n] = held
        slopes[n, 0] = slope[0]
        slopes[n, 1] = slope[1]


def run_feed(layer, place, stream, mine, other, mlp_w, mlp_o, sv, gv, gvo):
    rest = (mlp_w, mlp_o, sv, gv, gvo)
    return pl.pallas_call(
        functools.partial(feed_kernel, layer),
        grid=(NS // 2,),
        out_shape=[
            hbm(CANVAS, f32), hbm(CANVAS, f32), hbm((NS, ROWS, HALF), bf16), hbm((NS, 2, ROWS, HALF), bf16)
        ],
        in_specs=[smem_spec(), canvas_block(2)] + frame_specs(2) + [kept(x.shape) for x in rest],
        out_specs=[
            canvas_block(2), canvas_block(2), per_step((ROWS, HALF), 0, 2), per_step((2, ROWS, HALF), 0, 2)
        ],
        compiler_params=params(SMALL),
        cost_estimate=cost(10),
        name=f"layer{layer}_feed_forward",
    )(place, stream, *frame_views(mine, other), *rest)


def last_layer_kernel(
    layer, devices, place, stream, cot, att_w, mlp_w, near, far, sv, gv, gvo, ids_t,
    out, grad_in, send, keep,
    whole, att2, gv2, idc, mid, gmid, gb, qkv_s, e_s, rl_s, att_s, heads_s, active_s, a1_s, dqkv_s, gb_s,
    a2_s, gh_s, gm_s, acc_s, acc_b1, acc_g, tall,
):
    own = place[GROUP]
    assemble(whole, near, far, place[CORE])
    att2[own] = att_w[...]
    att2[1 - own] = whole[:, 0:HALF]
    gv2[own] = gv[layer]
    gv2[1 - own] = gvo[layer]
    spread_ids(ids_t, idc)
    acc_s[...] = jnp.zeros_like(acc_s)
    acc_b1[...] = jnp.zeros_like(acc_b1)
    acc_g[...] = jnp.zeros_like(acc_g)

    for g in range(2):
        def gang(first, carry, g=g):
            for n in range(GANG):
                s = GANG * first + n
                i = g * NS + s
                rows = stripe_of(stream, g, s)
                a1, qkv, e, rl, att, heads = attend(
                    g, rows, stripe_of(idc, g, s), qkv_of(att2[g]), gv2[g],
                    shared_of(sv, layer, 0), shared_of(sv, layer, 1),
                )
                qkv_s[i] = qkv
                e_s[i] = e
                rl_s[i] = rl
                att_s[i] = att
                part = dot(heads, proj_of(att2[g])).astype(bf16).astype(f32)
                if g == 0:
                    put_stripe(mid, g, s, part)
                else:
                    put_stripe(mid, g, s, rows + ((stripe_of(mid, g, s) + part) + shared_of(sv, layer, 2)))
                a1_s[g, s] = a1
                heads_s[g, s] = heads
            return carry

        lax.fori_loop(0, NS // GANG, gang, 0)

    def pairs():
        return [
            (up_of(mlp_w, 0), down_of(mlp_w, 0), gv[layer][:, 12 * CH :]),
            (up_of(whole, HALF), down_of(whole, HALF), gvo[layer][:, 12 * CH :]),
        ]

    tall[0 : SIDE * SIDE] = cot[...].astype(f32)
    spread_rows(tall, gmid)

    def block(s):
        rows = stripe_of(mid, 0, s)
        new, held, slope = mlp_forward(rows, sv, layer, pairs())
        put_stripe(grad_in, 0, s, new)
        active_s[s] = held
        grad = stripe_of(gmid, 0, s)
        new, low, gm, a2, gh, sums = mlp_backward(grad, rows, slope, sv, layer, pairs())
        put_stripe(gmid, 0, s, new)
        put_stripe(gb, 0, s, low.astype(f32))
        gm_s[s] = gm
        a2_s[s] = a2
        gh_s[s] = gh
        for index, value in zip((2, 3, 4, 5), sums):
            acc_s[index] += value
        acc_b1[...] += sums[4]

    def blocks(first, carry):
        block(2 * first)
        block(2 * first + 1)
        return carry

    lax.fori_loop(0, NS // 2, blocks, 0)
    pack_rows(grad_in, tall)
    out[...] = tall[0 : SIDE * SIDE].astype(bf16)

    for g in range(2):
        def gang(first, carry, g=g):
            def add(index, value):
                acc_g[g, index] += value

            for n in range(GANG):
                s = GANG * first + n
                i = g * NS + s
                gbs = stripe_of(gb, g, s).astype(bf16)
                dqkv, part = attend_back(
                    g, gbs, stripe_of(idc, g, s), qkv_of(att2[g]), proj_of(att2[g]), gv2[g], qkv_s[i], e_s[i],
                    rl_s[i], att_s[i], add,
                )
                if g == 0:
                    put_stripe(mid, g, s, part)
                else:
                    put_stripe(mid, g, s, stripe_of(mid, g, s) + part)
                dqkv_s[g, s] = dqkv
                gb_s[g, s] = gbs
            return carry

        lax.fori_loop(0, NS // GANG, gang, 0)

    def final(s, carry):
        hat, rstd = normed(stripe_of(stream, 0, s))
        da = stripe_of(mid, 0, s)
        acc_s[0] += tile_sum(da * hat)
        acc_s[1] += tile_sum(da)
        put_stripe(
            grad_in, 0, s, stripe_of(gmid, 0, s) + norm_back(da, hat, rstd, shared_of(sv, layer, 0))
        )
        return carry

    lax.fori_loop(0, NS, final, 0)

    def flat(ref):
        return ref[...].reshape(NS * ROWS, ref.shape[-1])

    core = place[CORE]
    put_chunks(send, keep, core, 0, dot_rows(flat(a1_s.at[own]), flat(dqkv_s.at[own])))
    put_chunks(send, keep, core, 3 * CH, dot_rows(flat(gb_s.at[own]), flat(heads_s.at[own])))
    put_chunks(send, keep, core, HALF, dot_rows(flat(a2_s), flat(gh_s)))
    put_chunks(send, keep, core, 2 * HALF, dot_rows(flat(gm_s), flat(active_s)))
    shared_row = jnp.concatenate([one_row(acc_s[index]) for index in range(6)], axis=1)
    group_row = jnp.concatenate([one_row(acc_g[own, index]) for index in range(12)] + [one_row(acc_b1[...])], axis=1)
    put_chunks(send, keep, core, 3 * HALF, pack_vectors(devices, shared_row, group_row))


def run_last_layer(layer, devices, place, args):
    return pl.pallas_call(
        functools.partial(last_layer_kernel, layer, devices),
        out_shape=[sds((SIDE * SIDE, WIDTH), bf16), sds(CANVAS, f32)] + chunk_shapes(devices),
        in_specs=[smem_spec()] + [vmem_spec()] * len(args),
        out_specs=[vmem_spec()] * 4,
        scratch_shapes=[
            pltpu.VMEM((WIDTH, 3 * HALF), bf16),
            pltpu.VMEM((2, WIDTH, HALF), bf16),
            pltpu.VMEM((2, 1, 16 * CH), f32),
            pltpu.VMEM((SIDE, NS, SLOT, CH), f32),
            pltpu.VMEM(CANVAS, f32),
            pltpu.VMEM(CANVAS, f32),
            pltpu.VMEM(CANVAS, f32),
            pltpu.VMEM((2 * NS, TOKENS, 3 * CH), bf16),
            pltpu.VMEM((2 * NS, TOKENS, KEYS), bf16),
            pltpu.VMEM((2 * NS, TOKENS, CH), f32),
            pltpu.VMEM((2 * NS, TOKENS, CH), bf16),
            pltpu.VMEM((2, NS, ROWS, CH), bf16),
            pltpu.VMEM((NS, ROWS, HALF), bf16),
            pltpu.VMEM((2, NS, ROWS, WIDTH), bf16),
            pltpu.VMEM((2, NS, ROWS, 3 * CH), bf16),
            pltpu.VMEM((2, NS, ROWS, WIDTH), bf16),
            pltpu.VMEM((NS, ROWS, WIDTH), bf16),
            pltpu.VMEM((NS, ROWS, HALF), bf16),
            pltpu.VMEM((NS, ROWS, WIDTH), bf16),
            pltpu.VMEM((6, SLOT, WIDTH), f32),
            pltpu.VMEM((SLOT, HALF), f32),
            pltpu.VMEM((2, 12, SLOT, CH), f32),
            pltpu.VMEM((SIDE * SIDE + 4, WIDTH), f32),
        ],
        compiler_params=params(LARGE),
        cost_estimate=cost(65),
        name=f"layer{layer}_forward_backward",
    )(place, *args)


def feed_back_kernel(
    layer, place, grad, mid, slopes, active, mlp_w, mlp_o, sv, gv, gvo, *refs,
):
    gmid, gb, big, rows_out, bias_out, a2_s, gh_s, gm_s, act_s, acc_s, acc_b1 = refs[-11:]
    s = pl.program_id(0)

    @pl.when(s == 0)
    def _():
        acc_s[...] = jnp.zeros_like(acc_s)
        acc_b1[...] = jnp.zeros_like(acc_b1)

    pairs = [
        (up_of(w, 0), down_of(w, 0), v[layer][:, 12 * CH :]) for w, v in ((mlp_w, gv), (mlp_o, gvo))
    ]
    new, low, gm, a2, gh, sums = mlp_backward(
        grad[...].reshape(ROWS, WIDTH), mid[...].reshape(ROWS, WIDTH), [slopes[0, 0], slopes[0, 1]], sv, layer, pairs
    )
    gmid[...] = new.reshape(STRIPE, NS, SLOT, WIDTH)
    gb[...] = low.astype(f32).reshape(STRIPE, NS, SLOT, WIDTH)
    gm_s[s] = gm
    a2_s[s] = a2
    gh_s[s] = gh
    act_s[s] = active[0]
    for index in range(4):
        acc_s[index] += sums[index]
    acc_b1[...] += sums[4]

    @pl.when(s == NS - 1)
    def _():
        def flat(ref):
            return ref[...].reshape(NS * ROWS, ref.shape[-1])

        big[:, 0:HALF] = dot_rows(flat(a2_s), flat(gh_s)).astype(bf16)
        big[:, HALF:] = dot_rows(flat(gm_s), flat(act_s)).astype(bf16)
        rows_out[...] = jnp.concatenate([one_row(acc_s[index]) for index in range(4)], axis=1)
        bias_out[...] = one_row(acc_b1[...])


def run_feed_back(layer, place, grad, mid, slopes, active, mlp_w, mlp_o, sv, gv, gvo, after):
    rest = (mlp_w, mlp_o, sv, gv, gvo)
    mid, slopes, active = (pltpu.with_memory_space_constraint(x, pltpu.HBM) for x in (mid, slopes, active))
    return pl.pallas_call(
        functools.partial(feed_back_kernel, layer),
        grid=(NS,),
        out_shape=[
            sds(CANVAS, f32), sds(CANVAS, f32), sds((WIDTH, 2 * HALF), bf16), sds((1, 4 * WIDTH), f32),
            sds((1, HALF), f32),
        ],
        in_specs=[smem_spec(), canvas_block(), canvas_block(), per_step((2, ROWS, HALF)), per_step((ROWS, HALF))]
        + [kept(x.shape) for x in rest]
        + waits(after),
        out_specs=[canvas_block(), canvas_block(), kept((WIDTH, 2 * HALF)), kept((1, 4 * WIDTH)), kept((1, HALF))],
        scratch_shapes=[
            pltpu.VMEM((NS, ROWS, WIDTH), bf16),
            pltpu.VMEM((NS, ROWS, HALF), bf16),
            pltpu.VMEM((NS, ROWS, WIDTH), bf16),
            pltpu.VMEM((NS, ROWS, HALF), bf16),
            pltpu.VMEM((4, SLOT, WIDTH), f32),
            pltpu.VMEM((SLOT, HALF), f32),
        ],
        compiler_params=params(SMALL),
        cost_estimate=cost(11),
        name=f"layer{layer}_feed_backward",
    )(place, grad, mid, slopes, active, *rest, *after)


def attention_back_kernel(layer, mine, devices, first, count, n_after, place, gb, qkv, e, rl, att, *refs):
    whole = first + count == NS
    if mine:
        att_w, sv, gv, ids_t, heads, a1 = refs[:6]
        idc, dqkv_s, gb_s, acc_g = refs[-4:]
        if whole:
            big_p, acc_p, big_m, rows_m, bias_m = refs[6:11]
            da, big = refs[-6:-4]
        else:
            da, big, acc_o = refs[-7:-4]
    else:
        att_w, sv, gv, ids_t = refs[:4]
        da, idc = refs[-2:]
    step = pl.program_id(0)

    @pl.when(step == 0)
    def _():
        spread_ids(ids_t, idc)
        if mine and whole:
            acc_g[...] = acc_p[...]
        elif mine:
            acc_g[...] = jnp.zeros_like(acc_g)

    def add(index, value):
        acc_g[index] += value

    frame = place[GROUP] if mine else 1 - place[GROUP]
    for g in range(2):
        @pl.when(frame == g)
        def _(g=g):
            for n in range(GANG):
                place_in = GANG * step + n
                s = place_in + first
                gbs = stripe_of(gb, g, s).astype(bf16)
                dqkv, part = attend_back(
                    g, gbs, stripe_of(idc, g, s), qkv_of(att_w), proj_of(att_w), gv[layer], qkv[n], e[n], rl[n], att[n],
                    add if mine else None,
                )
                da[n] = part
                if mine:
                    dqkv_s[place_in] = dqkv
                    gb_s[place_in] = gbs

    if mine:
        @pl.when(step == count // GANG - 1)
        def _():
            def flat(ref):
                return ref[...].reshape(count * ROWS, ref.shape[-1])

            part = jnp.concatenate(
                [
                    dot_rows(flat(a1.at[pl.ds(first, count)]), flat(dqkv_s)),
                    dot_rows(flat(gb_s), flat(heads.at[pl.ds(first, count)])),
                ],
                axis=1,
            )
            if not whole:
                big[...] = part
                acc_o[...] = acc_g[...]
                return
            big[:, 0:HALF] = (part + big_p[...]).astype(bf16)
            big[:, HALF : 3 * HALF] = big_m[...]
            shared_row = jnp.concatenate([jnp.zeros((1, 2 * WIDTH), f32), rows_m[...]], axis=1)
            group_row = jnp.concatenate([one_row(acc_g[index]) for index in range(12)] + [bias_m[...]], axis=1)
            big[:, 3 * HALF :] = pack_vectors(devices, shared_row, group_row).astype(bf16)


def run_attention_back(layer, mine, devices, first, count, place, gb, saved, weights, sv, gv, ids_t, extra, da, after):
    rest = (weights, sv, gv, ids_t, *extra)
    whole = first + count == NS
    last = (*after,) if da is None else (*after, da)
    outs = [sds((NS, ROWS, WIDTH), f32)]
    out_specs = [per_step((ROWS, WIDTH), first // GANG, GANG)]
    scratch = [pltpu.VMEM((SIDE, NS, SLOT, CH), f32)]
    if mine:
        if whole:
            outs.append(sds((WIDTH, 3 * HALF + 2 * CH), bf16))
        else:
            outs += [sds((WIDTH, HALF), f32), sds((12, SLOT, CH), f32)]
        out_specs += [kept(x.shape) for x in outs[1:]]
        scratch += [
            pltpu.VMEM((count, ROWS, 3 * CH), bf16),
            pltpu.VMEM((count, ROWS, WIDTH), bf16),
            pltpu.VMEM((12, SLOT, CH), f32),
        ]
    inputs = (place, gb, *saved, *rest, *last)
    return pl.pallas_call(
        functools.partial(attention_back_kernel, layer, mine, devices, first, count, len(last)),
        grid=(count // GANG,),
        out_shape=outs,
        in_specs=[smem_spec(), kept(CANVAS)]
        + [per_step(shape, first // GANG, GANG) for shape, _ in ATT_SAVED]
        + [kept(x.shape) for x in rest]
        + waits(last),
        out_specs=out_specs,
        scratch_shapes=scratch,
        input_output_aliases={} if da is None else {len(inputs) - 1: 0},
        compiler_params=params(SMALL),
        cost_estimate=cost(2.2 * count),
        name=f"layer{layer}_attention_back_{'own' if mine else 'other'}_{first}",
    )(*inputs)


def norm_back_kernel(layer, place, stream, gmid, mine_h, mine_v, other_h, other_v, sv, *refs):
    out, sums, grad_in, acc = refs[-4:]
    s = pl.program_id(0)

    @pl.when(s == 0)
    def _():
        acc[...] = jnp.zeros_like(acc)

    da = in_frames(place[GROUP], mine_h, mine_v, other_h, other_v)
    hat, rstd = normed(stream[...].reshape(ROWS, WIDTH))
    acc[0] += tile_sum(da * hat)
    acc[1] += tile_sum(da)
    new = gmid[...].reshape(ROWS, WIDTH) + norm_back(da, hat, rstd, shared_of(sv, layer, 0))
    put_stripe(grad_in, 0, s, new)

    @pl.when(s == NS - 1)
    def _():
        pack_rows(grad_in, out)
        sums[...] = jnp.concatenate([one_row(acc[0]), one_row(acc[1])], axis=1)


def run_norm_back(layer, place, stream, gmid, mine, other, sv, after):
    return pl.pallas_call(
        functools.partial(norm_back_kernel, layer),
        grid=(NS,),
        out_shape=[sds((SIDE * SIDE, WIDTH), f32), sds((1, 2 * WIDTH), f32)],
        in_specs=[smem_spec(), canvas_block(), canvas_block()] + frame_specs() + [kept(sv.shape)] + waits(after),
        out_specs=[kept((SIDE * SIDE, WIDTH)), kept((1, 2 * WIDTH))],
        scratch_shapes=[pltpu.VMEM(CANVAS, f32), pltpu.VMEM((2, SLOT, WIDTH), f32)],
        compiler_params=params(SMALL),
        cost_estimate=cost(4),
        name=f"layer{layer}_norm_backward",
    )(place, stream, gmid, *frame_views(mine, other), sv, *after)


def halves_of(x):
    high = x.astype(bf16)
    return high, (x - high.astype(f32)).astype(bf16)


def split_dot(a, b, dims):
    (a_high, a_low), (b_high, b_low) = halves_of(a), halves_of(b)
    left = jnp.concatenate([a_high, a_high, a_low], axis=1)
    right = jnp.concatenate([b_high, b_low, b_high], axis=dims[1][0])
    return lax.dot_general(left, right, (dims, ((), ())), preferred_element_type=f32)


SPANS = ((0, 3 * CH), (3 * CH, HALF), (HALF, 2 * HALF), (2 * HALF, 3 * HALF))


def own_rows(ref, index, rows):
    if rows % SLOT == 0:
        return ref[pl.ds(pl.multiple_of(index * rows, SLOT), rows)]
    start = index * rows
    base = pl.multiple_of((start // SLOT) * SLOT, SLOT)
    return pltpu.roll(ref[pl.ds(base, SLOT)], SLOT - (start - base), 0)[0:rows]


def sums_width(rows):
    return max(CH, SLOT * CH // rows)


def sums_blocks(rows):
    per = sums_width(rows) // CH
    return [(b // per, 3 * HALF + (b % per) * CH) for b in range(SLOT)]


def read_sums(ref, rows):
    blocks = [ref[row : row + 1, lane : lane + CH].astype(f32) for row, lane in sums_blocks(rows)]
    return jnp.concatenate([blocks[n] + blocks[n + 4] for n in range(4)], axis=1)


def with_sums(matrix, sums):
    rows, width = matrix.shape[0], sums_width(matrix.shape[0])
    high, low = halves_of(sums)
    parts = [x[:, n * CH : (n + 1) * CH] for x in (high, low) for n in range(4)]
    per = width // CH
    lines = [jnp.concatenate(parts[n : n + per], axis=1) for n in range(0, SLOT, per)]
    if rows > len(lines):
        lines.append(jnp.zeros((rows - len(lines), width), bf16))
    beside = jnp.concatenate([x.astype(f32) for x in lines], axis=0).astype(bf16)
    return jnp.concatenate([matrix, beside], axis=1)


def momentum_kernel(layer, place, keep, got, qkv, proj, up, down, extra, whole, fresh, vectors, *refs):
    total = keep[0].astype(f32) + got[0].astype(f32)
    matrix = total[:, 0 : 3 * HALF]
    old = jnp.concatenate([qkv[layer], proj[layer], up[layer], down[layer]], axis=1)
    new = momentum_decay * old + matrix
    fresh[...] = new
    ahead = (matrix + momentum_decay * new).astype(bf16)
    vectors[...] = total[0:1, 3 * HALF :]
    if layer == 0:
        whole[0] = with_sums(ahead, extra[...])
    else:
        whole[0] = ahead
        put_chunks(*refs, place[CORE], 0, extra[...].astype(f32))


def run_momentum(layer, devices, place, keep, got, moments, extra):
    rows = keep.shape[1]
    width = 3 * HALF + (0 if layer else sums_width(rows))
    outs = [sds((1, rows, width), bf16), sds((rows, 3 * HALF), f32), sds((1, 2 * CH), f32)]
    if layer:
        outs += chunk_shapes(devices)
    return pl.pallas_call(
        functools.partial(momentum_kernel, layer),
        out_shape=outs,
        in_specs=[smem_spec()] + [vmem_spec()] * 7,
        out_specs=[vmem_spec()] * len(outs),
        compiler_params=params(SMALL),
        cost_estimate=cost(1),
        name=f"layer{layer}_momentum",
    )(place, keep, got, *moments, extra)


def square_dot(x, dims):
    high, low = halves_of(x)
    mixed = lax.dot_general(high, low, (dims, ((), ())), preferred_element_type=f32)
    return lax.dot_general(high, high, (dims, ((), ())), preferred_element_type=f32) + (mixed + mixed.T)


def newton(works, steps):
    for _ in range(steps):
        grams = [square_dot(work, ((1,), (1,))) for work in works]
        blends = [coeff_second * gram + coeff_third * square_dot(gram, ((1,), (0,))) for gram in grams]
        works = [
            coeff_first * work + split_dot(blend, work, ((1,), (0,)))
            for work, blend in zip(works, blends)
        ]
    return works


def first_works(whole):
    works = []
    for which, (start, stop) in enumerate(SPANS):
        work = whole[:, start:stop].astype(f32)
        works.append(work.T if which == 1 else work)
    return [work / (jnp.sqrt(jnp.sum(work * work)) + 1e-07) for work in works]


def new_rows(layer, place, rows, works, masters, turned, rows_s):
    index = place[INDEX]
    for which, (work, master) in enumerate(zip(works, masters)):
        width = SPANS[which][1] - SPANS[which][0]
        rows_s[:, 0:width] = work.T if which == 1 else work
        step = own_rows(rows_s, index, rows)[:, 0:width]
        if which % 2 == 1:
            turned[:, 0:width] = master[layer].T
            old = own_rows(turned, index, rows)[:, 0:width]
        else:
            old = own_rows(master.at[layer], index, rows)
        size = matrix_rate * match_scale * math.sqrt(max(master.shape[1:]))
        yield which, old * (1.0 - matrix_rate * weight_decay) - size * step


def newton_begin_kernel(steps, whole, *refs):
    for out, work in zip(refs[-4:], newton(first_works(whole), steps)):
        out[...] = work


def newton_go_on_kernel(steps, *refs):
    for out, work in zip(refs[-4:], newton([ref[...] for ref in refs[:4]], steps)):
        out[...] = work


def newton_end_kernel(layer, steps, place, qkv, proj, up, down, *refs):
    out, turned, rows_s = refs[-3:]
    works = newton([ref[...] for ref in refs[:4]], steps)
    for which, new in new_rows(layer, place, out.shape[0], works, (qkv, proj, up, down), turned, rows_s):
        out[:, SPANS[which][0] : SPANS[which][1]] = new


WORKS = [sds((CH if n == 1 else WIDTH, WIDTH if n == 1 else stop - start), f32) for n, (start, stop) in enumerate(SPANS)]


def run_newton_part(layer, steps, inputs, after):
    kernel = newton_begin_kernel if len(inputs) == 1 else newton_go_on_kernel
    return pl.pallas_call(
        functools.partial(kernel, steps),
        out_shape=WORKS,
        in_specs=[vmem_spec()] * len(inputs) + waits(after),
        out_specs=[vmem_spec()] * 4,
        compiler_params=params(SMALL),
        cost_estimate=cost(2 * steps),
        name=f"layer{layer}_newton_{'begin' if len(inputs) == 1 else 'go_on'}",
    )(*inputs, *after)


NEWTON_SCRATCH = [pltpu.VMEM((WIDTH, HALF), f32), pltpu.VMEM((WIDTH, HALF), f32)]


def run_newton_end(layer, steps, place, rows, works, masters, after):
    return pl.pallas_call(
        functools.partial(newton_end_kernel, layer, steps),
        out_shape=sds((rows, 3 * HALF), f32),
        in_specs=[smem_spec()] + [vmem_spec()] * 8 + waits(after),
        out_specs=vmem_spec(),
        scratch_shapes=NEWTON_SCRATCH,
        compiler_params=params(SMALL),
        cost_estimate=cost(2 * steps),
        name=f"layer{layer}_newton_end",
    )(place, *masters, *works, *after)


def finish_kernel(place, whole, qkv, proj, up, down, fresh0, fresh1, step1, vectors0, vectors1, *refs):
    shared_m, group_m, shared_w, group_w = refs[0:4]
    outs = refs[4:-2]
    turned, rows_s = refs[-2:]
    for layer, fresh in enumerate((fresh0, fresh1)):
        for which, (start, stop) in enumerate(SPANS):
            outs[2 * which][layer] = fresh[:, start:stop]
    for which, (start, stop) in enumerate(SPANS):
        outs[2 * which + 1][1] = step1[:, start:stop]
    wide, own = shared_m.shape[1], group_m.shape[2]
    late = jnp.concatenate([read_sums(whole, fresh0.shape[0]), jnp.zeros((1, 4 * WIDTH), f32)], axis=1)
    late = jnp.broadcast_to(late, (SLOT, 6 * WIDTH))
    late = pltpu.roll(late, lax.rem(6 * WIDTH - place[INDEX] * wide, 6 * WIDTH), 1)[0:1, 0:wide]
    for layer, vectors in enumerate((vectors0, vectors1)):
        grad = vectors[:, 0:wide]
        if layer == 0:
            grad = grad + late
        new = momentum_decay * shared_m[layer : layer + 1, :] + grad
        outs[8][layer : layer + 1, :] = new
        outs[9][layer : layer + 1, :] = shared_w[layer : layer + 1, :] - vector_rate * new
        new = momentum_decay * group_m[layer] + vectors[:, CH : CH + own]
        outs[10][layer] = new
        outs[11][layer] = group_w[layer] - vector_rate * new
    works = newton(first_works(whole), NS_STEPS)
    for which, new in new_rows(0, place, fresh0.shape[0], works, (qkv, proj, up, down), turned, rows_s):
        outs[2 * which + 1][0] = new


def run_finish(rows, place, *args):
    shapes = []
    for start, stop in SPANS:
        shapes += [sds((LAYERS, rows, stop - start), f32)] * 2
    shapes += [sds(args[10].shape, f32)] * 2 + [sds(args[11].shape, f32)] * 2
    return pl.pallas_call(
        finish_kernel,
        out_shape=shapes,
        in_specs=[smem_spec()] + [vmem_spec()] * len(args),
        out_specs=[vmem_spec()] * len(shapes),
        scratch_shapes=NEWTON_SCRATCH,
        compiler_params=params(SMALL),
        cost_estimate=cost(10),
        name="layer0_newton_finish",
    )(place, *args)


def combine_kernel(bit, place, keep, got, *refs):
    send, stay = refs[-2:]
    side = (place[INDEX] // bit) % 2
    for m in range(send.shape[0]):
        for out, n in ((stay, 2 * m + side), (send, 2 * m + 1 - side)):
            out[m] = (keep[n].astype(f32) + got[n].astype(f32)).astype(bf16)


def run_combine(bit, place, keep, got, after=()):
    shape = (keep.shape[0] // 2,) + keep.shape[1:]
    return pl.pallas_call(
        functools.partial(combine_kernel, bit),
        out_shape=[sds(shape, bf16)] * 2,
        in_specs=[smem_spec(), vmem_spec(), vmem_spec()] + waits(after),
        out_specs=[vmem_spec()] * 2,
        compiler_params=params(SMALL),
        cost_estimate=cost(1),
        name=f"combine_{bit}",
    )(place, keep, got, *after)


def join_kernel(bit, place, held, got, *refs):
    out = refs[-1]
    side = (place[INDEX] // bit) % 2
    for m in range(held.shape[0]):
        out[2 * m + side] = held[m]
        out[2 * m + 1 - side] = got[m]
    if held.shape[2] > 3 * HALF:
        out[0] = with_sums(out[0, :, 0 : 3 * HALF], read_sums(held.at[0], held.shape[1]) + read_sums(got.at[0], held.shape[1]))


def run_join(bit, place, held, got, after=()):
    return pl.pallas_call(
        functools.partial(join_kernel, bit),
        out_shape=sds((2 * held.shape[0],) + held.shape[1:], bf16),
        in_specs=[smem_spec(), vmem_spec(), vmem_spec()] + waits(after),
        out_specs=vmem_spec(),
        compiler_params=params(SMALL),
        cost_estimate=cost(1),
        name=f"join_{bit}",
    )(place, held, got, *after)


def swap(x, axis, bit):
    n = lax.axis_size(axis)
    return lax.ppermute(x, axis, [(i, i ^ bit) for i in range(n)])


def local(
    tokens, cotangent, image_ids, qkv_weight, proj_weight, up_weight, down_weight, shared_vectors, group_vectors,
    qkv_moment, proj_moment, up_moment, down_moment, shared_moment, group_moment,
):
    devices = lax.axis_size("dp")
    index = lax.axis_index("dp")
    place = jnp.stack([index % 2, lax.axis_index("group"), index]).astype(jnp.int32)
    masters = (qkv_weight, proj_weight, up_weight, down_weight)
    moments = (qkv_moment, jnp.swapaxes(proj_moment, 1, 2), up_moment, jnp.swapaxes(down_moment, 1, 2))
    rows = WIDTH // devices
    bits = [1 << n for n in range(devices.bit_length() - 1)]

    att0, mlp0, att1, mlp1, send = run_prepare(place, *masters)
    att0_o = swap(att0, "group", 1)
    gv, gvo = group_vectors, swap(group_vectors, "group", 1)
    mlp0_o = swap(mlp0, "group", 1)
    near = swap(send, "group", 1)
    far = swap(near, "dp", 1)
    sv = shared_vectors

    columns = jnp.swapaxes(image_ids[0].astype(f32), 0, 1).reshape(NS, STRIPE, SIDE)
    ids_t = jnp.pad(columns, ((0, 0), (0, 1), (0, 0)), constant_values=-1.0).reshape(NS * SLOT, SIDE)

    part_own, *rest_own, stream = run_attention(0, True, place, tokens, att0, sv, gv, ids_t)
    saved_own, own_kept = rest_own[:4], rest_own[4:]
    part_other, *saved_other = run_attention(0, False, place, stream, att0_o, sv, gvo, ids_t)
    middle, mid, active, slopes = run_feed(0, place, stream, part_own, part_other, mlp0, mlp0_o, sv, gv, gvo)
    outputs, grad, send1, keep1 = run_last_layer(
        1, devices, place, (middle, cotangent, att1, mlp1, near, far, sv, gv, gvo, ids_t)
    )

    def hop(x, bit):
        return swap(x, "dp", bit)

    top = bits[-1]
    send1, keep1 = run_combine(bits[1], place, keep1, hop(send1, bits[0]))
    got1 = hop(send1, bits[1])
    gmid, gb, big_m, rows_m, bias_m = run_feed_back(
        0, place, grad, mid, slopes, active, mlp0, mlp0_o, sv, gv, gvo, (keep1,)
    )

    def back(mine, first, extra, da, after):
        saved, weights, vec = (saved_own, att0, gv) if mine else (saved_other, att0_o, gvo)
        return run_attention_back(
            0, mine, devices, first, NS // 2, place, gb, saved, weights, sv, vec, ids_t, extra, da, after
        )

    send1, keep1 = run_combine(bits[2], place, keep1, got1, (rows_m,))
    got1 = hop(send1, bits[2])
    da_own, big_p, acc_p = back(True, 0, own_kept, None, (keep1,))
    for bit in bits[3:]:
        send1, keep1 = run_combine(bit, place, keep1, got1, (acc_p,))
        got1 = hop(send1, bit)
    da_own, big0 = back(True, NS // 2, (*own_kept, big_p, acc_p, big_m, rows_m, bias_m), da_own, (keep1,))
    held1, fresh1, vectors1, send0, keep0 = run_momentum(1, devices, place, keep1, got1, moments, big0)
    got1 = hop(held1, top)
    send0, keep0 = run_combine(bits[1], place, keep0, hop(send0, bits[0]))
    got0 = hop(send0, bits[1])
    (da_other,) = back(False, 0, (), None, (keep0, held1))
    held1 = run_join(top, place, held1, got1, (da_other,))
    for bit in bits[-2:1:-1]:
        got1 = hop(held1, bit)
        if bit != bits[2]:
            held1 = run_join(bit, place, held1, got1)
    send0, keep0 = run_combine(bits[2], place, keep0, got0, (da_other,))
    got0 = hop(send0, bits[2])
    (da_other,) = back(False, NS // 2, (), da_other, (keep0, held1))
    held1 = run_join(bits[2], place, held1, got1, (da_other,))
    got1 = hop(held1, bits[1])
    for bit in bits[3:]:
        send0, keep0 = run_combine(bit, place, keep0, got0, (da_other,))
        got0 = hop(send0, bit)
    input_grad, norm_sums = run_norm_back(0, place, stream, gmid, da_own, da_other, sv, (keep0, held1))
    held0, fresh0, vectors0 = run_momentum(0, devices, place, keep0, got0, moments, norm_sums)
    got0 = hop(held0, top)
    held1 = run_join(bits[1], place, held1, got1, (held0,))
    held1 = run_join(bits[0], place, held1, hop(held1, bits[0]))

    works = run_newton_part(1, 2, (held1.reshape(WIDTH, 3 * HALF),), (held0,))
    held0 = run_join(top, place, held0, got0, (works[0],))
    for bit in bits[-2:2:-1]:
        held0 = run_join(bit, place, held0, hop(held0, bit))
    got0 = hop(held0, bits[2])
    works = run_newton_part(1, 2, works, (held0,))
    held0 = run_join(bits[2], place, held0, got0, (works[0],))
    got0 = hop(held0, bits[1])
    step1 = run_newton_end(1, NS_STEPS - 4, place, rows, works, masters, (held0,))
    held0 = run_join(bits[1], place, held0, got0, (step1,))
    held0 = run_join(bits[0], place, held0, hop(held0, bits[0]))
    whole0 = held0.reshape(WIDTH, held0.shape[2])

    length = shared_moment.shape[1]
    shared_w = lax.dynamic_slice_in_dim(shared_vectors, index * length, length, 1)
    length = group_moment.shape[2]
    group_w = lax.dynamic_slice_in_dim(group_vectors, index * length, length, 2)
    out = run_finish(
        rows, place, whole0, *masters, fresh0, fresh1, step1, vectors0, vectors1,
        shared_moment, group_moment, shared_w, group_w,
    )
    out = [jnp.swapaxes(x, 1, 2) if n in (2, 3, 6, 7) else x for n, x in enumerate(out)]
    return (outputs, input_grad, *out)


def solution(mesh):
    return jax.shard_map(
        local,
        mesh=mesh,
        in_specs=(
            P("dp", None),
            P("dp", None),
            P("dp", None, None),
            P(None, None, "group"),
            P(None, "group", None),
            P(None, None, "group"),
            P(None, "group", None),
            P(),
            P(None, "group", None),
            P(None, "dp", "group"),
            P(None, "group", "dp"),
            P(None, "dp", "group"),
            P(None, "group", "dp"),
            P(None, "dp"),
            P(None, "group", "dp"),
        ),
        out_specs=(
            P("dp", None),
            P("dp", None),
            P(None, "dp", "group"),
            P(None, "dp", "group"),
            P(None, "group", "dp"),
            P(None, "group", "dp"),
            P(None, "dp", "group"),
            P(None, "dp", "group"),
            P(None, "group", "dp"),
            P(None, "group", "dp"),
            P(None, "dp"),
            P(None, "dp"),
            P(None, "group", "dp"),
            P(None, "group", "dp"),
        ),
        check_vma=False,
    )
```

```python
import functools
import math

import jax
import jax.numpy as jnp
from jax import lax
from jax.experimental import pallas as pl
from jax.experimental.pallas import tpu as pltpu
from jax.sharding import PartitionSpec as P

HEADS = 8
STRIPE = 7
LAYERS = 2
NS_STEPS = 5

epsilon = 1e-05
coeff_first = 3.4445
coeff_second = -4.775
coeff_third = 2.0315
momentum_decay = 0.95
matrix_rate = 0.25
weight_decay = 0.1
vector_rate = 0.001
match_scale = 0.2
masked_score = -1e30

f32 = jnp.float32
bf16 = jnp.bfloat16
LOG2E = 1.4426950408889634
MIB = 1024 * 1024
SMALL, LARGE = 32, 62

SIDE = 42
NS = 6
GANG = 3
SLOT = 8
ROWS = SIDE * SLOT
KEPT = 208
TOKENS = 320
KEYS = 5 * 256
WIDTH = 256
CH = 128
HALF = 512
HL = 4
HEAD = 32


def dot(a, b):
    return jnp.dot(a, b, preferred_element_type=f32)


def dot_t(a, b):
    return lax.dot_general(a, b, (((1,), (1,)), ((), ())), preferred_element_type=f32)


def dot_rows(a, b):
    return lax.dot_general(a, b, (((0,), (0,)), ((), ())), preferred_element_type=f32)


def lane_head():
    return lax.broadcasted_iota(jnp.int32, (1, CH), 1) // HEAD


def stripe_of(ref, g, s):
    if g == 0:
        block = ref[pl.ds(STRIPE * s, STRIPE)]
    else:
        block = ref[:, pl.ds(s, 1)]
    return block.reshape(ROWS, block.shape[-1])


def put_stripe(ref, g, s, value):
    if g == 0:
        ref[pl.ds(STRIPE * s, STRIPE)] = value.reshape(STRIPE, NS, SLOT, value.shape[-1])
    else:
        ref[:, pl.ds(s, 1)] = value.reshape(SIDE, 1, SLOT, value.shape[-1])


def normed(rows):
    mean = jnp.mean(rows, axis=-1, keepdims=True)
    centred = rows - mean
    spread = jnp.mean(centred * centred, axis=-1, keepdims=True)
    rstd = lax.rsqrt(spread + epsilon)
    return centred * rstd, rstd


def norm_back(grad, hat, rstd, gain):
    scaled = grad * gain
    first = jnp.mean(scaled, axis=-1, keepdims=True)
    second = jnp.mean(scaled * hat, axis=-1, keepdims=True)
    return rstd * (scaled - first - hat * second)


def tile_sum(rows):
    return jnp.sum(rows.reshape(-1, SLOT, rows.shape[-1]), axis=0)


def gelu_parts(x):
    phi = 0.5 + 0.5 * lax.erf(x * math.sqrt(0.5))
    bell = jnp.exp2(x * x * (-0.5 * LOG2E))
    return x * phi, phi + x * bell * (1.0 / math.sqrt(2.0 * math.pi))


def places(ndim):
    shape = (1,) * (ndim - 2) + (SLOT, 1)
    return lax.broadcasted_iota(jnp.int32, shape, ndim - 2)


def fine_shifts(x, g, edge):
    axis = x.ndim - 2
    place = places(x.ndim)
    up = pltpu.roll(x, SLOT - 1, axis)
    down = pltpu.roll(x, 1, axis)
    if g == 0:
        end = x[:, :1] if edge is None else jnp.full_like(x[:, :1], edge)
        after = jnp.concatenate([x[:, 1:], end], axis=1)
        before = jnp.concatenate([end, x[:, :-1]], axis=1)
        up = jnp.where(place == STRIPE - 1, pltpu.roll(after, STRIPE - 1, axis), up)
        down = jnp.where(place == 0, pltpu.roll(before, 2, axis), down)
        if edge is not None:
            up = jnp.where(place == STRIPE, edge, up)
            down = jnp.where(place == STRIPE, edge, down)
    elif edge is not None:
        up = jnp.where(place >= STRIPE - 1, edge, up)
        down = jnp.where((place == 0) | (place == STRIPE), edge, down)
    return up, down


def coarse(x, step, fill):
    if step == 0:
        return x
    end = jnp.full_like(x[:1], fill)
    if step > 0:
        return jnp.concatenate([x[1:], end], axis=0)
    return jnp.concatenate([end, x[:-1]], axis=0)


def masked_neighbours(x, ids, g):
    shape = (STRIPE, NS, SLOT, CH) if g == 0 else (SIDE, SLOT, CH)
    x = x.reshape(shape)
    centre = ids.reshape(shape)
    up, down = fine_shifts(x, g, None)
    up_ids, down_ids = fine_shifts(centre, g, -3.0)
    around = {0: (x, centre), 1: (up, up_ids), -1: (down, down_ids)}
    for row_step in (-1, 0, 1):
        for col_step in (-1, 0, 1):
            tap = 3 * (row_step + 1) + col_step + 1
            coarse_step, fine_step = (row_step, col_step) if g == 0 else (col_step, row_step)
            source, source_ids = around[fine_step]
            if coarse_step == 0 and fine_step == 0:
                yield tap, source.reshape(ROWS, CH)
                continue
            source = coarse(source, coarse_step, 0.0)
            source_ids = coarse(source_ids, coarse_step, -9.0)
            yield tap, jnp.where(source_ids == centre, source, 0.0).reshape(ROWS, CH)


def compact(x):
    width = x.shape[1]
    tiles = x[KEPT:].reshape(2, SLOT, SLOT, width)
    place = lax.broadcasted_iota(jnp.int32, (1, SLOT, 1), 1)
    parts = []
    for j in range(STRIPE):
        first, second = tiles[:, j], pltpu.roll(tiles[:, j + 1], STRIPE - j, 1)
        if j:
            first = pltpu.roll(first, SLOT - j, 1)
        parts.append(jnp.where(place < STRIPE - j, first, second))
    return jnp.concatenate([x[:KEPT], jnp.stack(parts, axis=1).reshape(TOKENS - KEPT, width)], axis=0)


def expand(x):
    width = x.shape[1]
    tiles = x[KEPT:].reshape(2, STRIPE, SLOT, width)
    place = lax.broadcasted_iota(jnp.int32, (1, SLOT, 1), 1)
    parts = [tiles[:, 0]]
    for t in range(1, STRIPE):
        both = pltpu.roll(tiles[:, t - 1], t, 1), pltpu.roll(tiles[:, t], t, 1)
        parts.append(jnp.where(place < t, *both))
    parts.append(pltpu.roll(tiles[:, STRIPE - 1], STRIPE, 1))
    parts = [jnp.where(place < STRIPE, part, 0.0) for part in parts]
    return jnp.concatenate([x[:KEPT], jnp.stack(parts, axis=1).reshape(ROWS - KEPT, width)], axis=0)


WIDE, TAIL = 256, 64


def by_heads(pieces):
    parts = [pieces(h) for h in range(HL)]
    return jnp.concatenate([part[0] for part in parts] + [part[1] for part in parts], axis=0)


def block_diagonal(x):
    head = lane_head()

    def pieces(h):
        own = x * jnp.where(head == h, 1.0, 0.0).astype(bf16)
        return own[:WIDE], own[WIDE:]

    return by_heads(pieces)


def lane_marks(pick):
    lane = lax.broadcasted_iota(jnp.int32, (1, CH), 1)

    def pieces(h):
        mark = jnp.where(pick(lane, h), 1.0, 0.0).astype(bf16)
        return jnp.broadcast_to(mark, (WIDE, CH)), jnp.broadcast_to(mark, (TAIL, CH))

    return by_heads(pieces)


def turned(x):
    return jnp.concatenate([x, jnp.zeros((3 * CH - TOKENS, CH), x.dtype)], axis=0).T[:, 0:TOKENS]


def head_rows(x, h):
    return x[h * HEAD : (h + 1) * HEAD]


def over_queries(left, weights):
    main = [dot(head_rows(left, h), weights[:, h * WIDE : (h + 1) * WIDE]) for h in range(HL)]
    tails = dot(left, weights[:, HL * WIDE :])
    last = []
    for h in range(HL):
        own = head_rows(tails, h)[:, (h // 2) * CH : (h // 2 + 1) * CH]
        last.append(pltpu.roll(own, TAIL, 1) if h % 2 else own)
    return jnp.concatenate([jnp.concatenate(main, axis=0), jnp.concatenate(last, axis=0)], axis=1)


def masked_softmax(q, keys, bias):
    tails = dot_t(q, keys[HL * WIDE :])
    left = lax.broadcasted_iota(jnp.int32, (1, CH), 1) < TAIL
    lowest = jnp.finfo(f32).min
    parts, last = [], []
    for h in range(0, HL, 2):
        scores = dot_t(q, keys[h * WIDE : (h + 2) * WIDE])
        own = [scores[:, n * CH : (n + 1) * CH] + bias[n % 2] for n in range(4)]
        tail = tails[:, (h // 2) * CH : (h // 2 + 1) * CH] + bias[2]
        top = jnp.maximum(jnp.maximum(own[0], own[1]), jnp.where(left, tail, lowest))
        other = jnp.maximum(jnp.maximum(own[2], own[3]), jnp.where(left, lowest, tail))
        top = jnp.max(top, axis=-1, keepdims=True)
        other = jnp.max(other, axis=-1, keepdims=True)
        parts += [jnp.exp2(x - y).astype(bf16) for x, y in zip(own, (top, top, other, other))]
        last.append(jnp.exp2(tail - jnp.where(left, top, other)).astype(bf16))
    return jnp.concatenate(parts + last, axis=1)


def spread_ids(ids_t, idc):
    for r in range(SIDE):
        column = jnp.broadcast_to(ids_t[:, r : r + 1], (NS * SLOT, CH))
        idc[r] = column.reshape(NS, SLOT, CH)


def spread_rows(source, target):
    place = lax.broadcasted_iota(jnp.int32, (SLOT, 1), 0)
    for r in range(SIDE):
        for column in range(NS):
            tile = source[pl.ds(SIDE * r + STRIPE * column, SLOT)]
            target[r, column] = jnp.where(place < STRIPE, tile, 0.0)


def pack_rows(source, target):
    for r in range(SIDE):
        for column in range(NS):
            start = SIDE * r + STRIPE * column
            if start + SLOT <= SIDE * SIDE:
                target[pl.ds(start, SLOT)] = source[r, column]
            else:
                target[pl.ds(start, STRIPE)] = source[r, column, 0:STRIPE]


def attend(g, rows, ids, weights, vec, gain, shift):
    hat, _ = normed(rows)
    a1 = (hat * gain + shift).astype(bf16)
    mixed = dot(a1, weights)
    value = mixed[:, 2 * CH :] + vec[:, CH : 2 * CH]
    query = (mixed[:, :CH] + vec[:, :CH]) * (HEAD ** -0.5 * LOG2E)
    qkv = compact(jnp.concatenate([query, mixed[:, CH : 2 * CH], value], axis=1)).astype(bf16)
    q, k, v = qkv[:, :CH], qkv[:, CH : 2 * CH], qkv[:, 2 * CH :]
    ids_c = compact(ids)
    key_ids = jnp.concatenate([ids_c, jnp.full((3 * CH - TOKENS, CH), -5.0, f32)], axis=0).T[0:1]
    left = lax.broadcasted_iota(jnp.int32, (1, CH), 1) < TAIL
    last = key_ids[:, 2 * CH :]
    last = jnp.where(left, last, pltpu.roll(last, TAIL, 1))
    bias = [
        jnp.where(ids_c == part, 0.0, masked_score) for part in (key_ids[:, :CH], key_ids[:, CH : 2 * CH], last)
    ]
    e = masked_softmax(q, block_diagonal(k), bias)
    ones = lane_marks(lambda lane, h: lane // HEAD == h)
    both = dot(e, jnp.concatenate([block_diagonal(v), ones], axis=1))
    rl = 1.0 / both[:, CH:]
    att = both[:, :CH] * rl
    total = expand(att) + vec[:, 2 * CH : 3 * CH]
    for tap, near in masked_neighbours(value.astype(bf16).astype(f32), ids, g):
        total = total + near * vec[:, (3 + tap) * CH : (4 + tap) * CH]
    return a1, qkv, e, rl, att.astype(bf16), total.astype(bf16)


def attend_back(g, gbs, ids, weights, proj, vec, qkv, e, rl, att, add):
    d_out = dot_t(gbs, proj).astype(bf16).astype(f32)
    q, k, v = qkv[:, 0:CH], qkv[:, CH : 2 * CH], qkv[:, 2 * CH :]
    scaled = (compact(d_out) * rl).astype(bf16)
    prod = scaled.astype(f32) * att.astype(f32)
    prod_high = prod.astype(bf16)
    prod_low = (prod - prod_high.astype(f32)).astype(bf16)
    lanes = lax.broadcasted_iota(jnp.int32, (CH, CH), 1)
    rows_of = lax.broadcasted_iota(jnp.int32, (CH, CH), 0)
    gather = jnp.where((lanes % HEAD == rows_of // HEAD) & (lanes < 3 * HEAD), 1.0, 0.0).astype(bf16)
    centre = dot(
        jnp.concatenate([prod_high, prod_low], axis=1), jnp.concatenate([gather, gather], axis=0)
    )
    first = centre.astype(bf16).astype(f32)
    rest = centre - first
    second = rest.astype(bf16).astype(f32)
    lane = lax.broadcasted_iota(jnp.int32, (1, CH), 1)
    pieces = jnp.where(lane < HEAD, first, jnp.where(lane < 2 * HEAD, second, rest - second))
    left = jnp.concatenate([scaled, (-pieces).astype(bf16)], axis=1)
    marks = lane_marks(lambda lane, h: (lane % HEAD == h) & (lane < 3 * HEAD))
    right = jnp.concatenate([block_diagonal(v), marks], axis=1)
    ds = (e.astype(f32) * dot_t(left, right)).astype(bf16)
    dq = dot(ds, block_diagonal(k)) * HEAD ** -0.5
    turned_grads = [over_queries(turned(q), ds) * (1.0 / LOG2E), over_queries(turned(scaled), e)]
    grads = jnp.concatenate([dq, jnp.concatenate(turned_grads, axis=0).T[0:TOKENS]], axis=1)
    grads = expand(grads)
    vf = expand(v.astype(f32))
    dv = grads[:, 2 * CH :]
    for tap, near in masked_neighbours(d_out, ids, g):
        mirror = 8 - tap
        dv = dv + near * vec[:, (3 + mirror) * CH : (4 + mirror) * CH]
        if add is not None:
            add(3 + mirror, tile_sum(near * vf))
    dq, dk, dv = grads[:, :CH].astype(bf16), grads[:, CH : 2 * CH].astype(bf16), dv.astype(bf16)
    if add is not None:
        add(0, tile_sum(dq.astype(f32)))
        add(1, tile_sum(dv.astype(f32)))
        add(2, tile_sum(d_out))
    dqkv = jnp.concatenate([dq, dk, dv], axis=1)
    return dqkv, dot_t(dqkv, weights).astype(bf16).astype(f32)


def qkv_of(buffer):
    return buffer[:, 0 : 3 * CH]


def proj_of(buffer):
    return jnp.concatenate([buffer[0:CH, 3 * CH : 4 * CH], buffer[CH : 2 * CH, 3 * CH : 4 * CH]], axis=1)


def up_of(buffer, start):
    return buffer[:, start : start + HALF]


def down_of(buffer, start):
    return jnp.concatenate(
        [buffer[:, start + HALF : start + HALF + WIDTH], buffer[:, start + HALF + WIDTH : start + 2 * HALF]], axis=0
    )


def assemble(whole, near, far, core):
    half = WIDTH // 2
    whole[pl.ds(core * half, half)] = near[...]
    whole[pl.ds((1 - core) * half, half)] = far[...]


def shared_of(sv, layer, index):
    return sv[layer : layer + 1, index * WIDTH : (index + 1) * WIDTH]


def mlp_forward(rows, sv, layer, pairs):
    hat, _ = normed(rows)
    a2 = (hat * shared_of(sv, layer, 3) + shared_of(sv, layer, 4)).astype(bf16)
    parts, kept, slopes = [], [], []
    for up, down, bias in pairs:
        active, slope = gelu_parts(dot(a2, up) + bias)
        active = active.astype(bf16)
        kept.append(active)
        slopes.append(slope.astype(bf16))
        parts.append(dot(active, down).astype(bf16).astype(f32))
    return rows + ((parts[0] + parts[1]) + shared_of(sv, layer, 5)), kept[0], slopes


def mlp_backward(rows, mid, slopes, sv, layer, pairs):
    gm = rows.astype(bf16)
    hat, rstd = normed(mid)
    a2 = (hat * shared_of(sv, layer, 3) + shared_of(sv, layer, 4)).astype(bf16)
    parts, hidden = [], []
    for (up, down, _), slope in zip(pairs, slopes):
        gh = (dot_t(gm, down) * slope.astype(f32)).astype(bf16)
        hidden.append(gh)
        parts.append(dot_t(gh, up).astype(bf16).astype(f32))
    da2 = parts[0] + parts[1]
    new = rows + norm_back(da2, hat, rstd, shared_of(sv, layer, 3))
    low = new.astype(bf16)
    sums = (
        tile_sum(low.astype(f32)), tile_sum(da2 * hat), tile_sum(da2), tile_sum(gm.astype(f32)),
        tile_sum(hidden[0].astype(f32)),
    )
    return new, low, gm, a2, hidden[0], sums


def one_row(tile):
    return jnp.sum(tile, axis=0, keepdims=True)


def pack_vectors(devices, shared_row, group_row):
    rows = WIDTH // devices
    wide = shared_row.shape[1] // devices
    own = group_row.shape[1] // devices
    lines = []
    for i in range(devices):
        pieces = []
        for piece in (shared_row[:, i * wide : (i + 1) * wide], group_row[:, i * own : (i + 1) * own]):
            pieces.append(piece)
            if piece.shape[1] < CH:
                pieces.append(jnp.zeros((1, CH - piece.shape[1]), f32))
        line = jnp.concatenate(pieces, axis=1)
        lines.append(jnp.concatenate([line, jnp.zeros((rows - 1, 2 * CH), f32)], axis=0))
    return jnp.concatenate(lines, axis=0)


def sds(shape, dtype):
    return jax.ShapeDtypeStruct(shape, dtype)


def hbm(shape, dtype):
    return pltpu.HBM(shape, dtype)


def chunk_shapes(devices):
    return [sds((devices // 2, WIDTH // devices, 3 * HALF + 2 * CH), bf16)] * 2


def put_chunks(send, keep, core, start, value):
    rows, width = send.shape[1], value.shape[1]
    for m in range(send.shape[0]):
        even = value[2 * m * rows : (2 * m + 1) * rows]
        odd = value[(2 * m + 1) * rows : (2 * m + 2) * rows]
        keep[m, :, start : start + width] = jnp.where(core == 0, even, odd).astype(bf16)
        send[m, :, start : start + width] = jnp.where(core == 0, odd, even).astype(bf16)


def vmem_spec():
    return pl.BlockSpec(memory_space=pltpu.VMEM)


def smem_spec():
    return pl.BlockSpec(memory_space=pltpu.SMEM)


def waits(arrays):
    return [pl.BlockSpec(memory_space=pl.ANY)] * len(arrays)


def kept(shape):
    return pl.BlockSpec(shape, lambda s: (0,) * len(shape))


def per_step(shape, first=0, count=1):
    return pl.BlockSpec((count,) + shape, lambda s: (s + first,) + (0,) * len(shape))


def cost(us):
    return pl.CostEstimate(flops=int(us * 1.1e9), bytes_accessed=10**6, transcendentals=0)


def params(mib):
    return pltpu.CompilerParams(vmem_limit_bytes=mib * MIB)


CANVAS = (SIDE, NS, SLOT, WIDTH)
CORE, GROUP, INDEX = 0, 1, 2


def prepare_first_kernel(qkv, proj, att):
    att[:, 0 : 3 * CH] = qkv[0].astype(bf16)
    att[0:CH, 3 * CH :] = proj[0, :, 0:CH].astype(bf16)
    att[CH:, 3 * CH :] = proj[0, :, CH:].astype(bf16)


def prepare_rest_kernel(place, qkv, proj, up, down, mlp0, att1, mlp1, send):
    half = WIDTH // 2
    att1[:, 0 : 3 * CH] = qkv[0].astype(bf16)
    att1[0:CH, 3 * CH :] = proj[0, :, 0:CH].astype(bf16)
    att1[CH:, 3 * CH :] = proj[0, :, CH:].astype(bf16)
    for layer, mlp in enumerate((mlp0, mlp1)):
        mlp[:, 0:HALF] = up[layer].astype(bf16)
        mlp[:, HALF : HALF + WIDTH] = down[layer, 0:WIDTH].astype(bf16)
        mlp[:, HALF + WIDTH :] = down[layer, WIDTH:].astype(bf16)
    mine = pl.ds(place[CORE] * half, half)
    send[:, 0:HALF] = att1[mine]
    send[:, HALF:] = mlp1[mine]


def layer_spec(shape, layer):
    return pl.BlockSpec((1,) + shape[1:], lambda s: (layer, 0, 0))


def run_prepare(place, qkv, proj, up, down):
    half = WIDTH // 2
    qkv, proj, up, down = (pltpu.with_memory_space_constraint(x, pltpu.HBM) for x in (qkv, proj, up, down))
    att0 = pl.pallas_call(
        prepare_first_kernel,
        grid=(1,),
        out_shape=sds((WIDTH, HALF), bf16),
        in_specs=[layer_spec(qkv.shape, 0), layer_spec(proj.shape, 0)],
        out_specs=kept((WIDTH, HALF)),
        compiler_params=params(SMALL),
        cost_estimate=cost(1),
        name="prepare_first",
    )(qkv, proj)
    rest = pl.pallas_call(
        prepare_rest_kernel,
        grid=(1,),
        out_shape=[
            hbm((WIDTH, 2 * HALF), bf16), hbm((WIDTH, HALF), bf16), hbm((WIDTH, 2 * HALF), bf16),
            sds((half, 3 * HALF), bf16),
        ],
        in_specs=[smem_spec(), layer_spec(qkv.shape, 1), layer_spec(proj.shape, 1), kept(up.shape), kept(down.shape)],
        out_specs=[
            kept((WIDTH, 2 * HALF)), kept((WIDTH, HALF)), kept((WIDTH, 2 * HALF)), kept((half, 3 * HALF)),
        ],
        compiler_params=params(SMALL),
        cost_estimate=cost(3),
        name="prepare_rest",
    )(place, qkv, proj, up, down)
    return att0, *rest


def attention_kernel(layer, mine, place, given, *refs):
    if mine:
        att_w, sv, gv, ids_t, part, qkv_o, e_o, rl_o, att_o, heads_o, a1_o, stream, idc, tall = refs
    else:
        stream = given
        att_w, sv, gv, ids_t, part, qkv_o, e_o, rl_o, att_o, idc = refs
    s = pl.program_id(0)

    @pl.when(s == 0)
    def _():
        spread_ids(ids_t, idc)
        if mine:
            tall[0 : SIDE * SIDE] = given[...].astype(f32)
            spread_rows(tall, stream)

    frame = place[GROUP] if mine else 1 - place[GROUP]
    for g in range(2):
        @pl.when(frame == g)
        def _(g=g):
            for n in range(GANG):
                row = GANG * s + n
                a1, qkv, e, rl, att, heads = attend(
                    g, stripe_of(stream, g, row), stripe_of(idc, g, row), qkv_of(att_w), gv[layer],
                    shared_of(sv, layer, 0), shared_of(sv, layer, 1),
                )
                qkv_o[n] = qkv
                e_o[n] = e
                rl_o[n] = rl
                att_o[n] = att
                part[n] = dot(heads, proj_of(att_w)).astype(bf16).astype(f32)
                if mine:
                    heads_o[n] = heads
                    a1_o[n] = a1


ATT_SAVED = [((TOKENS, 3 * CH), bf16), ((TOKENS, KEYS), bf16), ((TOKENS, CH), f32), ((TOKENS, CH), bf16)]


def run_attention(layer, mine, place, stream, weights, sv, gv, ids_t):
    outs = [((ROWS, WIDTH), f32)] + ATT_SAVED + ([((ROWS, CH), bf16), ((ROWS, WIDTH), bf16)] if mine else [])
    inputs = (stream, weights, sv, gv, ids_t)
    return pl.pallas_call(
        functools.partial(attention_kernel, layer, mine),
        grid=(NS // GANG,),
        out_shape=[(sds if n == 0 else hbm)((NS,) + shape, dtype) for n, (shape, dtype) in enumerate(outs)]
        + ([sds(CANVAS, f32)] if mine else []),
        in_specs=[smem_spec()] + [kept(x.shape) for x in inputs],
        out_specs=[per_step(shape, 0, GANG) for shape, _ in outs] + ([kept(CANVAS)] if mine else []),
        scratch_shapes=[pltpu.VMEM((SIDE, NS, SLOT, CH), f32)]
        + ([pltpu.VMEM((SIDE * SIDE + 4, WIDTH), f32)] if mine else []),
        compiler_params=params(SMALL),
        cost_estimate=cost(11),
        name=f"layer{layer}_attention_{'own' if mine else 'other'}",
    )(place, *inputs)


def in_frames(own, mine_h, mine_v, other_h, other_v, n=0):
    def turned(ref):
        columns = [ref[column, pl.ds(STRIPE * n, STRIPE)] for column in range(NS)]
        return jnp.stack(columns, axis=1).reshape(ROWS, WIDTH)

    mine = jnp.where(own == 0, mine_h[n], turned(mine_v))
    other = jnp.where(own == 0, turned(other_v), other_h[n])
    return mine + other


def frame_specs(count=1):
    flat = per_step((ROWS, WIDTH), 0, count)
    tall = pl.BlockSpec((NS, STRIPE * count, SLOT, WIDTH), lambda s: (0, s, 0, 0))
    return [flat, tall, flat, tall]


def frame_views(mine, other):
    shape = (NS, SIDE, SLOT, WIDTH)
    return (mine, mine.reshape(shape), other, other.reshape(shape))


def canvas_block(count=1):
    return pl.BlockSpec((STRIPE * count, NS, SLOT, WIDTH), lambda s: (s, 0, 0, 0))


def feed_kernel(
    layer, place, stream, mine_h, mine_v, other_h, other_v, mlp_w, mlp_o, sv, gv, gvo,
    out, mid, active, slopes,
):
    pairs = [
        (up_of(w, 0), down_of(w, 0), v[layer][:, 12 * CH :]) for w, v in ((mlp_w, gv), (mlp_o, gvo))
    ]
    for n in range(GANG):
        both = in_frames(place[GROUP], mine_h, mine_v, other_h, other_v, n)
        rows = stripe_of(stream, 0, n) + (both + shared_of(sv, layer, 2))
        put_stripe(mid, 0, n, rows)
        new, held, slope = mlp_forward(rows, sv, layer, pairs)
        put_stripe(out, 0, n, new)
        active[n] = held
        slopes[n, 0] = slope[0]
        slopes[n, 1] = slope[1]


def run_feed(layer, place, stream, mine, other, mlp_w, mlp_o, sv, gv, gvo):
    rest = (mlp_w, mlp_o, sv, gv, gvo)
    return pl.pallas_call(
        functools.partial(feed_kernel, layer),
        grid=(NS // GANG,),
        out_shape=[
            hbm(CANVAS, f32), hbm(CANVAS, f32), hbm((NS, ROWS, HALF), bf16), hbm((NS, 2, ROWS, HALF), bf16)
        ],
        in_specs=[smem_spec(), canvas_block(GANG)] + frame_specs(GANG) + [kept(x.shape) for x in rest],
        out_specs=[
            canvas_block(GANG), canvas_block(GANG), per_step((ROWS, HALF), 0, GANG), per_step((2, ROWS, HALF), 0, GANG)
        ],
        compiler_params=params(SMALL),
        cost_estimate=cost(10),
        name=f"layer{layer}_feed_forward",
    )(place, stream, *frame_views(mine, other), *rest)


def last_layer_kernel(
    layer, devices, place, stream, cot, att_w, mlp_w, near, far, sv, gv, gvo, ids_t,
    out, grad_in, send, keep,
    whole, att2, gv2, idc, mid, gmid, gb, qkv_s, e_s, rl_s, att_s, heads_s, active_s, a1_s, dqkv_s, gb_s,
    a2_s, gh_s, gm_s, acc_s, acc_b1, acc_g, tall,
):
    own = place[GROUP]
    assemble(whole, near, far, place[CORE])
    att2[own] = att_w[...]
    att2[1 - own] = whole[:, 0:HALF]
    gv2[own] = gv[layer]
    gv2[1 - own] = gvo[layer]
    spread_ids(ids_t, idc)
    acc_s[...] = jnp.zeros_like(acc_s)
    acc_b1[...] = jnp.zeros_like(acc_b1)
    acc_g[...] = jnp.zeros_like(acc_g)

    for g in range(2):
        def gang(first, carry, g=g):
            for n in range(GANG):
                s = GANG * first + n
                i = g * NS + s
                rows = stripe_of(stream, g, s)
                a1, qkv, e, rl, att, heads = attend(
                    g, rows, stripe_of(idc, g, s), qkv_of(att2[g]), gv2[g],
                    shared_of(sv, layer, 0), shared_of(sv, layer, 1),
                )
                qkv_s[i] = qkv
                e_s[i] = e
                rl_s[i] = rl
                att_s[i] = att
                part = dot(heads, proj_of(att2[g])).astype(bf16).astype(f32)
                if g == 0:
                    put_stripe(mid, g, s, part)
                else:
                    put_stripe(mid, g, s, rows + ((stripe_of(mid, g, s) + part) + shared_of(sv, layer, 2)))
                a1_s[g, s] = a1
                heads_s[g, s] = heads
            return carry

        lax.fori_loop(0, NS // GANG, gang, 0)

    def pairs():
        return [
            (up_of(mlp_w, 0), down_of(mlp_w, 0), gv[layer][:, 12 * CH :]),
            (up_of(whole, HALF), down_of(whole, HALF), gvo[layer][:, 12 * CH :]),
        ]

    tall[0 : SIDE * SIDE] = cot[...].astype(f32)
    spread_rows(tall, gmid)

    def block(s):
        rows = stripe_of(mid, 0, s)
        new, held, slope = mlp_forward(rows, sv, layer, pairs())
        put_stripe(grad_in, 0, s, new)
        active_s[s] = held
        grad = stripe_of(gmid, 0, s)
        new, low, gm, a2, gh, sums = mlp_backward(grad, rows, slope, sv, layer, pairs())
        put_stripe(gmid, 0, s, new)
        put_stripe(gb, 0, s, low.astype(f32))
        gm_s[s] = gm
        a2_s[s] = a2
        gh_s[s] = gh
        for index, value in zip((2, 3, 4, 5), sums):
            acc_s[index] += value
        acc_b1[...] += sums[4]

    def blocks(first, carry):
        for n in range(GANG):
            block(GANG * first + n)
        return carry

    lax.fori_loop(0, NS // GANG, blocks, 0)
    pack_rows(grad_in, tall)
    out[...] = tall[0 : SIDE * SIDE].astype(bf16)

    for g in range(2):
        def gang(first, carry, g=g):
            def add(index, value):
                acc_g[g, index] += value

            for n in range(GANG):
                s = GANG * first + n
                i = g * NS + s
                gbs = stripe_of(gb, g, s).astype(bf16)
                dqkv, part = attend_back(
                    g, gbs, stripe_of(idc, g, s), qkv_of(att2[g]), proj_of(att2[g]), gv2[g], qkv_s[i], e_s[i],
                    rl_s[i], att_s[i], add,
                )
                if g == 0:
                    put_stripe(mid, g, s, part)
                else:
                    put_stripe(mid, g, s, stripe_of(mid, g, s) + part)
                dqkv_s[g, s] = dqkv
                gb_s[g, s] = gbs
            return carry

        lax.fori_loop(0, NS // GANG, gang, 0)

    def final(first, carry):
        for n in range(GANG):
            s = GANG * first + n
            hat, rstd = normed(stripe_of(stream, 0, s))
            da = stripe_of(mid, 0, s)
            acc_s[0] += tile_sum(da * hat)
            acc_s[1] += tile_sum(da)
            put_stripe(
                grad_in, 0, s, stripe_of(gmid, 0, s) + norm_back(da, hat, rstd, shared_of(sv, layer, 0))
            )
        return carry

    lax.fori_loop(0, NS // GANG, final, 0)

    def flat(ref):
        return ref[...].reshape(NS * ROWS, ref.shape[-1])

    core = place[CORE]
    put_chunks(send, keep, core, 0, dot_rows(flat(a1_s.at[own]), flat(dqkv_s.at[own])))
    put_chunks(send, keep, core, 3 * CH, dot_rows(flat(gb_s.at[own]), flat(heads_s.at[own])))
    put_chunks(send, keep, core, HALF, dot_rows(flat(a2_s), flat(gh_s)))
    put_chunks(send, keep, core, 2 * HALF, dot_rows(flat(gm_s), flat(active_s)))
    shared_row = jnp.concatenate([one_row(acc_s[index]) for index in range(6)], axis=1)
    group_row = jnp.concatenate([one_row(acc_g[own, index]) for index in range(12)] + [one_row(acc_b1[...])], axis=1)
    put_chunks(send, keep, core, 3 * HALF, pack_vectors(devices, shared_row, group_row))


def run_last_layer(layer, devices, place, args):
    return pl.pallas_call(
        functools.partial(last_layer_kernel, layer, devices),
        out_shape=[sds((SIDE * SIDE, WIDTH), bf16), sds(CANVAS, f32)] + chunk_shapes(devices),
        in_specs=[smem_spec()] + [vmem_spec()] * len(args),
        out_specs=[vmem_spec()] * 4,
        scratch_shapes=[
            pltpu.VMEM((WIDTH, 3 * HALF), bf16),
            pltpu.VMEM((2, WIDTH, HALF), bf16),
            pltpu.VMEM((2, 1, 16 * CH), f32),
            pltpu.VMEM((SIDE, NS, SLOT, CH), f32),
            pltpu.VMEM(CANVAS, f32),
            pltpu.VMEM(CANVAS, f32),
            pltpu.VMEM(CANVAS, f32),
            pltpu.VMEM((2 * NS, TOKENS, 3 * CH), bf16),
            pltpu.VMEM((2 * NS, TOKENS, KEYS), bf16),
            pltpu.VMEM((2 * NS, TOKENS, CH), f32),
            pltpu.VMEM((2 * NS, TOKENS, CH), bf16),
            pltpu.VMEM((2, NS, ROWS, CH), bf16),
            pltpu.VMEM((NS, ROWS, HALF), bf16),
            pltpu.VMEM((2, NS, ROWS, WIDTH), bf16),
            pltpu.VMEM((2, NS, ROWS, 3 * CH), bf16),
            pltpu.VMEM((2, NS, ROWS, WIDTH), bf16),
            pltpu.VMEM((NS, ROWS, WIDTH), bf16),
            pltpu.VMEM((NS, ROWS, HALF), bf16),
            pltpu.VMEM((NS, ROWS, WIDTH), bf16),
            pltpu.VMEM((6, SLOT, WIDTH), f32),
            pltpu.VMEM((SLOT, HALF), f32),
            pltpu.VMEM((2, 12, SLOT, CH), f32),
            pltpu.VMEM((SIDE * SIDE + 4, WIDTH), f32),
        ],
        compiler_params=params(LARGE),
        cost_estimate=cost(65),
        name=f"layer{layer}_forward_backward",
    )(place, *args)


def feed_back_kernel(
    layer, place, grad, mid, slopes, active, mlp_w, mlp_o, sv, gv, gvo, *refs,
):
    gmid, gb, big, rows_out, bias_out, a2_s, gh_s, gm_s, act_s, acc_s, acc_b1 = refs[-11:]
    s = pl.program_id(0)

    @pl.when(s == 0)
    def _():
        acc_s[...] = jnp.zeros_like(acc_s)
        acc_b1[...] = jnp.zeros_like(acc_b1)

    pairs = [
        (up_of(w, 0), down_of(w, 0), v[layer][:, 12 * CH :]) for w, v in ((mlp_w, gv), (mlp_o, gvo))
    ]
    for n in range(GANG):
        new, low, gm, a2, gh, sums = mlp_backward(
            stripe_of(grad, 0, n), stripe_of(mid, 0, n), [slopes[n, 0], slopes[n, 1]], sv, layer, pairs
        )
        put_stripe(gmid, 0, n, new)
        put_stripe(gb, 0, n, low.astype(f32))
        gm_s[GANG * s + n] = gm
        a2_s[GANG * s + n] = a2
        gh_s[GANG * s + n] = gh
        act_s[GANG * s + n] = active[n]
        for index in range(4):
            acc_s[index] += sums[index]
        acc_b1[...] += sums[4]

    @pl.when(s == NS // GANG - 1)
    def _():
        def flat(ref):
            return ref[...].reshape(NS * ROWS, ref.shape[-1])

        big[:, 0:HALF] = dot_rows(flat(a2_s), flat(gh_s)).astype(bf16)
        big[:, HALF:] = dot_rows(flat(gm_s), flat(act_s)).astype(bf16)
        rows_out[...] = jnp.concatenate([one_row(acc_s[index]) for index in range(4)], axis=1)
        bias_out[...] = one_row(acc_b1[...])


def run_feed_back(layer, place, grad, mid, slopes, active, mlp_w, mlp_o, sv, gv, gvo, after):
    rest = (mlp_w, mlp_o, sv, gv, gvo)
    mid, slopes, active = (pltpu.with_memory_space_constraint(x, pltpu.HBM) for x in (mid, slopes, active))
    return pl.pallas_call(
        functools.partial(feed_back_kernel, layer),
        grid=(NS // GANG,),
        out_shape=[
            sds(CANVAS, f32), sds(CANVAS, f32), sds((WIDTH, 2 * HALF), bf16), sds((1, 4 * WIDTH), f32),
            sds((1, HALF), f32),
        ],
        in_specs=[smem_spec(), canvas_block(GANG), canvas_block(GANG), per_step((2, ROWS, HALF), 0, GANG), per_step((ROWS, HALF), 0, GANG)]
        + [kept(x.shape) for x in rest]
        + waits(after),
        out_specs=[canvas_block(GANG), canvas_block(GANG), kept((WIDTH, 2 * HALF)), kept((1, 4 * WIDTH)), kept((1, HALF))],
        scratch_shapes=[
            pltpu.VMEM((NS, ROWS, WIDTH), bf16),
            pltpu.VMEM((NS, ROWS, HALF), bf16),
            pltpu.VMEM((NS, ROWS, WIDTH), bf16),
            pltpu.VMEM((NS, ROWS, HALF), bf16),
            pltpu.VMEM((4, SLOT, WIDTH), f32),
            pltpu.VMEM((SLOT, HALF), f32),
        ],
        compiler_params=params(SMALL),
        cost_estimate=cost(11),
        name=f"layer{layer}_feed_backward",
    )(place, grad, mid, slopes, active, *rest, *after)


def attention_back_kernel(layer, mine, devices, place, gb, qkv, e, rl, att, *refs):
    if mine:
        att_w, sv, gv, ids_t, heads, a1, big_m, rows_m, bias_m = refs[:9]
        da, big, idc, dqkv_s, gb_s, acc_g = refs[-6:]
    else:
        att_w, sv, gv, ids_t = refs[:4]
        da, idc = refs[-2:]
    step = pl.program_id(0)

    @pl.when(step == 0)
    def _():
        spread_ids(ids_t, idc)
        if mine:
            acc_g[...] = jnp.zeros_like(acc_g)

    def add(index, value):
        acc_g[index] += value

    frame = place[GROUP] if mine else 1 - place[GROUP]
    for g in range(2):
        @pl.when(frame == g)
        def _(g=g):
            for n in range(GANG):
                s = GANG * step + n
                gbs = stripe_of(gb, g, s).astype(bf16)
                dqkv, part = attend_back(
                    g, gbs, stripe_of(idc, g, s), qkv_of(att_w), proj_of(att_w), gv[layer], qkv[n], e[n], rl[n], att[n],
                    add if mine else None,
                )
                da[n] = part
                if mine:
                    dqkv_s[s] = dqkv
                    gb_s[s] = gbs

    if mine:
        @pl.when(step == NS // GANG - 1)
        def _():
            def flat(ref):
                return ref[...].reshape(NS * ROWS, ref.shape[-1])

            big[:, 0 : 3 * CH] = dot_rows(flat(a1), flat(dqkv_s)).astype(bf16)
            big[:, 3 * CH : HALF] = dot_rows(flat(gb_s), flat(heads)).astype(bf16)
            big[:, HALF : 3 * HALF] = big_m[...]
            shared_row = jnp.concatenate([jnp.zeros((1, 2 * WIDTH), f32), rows_m[...]], axis=1)
            group_row = jnp.concatenate([one_row(acc_g[index]) for index in range(12)] + [bias_m[...]], axis=1)
            big[:, 3 * HALF :] = pack_vectors(devices, shared_row, group_row).astype(bf16)


def run_attention_back(layer, mine, devices, place, gb, saved, weights, sv, gv, ids_t, extra, after):
    rest = (weights, sv, gv, ids_t, *extra)
    outs = [sds((NS, ROWS, WIDTH), f32)]
    out_specs = [per_step((ROWS, WIDTH), 0, GANG)]
    scratch = [pltpu.VMEM((SIDE, NS, SLOT, CH), f32)]
    if mine:
        outs.append(sds((WIDTH, 3 * HALF + 2 * CH), bf16))
        out_specs.append(kept(outs[1].shape))
        scratch += [
            pltpu.VMEM((NS, ROWS, 3 * CH), bf16),
            pltpu.VMEM((NS, ROWS, WIDTH), bf16),
            pltpu.VMEM((12, SLOT, CH), f32),
        ]
    inputs = (place, gb, *saved, *rest, *after)
    return pl.pallas_call(
        functools.partial(attention_back_kernel, layer, mine, devices),
        grid=(NS // GANG,),
        out_shape=outs,
        in_specs=[smem_spec(), kept(CANVAS)]
        + [per_step(shape, 0, GANG) for shape, _ in ATT_SAVED]
        + [kept(x.shape) for x in rest]
        + waits(after),
        out_specs=out_specs,
        scratch_shapes=scratch,
        compiler_params=params(SMALL),
        cost_estimate=cost(10),
        name=f"layer{layer}_attention_back_{'own' if mine else 'other'}",
    )(*inputs)


def norm_back_kernel(layer, place, stream, gmid, mine_h, mine_v, other_h, other_v, sv, *refs):
    out, sums, grad_in, acc = refs[-4:]
    s = pl.program_id(0)

    @pl.when(s == 0)
    def _():
        acc[...] = jnp.zeros_like(acc)

    for n in range(GANG):
        da = in_frames(place[GROUP], mine_h, mine_v, other_h, other_v, n)
        hat, rstd = normed(stripe_of(stream, 0, n))
        acc[0] += tile_sum(da * hat)
        acc[1] += tile_sum(da)
        new = stripe_of(gmid, 0, n) + norm_back(da, hat, rstd, shared_of(sv, layer, 0))
        put_stripe(grad_in, 0, GANG * s + n, new)

    @pl.when(s == NS // GANG - 1)
    def _():
        pack_rows(grad_in, out)
        sums[...] = jnp.concatenate([one_row(acc[0]), one_row(acc[1])], axis=1)


def run_norm_back(layer, place, stream, gmid, mine, other, sv, after):
    return pl.pallas_call(
        functools.partial(norm_back_kernel, layer),
        grid=(NS // GANG,),
        out_shape=[sds((SIDE * SIDE, WIDTH), f32), sds((1, 2 * WIDTH), f32)],
        in_specs=[smem_spec(), canvas_block(GANG), canvas_block(GANG)] + frame_specs(GANG) + [kept(sv.shape)] + waits(after),
        out_specs=[kept((SIDE * SIDE, WIDTH)), kept((1, 2 * WIDTH))],
        scratch_shapes=[pltpu.VMEM(CANVAS, f32), pltpu.VMEM((2, SLOT, WIDTH), f32)],
        compiler_params=params(SMALL),
        cost_estimate=cost(4),
        name=f"layer{layer}_norm_backward",
    )(place, stream, gmid, *frame_views(mine, other), sv, *after)


def halves_of(x):
    high = x.astype(bf16)
    return high, (x - high.astype(f32)).astype(bf16)


def split_dot(a, b, dims):
    (a_high, a_low), (b_high, b_low) = halves_of(a), halves_of(b)
    left = jnp.concatenate([a_high, a_high, a_low], axis=1)
    right = jnp.concatenate([b_high, b_low, b_high], axis=dims[1][0])
    return lax.dot_general(left, right, (dims, ((), ())), preferred_element_type=f32)


SPANS = ((0, 3 * CH), (3 * CH, HALF), (HALF, 2 * HALF), (2 * HALF, 3 * HALF))


def own_rows(ref, index, rows):
    if rows % SLOT == 0:
        return ref[pl.ds(pl.multiple_of(index * rows, SLOT), rows)]
    start = index * rows
    base = pl.multiple_of((start // SLOT) * SLOT, SLOT)
    return pltpu.roll(ref[pl.ds(base, SLOT)], SLOT - (start - base), 0)[0:rows]


def sums_width(rows):
    return max(CH, SLOT * CH // rows)


def sums_blocks(rows):
    per = sums_width(rows) // CH
    return [(b // per, 3 * HALF + (b % per) * CH) for b in range(SLOT)]


def read_sums(ref, rows):
    blocks = [ref[row : row + 1, lane : lane + CH].astype(f32) for row, lane in sums_blocks(rows)]
    return jnp.concatenate([blocks[n] + blocks[n + 4] for n in range(4)], axis=1)


def with_sums(matrix, sums):
    rows, width = matrix.shape[0], sums_width(matrix.shape[0])
    high, low = halves_of(sums)
    parts = [x[:, n * CH : (n + 1) * CH] for x in (high, low) for n in range(4)]
    per = width // CH
    lines = [jnp.concatenate(parts[n : n + per], axis=1) for n in range(0, SLOT, per)]
    if rows > len(lines):
        lines.append(jnp.zeros((rows - len(lines), width), bf16))
    beside = jnp.concatenate([x.astype(f32) for x in lines], axis=0).astype(bf16)
    return jnp.concatenate([matrix, beside], axis=1)


def momentum_kernel(layer, n_got, place, keep, *refs):
    gots, (qkv, proj, up, down, extra, whole, fresh, vectors), refs = refs[:n_got], refs[n_got : n_got + 8], refs[n_got + 8 :]
    total = keep[0].astype(f32)
    for got in gots:
        total = total + got[0].astype(f32)
    matrix = total[:, 0 : 3 * HALF]
    old = jnp.concatenate([qkv[layer], proj[layer], up[layer], down[layer]], axis=1)
    new = momentum_decay * old + matrix
    fresh[...] = new
    ahead = (matrix + momentum_decay * new).astype(bf16)
    vectors[...] = total[0:1, 3 * HALF :]
    if layer == 0:
        whole[0] = with_sums(ahead, extra[...])
    else:
        whole[0] = ahead
        put_chunks(*refs, place[CORE], 0, extra[...].astype(f32))


def run_momentum(layer, devices, place, keep, gots, moments, extra):
    rows = keep.shape[1]
    width = 3 * HALF + (0 if layer else sums_width(rows))
    outs = [sds((1, rows, width), bf16), hbm((rows, 3 * HALF), f32), sds((1, 2 * CH), f32)]
    if layer:
        outs += chunk_shapes(devices)
    return pl.pallas_call(
        functools.partial(momentum_kernel, layer, len(gots)),
        out_shape=outs,
        in_specs=[smem_spec()] + [vmem_spec()] * (6 + len(gots)),
        out_specs=[vmem_spec()] * len(outs),
        compiler_params=params(SMALL),
        cost_estimate=cost(1),
        name=f"layer{layer}_momentum",
    )(place, keep, *gots, *moments, extra)


def square_dot(x, dims):
    high, low = halves_of(x)
    mixed = lax.dot_general(high, low, (dims, ((), ())), preferred_element_type=f32)
    return lax.dot_general(high, high, (dims, ((), ())), preferred_element_type=f32) + (mixed + mixed.T)


def newton(works, steps):
    for _ in range(steps):
        grams = [square_dot(work, ((1,), (1,))) for work in works]
        blends = [coeff_second * gram + coeff_third * square_dot(gram, ((1,), (0,))) for gram in grams]
        works = [
            coeff_first * work + split_dot(blend, work, ((1,), (0,)))
            for work, blend in zip(works, blends)
        ]
    return works


def newton_from(whole, steps):
    lows = [whole[:, start:stop] for start, stop in SPANS]
    works = [low.astype(f32) for low in lows]
    works[1] = works[1].T
    lows[1] = works[1].astype(bf16)
    factors = [1.0 / (jnp.sqrt(jnp.sum(work * work)) + 1e-07) for work in works]
    grams = [dot_t(low, low) * (factor * factor) for low, factor in zip(lows, factors)]
    blends = [coeff_second * gram + coeff_third * square_dot(gram, ((1,), (0,))) for gram in grams]
    works = [
        (coeff_first * work + dot(jnp.concatenate(halves_of(blend), axis=1), jnp.concatenate([low, low], axis=0))) * factor
        for work, low, blend, factor in zip(works, lows, blends, factors)
    ]
    return newton(works, steps - 1)


def old_rows(layer, index, rows, masters, turned):
    parts = []
    for which, master in enumerate(masters):
        width = SPANS[which][1] - SPANS[which][0]
        if which % 2 == 1:
            turned[:, 0:width] = master[layer].T
            parts.append(own_rows(turned, index, rows)[:, 0:width])
        else:
            parts.append(own_rows(master.at[layer], index, rows))
    return parts


def new_rows(index, rows, works, old, rows_s):
    for which, work in enumerate(works):
        start, stop = SPANS[which]
        rows_s[:, 0 : stop - start] = work.T if which == 1 else work
        step = own_rows(rows_s, index, rows)[:, 0 : stop - start]
        size = matrix_rate * match_scale * math.sqrt(max(work.shape) if which != 3 else HALF)
        yield which, old[:, start:stop] * (1.0 - matrix_rate * weight_decay) - size * step


def newton_begin_kernel(steps, place, whole, qkv, proj, up, down, *refs):
    old = refs[-3:-1]
    for layer in range(LAYERS):
        parts = old_rows(layer, place[INDEX], old[layer].shape[0], (qkv, proj, up, down), refs[-1])
        for (start, stop), part in zip(SPANS, parts):
            old[layer][:, start:stop] = part
    for out, work in zip(refs[-7:-3], newton_from(whole, steps)):
        out[...] = work


def newton_go_on_kernel(steps, *refs):
    for out, work in zip(refs[-4:], newton([ref[...] for ref in refs[:4]], steps)):
        out[...] = work


def newton_end_kernel(steps, place, old, *refs):
    out, rows_s = refs[-2:]
    works = newton([ref[...] for ref in refs[:4]], steps)
    for which, new in new_rows(place[INDEX], out.shape[0], works, old, rows_s):
        out[:, SPANS[which][0] : SPANS[which][1]] = new


WORKS = [sds((CH if n == 1 else WIDTH, WIDTH if n == 1 else stop - start), f32) for n, (start, stop) in enumerate(SPANS)]


def run_newton_begin(steps, place, rows, whole, masters, after):
    return pl.pallas_call(
        functools.partial(newton_begin_kernel, steps),
        out_shape=WORKS + [hbm((rows, 3 * HALF), f32)] * 2,
        in_specs=[smem_spec()] + [vmem_spec()] * 5 + waits(after),
        out_specs=[vmem_spec()] * 6,
        scratch_shapes=[pltpu.VMEM((WIDTH, HALF), f32)],
        compiler_params=params(SMALL),
        cost_estimate=cost(2 * steps),
        name="layer1_newton_begin",
    )(place, whole, *masters, *after)


def run_newton_go_on(steps, works, after):
    return pl.pallas_call(
        functools.partial(newton_go_on_kernel, steps),
        out_shape=WORKS,
        in_specs=[vmem_spec()] * 4 + waits(after),
        out_specs=[vmem_spec()] * 4,
        compiler_params=params(SMALL),
        cost_estimate=cost(2 * steps),
        name="layer1_newton_go_on",
    )(*works, *after)


def run_newton_end(steps, place, old, works, after):
    return pl.pallas_call(
        functools.partial(newton_end_kernel, steps),
        out_shape=sds(old.shape, f32),
        in_specs=[smem_spec()] + [vmem_spec()] * 5 + waits(after),
        out_specs=vmem_spec(),
        scratch_shapes=[pltpu.VMEM((WIDTH, HALF), f32)],
        compiler_params=params(SMALL),
        cost_estimate=cost(2 * steps),
        name="layer1_newton_end",
    )(place, old, *works, *after)


def finish_kernel(place, whole, old, fresh0, fresh1, step1, vectors0, vectors1, *refs):
    shared_m, group_m, shared_w, group_w = refs[0:4]
    outs = refs[4:-1]
    rows_s = refs[-1]
    for layer, fresh in enumerate((fresh0, fresh1)):
        for which, (start, stop) in enumerate(SPANS):
            outs[2 * which][layer] = fresh[:, start:stop]
    for which, (start, stop) in enumerate(SPANS):
        outs[2 * which + 1][1] = step1[:, start:stop]
    wide, own = shared_m.shape[1], group_m.shape[2]
    late = jnp.concatenate([read_sums(whole, fresh0.shape[0]), jnp.zeros((1, 4 * WIDTH), f32)], axis=1)
    late = jnp.broadcast_to(late, (SLOT, 6 * WIDTH))
    late = pltpu.roll(late, lax.rem(6 * WIDTH - place[INDEX] * wide, 6 * WIDTH), 1)[0:1, 0:wide]
    for layer, vectors in enumerate((vectors0, vectors1)):
        grad = vectors[:, 0:wide]
        if layer == 0:
            grad = grad + late
        new = momentum_decay * shared_m[layer : layer + 1, :] + grad
        outs[8][layer : layer + 1, :] = new
        outs[9][layer : layer + 1, :] = shared_w[layer : layer + 1, :] - vector_rate * new
        new = momentum_decay * group_m[layer] + vectors[:, CH : CH + own]
        outs[10][layer] = new
        outs[11][layer] = group_w[layer] - vector_rate * new
    works = newton_from(whole, NS_STEPS)
    for which, new in new_rows(place[INDEX], fresh0.shape[0], works, old, rows_s):
        outs[2 * which + 1][0] = new


def run_finish(rows, place, *args):
    shapes = []
    for start, stop in SPANS:
        shapes += [sds((LAYERS, rows, stop - start), f32)] * 2
    shapes += [sds(args[7].shape, f32)] * 2 + [sds(args[8].shape, f32)] * 2
    return pl.pallas_call(
        finish_kernel,
        out_shape=shapes,
        in_specs=[smem_spec()] + [vmem_spec()] * len(args),
        out_specs=[vmem_spec()] * len(shapes),
        scratch_shapes=[pltpu.VMEM((WIDTH, HALF), f32)],
        compiler_params=params(SMALL),
        cost_estimate=cost(10),
        name="layer0_newton_finish",
    )(place, *args)


def stages_of(devices):
    bits = [1 << n for n in range(devices.bit_length() - 1)]
    stages = [(bit,) for bit in bits[:2]]
    return stages + [tuple(bits[n : n + 2]) for n in range(2, len(bits), 2)]


def peers(stage):
    return [x * stage[0] for x in range(1, 1 << len(stage))]


def swap(x, axis, mask):
    n = lax.axis_size(axis)
    return lax.ppermute(x, axis, [(i, i ^ mask) for i in range(n)])


def send_parts(parts, stage):
    return [swap(part, "dp", mask) for part, mask in zip(parts, peers(stage))]


def send_all(held, stage):
    return [swap(held, "dp", mask) for mask in peers(stage)]


def part_chunks(stage, index, total, outs):
    radix = 1 << len(stage)
    own = (index // stage[0]) % radix
    for m in range(outs[0].shape[0]):
        for x in range(radix):
            outs[x - 1][m] = total(radix * m + (own ^ x)).astype(bf16)


def join_chunks(stage, index, held, gots, out):
    radix = 1 << len(stage)
    own = (index // stage[0]) % radix
    for m in range(held.shape[0]):
        for x, ref in enumerate((held, *gots)):
            out[radix * m + (own ^ x)] = ref[m]
    rows = held.shape[1]
    if held.shape[2] > 3 * HALF:
        sums = read_sums(held.at[0], rows)
        for ref in gots:
            sums = sums + read_sums(ref.at[0], rows)
        out[0] = with_sums(out[0, :, 0 : 3 * HALF], sums)


def hop_kernel(joined, parted, place, *refs):
    index = place[INDEX]
    counts = [0 if stage is None else 1 << len(stage) for stage in (joined, parted and parted[0])]
    given, taken = refs[: counts[0]], refs[counts[0] : counts[0] + counts[1]]
    outs = list(refs[len(refs) - (joined is not None) - (0 if parted is None else 1 << len(parted[1])) :])
    if joined is not None:
        join_chunks(joined, index, given[0], given[1:], outs.pop(0))
    if parted is not None:
        def total(n):
            value = taken[0][n].astype(f32)
            for ref in taken[1:]:
                value = value + ref[n].astype(f32)
            return value

        part_chunks(parted[1], index, total, outs)


def run_hop(place, join=None, part=None, after=()):
    shapes, inputs = [], []
    if join is not None:
        stage, held, gots = join
        shapes.append(sds((held.shape[0] << len(stage),) + held.shape[1:], bf16))
        inputs += [held, *gots]
    if part is not None:
        _, stage, keep, gots = part
        shapes += [sds((keep.shape[0] >> len(stage),) + keep.shape[1:], bf16)] * (1 << len(stage))
        inputs += [keep, *gots]
    kernel = functools.partial(hop_kernel, join and join[0], part and part[:2])
    outs = pl.pallas_call(
        kernel,
        out_shape=shapes,
        in_specs=[smem_spec()] + [vmem_spec()] * len(inputs) + waits(after),
        out_specs=[vmem_spec()] * len(shapes),
        compiler_params=params(SMALL),
        cost_estimate=cost(1),
        name="hop",
    )(place, *inputs, *after)
    joined = outs[0] if join is not None else None
    parts = outs[(join is not None) :]
    return (joined, parts[:-1], parts[-1]) if part is not None else joined


def local(
    tokens, cotangent, image_ids, qkv_weight, proj_weight, up_weight, down_weight, shared_vectors, group_vectors,
    qkv_moment, proj_moment, up_moment, down_moment, shared_moment, group_moment,
):
    devices = lax.axis_size("dp")
    index = lax.axis_index("dp")
    place = jnp.stack([index % 2, lax.axis_index("group"), index]).astype(jnp.int32)
    masters = (qkv_weight, proj_weight, up_weight, down_weight)
    moments = (qkv_moment, jnp.swapaxes(proj_moment, 1, 2), up_moment, jnp.swapaxes(down_moment, 1, 2))
    rows = WIDTH // devices
    stages = stages_of(devices)

    att0, mlp0, att1, mlp1, send = run_prepare(place, *masters)
    att0_o = swap(att0, "group", 1)
    gv, gvo = group_vectors, swap(group_vectors, "group", 1)
    mlp0_o = swap(mlp0, "group", 1)
    near = swap(send, "group", 1)
    far = swap(near, "dp", 1)
    sv = shared_vectors

    columns = jnp.swapaxes(image_ids[0].astype(f32), 0, 1).reshape(NS, STRIPE, SIDE)
    ids_t = jnp.pad(columns, ((0, 0), (0, 1), (0, 0)), constant_values=-1.0).reshape(NS * SLOT, SIDE)

    part_own, *rest_own, stream = run_attention(0, True, place, tokens, att0, sv, gv, ids_t)
    saved_own, own_kept = rest_own[:4], rest_own[4:]
    part_other, *saved_other = run_attention(0, False, place, stream, att0_o, sv, gvo, ids_t)
    middle, mid, active, slopes = run_feed(0, place, stream, part_own, part_other, mlp0, mlp0_o, sv, gv, gvo)
    outputs, grad, send1, keep1 = run_last_layer(
        1, devices, place, (middle, cotangent, att1, mlp1, near, far, sv, gv, gvo, ids_t)
    )

    def reduce_late(keep, gots, first):
        for stage, after in zip(stages[first:], stages[first + 1 :]):
            _, parts, keep = run_hop(place, part=(stage, after, keep, gots))
            gots = send_parts(parts, after)
        return keep, gots

    keep1 = pltpu.with_memory_space_constraint(keep1, pltpu.HBM)
    got1 = send_parts([send1], stages[0])
    _, parts, keep1 = run_hop(place, part=(stages[0], stages[1], keep1, got1))
    got1 = send_parts(parts, stages[1])
    gmid, gb, big_m, rows_m, bias_m = run_feed_back(
        0, place, grad, mid, slopes, active, mlp0, mlp0_o, sv, gv, gvo, (keep1,)
    )

    def back(mine, extra, after):
        saved, weights, vec = (saved_own, att0, gv) if mine else (saved_other, att0_o, gvo)
        return run_attention_back(0, mine, devices, place, gb, saved, weights, sv, vec, ids_t, extra, after)

    _, parts, keep1 = run_hop(place, part=(stages[1], stages[2], keep1, got1), after=(rows_m,))
    got1 = send_parts(parts, stages[2])
    da_own, big0 = back(True, (*own_kept, big_m, rows_m, bias_m), (keep1,))
    keep1, got1 = reduce_late(keep1, got1, 2)
    held1, fresh1, vectors1, send0, keep0 = run_momentum(1, devices, place, keep1, got1, moments, big0)
    got1 = send_all(held1, stages[-1])
    got0 = send_parts([send0], stages[0])
    _, parts, keep0 = run_hop(place, part=(stages[0], stages[1], keep0, got0))
    got0 = send_parts(parts, stages[1])
    (da_other,) = back(False, (), (keep0, held1))
    for stage in stages[-1:2:-1]:
        held1 = run_hop(place, join=(stage, held1, got1))
        got1 = send_all(held1, stages[stages.index(stage) - 1])
    held1, parts, keep0 = run_hop(
        place, join=(stages[2], held1, got1), part=(stages[1], stages[2], keep0, got0), after=(da_other,)
    )
    got1 = send_all(held1, stages[1])
    got0 = send_parts(parts, stages[2])
    input_grad, norm_sums = run_norm_back(0, place, stream, gmid, da_own, da_other, sv, (keep0, held1))
    keep0, got0 = reduce_late(keep0, got0, 2)
    held0, fresh0, vectors0 = run_momentum(0, devices, place, keep0, got0, moments, norm_sums)
    got0 = send_all(held0, stages[-1])
    held1 = run_hop(place, join=(stages[1], held1, got1), after=(held0,))
    held1 = run_hop(place, join=(stages[0], held1, send_all(held1, stages[0])))

    *works, old0, old1 = run_newton_begin(3, place, rows, held1.reshape(WIDTH, 3 * HALF), masters, (held0,))
    for stage in stages[-1:2:-1]:
        held0 = run_hop(place, join=(stage, held0, got0))
        got0 = send_all(held0, stages[stages.index(stage) - 1])
    held0 = run_hop(place, join=(stages[2], held0, got0), after=(works[0],))
    got0 = send_all(held0, stages[1])
    step1 = run_newton_end(NS_STEPS - 3, place, old1, works, (held0,))
    held0 = run_hop(place, join=(stages[1], held0, got0), after=(step1,))
    held0 = run_hop(place, join=(stages[0], held0, send_all(held0, stages[0])))
    whole0 = held0.reshape(WIDTH, held0.shape[2])

    length = shared_moment.shape[1]
    shared_w = lax.dynamic_slice_in_dim(shared_vectors, index * length, length, 1)
    length = group_moment.shape[2]
    group_w = lax.dynamic_slice_in_dim(group_vectors, index * length, length, 2)
    out = run_finish(
        rows, place, whole0, old0, fresh0, fresh1, step1, vectors0, vectors1,
        shared_moment, group_moment, shared_w, group_w,
    )
    out = [jnp.swapaxes(x, 1, 2) if n in (2, 3, 6, 7) else x for n, x in enumerate(out)]
    return (outputs, input_grad, *out)


def solution(mesh):
    return jax.shard_map(
        local,
        mesh=mesh,
        in_specs=(
            P("dp", None),
            P("dp", None),
            P("dp", None, None),
            P(None, None, "group"),
            P(None, "group", None),
            P(None, None, "group"),
            P(None, "group", None),
            P(),
            P(None, "group", None),
            P(None, "dp", "group"),
            P(None, "group", "dp"),
            P(None, "dp", "group"),
            P(None, "group", "dp"),
            P(None, "dp"),
            P(None, "group", "dp"),
        ),
        out_specs=(
            P("dp", None),
            P("dp", None),
            P(None, "dp", "group"),
            P(None, "dp", "group"),
            P(None, "group", "dp"),
            P(None, "group", "dp"),
            P(None, "dp", "group"),
            P(None, "dp", "group"),
            P(None, "group", "dp"),
            P(None, "group", "dp"),
            P(None, "dp"),
            P(None, "dp"),
            P(None, "group", "dp"),
            P(None, "group", "dp"),
        ),
        check_vma=False,
    )
```

```python
import functools
import math

import jax
import jax.numpy as jnp
from jax import lax
from jax.experimental import pallas as pl
from jax.experimental.pallas import tpu as pltpu
from jax.sharding import PartitionSpec as P

HEADS = 8
STRIPE = 7
LAYERS = 2
NS_STEPS = 5

epsilon = 1e-05
coeff_first = 3.4445
coeff_second = -4.775
coeff_third = 2.0315
momentum_decay = 0.95
matrix_rate = 0.25
weight_decay = 0.1
vector_rate = 0.001
match_scale = 0.2
masked_score = -1e30

f32 = jnp.float32
bf16 = jnp.bfloat16
LOG2E = 1.4426950408889634
MIB = 1024 * 1024
SMALL, LARGE = 32, 62

SIDE = 42
NS = 6
FA_GANG = 2
GANG = 3
SLOT = 8
ROWS = SIDE * SLOT
KEPT = 208
TOKENS = 320
KEYS = 5 * 256
WIDTH = 256
CH = 128
HALF = 512
HL = 4
HEAD = 32


def dot(a, b):
    return jnp.dot(a, b, preferred_element_type=f32)


def dot_t(a, b):
    return lax.dot_general(a, b, (((1,), (1,)), ((), ())), preferred_element_type=f32)


def dot_rows(a, b):
    return lax.dot_general(a, b, (((0,), (0,)), ((), ())), preferred_element_type=f32)


def lane_head():
    return lax.broadcasted_iota(jnp.int32, (1, CH), 1) // HEAD


def stripe_of(ref, g, s):
    if g == 0:
        block = ref[pl.ds(STRIPE * s, STRIPE)]
    else:
        block = ref[:, pl.ds(s, 1)]
    return block.reshape(ROWS, block.shape[-1])


def put_stripe(ref, g, s, value):
    if g == 0:
        ref[pl.ds(STRIPE * s, STRIPE)] = value.reshape(STRIPE, NS, SLOT, value.shape[-1])
    else:
        ref[:, pl.ds(s, 1)] = value.reshape(SIDE, 1, SLOT, value.shape[-1])


def normed(rows):
    mean = jnp.mean(rows, axis=-1, keepdims=True)
    centred = rows - mean
    spread = jnp.mean(centred * centred, axis=-1, keepdims=True)
    rstd = lax.rsqrt(spread + epsilon)
    return centred * rstd, rstd


def norm_back(grad, hat, rstd, gain):
    scaled = grad * gain
    first = jnp.mean(scaled, axis=-1, keepdims=True)
    second = jnp.mean(scaled * hat, axis=-1, keepdims=True)
    return rstd * (scaled - first - hat * second)


def tile_sum(rows):
    return jnp.sum(rows.reshape(-1, SLOT, rows.shape[-1]), axis=0)


def gelu_parts(x):
    phi = 0.5 + 0.5 * lax.erf(x * math.sqrt(0.5))
    bell = jnp.exp2(x * x * (-0.5 * LOG2E))
    return x * phi, phi + x * bell * (1.0 / math.sqrt(2.0 * math.pi))


def places(ndim):
    shape = (1,) * (ndim - 2) + (SLOT, 1)
    return lax.broadcasted_iota(jnp.int32, shape, ndim - 2)


def fine_shifts(x, g, edge):
    axis = x.ndim - 2
    place = places(x.ndim)
    up = pltpu.roll(x, SLOT - 1, axis)
    down = pltpu.roll(x, 1, axis)
    if g == 0:
        end = x[:, :1] if edge is None else jnp.full_like(x[:, :1], edge)
        after = jnp.concatenate([x[:, 1:], end], axis=1)
        before = jnp.concatenate([end, x[:, :-1]], axis=1)
        up = jnp.where(place == STRIPE - 1, pltpu.roll(after, STRIPE - 1, axis), up)
        down = jnp.where(place == 0, pltpu.roll(before, 2, axis), down)
        if edge is not None:
            up = jnp.where(place == STRIPE, edge, up)
            down = jnp.where(place == STRIPE, edge, down)
    elif edge is not None:
        up = jnp.where(place >= STRIPE - 1, edge, up)
        down = jnp.where((place == 0) | (place == STRIPE), edge, down)
    return up, down


def coarse(x, step, fill):
    if step == 0:
        return x
    end = jnp.full_like(x[:1], fill)
    if step > 0:
        return jnp.concatenate([x[1:], end], axis=0)
    return jnp.concatenate([end, x[:-1]], axis=0)


def masked_neighbours(x, ids, g):
    shape = (STRIPE, NS, SLOT, CH) if g == 0 else (SIDE, SLOT, CH)
    x = x.reshape(shape)
    centre = ids.reshape(shape)
    up, down = fine_shifts(x, g, None)
    up_ids, down_ids = fine_shifts(centre, g, -3.0)
    around = {0: (x, centre), 1: (up, up_ids), -1: (down, down_ids)}
    for row_step in (-1, 0, 1):
        for col_step in (-1, 0, 1):
            tap = 3 * (row_step + 1) + col_step + 1
            coarse_step, fine_step = (row_step, col_step) if g == 0 else (col_step, row_step)
            source, source_ids = around[fine_step]
            if coarse_step == 0 and fine_step == 0:
                yield tap, source.reshape(ROWS, CH)
                continue
            source = coarse(source, coarse_step, 0.0)
            source_ids = coarse(source_ids, coarse_step, -9.0)
            yield tap, jnp.where(source_ids == centre, source, 0.0).reshape(ROWS, CH)


def compact(x):
    width = x.shape[1]
    tiles = x[KEPT:].reshape(2, SLOT, SLOT, width)
    place = lax.broadcasted_iota(jnp.int32, (1, SLOT, 1), 1)
    parts = []
    for j in range(STRIPE):
        first, second = tiles[:, j], pltpu.roll(tiles[:, j + 1], STRIPE - j, 1)
        if j:
            first = pltpu.roll(first, SLOT - j, 1)
        parts.append(jnp.where(place < STRIPE - j, first, second))
    return jnp.concatenate([x[:KEPT], jnp.stack(parts, axis=1).reshape(TOKENS - KEPT, width)], axis=0)


def expand(x):
    width = x.shape[1]
    tiles = x[KEPT:].reshape(2, STRIPE, SLOT, width)
    place = lax.broadcasted_iota(jnp.int32, (1, SLOT, 1), 1)
    parts = [tiles[:, 0]]
    for t in range(1, STRIPE):
        both = pltpu.roll(tiles[:, t - 1], t, 1), pltpu.roll(tiles[:, t], t, 1)
        parts.append(jnp.where(place < t, *both))
    parts.append(pltpu.roll(tiles[:, STRIPE - 1], STRIPE, 1))
    parts = [jnp.where(place < STRIPE, part, 0.0) for part in parts]
    return jnp.concatenate([x[:KEPT], jnp.stack(parts, axis=1).reshape(ROWS - KEPT, width)], axis=0)


WIDE, TAIL = 256, 64


def by_heads(pieces):
    parts = [pieces(h) for h in range(HL)]
    return jnp.concatenate([part[0] for part in parts] + [part[1] for part in parts], axis=0)


def block_diagonal(x):
    head = lane_head()

    def pieces(h):
        own = x * jnp.where(head == h, 1.0, 0.0).astype(bf16)
        return own[:WIDE], own[WIDE:]

    return by_heads(pieces)


def lane_marks(pick):
    lane = lax.broadcasted_iota(jnp.int32, (1, CH), 1)

    def pieces(h):
        mark = jnp.where(pick(lane, h), 1.0, 0.0).astype(bf16)
        return jnp.broadcast_to(mark, (WIDE, CH)), jnp.broadcast_to(mark, (TAIL, CH))

    return by_heads(pieces)


def turned(x):
    return jnp.concatenate([x, jnp.zeros((3 * CH - TOKENS, CH), x.dtype)], axis=0).T[:, 0:TOKENS]


def head_rows(x, h):
    return x[h * HEAD : (h + 1) * HEAD]


def over_queries(left, weights):
    main = [dot(head_rows(left, h), weights[:, h * WIDE : (h + 1) * WIDE]) for h in range(HL)]
    tails = dot(left, weights[:, HL * WIDE :])
    last = []
    for h in range(HL):
        own = head_rows(tails, h)[:, (h // 2) * CH : (h // 2 + 1) * CH]
        last.append(pltpu.roll(own, TAIL, 1) if h % 2 else own)
    return jnp.concatenate([jnp.concatenate(main, axis=0), jnp.concatenate(last, axis=0)], axis=1)


def masked_softmax(q, keys, bias):
    tails = dot_t(q, keys[HL * WIDE :])
    left = lax.broadcasted_iota(jnp.int32, (1, CH), 1) < TAIL
    lowest = jnp.finfo(f32).min
    parts, last = [], []
    for h in range(0, HL, 2):
        scores = dot_t(q, keys[h * WIDE : (h + 2) * WIDE])
        own = [scores[:, n * CH : (n + 1) * CH] + bias[n % 2] for n in range(4)]
        tail = tails[:, (h // 2) * CH : (h // 2 + 1) * CH] + bias[2]
        top = jnp.maximum(jnp.maximum(own[0], own[1]), jnp.where(left, tail, lowest))
        other = jnp.maximum(jnp.maximum(own[2], own[3]), jnp.where(left, lowest, tail))
        top = jnp.max(top, axis=-1, keepdims=True)
        other = jnp.max(other, axis=-1, keepdims=True)
        parts += [jnp.exp2(x - y).astype(bf16) for x, y in zip(own, (top, top, other, other))]
        last.append(jnp.exp2(tail - jnp.where(left, top, other)).astype(bf16))
    return jnp.concatenate(parts + last, axis=1)


def spread_ids(ids_t, idc):
    for r in range(SIDE):
        column = jnp.broadcast_to(ids_t[:, r : r + 1], (NS * SLOT, CH))
        idc[r] = column.reshape(NS, SLOT, CH)


def spread_rows(source, target):
    place = lax.broadcasted_iota(jnp.int32, (SLOT, 1), 0)
    for r in range(SIDE):
        for column in range(NS):
            tile = source[pl.ds(SIDE * r + STRIPE * column, SLOT)]
            target[r, column] = jnp.where(place < STRIPE, tile, 0.0)


def pack_rows(source, target):
    for r in range(SIDE):
        for column in range(NS):
            start = SIDE * r + STRIPE * column
            if start + SLOT <= SIDE * SIDE:
                target[pl.ds(start, SLOT)] = source[r, column]
            else:
                target[pl.ds(start, STRIPE)] = source[r, column, 0:STRIPE]


def first_norm(rows, sv, layer):
    hat, _ = normed(rows)
    return (hat * shared_of(sv, layer, 0) + shared_of(sv, layer, 1)).astype(bf16)


def attend(g, a1, ids, weights, vec):
    mixed = dot(a1, weights)
    value = mixed[:, 2 * CH :] + vec[:, CH : 2 * CH]
    query = (mixed[:, :CH] + vec[:, :CH]) * (HEAD ** -0.5 * LOG2E)
    qkv = compact(jnp.concatenate([query, mixed[:, CH : 2 * CH], value], axis=1)).astype(bf16)
    q, k, v = qkv[:, :CH], qkv[:, CH : 2 * CH], qkv[:, 2 * CH :]
    ids_c = compact(ids)
    key_ids = jnp.concatenate([ids_c, jnp.full((3 * CH - TOKENS, CH), -5.0, f32)], axis=0).T[0:1]
    left = lax.broadcasted_iota(jnp.int32, (1, CH), 1) < TAIL
    last = key_ids[:, 2 * CH :]
    last = jnp.where(left, last, pltpu.roll(last, TAIL, 1))
    bias = [
        jnp.where(ids_c == part, 0.0, masked_score) for part in (key_ids[:, :CH], key_ids[:, CH : 2 * CH], last)
    ]
    e = masked_softmax(q, block_diagonal(k), bias)
    ones = lane_marks(lambda lane, h: lane // HEAD == h)
    both = dot(e, jnp.concatenate([block_diagonal(v), ones], axis=1))
    rl = 1.0 / both[:, CH:]
    att = both[:, :CH] * rl
    total = expand(att) + vec[:, 2 * CH : 3 * CH]
    for tap, near in masked_neighbours(value.astype(bf16).astype(f32), ids, g):
        total = total + near * vec[:, (3 + tap) * CH : (4 + tap) * CH]
    return qkv, e, rl, att.astype(bf16), total.astype(bf16)


def attend_back(g, gbs, ids, weights, proj, vec, qkv, e, rl, att, add):
    d_out = dot_t(gbs, proj).astype(bf16).astype(f32)
    q, k, v = qkv[:, 0:CH], qkv[:, CH : 2 * CH], qkv[:, 2 * CH :]
    scaled = (compact(d_out) * rl).astype(bf16)
    prod = scaled.astype(f32) * att.astype(f32)
    prod_high = prod.astype(bf16)
    prod_low = (prod - prod_high.astype(f32)).astype(bf16)
    lanes = lax.broadcasted_iota(jnp.int32, (CH, CH), 1)
    rows_of = lax.broadcasted_iota(jnp.int32, (CH, CH), 0)
    gather = jnp.where((lanes % HEAD == rows_of // HEAD) & (lanes < 3 * HEAD), 1.0, 0.0).astype(bf16)
    centre = dot(
        jnp.concatenate([prod_high, prod_low], axis=1), jnp.concatenate([gather, gather], axis=0)
    )
    first = centre.astype(bf16).astype(f32)
    rest = centre - first
    second = rest.astype(bf16).astype(f32)
    lane = lax.broadcasted_iota(jnp.int32, (1, CH), 1)
    pieces = jnp.where(lane < HEAD, first, jnp.where(lane < 2 * HEAD, second, rest - second))
    left = jnp.concatenate([scaled, (-pieces).astype(bf16)], axis=1)
    marks = lane_marks(lambda lane, h: (lane % HEAD == h) & (lane < 3 * HEAD))
    right = jnp.concatenate([block_diagonal(v), marks], axis=1)
    ds = (e.astype(f32) * dot_t(left, right)).astype(bf16)
    dq = dot(ds, block_diagonal(k)) * HEAD ** -0.5
    turned_grads = [over_queries(turned(q), ds) * (1.0 / LOG2E), over_queries(turned(scaled), e)]
    grads = jnp.concatenate([dq, jnp.concatenate(turned_grads, axis=0).T[0:TOKENS]], axis=1)
    grads = expand(grads)
    vf = expand(v.astype(f32))
    dv = grads[:, 2 * CH :]
    for tap, near in masked_neighbours(d_out, ids, g):
        mirror = 8 - tap
        dv = dv + near * vec[:, (3 + mirror) * CH : (4 + mirror) * CH]
        if add is not None:
            add(3 + mirror, tile_sum(near * vf))
    dq, dk, dv = grads[:, :CH].astype(bf16), grads[:, CH : 2 * CH].astype(bf16), dv.astype(bf16)
    if add is not None:
        add(0, tile_sum(dq.astype(f32)))
        add(1, tile_sum(dv.astype(f32)))
        add(2, tile_sum(d_out))
    dqkv = jnp.concatenate([dq, dk, dv], axis=1)
    return dqkv, dot_t(dqkv, weights).astype(bf16).astype(f32)


def qkv_of(buffer):
    return buffer[:, 0 : 3 * CH]


def proj_of(buffer):
    return jnp.concatenate([buffer[0:CH, 3 * CH : 4 * CH], buffer[CH : 2 * CH, 3 * CH : 4 * CH]], axis=1)


def up_of(buffer, start):
    return buffer[:, start : start + HALF]


def down_of(buffer, start):
    return jnp.concatenate(
        [buffer[:, start + HALF : start + HALF + WIDTH], buffer[:, start + HALF + WIDTH : start + 2 * HALF]], axis=0
    )


def assemble(whole, near, far, core):
    half = WIDTH // 2
    whole[pl.ds(core * half, half)] = near[...]
    whole[pl.ds((1 - core) * half, half)] = far[...]


def shared_of(sv, layer, index):
    return sv[layer : layer + 1, index * WIDTH : (index + 1) * WIDTH]


def mlp_forward(rows, sv, layer, pairs):
    hat, _ = normed(rows)
    a2 = (hat * shared_of(sv, layer, 3) + shared_of(sv, layer, 4)).astype(bf16)
    parts, kept, slopes = [], [], []
    for up, down, bias in pairs:
        active, slope = gelu_parts(dot(a2, up) + bias)
        active = active.astype(bf16)
        kept.append(active)
        slopes.append(slope.astype(bf16))
        parts.append(dot(active, down).astype(bf16).astype(f32))
    return rows + ((parts[0] + parts[1]) + shared_of(sv, layer, 5)), kept[0], slopes


def mlp_backward(rows, mid, slopes, sv, layer, pairs):
    gm = rows.astype(bf16)
    hat, rstd = normed(mid)
    a2 = (hat * shared_of(sv, layer, 3) + shared_of(sv, layer, 4)).astype(bf16)
    parts, hidden = [], []
    for (up, down, _), slope in zip(pairs, slopes):
        gh = (dot_t(gm, down) * slope.astype(f32)).astype(bf16)
        hidden.append(gh)
        parts.append(dot_t(gh, up).astype(bf16).astype(f32))
    da2 = parts[0] + parts[1]
    new = rows + norm_back(da2, hat, rstd, shared_of(sv, layer, 3))
    low = new.astype(bf16)
    sums = (
        tile_sum(low.astype(f32)), tile_sum(da2 * hat), tile_sum(da2), tile_sum(gm.astype(f32)),
        tile_sum(hidden[0].astype(f32)),
    )
    return new, low, gm, a2, hidden[0], sums


def one_row(tile):
    return jnp.sum(tile, axis=0, keepdims=True)


def pack_vectors(devices, shared_row, group_row):
    rows = WIDTH // devices
    wide = shared_row.shape[1] // devices
    own = group_row.shape[1] // devices
    lines = []
    for i in range(devices):
        pieces = []
        for piece in (shared_row[:, i * wide : (i + 1) * wide], group_row[:, i * own : (i + 1) * own]):
            pieces.append(piece)
            if piece.shape[1] < CH:
                pieces.append(jnp.zeros((1, CH - piece.shape[1]), f32))
        line = jnp.concatenate(pieces, axis=1)
        lines.append(jnp.concatenate([line, jnp.zeros((rows - 1, 2 * CH), f32)], axis=0))
    return jnp.concatenate(lines, axis=0)


def sds(shape, dtype):
    return jax.ShapeDtypeStruct(shape, dtype)


def hbm(shape, dtype):
    return pltpu.HBM(shape, dtype)


def chunk_shapes(devices):
    return [sds((devices // 2, WIDTH // devices, 3 * HALF + 2 * CH), bf16)] * 2


def put_chunks(send, keep, core, start, value):
    rows, width = send.shape[1], value.shape[1]
    for m in range(send.shape[0]):
        even = value[2 * m * rows : (2 * m + 1) * rows]
        odd = value[(2 * m + 1) * rows : (2 * m + 2) * rows]
        keep[m, :, start : start + width] = jnp.where(core == 0, even, odd).astype(bf16)
        send[m, :, start : start + width] = jnp.where(core == 0, odd, even).astype(bf16)


def vmem_spec():
    return pl.BlockSpec(memory_space=pltpu.VMEM)


def smem_spec():
    return pl.BlockSpec(memory_space=pltpu.SMEM)


def waits(arrays):
    return [pl.BlockSpec(memory_space=pl.ANY)] * len(arrays)


def kept(shape):
    return pl.BlockSpec(shape, lambda s: (0,) * len(shape))


def per_step(shape, first=0, count=1):
    return pl.BlockSpec((count,) + shape, lambda s: (s + first,) + (0,) * len(shape))


def cost(us):
    return pl.CostEstimate(flops=int(us * 1.1e9), bytes_accessed=10**6, transcendentals=0)


def params(mib):
    return pltpu.CompilerParams(vmem_limit_bytes=mib * MIB)


CANVAS = (SIDE, NS, SLOT, WIDTH)
CORE, GROUP, INDEX = 0, 1, 2


def prepare_first_kernel(qkv, proj, att):
    att[:, 0 : 3 * CH] = qkv[0].astype(bf16)
    att[0:CH, 3 * CH :] = proj[0, :, 0:CH].astype(bf16)
    att[CH:, 3 * CH :] = proj[0, :, CH:].astype(bf16)


def prepare_rest_kernel(place, qkv, proj, up, down, mlp0, att1, mlp1, send):
    half = WIDTH // 2
    att1[:, 0 : 3 * CH] = qkv[0].astype(bf16)
    att1[0:CH, 3 * CH :] = proj[0, :, 0:CH].astype(bf16)
    att1[CH:, 3 * CH :] = proj[0, :, CH:].astype(bf16)
    for layer, mlp in enumerate((mlp0, mlp1)):
        mlp[:, 0:HALF] = up[layer].astype(bf16)
        mlp[:, HALF : HALF + WIDTH] = down[layer, 0:WIDTH].astype(bf16)
        mlp[:, HALF + WIDTH :] = down[layer, WIDTH:].astype(bf16)
    mine = pl.ds(place[CORE] * half, half)
    send[:, 0:HALF] = att1[mine]
    send[:, HALF:] = mlp1[mine]


def layer_spec(shape, layer):
    return pl.BlockSpec((1,) + shape[1:], lambda s: (layer, 0, 0))


def run_prepare(place, qkv, proj, up, down):
    half = WIDTH // 2
    qkv, proj, up, down = (pltpu.with_memory_space_constraint(x, pltpu.HBM) for x in (qkv, proj, up, down))
    att0 = pl.pallas_call(
        prepare_first_kernel,
        grid=(1,),
        out_shape=sds((WIDTH, HALF), bf16),
        in_specs=[layer_spec(qkv.shape, 0), layer_spec(proj.shape, 0)],
        out_specs=kept((WIDTH, HALF)),
        compiler_params=params(SMALL),
        cost_estimate=cost(1),
        name="prepare_first",
    )(qkv, proj)
    rest = pl.pallas_call(
        prepare_rest_kernel,
        grid=(1,),
        out_shape=[
            hbm((WIDTH, 2 * HALF), bf16), hbm((WIDTH, HALF), bf16), hbm((WIDTH, 2 * HALF), bf16),
            sds((half, 3 * HALF), bf16),
        ],
        in_specs=[smem_spec(), layer_spec(qkv.shape, 1), layer_spec(proj.shape, 1), kept(up.shape), kept(down.shape)],
        out_specs=[
            kept((WIDTH, 2 * HALF)), kept((WIDTH, HALF)), kept((WIDTH, 2 * HALF)), kept((half, 3 * HALF)),
        ],
        compiler_params=params(SMALL),
        cost_estimate=cost(3),
        name="prepare_rest",
    )(place, qkv, proj, up, down)
    return att0, *rest


def attention_kernel(layer, mine, place, given, *refs):
    if mine:
        att_w, sv, gv, ids_t, part, qkv_o, e_o, rl_o, att_o, heads_o, a1_o, stream, idc, tall = refs
    else:
        stream = given
        att_w, sv, gv, ids_t, part, qkv_o, e_o, rl_o, att_o, idc = refs
    s = pl.program_id(0)

    @pl.when(s == 0)
    def _():
        spread_ids(ids_t, idc)
        if mine:
            tall[0 : SIDE * SIDE] = given[...].astype(f32)
            spread_rows(tall, stream)

    frame = place[GROUP] if mine else 1 - place[GROUP]
    for g in range(2):
        @pl.when(frame == g)
        def _(g=g):
            for n in range(FA_GANG):
                row = FA_GANG * s + n
                a1 = first_norm(stripe_of(stream, g, row), sv, layer)
                qkv, e, rl, att, heads = attend(g, a1, stripe_of(idc, g, row), qkv_of(att_w), gv[layer])
                qkv_o[n] = qkv
                e_o[n] = e
                rl_o[n] = rl
                att_o[n] = att
                part[n] = dot(heads, proj_of(att_w)).astype(bf16).astype(f32)
                if mine:
                    heads_o[n] = heads
                    a1_o[n] = a1


ATT_SAVED = [((TOKENS, 3 * CH), bf16), ((TOKENS, KEYS), bf16), ((TOKENS, CH), f32), ((TOKENS, CH), bf16)]


def run_attention(layer, mine, place, stream, weights, sv, gv, ids_t):
    outs = [((ROWS, WIDTH), f32)] + ATT_SAVED + ([((ROWS, CH), bf16), ((ROWS, WIDTH), bf16)] if mine else [])
    inputs = (stream, weights, sv, gv, ids_t)
    return pl.pallas_call(
        functools.partial(attention_kernel, layer, mine),
        grid=(NS // FA_GANG,),
        out_shape=[(sds if n == 0 else hbm)((NS,) + shape, dtype) for n, (shape, dtype) in enumerate(outs)]
        + ([sds(CANVAS, f32)] if mine else []),
        in_specs=[smem_spec()] + [kept(x.shape) for x in inputs],
        out_specs=[per_step(shape, 0, FA_GANG) for shape, _ in outs] + ([kept(CANVAS)] if mine else []),
        scratch_shapes=[pltpu.VMEM((SIDE, NS, SLOT, CH), f32)]
        + ([pltpu.VMEM((SIDE * SIDE + 4, WIDTH), f32)] if mine else []),
        compiler_params=params(SMALL),
        cost_estimate=cost(11),
        name=f"layer{layer}_attention_{'own' if mine else 'other'}",
    )(place, *inputs)


def in_frames(own, mine_h, mine_v, other_h, other_v, n=0):
    def turned(ref):
        columns = [ref[column, pl.ds(STRIPE * n, STRIPE)] for column in range(NS)]
        return jnp.stack(columns, axis=1).reshape(ROWS, WIDTH)

    mine = jnp.where(own == 0, mine_h[n], turned(mine_v))
    other = jnp.where(own == 0, turned(other_v), other_h[n])
    return mine + other


def frame_specs(count=1):
    flat = per_step((ROWS, WIDTH), 0, count)
    tall = pl.BlockSpec((NS, STRIPE * count, SLOT, WIDTH), lambda s: (0, s, 0, 0))
    return [flat, tall, flat, tall]


def frame_views(mine, other):
    shape = (NS, SIDE, SLOT, WIDTH)
    return (mine, mine.reshape(shape), other, other.reshape(shape))


def canvas_block(count=1):
    return pl.BlockSpec((STRIPE * count, NS, SLOT, WIDTH), lambda s: (s, 0, 0, 0))


def feed_kernel(
    layer, place, stream, mine_h, mine_v, other_h, other_v, mlp_w, mlp_o, sv, gv, gvo,
    out, mid, active, slopes,
):
    pairs = [
        (up_of(w, 0), down_of(w, 0), v[layer][:, 12 * CH :]) for w, v in ((mlp_w, gv), (mlp_o, gvo))
    ]
    for n in range(GANG):
        both = in_frames(place[GROUP], mine_h, mine_v, other_h, other_v, n)
        rows = stripe_of(stream, 0, n) + (both + shared_of(sv, layer, 2))
        put_stripe(mid, 0, n, rows)
        new, held, slope = mlp_forward(rows, sv, layer, pairs)
        put_stripe(out, 0, n, new)
        active[n] = held
        slopes[n, 0] = slope[0]
        slopes[n, 1] = slope[1]


def run_feed(layer, place, stream, mine, other, mlp_w, mlp_o, sv, gv, gvo):
    rest = (mlp_w, mlp_o, sv, gv, gvo)
    return pl.pallas_call(
        functools.partial(feed_kernel, layer),
        grid=(NS // GANG,),
        out_shape=[
            hbm(CANVAS, f32), hbm(CANVAS, f32), hbm((NS, ROWS, HALF), bf16), hbm((NS, 2, ROWS, HALF), bf16)
        ],
        in_specs=[smem_spec(), canvas_block(GANG)] + frame_specs(GANG) + [kept(x.shape) for x in rest],
        out_specs=[
            canvas_block(GANG), canvas_block(GANG), per_step((ROWS, HALF), 0, GANG), per_step((2, ROWS, HALF), 0, GANG)
        ],
        compiler_params=params(SMALL),
        cost_estimate=cost(10),
        name=f"layer{layer}_feed_forward",
    )(place, stream, *frame_views(mine, other), *rest)


def last_layer_kernel(
    layer, devices, place, stream, cot, att_w, mlp_w, near, far, sv, gv, gvo, ids_t,
    out, grad_in, send, keep,
    whole, att2, gv2, idc, mid, gmid, gb, qkv_s, e_s, rl_s, att_s, heads_s, active_s, a1_s, dqkv_s, gb_s,
    a2_s, gh_s, gm_s, acc_s, acc_b1, acc_g, tall,
):
    own = place[GROUP]
    assemble(whole, near, far, place[CORE])
    att2[own] = att_w[...]
    att2[1 - own] = whole[:, 0:HALF]
    gv2[own] = gv[layer]
    gv2[1 - own] = gvo[layer]
    spread_ids(ids_t, idc)
    acc_s[...] = jnp.zeros_like(acc_s)
    acc_b1[...] = jnp.zeros_like(acc_b1)
    acc_g[...] = jnp.zeros_like(acc_g)

    def norms(first, carry):
        for n in range(GANG):
            s = GANG * first + n
            put_stripe(gmid, 0, s, first_norm(stripe_of(stream, 0, s), sv, layer).astype(f32))
        return carry

    lax.fori_loop(0, NS // GANG, norms, 0)

    for g in range(2):
        def gang(first, carry, g=g):
            for n in range(GANG):
                s = GANG * first + n
                i = g * NS + s
                a1 = stripe_of(gmid, g, s).astype(bf16)
                qkv, e, rl, att, heads = attend(g, a1, stripe_of(idc, g, s), qkv_of(att2[g]), gv2[g])
                qkv_s[i] = qkv
                e_s[i] = e
                rl_s[i] = rl
                att_s[i] = att
                part = dot(heads, proj_of(att2[g])).astype(bf16).astype(f32)
                if g == 0:
                    put_stripe(mid, g, s, part)
                else:
                    rows = stripe_of(stream, g, s)
                    put_stripe(mid, g, s, rows + ((stripe_of(mid, g, s) + part) + shared_of(sv, layer, 2)))
                a1_s[g, s] = a1
                heads_s[g, s] = heads
            return carry

        lax.fori_loop(0, NS // GANG, gang, 0)

    def pairs():
        return [
            (up_of(mlp_w, 0), down_of(mlp_w, 0), gv[layer][:, 12 * CH :]),
            (up_of(whole, HALF), down_of(whole, HALF), gvo[layer][:, 12 * CH :]),
        ]

    tall[0 : SIDE * SIDE] = cot[...].astype(f32)
    spread_rows(tall, gmid)

    def block(s):
        rows = stripe_of(mid, 0, s)
        new, held, slope = mlp_forward(rows, sv, layer, pairs())
        put_stripe(grad_in, 0, s, new)
        active_s[s] = held
        grad = stripe_of(gmid, 0, s)
        new, low, gm, a2, gh, sums = mlp_backward(grad, rows, slope, sv, layer, pairs())
        put_stripe(gmid, 0, s, new)
        put_stripe(gb, 0, s, low.astype(f32))
        gm_s[s] = gm
        a2_s[s] = a2
        gh_s[s] = gh
        for index, value in zip((2, 3, 4, 5), sums):
            acc_s[index] += value
        acc_b1[...] += sums[4]

    def blocks(first, carry):
        for n in range(GANG):
            block(GANG * first + n)
        return carry

    lax.fori_loop(0, NS // GANG, blocks, 0)
    pack_rows(grad_in, tall)
    out[...] = tall[0 : SIDE * SIDE].astype(bf16)

    for g in range(2):
        def gang(first, carry, g=g):
            def add(index, value):
                acc_g[g, index] += value

            for n in range(GANG):
                s = GANG * first + n
                i = g * NS + s
                gbs = stripe_of(gb, g, s).astype(bf16)
                dqkv, part = attend_back(
                    g, gbs, stripe_of(idc, g, s), qkv_of(att2[g]), proj_of(att2[g]), gv2[g], qkv_s[i], e_s[i],
                    rl_s[i], att_s[i], add,
                )
                if g == 0:
                    put_stripe(mid, g, s, part)
                else:
                    put_stripe(mid, g, s, stripe_of(mid, g, s) + part)
                dqkv_s[g, s] = dqkv
                gb_s[g, s] = gbs
            return carry

        lax.fori_loop(0, NS // GANG, gang, 0)

    def final(first, carry):
        for n in range(GANG):
            s = GANG * first + n
            hat, rstd = normed(stripe_of(stream, 0, s))
            da = stripe_of(mid, 0, s)
            acc_s[0] += tile_sum(da * hat)
            acc_s[1] += tile_sum(da)
            put_stripe(
                grad_in, 0, s, stripe_of(gmid, 0, s) + norm_back(da, hat, rstd, shared_of(sv, layer, 0))
            )
        return carry

    lax.fori_loop(0, NS // GANG, final, 0)

    def flat(ref):
        return ref[...].reshape(NS * ROWS, ref.shape[-1])

    core = place[CORE]
    put_chunks(send, keep, core, 0, dot_rows(flat(a1_s.at[own]), flat(dqkv_s.at[own])))
    put_chunks(send, keep, core, 3 * CH, dot_rows(flat(gb_s.at[own]), flat(heads_s.at[own])))
    put_chunks(send, keep, core, HALF, dot_rows(flat(a2_s), flat(gh_s)))
    put_chunks(send, keep, core, 2 * HALF, dot_rows(flat(gm_s), flat(active_s)))
    shared_row = jnp.concatenate([one_row(acc_s[index]) for index in range(6)], axis=1)
    group_row = jnp.concatenate([one_row(acc_g[own, index]) for index in range(12)] + [one_row(acc_b1[...])], axis=1)
    put_chunks(send, keep, core, 3 * HALF, pack_vectors(devices, shared_row, group_row))


def run_last_layer(layer, devices, place, args):
    return pl.pallas_call(
        functools.partial(last_layer_kernel, layer, devices),
        out_shape=[sds((SIDE * SIDE, WIDTH), bf16), sds(CANVAS, f32)] + chunk_shapes(devices),
        in_specs=[smem_spec()] + [vmem_spec()] * len(args),
        out_specs=[vmem_spec()] * 4,
        scratch_shapes=[
            pltpu.VMEM((WIDTH, 3 * HALF), bf16),
            pltpu.VMEM((2, WIDTH, HALF), bf16),
            pltpu.VMEM((2, 1, 16 * CH), f32),
            pltpu.VMEM((SIDE, NS, SLOT, CH), f32),
            pltpu.VMEM(CANVAS, f32),
            pltpu.VMEM(CANVAS, f32),
            pltpu.VMEM(CANVAS, f32),
            pltpu.VMEM((2 * NS, TOKENS, 3 * CH), bf16),
            pltpu.VMEM((2 * NS, TOKENS, KEYS), bf16),
            pltpu.VMEM((2 * NS, TOKENS, CH), f32),
            pltpu.VMEM((2 * NS, TOKENS, CH), bf16),
            pltpu.VMEM((2, NS, ROWS, CH), bf16),
            pltpu.VMEM((NS, ROWS, HALF), bf16),
            pltpu.VMEM((2, NS, ROWS, WIDTH), bf16),
            pltpu.VMEM((2, NS, ROWS, 3 * CH), bf16),
            pltpu.VMEM((2, NS, ROWS, WIDTH), bf16),
            pltpu.VMEM((NS, ROWS, WIDTH), bf16),
            pltpu.VMEM((NS, ROWS, HALF), bf16),
            pltpu.VMEM((NS, ROWS, WIDTH), bf16),
            pltpu.VMEM((6, SLOT, WIDTH), f32),
            pltpu.VMEM((SLOT, HALF), f32),
            pltpu.VMEM((2, 12, SLOT, CH), f32),
            pltpu.VMEM((SIDE * SIDE + 4, WIDTH), f32),
        ],
        compiler_params=params(LARGE),
        cost_estimate=cost(65),
        name=f"layer{layer}_forward_backward",
    )(place, *args)


def feed_back_kernel(
    layer, place, grad, mid, slopes, active, mlp_w, mlp_o, sv, gv, gvo, *refs,
):
    gmid, gb, big, rows_out, bias_out, a2_s, gh_s, gm_s, act_s, acc_s, acc_b1 = refs[-11:]
    s = pl.program_id(0)

    @pl.when(s == 0)
    def _():
        acc_s[...] = jnp.zeros_like(acc_s)
        acc_b1[...] = jnp.zeros_like(acc_b1)

    pairs = [
        (up_of(w, 0), down_of(w, 0), v[layer][:, 12 * CH :]) for w, v in ((mlp_w, gv), (mlp_o, gvo))
    ]
    for n in range(GANG):
        new, low, gm, a2, gh, sums = mlp_backward(
            stripe_of(grad, 0, n), stripe_of(mid, 0, n), [slopes[n, 0], slopes[n, 1]], sv, layer, pairs
        )
        put_stripe(gmid, 0, n, new)
        put_stripe(gb, 0, n, low.astype(f32))
        gm_s[GANG * s + n] = gm
        a2_s[GANG * s + n] = a2
        gh_s[GANG * s + n] = gh
        act_s[GANG * s + n] = active[n]
        for index in range(4):
            acc_s[index] += sums[index]
        acc_b1[...] += sums[4]

    @pl.when(s == NS // GANG - 1)
    def _():
        def flat(ref):
            return ref[...].reshape(NS * ROWS, ref.shape[-1])

        big[:, 0:HALF] = dot_rows(flat(a2_s), flat(gh_s)).astype(bf16)
        big[:, HALF:] = dot_rows(flat(gm_s), flat(act_s)).astype(bf16)
        rows_out[...] = jnp.concatenate([one_row(acc_s[index]) for index in range(4)], axis=1)
        bias_out[...] = one_row(acc_b1[...])


def run_feed_back(layer, place, grad, mid, slopes, active, mlp_w, mlp_o, sv, gv, gvo, after):
    rest = (mlp_w, mlp_o, sv, gv, gvo)
    mid, slopes, active = (pltpu.with_memory_space_constraint(x, pltpu.HBM) for x in (mid, slopes, active))
    return pl.pallas_call(
        functools.partial(feed_back_kernel, layer),
        grid=(NS // GANG,),
        out_shape=[
            sds(CANVAS, f32), sds(CANVAS, f32), sds((WIDTH, 2 * HALF), bf16), sds((1, 4 * WIDTH), f32),
            sds((1, HALF), f32),
        ],
        in_specs=[smem_spec(), canvas_block(GANG), canvas_block(GANG), per_step((2, ROWS, HALF), 0, GANG), per_step((ROWS, HALF), 0, GANG)]
        + [kept(x.shape) for x in rest]
        + waits(after),
        out_specs=[canvas_block(GANG), canvas_block(GANG), kept((WIDTH, 2 * HALF)), kept((1, 4 * WIDTH)), kept((1, HALF))],
        scratch_shapes=[
            pltpu.VMEM((NS, ROWS, WIDTH), bf16),
            pltpu.VMEM((NS, ROWS, HALF), bf16),
            pltpu.VMEM((NS, ROWS, WIDTH), bf16),
            pltpu.VMEM((NS, ROWS, HALF), bf16),
            pltpu.VMEM((4, SLOT, WIDTH), f32),
            pltpu.VMEM((SLOT, HALF), f32),
        ],
        compiler_params=params(SMALL),
        cost_estimate=cost(11),
        name=f"layer{layer}_feed_backward",
    )(place, grad, mid, slopes, active, *rest, *after)


def attention_back_kernel(layer, mine, devices, place, gb, qkv, e, rl, att, *refs):
    if mine:
        att_w, sv, gv, ids_t, heads, a1, big_m, rows_m, bias_m = refs[:9]
        da, big, idc, dqkv_s, gb_s, acc_g = refs[-6:]
    else:
        att_w, sv, gv, ids_t = refs[:4]
        da, idc = refs[-2:]
    step = pl.program_id(0)

    @pl.when(step == 0)
    def _():
        spread_ids(ids_t, idc)
        if mine:
            acc_g[...] = jnp.zeros_like(acc_g)

    def add(index, value):
        acc_g[index] += value

    frame = place[GROUP] if mine else 1 - place[GROUP]
    for g in range(2):
        @pl.when(frame == g)
        def _(g=g):
            for n in range(GANG):
                s = GANG * step + n
                gbs = stripe_of(gb, g, s).astype(bf16)
                dqkv, part = attend_back(
                    g, gbs, stripe_of(idc, g, s), qkv_of(att_w), proj_of(att_w), gv[layer], qkv[n], e[n], rl[n], att[n],
                    add if mine else None,
                )
                da[n] = part
                if mine:
                    dqkv_s[s] = dqkv
                    gb_s[s] = gbs

    if mine:
        @pl.when(step == NS // GANG - 1)
        def _():
            def flat(ref):
                return ref[...].reshape(NS * ROWS, ref.shape[-1])

            big[:, 0 : 3 * CH] = dot_rows(flat(a1), flat(dqkv_s)).astype(bf16)
            big[:, 3 * CH : HALF] = dot_rows(flat(gb_s), flat(heads)).astype(bf16)
            big[:, HALF : 3 * HALF] = big_m[...]
            shared_row = jnp.concatenate([jnp.zeros((1, 2 * WIDTH), f32), rows_m[...]], axis=1)
            group_row = jnp.concatenate([one_row(acc_g[index]) for index in range(12)] + [bias_m[...]], axis=1)
            big[:, 3 * HALF :] = pack_vectors(devices, shared_row, group_row).astype(bf16)


def run_attention_back(layer, mine, devices, place, gb, saved, weights, sv, gv, ids_t, extra, after):
    rest = (weights, sv, gv, ids_t, *extra)
    outs = [sds((NS, ROWS, WIDTH), f32)]
    out_specs = [per_step((ROWS, WIDTH), 0, GANG)]
    scratch = [pltpu.VMEM((SIDE, NS, SLOT, CH), f32)]
    if mine:
        outs.append(sds((WIDTH, 3 * HALF + 2 * CH), bf16))
        out_specs.append(kept(outs[1].shape))
        scratch += [
            pltpu.VMEM((NS, ROWS, 3 * CH), bf16),
            pltpu.VMEM((NS, ROWS, WIDTH), bf16),
            pltpu.VMEM((12, SLOT, CH), f32),
        ]
    inputs = (place, gb, *saved, *rest, *after)
    return pl.pallas_call(
        functools.partial(attention_back_kernel, layer, mine, devices),
        grid=(NS // GANG,),
        out_shape=outs,
        in_specs=[smem_spec(), kept(CANVAS)]
        + [per_step(shape, 0, GANG) for shape, _ in ATT_SAVED]
        + [kept(x.shape) for x in rest]
        + waits(after),
        out_specs=out_specs,
        scratch_shapes=scratch,
        compiler_params=params(SMALL),
        cost_estimate=cost(10),
        name=f"layer{layer}_attention_back_{'own' if mine else 'other'}",
    )(*inputs)


def norm_back_kernel(layer, place, stream, gmid, mine_h, mine_v, other_h, other_v, sv, *refs):
    out, sums, grad_in, acc = refs[-4:]
    s = pl.program_id(0)

    @pl.when(s == 0)
    def _():
        acc[...] = jnp.zeros_like(acc)

    for n in range(GANG):
        da = in_frames(place[GROUP], mine_h, mine_v, other_h, other_v, n)
        hat, rstd = normed(stripe_of(stream, 0, n))
        acc[0] += tile_sum(da * hat)
        acc[1] += tile_sum(da)
        new = stripe_of(gmid, 0, n) + norm_back(da, hat, rstd, shared_of(sv, layer, 0))
        put_stripe(grad_in, 0, GANG * s + n, new)

    @pl.when(s == NS // GANG - 1)
    def _():
        pack_rows(grad_in, out)
        sums[...] = jnp.concatenate([one_row(acc[0]), one_row(acc[1])], axis=1)


def run_norm_back(layer, place, stream, gmid, mine, other, sv, after):
    return pl.pallas_call(
        functools.partial(norm_back_kernel, layer),
        grid=(NS // GANG,),
        out_shape=[sds((SIDE * SIDE, WIDTH), f32), sds((1, 2 * WIDTH), f32)],
        in_specs=[smem_spec(), canvas_block(GANG), canvas_block(GANG)] + frame_specs(GANG) + [kept(sv.shape)] + waits(after),
        out_specs=[kept((SIDE * SIDE, WIDTH)), kept((1, 2 * WIDTH))],
        scratch_shapes=[pltpu.VMEM(CANVAS, f32), pltpu.VMEM((2, SLOT, WIDTH), f32)],
        compiler_params=params(SMALL),
        cost_estimate=cost(4),
        name=f"layer{layer}_norm_backward",
    )(place, stream, gmid, *frame_views(mine, other), sv, *after)


def halves_of(x):
    high = x.astype(bf16)
    return high, (x - high.astype(f32)).astype(bf16)


def split_dot(a, b, dims):
    (a_high, a_low), (b_high, b_low) = halves_of(a), halves_of(b)
    left = jnp.concatenate([a_high, a_high, a_low], axis=1)
    right = jnp.concatenate([b_high, b_low, b_high], axis=dims[1][0])
    return lax.dot_general(left, right, (dims, ((), ())), preferred_element_type=f32)


SPANS = ((0, 3 * CH), (3 * CH, HALF), (HALF, 2 * HALF), (2 * HALF, 3 * HALF))


def own_rows(ref, index, rows):
    if rows % SLOT == 0:
        return ref[pl.ds(pl.multiple_of(index * rows, SLOT), rows)]
    start = index * rows
    base = pl.multiple_of((start // SLOT) * SLOT, SLOT)
    return pltpu.roll(ref[pl.ds(base, SLOT)], SLOT - (start - base), 0)[0:rows]


def sums_width(rows):
    return max(CH, SLOT * CH // rows)


def sums_blocks(rows):
    per = sums_width(rows) // CH
    return [(b // per, 3 * HALF + (b % per) * CH) for b in range(SLOT)]


def read_sums(ref, rows):
    blocks = [ref[row : row + 1, lane : lane + CH].astype(f32) for row, lane in sums_blocks(rows)]
    return jnp.concatenate([blocks[n] + blocks[n + 4] for n in range(4)], axis=1)


def with_sums(matrix, sums):
    rows, width = matrix.shape[0], sums_width(matrix.shape[0])
    high, low = halves_of(sums)
    parts = [x[:, n * CH : (n + 1) * CH] for x in (high, low) for n in range(4)]
    per = width // CH
    lines = [jnp.concatenate(parts[n : n + per], axis=1) for n in range(0, SLOT, per)]
    if rows > len(lines):
        lines.append(jnp.zeros((rows - len(lines), width), bf16))
    beside = jnp.concatenate([x.astype(f32) for x in lines], axis=0).astype(bf16)
    return jnp.concatenate([matrix, beside], axis=1)


def momentum_kernel(layer, n_got, place, keep, *refs):
    gots, (qkv, proj, up, down, extra, whole, fresh, vectors), refs = refs[:n_got], refs[n_got : n_got + 8], refs[n_got + 8 :]
    total = keep[0].astype(f32)
    for got in gots:
        total = total + got[0].astype(f32)
    matrix = total[:, 0 : 3 * HALF]
    old = jnp.concatenate([qkv[layer], proj[layer], up[layer], down[layer]], axis=1)
    new = momentum_decay * old + matrix
    fresh[...] = new
    ahead = (matrix + momentum_decay * new).astype(bf16)
    vectors[...] = total[0:1, 3 * HALF :]
    if layer == 0:
        whole[0] = with_sums(ahead, extra[...])
    else:
        whole[0] = ahead
        put_chunks(*refs, place[CORE], 0, extra[...].astype(f32))


def run_momentum(layer, devices, place, keep, gots, moments, extra):
    rows = keep.shape[1]
    width = 3 * HALF + (0 if layer else sums_width(rows))
    outs = [sds((1, rows, width), bf16), hbm((rows, 3 * HALF), f32), sds((1, 2 * CH), f32)]
    if layer:
        outs += chunk_shapes(devices)
    return pl.pallas_call(
        functools.partial(momentum_kernel, layer, len(gots)),
        out_shape=outs,
        in_specs=[smem_spec()] + [vmem_spec()] * (6 + len(gots)),
        out_specs=[vmem_spec()] * len(outs),
        compiler_params=params(SMALL),
        cost_estimate=cost(1),
        name=f"layer{layer}_momentum",
    )(place, keep, *gots, *moments, extra)


def square_dot(x, dims):
    high, low = halves_of(x)
    mixed = lax.dot_general(high, low, (dims, ((), ())), preferred_element_type=f32)
    return lax.dot_general(high, high, (dims, ((), ())), preferred_element_type=f32) + (mixed + mixed.T)


def newton(works, steps):
    for _ in range(steps):
        grams = [square_dot(work, ((1,), (1,))) for work in works]
        blends = [coeff_second * gram + coeff_third * square_dot(gram, ((1,), (0,))) for gram in grams]
        works = [
            coeff_first * work + split_dot(blend, work, ((1,), (0,)))
            for work, blend in zip(works, blends)
        ]
    return works


def joined(stage, place, given, scratch):
    if len(given) == 1:
        return given[0][...]
    join_chunks(stage, place[INDEX], given[0], given[1:], scratch)
    return scratch[...].reshape(WIDTH, scratch.shape[2])


def newton_from(whole, picks, steps):
    works = [whole[:, SPANS[which][0] : SPANS[which][1]].astype(f32) for which in picks]
    works = [work.T if which == 1 else work for which, work in zip(picks, works)]
    lows = [work.astype(bf16) for work in works]
    factors = [1.0 / (jnp.sqrt(jnp.sum(work * work)) + 1e-07) for work in works]
    grams = [dot_t(low, low) * (factor * factor) for low, factor in zip(lows, factors)]
    blends = [coeff_second * gram + coeff_third * square_dot(gram, ((1,), (0,))) for gram in grams]
    works = [
        (coeff_first * work + dot(jnp.concatenate(halves_of(blend), axis=1), jnp.concatenate([low, low], axis=0))) * factor
        for work, low, blend, factor in zip(works, lows, blends, factors)
    ]
    return newton(works, steps - 1)


def old_rows(layer, index, rows, masters, turned):
    parts = []
    for which, master in enumerate(masters):
        width = SPANS[which][1] - SPANS[which][0]
        if which % 2 == 1:
            tile = (index * rows) // CH
            columns = pl.ds(pl.multiple_of(tile * CH, CH), CH)
            turned[0:CH, 0:width] = master[layer, :, columns].T
            parts.append(own_rows(turned, index - tile * (CH // rows), rows)[:, 0:width])
        else:
            parts.append(own_rows(master.at[layer], index, rows))
    return parts


def put_turned(work, which, rows_s):
    rows_s[:, 0 : SPANS[which][1] - SPANS[which][0]] = work.T if which == 1 else work


def new_rows(which, old, step):
    size = matrix_rate * match_scale * math.sqrt((3 * CH, WIDTH, HALF, HALF)[which])
    return old * (1.0 - matrix_rate * weight_decay) - size * step


SHARES = ((0, 2), (1, 3))
SHARE_WIDTH = 3 * CH + HALF


EARLY_STEPS = 2


def share_spots(picks):
    start, spots = 0, []
    for which in picks:
        width = SPANS[which][1] - SPANS[which][0]
        spots.append((which, CH if which == 1 else WIDTH, start, start + (WIDTH if which == 1 else width)))
        start += max(width, WIDTH)
    return spots


def newton_begin_kernel(stage, n_given, n_after, place, *refs):
    given, masters = refs[:n_given], refs[n_given : n_given + 4]
    old0, old1, works_o, turned_s, *scratch = refs[n_given + 4 + n_after :]
    index, rows = place[INDEX], old0.shape[0]
    whole = joined(stage, place, given, scratch[0] if scratch else None)
    for core, picks in enumerate(SHARES):
        @pl.when(place[CORE] == core)
        def _(picks=picks):
            for layer, old in enumerate((old0, old1)):
                for (start, stop), part in zip(SPANS, old_rows(layer, index, rows, masters, turned_s)):
                    old[:, start:stop] = part
            for (_, height, start, stop), work in zip(share_spots(picks), newton_from(whole, picks, EARLY_STEPS)):
                works_o[0:height, start:stop] = work


def newton_end_kernel(place, works, *refs):
    mine, theirs, rows_s = refs[-3:]
    index, rows = place[INDEX], mine.shape[0]
    for core, picks in enumerate(SHARES):
        @pl.when(place[CORE] == core)
        def _(picks=picks):
            spots = share_spots(picks)
            begun = [works[0:height, start:stop] for _, height, start, stop in spots]
            mine[...] = jnp.zeros_like(mine)
            theirs[...] = jnp.zeros_like(theirs)
            for (which, _, start, _), work in zip(spots, newton(begun, NS_STEPS - EARLY_STEPS)):
                width = SPANS[which][1] - SPANS[which][0]
                put_turned(work, which, rows_s)
                mine[:, start : start + width] = own_rows(rows_s, index, rows)[:, 0:width]
                theirs[:, start : start + width] = own_rows(rows_s, index + 1 - 2 * place[CORE], rows)[:, 0:width]


def run_newton_begin(stage, place, rows, given, masters, after):
    return pl.pallas_call(
        functools.partial(newton_begin_kernel, stage, len(given), len(after)),
        out_shape=[hbm((rows, 3 * HALF), f32)] * 2 + [sds((WIDTH, SHARE_WIDTH), f32)],
        in_specs=[smem_spec()] + [vmem_spec()] * (len(given) + 4) + waits(after),
        out_specs=[vmem_spec()] * 3,
        scratch_shapes=[pltpu.VMEM((WIDTH, HALF), f32)]
        + ([pltpu.VMEM((WIDTH // rows, rows, 3 * HALF), bf16)] if len(given) > 1 else []),
        compiler_params=params(SMALL),
        cost_estimate=cost(3),
        name="layer1_newton_begin",
    )(place, *given, *masters, *after)


def run_newton_end(place, rows, works, after):
    return pl.pallas_call(
        newton_end_kernel,
        out_shape=[sds((rows, SHARE_WIDTH), f32)] * 2,
        in_specs=[smem_spec(), vmem_spec()] + waits(after),
        out_specs=[vmem_spec()] * 2,
        scratch_shapes=[pltpu.VMEM((WIDTH, HALF), f32)],
        compiler_params=params(SMALL),
        cost_estimate=cost(4),
        name="layer1_newton_end",
    )(place, works, *after)


def finish_kernel(stage, n_given, place, *refs):
    given, refs = refs[:n_given], refs[n_given:]
    old0, old1, fresh0, fresh1, mine, theirs, vectors0, vectors1, shared_m, group_m, shared_w, group_w = refs[:12]
    outs, (rows_s, *scratch) = refs[12:24], refs[24:]
    whole = joined(stage, place, given, scratch[0] if scratch else None)
    for layer, fresh in enumerate((fresh0, fresh1)):
        for which, (start, stop) in enumerate(SPANS):
            outs[2 * which][layer] = fresh[:, start:stop]
    for core, picks in enumerate(SHARES):
        share = jnp.where(place[CORE] == core, mine[...], theirs[...])
        for which, _, first, _ in share_spots(picks):
            start, stop = SPANS[which]
            outs[2 * which + 1][1] = new_rows(which, old1[:, start:stop], share[:, first : first + stop - start])
    wide, own = shared_m.shape[1], group_m.shape[2]
    late = jnp.concatenate([read_sums(whole, fresh0.shape[0]), jnp.zeros((1, 4 * WIDTH), f32)], axis=1)
    late = jnp.broadcast_to(late, (SLOT, 6 * WIDTH))
    late = pltpu.roll(late, lax.rem(6 * WIDTH - place[INDEX] * wide, 6 * WIDTH), 1)[0:1, 0:wide]
    for layer, vectors in enumerate((vectors0, vectors1)):
        grad = vectors[:, 0:wide]
        if layer == 0:
            grad = grad + late
        new = momentum_decay * shared_m[layer : layer + 1, :] + grad
        outs[8][layer : layer + 1, :] = new
        outs[9][layer : layer + 1, :] = shared_w[layer : layer + 1, :] - vector_rate * new
        new = momentum_decay * group_m[layer] + vectors[:, CH : CH + own]
        outs[10][layer] = new
        outs[11][layer] = group_w[layer] - vector_rate * new
    rows = fresh0.shape[0]
    for which, work in enumerate(newton_from(whole, range(4), NS_STEPS)):
        start, stop = SPANS[which]
        put_turned(work, which, rows_s)
        step = own_rows(rows_s, place[INDEX], rows)[:, 0 : stop - start]
        outs[2 * which + 1][0] = new_rows(which, old0[:, start:stop], step)


def run_finish(stage, rows, place, given, *args):
    shapes = []
    for start, stop in SPANS:
        shapes += [sds((LAYERS, rows, stop - start), f32)] * 2
    shapes += [sds(args[8].shape, f32)] * 2 + [sds(args[9].shape, f32)] * 2
    return pl.pallas_call(
        functools.partial(finish_kernel, stage, len(given)),
        out_shape=shapes,
        in_specs=[smem_spec()] + [vmem_spec()] * (len(given) + len(args)),
        out_specs=[vmem_spec()] * len(shapes),
        scratch_shapes=[pltpu.VMEM((WIDTH, HALF), f32)]
        + ([pltpu.VMEM((WIDTH // rows, rows, given[0].shape[2]), bf16)] if len(given) > 1 else []),
        compiler_params=params(SMALL),
        cost_estimate=cost(10),
        name="layer0_newton_finish",
    )(place, *given, *args)


def stages_of(devices):
    bits = [1 << n for n in range(devices.bit_length() - 1)]
    stages = [(bit,) for bit in bits[:2]]
    return stages + [tuple(bits[n : n + 2]) for n in range(2, len(bits), 2)]


def peers(stage):
    return [x * stage[0] for x in range(1, 1 << len(stage))]


def swap(x, axis, mask):
    n = lax.axis_size(axis)
    return lax.ppermute(x, axis, [(i, i ^ mask) for i in range(n)])


def send_parts(parts, stage):
    return [swap(part, "dp", mask) for part, mask in zip(parts, peers(stage))]


def send_all(held, stage):
    return [swap(held, "dp", mask) for mask in peers(stage)]


def part_chunks(stage, index, total, outs):
    radix = 1 << len(stage)
    own = (index // stage[0]) % radix
    for m in range(outs[0].shape[0]):
        for x in range(radix):
            outs[x - 1][m] = total(radix * m + (own ^ x)).astype(bf16)


def join_chunks(stage, index, held, gots, out):
    radix = 1 << len(stage)
    own = (index // stage[0]) % radix
    for m in range(held.shape[0]):
        for x, ref in enumerate((held, *gots)):
            out[radix * m + (own ^ x)] = ref[m]
    rows = held.shape[1]
    if held.shape[2] > 3 * HALF:
        sums = read_sums(held.at[0], rows)
        for ref in gots:
            sums = sums + read_sums(ref.at[0], rows)
        out[0] = with_sums(out[0, :, 0 : 3 * HALF], sums)


def sum_of(refs, n):
    total = refs[0][n].astype(f32)
    for ref in refs[1:]:
        total = total + ref[n].astype(f32)
    return total


def hop_kernel(joined, parted, place, *refs):
    index = place[INDEX]
    n_parts = 0 if parted is None else 1 << len(parted[1])
    outs = refs[len(refs) - len(joined) - n_parts :]
    for stage, out in zip(joined, outs):
        given, refs = refs[: 1 << len(stage)], refs[1 << len(stage) :]
        join_chunks(stage, index, given[0], given[1:], out)
    if parted is not None:
        given = refs[: 1 << len(parted[0])]
        part_chunks(parted[1], index, lambda n: sum_of(given, n), outs[len(joined) :])


def run_hop(place, joins=(), part=None, after=()):
    shapes, inputs = [], []
    for stage, held, gots in joins:
        shapes.append(sds((held.shape[0] << len(stage),) + held.shape[1:], bf16))
        inputs += [held, *gots]
    if part is not None:
        _, stage, keep, gots = part
        shapes += [sds((keep.shape[0] >> len(stage),) + keep.shape[1:], bf16)] * (1 << len(stage))
        inputs += [keep, *gots]
    outs = pl.pallas_call(
        functools.partial(hop_kernel, [join[0] for join in joins], part and part[:2]),
        out_shape=shapes,
        in_specs=[smem_spec()] + [vmem_spec()] * len(inputs) + waits(after),
        out_specs=[vmem_spec()] * len(shapes),
        compiler_params=params(SMALL),
        cost_estimate=cost(1),
        name="hop",
    )(place, *inputs, *after)
    return outs if part is None else (outs[:-1], outs[-1])


def local(
    tokens, cotangent, image_ids, qkv_weight, proj_weight, up_weight, down_weight, shared_vectors, group_vectors,
    qkv_moment, proj_moment, up_moment, down_moment, shared_moment, group_moment,
):
    devices = lax.axis_size("dp")
    index = lax.axis_index("dp")
    place = jnp.stack([index % 2, lax.axis_index("group"), index]).astype(jnp.int32)
    masters = (qkv_weight, proj_weight, up_weight, down_weight)
    moments = (qkv_moment, jnp.swapaxes(proj_moment, 1, 2), up_moment, jnp.swapaxes(down_moment, 1, 2))
    rows = WIDTH // devices
    stages = stages_of(devices)

    att0, mlp0, att1, mlp1, send = run_prepare(place, *masters)
    att0_o = swap(att0, "group", 1)
    gv, gvo = group_vectors, swap(group_vectors, "group", 1)
    mlp0_o = swap(mlp0, "group", 1)
    near = swap(send, "group", 1)
    far = swap(near, "dp", 1)
    sv = shared_vectors

    columns = jnp.swapaxes(image_ids[0].astype(f32), 0, 1).reshape(NS, STRIPE, SIDE)
    ids_t = jnp.pad(columns, ((0, 0), (0, 1), (0, 0)), constant_values=-1.0).reshape(NS * SLOT, SIDE)

    part_own, *rest_own, stream = run_attention(0, True, place, tokens, att0, sv, gv, ids_t)
    saved_own, own_kept = rest_own[:4], rest_own[4:]
    part_other, *saved_other = run_attention(0, False, place, stream, att0_o, sv, gvo, ids_t)
    middle, mid, active, slopes = run_feed(0, place, stream, part_own, part_other, mlp0, mlp0_o, sv, gv, gvo)
    outputs, grad, send1, keep1 = run_last_layer(
        1, devices, place, (middle, cotangent, att1, mlp1, near, far, sv, gv, gvo, ids_t)
    )

    def reduce_late(keep, gots, first):
        for stage, after in zip(stages[first:], stages[first + 1 :]):
            parts, keep = run_hop(place, part=(stage, after, keep, gots))
            gots = send_parts(parts, after)
        return keep, gots

    keep1 = pltpu.with_memory_space_constraint(keep1, pltpu.HBM)
    got1 = send_parts([send1], stages[0])
    parts, keep1 = run_hop(place, part=(stages[0], stages[1], keep1, got1))
    got1 = send_parts(parts, stages[1])
    gmid, gb, big_m, rows_m, bias_m = run_feed_back(
        0, place, grad, mid, slopes, active, mlp0, mlp0_o, sv, gv, gvo, (keep1,)
    )

    def back(mine, extra, after):
        saved, weights, vec = (saved_own, att0, gv) if mine else (saved_other, att0_o, gvo)
        return run_attention_back(0, mine, devices, place, gb, saved, weights, sv, vec, ids_t, extra, after)

    parts, keep1 = run_hop(place, part=(stages[1], stages[2], keep1, got1), after=(rows_m,))
    got1 = send_parts(parts, stages[2])
    da_own, big0 = back(True, (*own_kept, big_m, rows_m, bias_m), (keep1,))
    keep1, got1 = reduce_late(keep1, got1, 2)
    held1, fresh1, vectors1, send0, keep0 = run_momentum(1, devices, place, keep1, got1, moments, big0)
    got1 = send_all(held1, stages[-1])
    got0 = send_parts([send0], stages[0])
    parts, keep0 = run_hop(place, part=(stages[0], stages[1], keep0, got0))
    got0 = send_parts(parts, stages[1])
    (da_other,) = back(False, (), (keep0, held1))
    for stage in stages[-1:2:-1]:
        (held1,) = run_hop(place, joins=[(stage, held1, got1)])
        got1 = send_all(held1, stages[stages.index(stage) - 1])
    (held1, *parts), keep0 = run_hop(
        place, joins=[(stages[2], held1, got1)], part=(stages[1], stages[2], keep0, got0), after=(da_other,)
    )
    got1 = send_all(held1, stages[1])
    got0 = send_parts(parts, stages[2])
    input_grad, norm_sums = run_norm_back(0, place, stream, gmid, da_own, da_other, sv, (keep0, held1))
    keep0, got0 = reduce_late(keep0, got0, 2)
    held0, fresh0, vectors0 = run_momentum(0, devices, place, keep0, got0, moments, norm_sums)
    got0 = send_all(held0, stages[-1])
    def last_join(held, gots):
        if rows % 16 == 0:
            return (held, *gots)
        return (run_hop(place, joins=[(stages[0], held, gots)])[0].reshape(WIDTH, held.shape[2]),)

    (held1,) = run_hop(place, joins=[(stages[1], held1, got1)], after=(held0,))
    given1 = last_join(held1, send_all(held1, stages[0]))
    old0, old1, works = run_newton_begin(stages[0], place, rows, given1, masters, (held0,))
    for stage in stages[-1:2:-1]:
        (held0,) = run_hop(place, joins=[(stage, held0, got0)])
        got0 = send_all(held0, stages[stages.index(stage) - 1])
    (held0,) = run_hop(place, joins=[(stages[2], held0, got0)], after=(works,))
    got0 = send_all(held0, stages[1])
    mine, theirs = run_newton_end(place, rows, works, (held0,))
    theirs = swap(theirs, "dp", 1)
    (held0,) = run_hop(place, joins=[(stages[1], held0, got0)], after=(mine,))
    given0 = last_join(held0, send_all(held0, stages[0]))

    length = shared_moment.shape[1]
    shared_w = lax.dynamic_slice_in_dim(shared_vectors, index * length, length, 1)
    length = group_moment.shape[2]
    group_w = lax.dynamic_slice_in_dim(group_vectors, index * length, length, 2)
    out = run_finish(
        stages[0], rows, place, given0, old0, old1, fresh0, fresh1, mine, theirs, vectors0, vectors1,
        shared_moment, group_moment, shared_w, group_w,
    )
    out = [jnp.swapaxes(x, 1, 2) if n in (2, 3, 6, 7) else x for n, x in enumerate(out)]
    return (outputs, input_grad, *out)


def solution(mesh):
    return jax.shard_map(
        local,
        mesh=mesh,
        in_specs=(
            P("dp", None),
            P("dp", None),
            P("dp", None, None),
            P(None, None, "group"),
            P(None, "group", None),
            P(None, None, "group"),
            P(None, "group", None),
            P(),
            P(None, "group", None),
            P(None, "dp", "group"),
            P(None, "group", "dp"),
            P(None, "dp", "group"),
            P(None, "group", "dp"),
            P(None, "dp"),
            P(None, "group", "dp"),
        ),
        out_specs=(
            P("dp", None),
            P("dp", None),
            P(None, "dp", "group"),
            P(None, "dp", "group"),
            P(None, "group", "dp"),
            P(None, "group", "dp"),
            P(None, "dp", "group"),
            P(None, "dp", "group"),
            P(None, "group", "dp"),
            P(None, "group", "dp"),
            P(None, "dp"),
            P(None, "dp"),
            P(None, "group", "dp"),
            P(None, "group", "dp"),
        ),
        check_vma=False,
    )
```

```python
import functools
import math

import jax
import jax.numpy as jnp
from jax import lax
from jax.experimental import pallas as pl
from jax.experimental.pallas import tpu as pltpu
from jax.sharding import PartitionSpec as P

HEADS = 8
STRIPE = 7
LAYERS = 2
NS_STEPS = 5

epsilon = 1e-05
coeff_first = 3.4445
coeff_second = -4.775
coeff_third = 2.0315
momentum_decay = 0.95
matrix_rate = 0.25
weight_decay = 0.1
vector_rate = 0.001
match_scale = 0.2
masked_score = -1e30

f32 = jnp.float32
bf16 = jnp.bfloat16
LOG2E = 1.4426950408889634
MIB = 1024 * 1024
SMALL, LARGE = 32, 62

SIDE = 42
NS = 6
FA_GANG = 2
GANG = 3
SLOT = 8
ROWS = SIDE * SLOT
KEPT = 208
TOKENS = 320
KEYS = 5 * 256
WIDTH = 256
CH = 128
HALF = 512
HL = 4
HEAD = 32


def dot(a, b):
    return jnp.dot(a, b, preferred_element_type=f32)


def dot_t(a, b):
    return lax.dot_general(a, b, (((1,), (1,)), ((), ())), preferred_element_type=f32)


def dot_rows(a, b):
    return lax.dot_general(a, b, (((0,), (0,)), ((), ())), preferred_element_type=f32)


def lane_head():
    return lax.broadcasted_iota(jnp.int32, (1, CH), 1) // HEAD


def stripe_of(ref, g, s):
    if g == 0:
        block = ref[pl.ds(STRIPE * s, STRIPE)]
    else:
        block = ref[:, pl.ds(s, 1)]
    return block.reshape(ROWS, block.shape[-1])


def put_stripe(ref, g, s, value):
    if g == 0:
        ref[pl.ds(STRIPE * s, STRIPE)] = value.reshape(STRIPE, NS, SLOT, value.shape[-1])
    else:
        ref[:, pl.ds(s, 1)] = value.reshape(SIDE, 1, SLOT, value.shape[-1])


def normed(rows):
    mean = jnp.mean(rows, axis=-1, keepdims=True)
    centred = rows - mean
    spread = jnp.mean(centred * centred, axis=-1, keepdims=True)
    rstd = lax.rsqrt(spread + epsilon)
    return centred * rstd, rstd


def norm_back(grad, hat, rstd, gain):
    scaled = grad * gain
    first = jnp.mean(scaled, axis=-1, keepdims=True)
    second = jnp.mean(scaled * hat, axis=-1, keepdims=True)
    return rstd * (scaled - first - hat * second)


def tile_sum(rows):
    return jnp.sum(rows.reshape(-1, SLOT, rows.shape[-1]), axis=0)


def gelu_parts(x):
    phi = 0.5 + 0.5 * lax.erf(x * math.sqrt(0.5))
    bell = jnp.exp2(x * x * (-0.5 * LOG2E))
    return x * phi, phi + x * bell * (1.0 / math.sqrt(2.0 * math.pi))


def places(ndim):
    shape = (1,) * (ndim - 2) + (SLOT, 1)
    return lax.broadcasted_iota(jnp.int32, shape, ndim - 2)


def fine_shifts(x, g, edge):
    axis = x.ndim - 2
    place = places(x.ndim)
    up = pltpu.roll(x, SLOT - 1, axis)
    down = pltpu.roll(x, 1, axis)
    if g == 0:
        end = x[:, :1] if edge is None else jnp.full_like(x[:, :1], edge)
        after = jnp.concatenate([x[:, 1:], end], axis=1)
        before = jnp.concatenate([end, x[:, :-1]], axis=1)
        up = jnp.where(place == STRIPE - 1, pltpu.roll(after, STRIPE - 1, axis), up)
        down = jnp.where(place == 0, pltpu.roll(before, 2, axis), down)
        if edge is not None:
            up = jnp.where(place == STRIPE, edge, up)
            down = jnp.where(place == STRIPE, edge, down)
    elif edge is not None:
        up = jnp.where(place >= STRIPE - 1, edge, up)
        down = jnp.where((place == 0) | (place == STRIPE), edge, down)
    return up, down


def coarse(x, step, fill):
    if step == 0:
        return x
    end = jnp.full_like(x[:1], fill)
    if step > 0:
        return jnp.concatenate([x[1:], end], axis=0)
    return jnp.concatenate([end, x[:-1]], axis=0)


def masked_neighbours(x, ids, g):
    shape = (STRIPE, NS, SLOT, CH) if g == 0 else (SIDE, SLOT, CH)
    x = x.reshape(shape)
    centre = ids.reshape(shape)
    up, down = fine_shifts(x, g, None)
    up_ids, down_ids = fine_shifts(centre, g, -3.0)
    around = {0: (x, centre), 1: (up, up_ids), -1: (down, down_ids)}
    for row_step in (-1, 0, 1):
        for col_step in (-1, 0, 1):
            tap = 3 * (row_step + 1) + col_step + 1
            coarse_step, fine_step = (row_step, col_step) if g == 0 else (col_step, row_step)
            source, source_ids = around[fine_step]
            if coarse_step == 0 and fine_step == 0:
                yield tap, source.reshape(ROWS, CH)
                continue
            source = coarse(source, coarse_step, 0.0)
            source_ids = coarse(source_ids, coarse_step, -9.0)
            yield tap, jnp.where(source_ids == centre, source, 0.0).reshape(ROWS, CH)


def compact(x):
    width = x.shape[1]
    tiles = x[KEPT:].reshape(2, SLOT, SLOT, width)
    place = lax.broadcasted_iota(jnp.int32, (1, SLOT, 1), 1)
    parts = []
    for j in range(STRIPE):
        first, second = tiles[:, j], pltpu.roll(tiles[:, j + 1], STRIPE - j, 1)
        if j:
            first = pltpu.roll(first, SLOT - j, 1)
        parts.append(jnp.where(place < STRIPE - j, first, second))
    return jnp.concatenate([x[:KEPT], jnp.stack(parts, axis=1).reshape(TOKENS - KEPT, width)], axis=0)


def expand(x):
    width = x.shape[1]
    tiles = x[KEPT:].reshape(2, STRIPE, SLOT, width)
    place = lax.broadcasted_iota(jnp.int32, (1, SLOT, 1), 1)
    parts = [tiles[:, 0]]
    for t in range(1, STRIPE):
        both = pltpu.roll(tiles[:, t - 1], t, 1), pltpu.roll(tiles[:, t], t, 1)
        parts.append(jnp.where(place < t, *both))
    parts.append(pltpu.roll(tiles[:, STRIPE - 1], STRIPE, 1))
    parts = [jnp.where(place < STRIPE, part, 0.0) for part in parts]
    return jnp.concatenate([x[:KEPT], jnp.stack(parts, axis=1).reshape(ROWS - KEPT, width)], axis=0)


WIDE, TAIL = 256, 64


def by_heads(pieces):
    parts = [pieces(h) for h in range(HL)]
    return jnp.concatenate([part[0] for part in parts] + [part[1] for part in parts], axis=0)


def block_diagonal(x):
    head = lane_head()

    def pieces(h):
        own = x * jnp.where(head == h, 1.0, 0.0).astype(bf16)
        return own[:WIDE], own[WIDE:]

    return by_heads(pieces)


def lane_marks(pick):
    lane = lax.broadcasted_iota(jnp.int32, (1, CH), 1)

    def pieces(h):
        mark = jnp.where(pick(lane, h), 1.0, 0.0).astype(bf16)
        return jnp.broadcast_to(mark, (WIDE, CH)), jnp.broadcast_to(mark, (TAIL, CH))

    return by_heads(pieces)


def turned(x):
    return jnp.concatenate([x, jnp.zeros((3 * CH - TOKENS, CH), x.dtype)], axis=0).T[:, 0:TOKENS]


def head_rows(x, h):
    return x[h * HEAD : (h + 1) * HEAD]


def over_queries(left, weights):
    main = [dot(head_rows(left, h), weights[:, h * WIDE : (h + 1) * WIDE]) for h in range(HL)]
    tails = dot(left, weights[:, HL * WIDE :])
    last = []
    for h in range(HL):
        own = head_rows(tails, h)[:, (h // 2) * CH : (h // 2 + 1) * CH]
        last.append(pltpu.roll(own, TAIL, 1) if h % 2 else own)
    return jnp.concatenate([jnp.concatenate(main, axis=0), jnp.concatenate(last, axis=0)], axis=1)


def masked_softmax(q, keys, bias):
    tails = dot_t(q, keys[HL * WIDE :])
    left = lax.broadcasted_iota(jnp.int32, (1, CH), 1) < TAIL
    lowest = jnp.finfo(f32).min
    parts, last = [], []
    for h in range(0, HL, 2):
        scores = dot_t(q, keys[h * WIDE : (h + 2) * WIDE])
        own = [scores[:, n * CH : (n + 1) * CH] + bias[n % 2] for n in range(4)]
        tail = tails[:, (h // 2) * CH : (h // 2 + 1) * CH] + bias[2]
        top = jnp.maximum(jnp.maximum(own[0], own[1]), jnp.where(left, tail, lowest))
        other = jnp.maximum(jnp.maximum(own[2], own[3]), jnp.where(left, lowest, tail))
        top = jnp.max(top, axis=-1, keepdims=True)
        other = jnp.max(other, axis=-1, keepdims=True)
        parts += [jnp.exp2(x - y).astype(bf16) for x, y in zip(own, (top, top, other, other))]
        last.append(jnp.exp2(tail - jnp.where(left, top, other)).astype(bf16))
    return jnp.concatenate(parts + last, axis=1)


def spread_ids(ids_t, idc):
    for r in range(SIDE):
        column = jnp.broadcast_to(ids_t[:, r : r + 1], (NS * SLOT, CH))
        idc[r] = column.reshape(NS, SLOT, CH)


def spread_rows(source, target):
    place = lax.broadcasted_iota(jnp.int32, (SLOT, 1), 0)
    for r in range(SIDE):
        for column in range(NS):
            tile = source[pl.ds(SIDE * r + STRIPE * column, SLOT)]
            target[r, column] = jnp.where(place < STRIPE, tile, 0.0)


def pack_rows(source, target):
    for r in range(SIDE):
        for column in range(NS):
            start = SIDE * r + STRIPE * column
            if start + SLOT <= SIDE * SIDE:
                target[pl.ds(start, SLOT)] = source[r, column]
            else:
                target[pl.ds(start, STRIPE)] = source[r, column, 0:STRIPE]


def first_norm(rows, sv, layer):
    hat, _ = normed(rows)
    return (hat * shared_of(sv, layer, 0) + shared_of(sv, layer, 1)).astype(bf16)


def attend(g, a1, ids, weights, vec):
    mixed = dot(a1, weights)
    value = mixed[:, 2 * CH :] + vec[:, CH : 2 * CH]
    query = (mixed[:, :CH] + vec[:, :CH]) * (HEAD ** -0.5 * LOG2E)
    qkv = compact(jnp.concatenate([query, mixed[:, CH : 2 * CH], value], axis=1)).astype(bf16)
    q, k, v = qkv[:, :CH], qkv[:, CH : 2 * CH], qkv[:, 2 * CH :]
    ids_c = compact(ids)
    key_ids = jnp.concatenate([ids_c, jnp.full((3 * CH - TOKENS, CH), -5.0, f32)], axis=0).T[0:1]
    left = lax.broadcasted_iota(jnp.int32, (1, CH), 1) < TAIL
    last = key_ids[:, 2 * CH :]
    last = jnp.where(left, last, pltpu.roll(last, TAIL, 1))
    bias = [
        jnp.where(ids_c == part, 0.0, masked_score) for part in (key_ids[:, :CH], key_ids[:, CH : 2 * CH], last)
    ]
    e = masked_softmax(q, block_diagonal(k), bias)
    ones = lane_marks(lambda lane, h: lane // HEAD == h)
    both = dot(e, jnp.concatenate([block_diagonal(v), ones], axis=1))
    rl = 1.0 / both[:, CH:]
    att = both[:, :CH] * rl
    total = expand(att) + vec[:, 2 * CH : 3 * CH]
    for tap, near in masked_neighbours(value.astype(bf16).astype(f32), ids, g):
        total = total + near * vec[:, (3 + tap) * CH : (4 + tap) * CH]
    return qkv, e, rl, att.astype(bf16), total.astype(bf16)


def attend_back(g, gbs, ids, weights, proj, vec, qkv, e, rl, att, add):
    d_out = dot_t(gbs, proj).astype(bf16).astype(f32)
    q, k, v = qkv[:, 0:CH], qkv[:, CH : 2 * CH], qkv[:, 2 * CH :]
    scaled = (compact(d_out) * rl).astype(bf16)
    prod = scaled.astype(f32) * att.astype(f32)
    prod_high = prod.astype(bf16)
    prod_low = (prod - prod_high.astype(f32)).astype(bf16)
    lanes = lax.broadcasted_iota(jnp.int32, (CH, CH), 1)
    rows_of = lax.broadcasted_iota(jnp.int32, (CH, CH), 0)
    gather = jnp.where((lanes % HEAD == rows_of // HEAD) & (lanes < 3 * HEAD), 1.0, 0.0).astype(bf16)
    centre = dot(
        jnp.concatenate([prod_high, prod_low], axis=1), jnp.concatenate([gather, gather], axis=0)
    )
    first = centre.astype(bf16).astype(f32)
    rest = centre - first
    second = rest.astype(bf16).astype(f32)
    lane = lax.broadcasted_iota(jnp.int32, (1, CH), 1)
    pieces = jnp.where(lane < HEAD, first, jnp.where(lane < 2 * HEAD, second, rest - second))
    left = jnp.concatenate([scaled, (-pieces).astype(bf16)], axis=1)
    marks = lane_marks(lambda lane, h: (lane % HEAD == h) & (lane < 3 * HEAD))
    right = jnp.concatenate([block_diagonal(v), marks], axis=1)
    ds = (e.astype(f32) * dot_t(left, right)).astype(bf16)
    dq = dot(ds, block_diagonal(k)) * HEAD ** -0.5
    turned_grads = [over_queries(turned(q), ds) * (1.0 / LOG2E), over_queries(turned(scaled), e)]
    grads = jnp.concatenate([dq, jnp.concatenate(turned_grads, axis=0).T[0:TOKENS]], axis=1)
    grads = expand(grads)
    vf = expand(v.astype(f32))
    dv = grads[:, 2 * CH :]
    for tap, near in masked_neighbours(d_out, ids, g):
        mirror = 8 - tap
        dv = dv + near * vec[:, (3 + mirror) * CH : (4 + mirror) * CH]
        if add is not None:
            add(3 + mirror, tile_sum(near * vf))
    dq, dk, dv = grads[:, :CH].astype(bf16), grads[:, CH : 2 * CH].astype(bf16), dv.astype(bf16)
    if add is not None:
        add(0, tile_sum(dq.astype(f32)))
        add(1, tile_sum(dv.astype(f32)))
        add(2, tile_sum(d_out))
    dqkv = jnp.concatenate([dq, dk, dv], axis=1)
    return dqkv, dot_t(dqkv, weights).astype(bf16).astype(f32)


def qkv_of(buffer):
    return buffer[:, 0 : 3 * CH]


def proj_of(buffer):
    return jnp.concatenate([buffer[0:CH, 3 * CH : 4 * CH], buffer[CH : 2 * CH, 3 * CH : 4 * CH]], axis=1)


def up_of(buffer, start):
    return buffer[:, start : start + HALF]


def down_of(buffer, start):
    return jnp.concatenate(
        [buffer[:, start + HALF : start + HALF + WIDTH], buffer[:, start + HALF + WIDTH : start + 2 * HALF]], axis=0
    )


def assemble(whole, near, far, core):
    half = WIDTH // 2
    whole[pl.ds(core * half, half)] = near[...]
    whole[pl.ds((1 - core) * half, half)] = far[...]


def shared_of(sv, layer, index):
    return sv[layer : layer + 1, index * WIDTH : (index + 1) * WIDTH]


def mlp_forward(rows, sv, layer, pairs):
    hat, _ = normed(rows)
    a2 = (hat * shared_of(sv, layer, 3) + shared_of(sv, layer, 4)).astype(bf16)
    parts, kept, slopes = [], [], []
    for up, down, bias in pairs:
        active, slope = gelu_parts(dot(a2, up) + bias)
        active = active.astype(bf16)
        kept.append(active)
        slopes.append(slope.astype(bf16))
        parts.append(dot(active, down).astype(bf16).astype(f32))
    return rows + ((parts[0] + parts[1]) + shared_of(sv, layer, 5)), kept[0], slopes


def mlp_backward(rows, mid, slopes, sv, layer, pairs):
    gm = rows.astype(bf16)
    hat, rstd = normed(mid)
    a2 = (hat * shared_of(sv, layer, 3) + shared_of(sv, layer, 4)).astype(bf16)
    parts, hidden = [], []
    for (up, down, _), slope in zip(pairs, slopes):
        gh = (dot_t(gm, down) * slope.astype(f32)).astype(bf16)
        hidden.append(gh)
        parts.append(dot_t(gh, up).astype(bf16).astype(f32))
    da2 = parts[0] + parts[1]
    new = rows + norm_back(da2, hat, rstd, shared_of(sv, layer, 3))
    low = new.astype(bf16)
    sums = (
        tile_sum(low.astype(f32)), tile_sum(da2 * hat), tile_sum(da2), tile_sum(gm.astype(f32)),
        tile_sum(hidden[0].astype(f32)),
    )
    return new, low, gm, a2, hidden[0], sums


def one_row(tile):
    return jnp.sum(tile, axis=0, keepdims=True)


def pack_vectors(devices, shared_row, group_row):
    rows = WIDTH // devices
    wide = shared_row.shape[1] // devices
    own = group_row.shape[1] // devices
    lines = []
    for i in range(devices):
        pieces = []
        for piece in (shared_row[:, i * wide : (i + 1) * wide], group_row[:, i * own : (i + 1) * own]):
            pieces.append(piece)
            if piece.shape[1] < CH:
                pieces.append(jnp.zeros((1, CH - piece.shape[1]), f32))
        line = jnp.concatenate(pieces, axis=1)
        lines.append(jnp.concatenate([line, jnp.zeros((rows - 1, 2 * CH), f32)], axis=0))
    return jnp.concatenate(lines, axis=0)


def sds(shape, dtype):
    return jax.ShapeDtypeStruct(shape, dtype)


def hbm(shape, dtype):
    return pltpu.HBM(shape, dtype)


def chunk_shapes(devices):
    return [sds((devices // 2, WIDTH // devices, 3 * HALF + 2 * CH), bf16)] * 2


def put_chunks(send, keep, core, start, value):
    rows, width = send.shape[1], value.shape[1]
    for m in range(send.shape[0]):
        even = value[2 * m * rows : (2 * m + 1) * rows]
        odd = value[(2 * m + 1) * rows : (2 * m + 2) * rows]
        keep[m, :, start : start + width] = jnp.where(core == 0, even, odd).astype(bf16)
        send[m, :, start : start + width] = jnp.where(core == 0, odd, even).astype(bf16)


def vmem_spec():
    return pl.BlockSpec(memory_space=pltpu.VMEM)


def smem_spec():
    return pl.BlockSpec(memory_space=pltpu.SMEM)


def waits(arrays):
    return [pl.BlockSpec(memory_space=pl.ANY)] * len(arrays)


def kept(shape):
    return pl.BlockSpec(shape, lambda s: (0,) * len(shape))


def per_step(shape, first=0, count=1):
    return pl.BlockSpec((count,) + shape, lambda s: (s + first,) + (0,) * len(shape))


def cost(us):
    return pl.CostEstimate(flops=int(us * 1.1e9), bytes_accessed=10**6, transcendentals=0)


def params(mib):
    return pltpu.CompilerParams(vmem_limit_bytes=mib * MIB)


CANVAS = (SIDE, NS, SLOT, WIDTH)
CORE, GROUP, INDEX = 0, 1, 2


def prepare_first_kernel(qkv, proj, att):
    att[:, 0 : 3 * CH] = qkv[0].astype(bf16)
    att[0:CH, 3 * CH :] = proj[0, :, 0:CH].astype(bf16)
    att[CH:, 3 * CH :] = proj[0, :, CH:].astype(bf16)


def prepare_rest_kernel(place, qkv, proj, up, down, mlp0, att1, mlp1, send):
    half = WIDTH // 2
    att1[:, 0 : 3 * CH] = qkv[0].astype(bf16)
    att1[0:CH, 3 * CH :] = proj[0, :, 0:CH].astype(bf16)
    att1[CH:, 3 * CH :] = proj[0, :, CH:].astype(bf16)
    for layer, mlp in enumerate((mlp0, mlp1)):
        mlp[:, 0:HALF] = up[layer].astype(bf16)
        mlp[:, HALF : HALF + WIDTH] = down[layer, 0:WIDTH].astype(bf16)
        mlp[:, HALF + WIDTH :] = down[layer, WIDTH:].astype(bf16)
    mine = pl.ds(place[CORE] * half, half)
    send[:, 0:HALF] = att1[mine]
    send[:, HALF:] = mlp1[mine]


def layer_spec(shape, layer):
    return pl.BlockSpec((1,) + shape[1:], lambda s: (layer, 0, 0))


def run_prepare(place, qkv, proj, up, down):
    half = WIDTH // 2
    qkv, proj, up, down = (pltpu.with_memory_space_constraint(x, pltpu.HBM) for x in (qkv, proj, up, down))
    att0 = pl.pallas_call(
        prepare_first_kernel,
        grid=(1,),
        out_shape=sds((WIDTH, HALF), bf16),
        in_specs=[layer_spec(qkv.shape, 0), layer_spec(proj.shape, 0)],
        out_specs=kept((WIDTH, HALF)),
        compiler_params=params(SMALL),
        cost_estimate=cost(1),
        name="prepare_first",
    )(qkv, proj)
    rest = pl.pallas_call(
        prepare_rest_kernel,
        grid=(1,),
        out_shape=[
            hbm((WIDTH, 2 * HALF), bf16), hbm((WIDTH, HALF), bf16), hbm((WIDTH, 2 * HALF), bf16),
            sds((half, 3 * HALF), bf16),
        ],
        in_specs=[smem_spec(), layer_spec(qkv.shape, 1), layer_spec(proj.shape, 1), kept(up.shape), kept(down.shape)],
        out_specs=[
            kept((WIDTH, 2 * HALF)), kept((WIDTH, HALF)), kept((WIDTH, 2 * HALF)), kept((half, 3 * HALF)),
        ],
        compiler_params=params(SMALL),
        cost_estimate=cost(3),
        name="prepare_rest",
    )(place, qkv, proj, up, down)
    return att0, *rest


def attention_kernel(layer, mine, place, given, *refs):
    if mine:
        att_w, sv, gv, ids_t, part, qkv_o, e_o, rl_o, att_o, heads_o, a1_o, stream, idc, tall = refs
    else:
        stream = given
        att_w, sv, gv, ids_t, part, qkv_o, e_o, rl_o, att_o, idc = refs
    s = pl.program_id(0)

    @pl.when(s == 0)
    def _():
        spread_ids(ids_t, idc)
        if mine:
            tall[0 : SIDE * SIDE] = given[...].astype(f32)
            spread_rows(tall, stream)

    frame = place[GROUP] if mine else 1 - place[GROUP]
    for g in range(2):
        @pl.when(frame == g)
        def _(g=g):
            for n in range(FA_GANG):
                row = FA_GANG * s + n
                a1 = first_norm(stripe_of(stream, g, row), sv, layer)
                qkv, e, rl, att, heads = attend(g, a1, stripe_of(idc, g, row), qkv_of(att_w), gv[layer])
                qkv_o[n] = qkv
                e_o[n] = e
                rl_o[n] = rl
                att_o[n] = att
                part[n] = dot(heads, proj_of(att_w)).astype(bf16).astype(f32)
                if mine:
                    heads_o[n] = heads
                    a1_o[n] = a1


ATT_SAVED = [((TOKENS, 3 * CH), bf16), ((TOKENS, KEYS), bf16), ((TOKENS, CH), f32), ((TOKENS, CH), bf16)]


def run_attention(layer, mine, place, stream, weights, sv, gv, ids_t):
    outs = [((ROWS, WIDTH), f32)] + ATT_SAVED + ([((ROWS, CH), bf16), ((ROWS, WIDTH), bf16)] if mine else [])
    inputs = (stream, weights, sv, gv, ids_t)
    return pl.pallas_call(
        functools.partial(attention_kernel, layer, mine),
        grid=(NS // FA_GANG,),
        out_shape=[(sds if n == 0 else hbm)((NS,) + shape, dtype) for n, (shape, dtype) in enumerate(outs)]
        + ([sds(CANVAS, f32)] if mine else []),
        in_specs=[smem_spec(), kept(stream.shape) if mine else vmem_spec()] + [kept(x.shape) for x in inputs[1:]],
        out_specs=[per_step(shape, 0, FA_GANG) for shape, _ in outs] + ([kept(CANVAS)] if mine else []),
        scratch_shapes=[pltpu.VMEM((SIDE, NS, SLOT, CH), f32)]
        + ([pltpu.VMEM((SIDE * SIDE + 4, WIDTH), f32)] if mine else []),
        compiler_params=params(SMALL),
        cost_estimate=cost(11),
        name=f"layer{layer}_attention_{'own' if mine else 'other'}",
    )(place, *inputs)


def in_frames(own, mine, other, n):
    def across(ref):
        return ref[n].reshape(ROWS, WIDTH)

    def down(ref):
        columns = [ref[column, pl.ds(STRIPE * n, STRIPE)] for column in range(NS)]
        return jnp.stack(columns, axis=1).reshape(ROWS, WIDTH)

    return jnp.where(own == 0, across(mine), down(mine)) + jnp.where(own == 0, down(other), across(other))


def frame_views(mine, other):
    return [x.reshape(NS, SIDE, SLOT, WIDTH) for x in (mine, other)]


def canvas_block(count=1):
    return pl.BlockSpec((STRIPE * count, NS, SLOT, WIDTH), lambda s: (s, 0, 0, 0))


def feed_kernel(
    layer, place, stream, mine, other, mlp_w, mlp_o, sv, gv, gvo,
    out, mid, active, slopes,
):
    pairs = [
        (up_of(w, 0), down_of(w, 0), v[layer][:, 12 * CH :]) for w, v in ((mlp_w, gv), (mlp_o, gvo))
    ]
    for n in range(GANG):
        both = in_frames(place[GROUP], mine, other, GANG * pl.program_id(0) + n)
        rows = stripe_of(stream, 0, n) + (both + shared_of(sv, layer, 2))
        put_stripe(mid, 0, n, rows)
        new, held, slope = mlp_forward(rows, sv, layer, pairs)
        put_stripe(out, 0, n, new)
        active[n] = held
        slopes[n, 0] = slope[0]
        slopes[n, 1] = slope[1]


def run_feed(layer, place, stream, mine, other, mlp_w, mlp_o, sv, gv, gvo):
    rest = (mlp_w, mlp_o, sv, gv, gvo)
    return pl.pallas_call(
        functools.partial(feed_kernel, layer),
        grid=(NS // GANG,),
        out_shape=[
            hbm(CANVAS, f32), hbm(CANVAS, f32), hbm((NS, ROWS, HALF), bf16), hbm((NS, 2, ROWS, HALF), bf16)
        ],
        in_specs=[smem_spec(), canvas_block(GANG)] + [vmem_spec()] * 2 + [kept(x.shape) for x in rest],
        out_specs=[
            canvas_block(GANG), canvas_block(GANG), per_step((ROWS, HALF), 0, GANG), per_step((2, ROWS, HALF), 0, GANG)
        ],
        compiler_params=params(SMALL),
        cost_estimate=cost(10),
        name=f"layer{layer}_feed_forward",
    )(place, stream, *frame_views(mine, other), *rest)


def last_layer_kernel(
    layer, devices, place, stream, cot, att_w, mlp_w, near, far, sv, gv, gvo, ids_t,
    out, grad_in, send, keep,
    whole, att2, gv2, idc, mid, gmid, gb, qkv_s, e_s, rl_s, att_s, heads_s, active_s, a1_s, dqkv_s, gb_s,
    a2_s, gh_s, gm_s, acc_s, acc_b1, acc_g, tall,
):
    own = place[GROUP]
    assemble(whole, near, far, place[CORE])
    att2[own] = att_w[...]
    att2[1 - own] = whole[:, 0:HALF]
    gv2[own] = gv[layer]
    gv2[1 - own] = gvo[layer]
    spread_ids(ids_t, idc)
    acc_s[...] = jnp.zeros_like(acc_s)
    acc_b1[...] = jnp.zeros_like(acc_b1)
    acc_g[...] = jnp.zeros_like(acc_g)

    def norms(first, carry):
        for n in range(GANG):
            s = GANG * first + n
            put_stripe(gmid, 0, s, first_norm(stripe_of(stream, 0, s), sv, layer).astype(f32))
        return carry

    lax.fori_loop(0, NS // GANG, norms, 0)

    for g in range(2):
        def gang(first, carry, g=g):
            for n in range(GANG):
                s = GANG * first + n
                i = g * NS + s
                a1 = stripe_of(gmid, g, s).astype(bf16)
                qkv, e, rl, att, heads = attend(g, a1, stripe_of(idc, g, s), qkv_of(att2[g]), gv2[g])
                qkv_s[i] = qkv
                e_s[i] = e
                rl_s[i] = rl
                att_s[i] = att
                part = dot(heads, proj_of(att2[g])).astype(bf16).astype(f32)
                if g == 0:
                    put_stripe(mid, g, s, part)
                else:
                    rows = stripe_of(stream, g, s)
                    put_stripe(mid, g, s, rows + ((stripe_of(mid, g, s) + part) + shared_of(sv, layer, 2)))
                a1_s[g, s] = a1
                heads_s[g, s] = heads
            return carry

        lax.fori_loop(0, NS // GANG, gang, 0)

    def pairs():
        return [
            (up_of(mlp_w, 0), down_of(mlp_w, 0), gv[layer][:, 12 * CH :]),
            (up_of(whole, HALF), down_of(whole, HALF), gvo[layer][:, 12 * CH :]),
        ]

    tall[0 : SIDE * SIDE] = cot[...].astype(f32)
    spread_rows(tall, gmid)

    def block(s):
        rows = stripe_of(mid, 0, s)
        new, held, slope = mlp_forward(rows, sv, layer, pairs())
        put_stripe(grad_in, 0, s, new)
        active_s[s] = held
        grad = stripe_of(gmid, 0, s)
        new, low, gm, a2, gh, sums = mlp_backward(grad, rows, slope, sv, layer, pairs())
        put_stripe(gmid, 0, s, new)
        put_stripe(gb, 0, s, low.astype(f32))
        gm_s[s] = gm
        a2_s[s] = a2
        gh_s[s] = gh
        for index, value in zip((2, 3, 4, 5), sums):
            acc_s[index] += value
        acc_b1[...] += sums[4]

    def blocks(first, carry):
        for n in range(GANG):
            block(GANG * first + n)
        return carry

    lax.fori_loop(0, NS // GANG, blocks, 0)
    pack_rows(grad_in, tall)
    out[...] = tall[0 : SIDE * SIDE].astype(bf16)

    for g in range(2):
        def gang(first, carry, g=g):
            def add(index, value):
                acc_g[g, index] += value

            for n in range(GANG):
                s = GANG * first + n
                i = g * NS + s
                gbs = stripe_of(gb, g, s).astype(bf16)
                dqkv, part = attend_back(
                    g, gbs, stripe_of(idc, g, s), qkv_of(att2[g]), proj_of(att2[g]), gv2[g], qkv_s[i], e_s[i],
                    rl_s[i], att_s[i], add,
                )
                if g == 0:
                    put_stripe(mid, g, s, part)
                else:
                    put_stripe(mid, g, s, stripe_of(mid, g, s) + part)
                dqkv_s[g, s] = dqkv
                gb_s[g, s] = gbs
            return carry

        lax.fori_loop(0, NS // GANG, gang, 0)

    def final(first, carry):
        for n in range(GANG):
            s = GANG * first + n
            hat, rstd = normed(stripe_of(stream, 0, s))
            da = stripe_of(mid, 0, s)
            acc_s[0] += tile_sum(da * hat)
            acc_s[1] += tile_sum(da)
            put_stripe(
                grad_in, 0, s, stripe_of(gmid, 0, s) + norm_back(da, hat, rstd, shared_of(sv, layer, 0))
            )
        return carry

    lax.fori_loop(0, NS // GANG, final, 0)

    def flat(ref):
        return ref[...].reshape(NS * ROWS, ref.shape[-1])

    core = place[CORE]
    put_chunks(send, keep, core, 0, dot_rows(flat(a1_s.at[own]), flat(dqkv_s.at[own])))
    put_chunks(send, keep, core, 3 * CH, dot_rows(flat(gb_s.at[own]), flat(heads_s.at[own])))
    put_chunks(send, keep, core, HALF, dot_rows(flat(a2_s), flat(gh_s)))
    put_chunks(send, keep, core, 2 * HALF, dot_rows(flat(gm_s), flat(active_s)))
    shared_row = jnp.concatenate([one_row(acc_s[index]) for index in range(6)], axis=1)
    group_row = jnp.concatenate([one_row(acc_g[own, index]) for index in range(12)] + [one_row(acc_b1[...])], axis=1)
    put_chunks(send, keep, core, 3 * HALF, pack_vectors(devices, shared_row, group_row))


def run_last_layer(layer, devices, place, args):
    return pl.pallas_call(
        functools.partial(last_layer_kernel, layer, devices),
        out_shape=[sds((SIDE * SIDE, WIDTH), bf16), sds(CANVAS, f32)] + chunk_shapes(devices),
        in_specs=[smem_spec()] + [vmem_spec()] * len(args),
        out_specs=[vmem_spec()] * 4,
        scratch_shapes=[
            pltpu.VMEM((WIDTH, 3 * HALF), bf16),
            pltpu.VMEM((2, WIDTH, HALF), bf16),
            pltpu.VMEM((2, 1, 16 * CH), f32),
            pltpu.VMEM((SIDE, NS, SLOT, CH), f32),
            pltpu.VMEM(CANVAS, f32),
            pltpu.VMEM(CANVAS, f32),
            pltpu.VMEM(CANVAS, f32),
            pltpu.VMEM((2 * NS, TOKENS, 3 * CH), bf16),
            pltpu.VMEM((2 * NS, TOKENS, KEYS), bf16),
            pltpu.VMEM((2 * NS, TOKENS, CH), f32),
            pltpu.VMEM((2 * NS, TOKENS, CH), bf16),
            pltpu.VMEM((2, NS, ROWS, CH), bf16),
            pltpu.VMEM((NS, ROWS, HALF), bf16),
            pltpu.VMEM((2, NS, ROWS, WIDTH), bf16),
            pltpu.VMEM((2, NS, ROWS, 3 * CH), bf16),
            pltpu.VMEM((2, NS, ROWS, WIDTH), bf16),
            pltpu.VMEM((NS, ROWS, WIDTH), bf16),
            pltpu.VMEM((NS, ROWS, HALF), bf16),
            pltpu.VMEM((NS, ROWS, WIDTH), bf16),
            pltpu.VMEM((6, SLOT, WIDTH), f32),
            pltpu.VMEM((SLOT, HALF), f32),
            pltpu.VMEM((2, 12, SLOT, CH), f32),
            pltpu.VMEM((SIDE * SIDE + 4, WIDTH), f32),
        ],
        compiler_params=params(LARGE),
        cost_estimate=cost(65),
        name=f"layer{layer}_forward_backward",
    )(place, *args)


def feed_back_kernel(
    layer, place, grad, mid, slopes, active, mlp_w, mlp_o, sv, gv, gvo, *refs,
):
    gmid, gb, big, rows_out, bias_out, a2_s, gh_s, gm_s, act_s, acc_s, acc_b1 = refs[-11:]
    s = pl.program_id(0)

    @pl.when(s == 0)
    def _():
        acc_s[...] = jnp.zeros_like(acc_s)
        acc_b1[...] = jnp.zeros_like(acc_b1)

    pairs = [
        (up_of(w, 0), down_of(w, 0), v[layer][:, 12 * CH :]) for w, v in ((mlp_w, gv), (mlp_o, gvo))
    ]
    for n in range(GANG):
        new, low, gm, a2, gh, sums = mlp_backward(
            stripe_of(grad, 0, n), stripe_of(mid, 0, n), [slopes[n, 0], slopes[n, 1]], sv, layer, pairs
        )
        put_stripe(gmid, 0, n, new)
        put_stripe(gb, 0, n, low.astype(f32))
        gm_s[GANG * s + n] = gm
        a2_s[GANG * s + n] = a2
        gh_s[GANG * s + n] = gh
        act_s[GANG * s + n] = active[n]
        for index in range(4):
            acc_s[index] += sums[index]
        acc_b1[...] += sums[4]

    @pl.when(s == NS // GANG - 1)
    def _():
        def flat(ref):
            return ref[...].reshape(NS * ROWS, ref.shape[-1])

        big[:, 0:HALF] = dot_rows(flat(a2_s), flat(gh_s)).astype(bf16)
        big[:, HALF:] = dot_rows(flat(gm_s), flat(act_s)).astype(bf16)
        rows_out[...] = jnp.concatenate([one_row(acc_s[index]) for index in range(4)], axis=1)
        bias_out[...] = one_row(acc_b1[...])


def run_feed_back(layer, place, grad, mid, slopes, active, mlp_w, mlp_o, sv, gv, gvo, after):
    rest = (mlp_w, mlp_o, sv, gv, gvo)
    mid, slopes, active = (pltpu.with_memory_space_constraint(x, pltpu.HBM) for x in (mid, slopes, active))
    return pl.pallas_call(
        functools.partial(feed_back_kernel, layer),
        grid=(NS // GANG,),
        out_shape=[
            sds(CANVAS, f32), sds(CANVAS, f32), sds((WIDTH, 2 * HALF), bf16), sds((1, 4 * WIDTH), f32),
            sds((1, HALF), f32),
        ],
        in_specs=[smem_spec(), canvas_block(GANG), canvas_block(GANG), per_step((2, ROWS, HALF), 0, GANG), per_step((ROWS, HALF), 0, GANG)]
        + [kept(x.shape) for x in rest]
        + waits(after),
        out_specs=[canvas_block(GANG), canvas_block(GANG), kept((WIDTH, 2 * HALF)), kept((1, 4 * WIDTH)), kept((1, HALF))],
        scratch_shapes=[
            pltpu.VMEM((NS, ROWS, WIDTH), bf16),
            pltpu.VMEM((NS, ROWS, HALF), bf16),
            pltpu.VMEM((NS, ROWS, WIDTH), bf16),
            pltpu.VMEM((NS, ROWS, HALF), bf16),
            pltpu.VMEM((4, SLOT, WIDTH), f32),
            pltpu.VMEM((SLOT, HALF), f32),
        ],
        compiler_params=params(SMALL),
        cost_estimate=cost(11),
        name=f"layer{layer}_feed_backward",
    )(place, grad, mid, slopes, active, *rest, *after)


def attention_back_kernel(layer, mine, devices, place, gb, qkv, e, rl, att, *refs):
    if mine:
        att_w, sv, gv, ids_t, heads, a1, big_m, rows_m, bias_m = refs[:9]
        da, big, idc, dqkv_s, gb_s, acc_g = refs[-6:]
    else:
        att_w, sv, gv, ids_t = refs[:4]
        da, idc = refs[-2:]
    step = pl.program_id(0)

    @pl.when(step == 0)
    def _():
        spread_ids(ids_t, idc)
        if mine:
            acc_g[...] = jnp.zeros_like(acc_g)

    def add(index, value):
        acc_g[index] += value

    frame = place[GROUP] if mine else 1 - place[GROUP]
    for g in range(2):
        @pl.when(frame == g)
        def _(g=g):
            for n in range(GANG):
                s = GANG * step + n
                gbs = stripe_of(gb, g, s).astype(bf16)
                dqkv, part = attend_back(
                    g, gbs, stripe_of(idc, g, s), qkv_of(att_w), proj_of(att_w), gv[layer], qkv[n], e[n], rl[n], att[n],
                    add if mine else None,
                )
                da[n] = part
                if mine:
                    dqkv_s[s] = dqkv
                    gb_s[s] = gbs

    if mine:
        @pl.when(step == NS // GANG - 1)
        def _():
            def flat(ref):
                return ref[...].reshape(NS * ROWS, ref.shape[-1])

            big[:, 0 : 3 * CH] = dot_rows(flat(a1), flat(dqkv_s)).astype(bf16)
            big[:, 3 * CH : HALF] = dot_rows(flat(gb_s), flat(heads)).astype(bf16)
            big[:, HALF : 3 * HALF] = big_m[...]
            shared_row = jnp.concatenate([jnp.zeros((1, 2 * WIDTH), f32), rows_m[...]], axis=1)
            group_row = jnp.concatenate([one_row(acc_g[index]) for index in range(12)] + [bias_m[...]], axis=1)
            big[:, 3 * HALF :] = pack_vectors(devices, shared_row, group_row).astype(bf16)


def run_attention_back(layer, mine, devices, place, gb, saved, weights, sv, gv, ids_t, extra, after):
    rest = (weights, sv, gv, ids_t, *extra)
    outs = [sds((NS, ROWS, WIDTH), f32)]
    out_specs = [per_step((ROWS, WIDTH), 0, GANG)]
    scratch = [pltpu.VMEM((SIDE, NS, SLOT, CH), f32)]
    if mine:
        outs.append(sds((WIDTH, 3 * HALF + 2 * CH), bf16))
        out_specs.append(kept(outs[1].shape))
        scratch += [
            pltpu.VMEM((NS, ROWS, 3 * CH), bf16),
            pltpu.VMEM((NS, ROWS, WIDTH), bf16),
            pltpu.VMEM((12, SLOT, CH), f32),
        ]
    inputs = (place, gb, *saved, *rest, *after)
    return pl.pallas_call(
        functools.partial(attention_back_kernel, layer, mine, devices),
        grid=(NS // GANG,),
        out_shape=outs,
        in_specs=[smem_spec(), vmem_spec()]
        + [per_step(shape, 0, GANG) for shape, _ in ATT_SAVED]
        + [kept(x.shape) for x in rest]
        + waits(after),
        out_specs=out_specs,
        scratch_shapes=scratch,
        compiler_params=params(SMALL),
        cost_estimate=cost(10),
        name=f"layer{layer}_attention_back_{'own' if mine else 'other'}",
    )(*inputs)


def norm_back_kernel(layer, place, stream, gmid, mine, other, sv, *refs):
    out, sums, grad_in, acc = refs[-4:]
    s = pl.program_id(0)

    @pl.when(s == 0)
    def _():
        acc[...] = jnp.zeros_like(acc)

    for n in range(GANG):
        da = in_frames(place[GROUP], mine, other, GANG * s + n)
        hat, rstd = normed(stripe_of(stream, 0, n))
        acc[0] += tile_sum(da * hat)
        acc[1] += tile_sum(da)
        new = stripe_of(gmid, 0, n) + norm_back(da, hat, rstd, shared_of(sv, layer, 0))
        put_stripe(grad_in, 0, GANG * s + n, new)

    @pl.when(s == NS // GANG - 1)
    def _():
        pack_rows(grad_in, out)
        sums[...] = jnp.concatenate([one_row(acc[0]), one_row(acc[1])], axis=1)


def run_norm_back(layer, place, stream, gmid, mine, other, sv, after):
    return pl.pallas_call(
        functools.partial(norm_back_kernel, layer),
        grid=(NS // GANG,),
        out_shape=[sds((SIDE * SIDE, WIDTH), f32), sds((1, 2 * WIDTH), f32)],
        in_specs=[smem_spec(), canvas_block(GANG), canvas_block(GANG)] + [vmem_spec()] * 2 + [kept(sv.shape)] + waits(after),
        out_specs=[kept((SIDE * SIDE, WIDTH)), kept((1, 2 * WIDTH))],
        scratch_shapes=[pltpu.VMEM(CANVAS, f32), pltpu.VMEM((2, SLOT, WIDTH), f32)],
        compiler_params=params(SMALL),
        cost_estimate=cost(4),
        name=f"layer{layer}_norm_backward",
    )(place, stream, gmid, *frame_views(mine, other), sv, *after)


def halves_of(x):
    high = x.astype(bf16)
    return high, (x - high.astype(f32)).astype(bf16)


def split_dot(a, b, dims):
    (a_high, a_low), (b_high, b_low) = halves_of(a), halves_of(b)
    left = jnp.concatenate([a_high, a_high, a_low], axis=1)
    right = jnp.concatenate([b_high, b_low, b_high], axis=dims[1][0])
    return lax.dot_general(left, right, (dims, ((), ())), preferred_element_type=f32)


SPANS = ((0, 3 * CH), (3 * CH, HALF), (HALF, 2 * HALF), (2 * HALF, 3 * HALF))


def own_rows(ref, index, rows):
    if rows % SLOT == 0:
        return ref[pl.ds(pl.multiple_of(index * rows, SLOT), rows)]
    start = index * rows
    base = pl.multiple_of((start // SLOT) * SLOT, SLOT)
    return pltpu.roll(ref[pl.ds(base, SLOT)], SLOT - (start - base), 0)[0:rows]


def sums_width(rows):
    return max(CH, SLOT * CH // rows)


def sums_blocks(rows):
    per = sums_width(rows) // CH
    return [(b // per, 3 * HALF + (b % per) * CH) for b in range(SLOT)]


def read_sums(ref, rows):
    blocks = [ref[row : row + 1, lane : lane + CH].astype(f32) for row, lane in sums_blocks(rows)]
    return jnp.concatenate([blocks[n] + blocks[n + 4] for n in range(4)], axis=1)


def with_sums(matrix, sums):
    rows, width = matrix.shape[0], sums_width(matrix.shape[0])
    high, low = halves_of(sums)
    parts = [x[:, n * CH : (n + 1) * CH] for x in (high, low) for n in range(4)]
    per = width // CH
    lines = [jnp.concatenate(parts[n : n + per], axis=1) for n in range(0, SLOT, per)]
    if rows > len(lines):
        lines.append(jnp.zeros((rows - len(lines), width), bf16))
    beside = jnp.concatenate([x.astype(f32) for x in lines], axis=0).astype(bf16)
    return jnp.concatenate([matrix, beside], axis=1)


def momentum_kernel(layer, n_got, place, keep, *refs):
    gots, (qkv, proj, up, down, extra, whole, fresh, vectors), refs = refs[:n_got], refs[n_got : n_got + 8], refs[n_got + 8 :]
    total = keep[0].astype(f32)
    for got in gots:
        total = total + got[0].astype(f32)
    matrix = total[:, 0 : 3 * HALF]
    old = jnp.concatenate([qkv[layer], proj[layer], up[layer], down[layer]], axis=1)
    new = momentum_decay * old + matrix
    fresh[...] = new
    ahead = (matrix + momentum_decay * new).astype(bf16)
    vectors[...] = total[0:1, 3 * HALF :]
    if layer == 0:
        whole[0] = with_sums(ahead, extra[...])
    else:
        whole[0] = ahead
        put_chunks(*refs, place[CORE], 0, extra[...].astype(f32))


def run_momentum(layer, devices, place, keep, gots, moments, extra):
    rows = keep.shape[1]
    width = 3 * HALF + (0 if layer else sums_width(rows))
    outs = [sds((1, rows, width), bf16), hbm((rows, 3 * HALF), f32), sds((1, 2 * CH), f32)]
    if layer:
        outs += chunk_shapes(devices)
    return pl.pallas_call(
        functools.partial(momentum_kernel, layer, len(gots)),
        out_shape=outs,
        in_specs=[smem_spec()] + [vmem_spec()] * (6 + len(gots)),
        out_specs=[vmem_spec()] * len(outs),
        compiler_params=params(SMALL),
        cost_estimate=cost(1),
        name=f"layer{layer}_momentum",
    )(place, keep, *gots, *moments, extra)


def square_dot(x, dims):
    high, low = halves_of(x)
    mixed = lax.dot_general(high, low, (dims, ((), ())), preferred_element_type=f32)
    return lax.dot_general(high, high, (dims, ((), ())), preferred_element_type=f32) + (mixed + mixed.T)


def newton(works, steps):
    for _ in range(steps):
        grams = [square_dot(work, ((1,), (1,))) for work in works]
        blends = [coeff_second * gram + coeff_third * square_dot(gram, ((1,), (0,))) for gram in grams]
        works = [
            coeff_first * work + split_dot(blend, work, ((1,), (0,)))
            for work, blend in zip(works, blends)
        ]
    return works


def joined(stage, place, given, scratch):
    if len(given) == 1:
        return given[0][...]
    join_chunks(stage, place[INDEX], given[0], given[1:], scratch)
    return scratch[...].reshape(WIDTH, scratch.shape[2])


def newton_from(whole, picks, steps):
    works = [whole[:, SPANS[which][0] : SPANS[which][1]].astype(f32) for which in picks]
    works = [work.T if which == 1 else work for which, work in zip(picks, works)]
    lows = [work.astype(bf16) for work in works]
    factors = [1.0 / (jnp.sqrt(jnp.sum(work * work)) + 1e-07) for work in works]
    grams = [dot_t(low, low) * (factor * factor) for low, factor in zip(lows, factors)]
    blends = [coeff_second * gram + coeff_third * square_dot(gram, ((1,), (0,))) for gram in grams]
    works = [
        (coeff_first * work + dot(jnp.concatenate(halves_of(blend), axis=1), jnp.concatenate([low, low], axis=0))) * factor
        for work, low, blend, factor in zip(works, lows, blends, factors)
    ]
    return newton(works, steps - 1)


def old_rows(layer, index, rows, masters, turned):
    parts = []
    for which, master in enumerate(masters):
        width = SPANS[which][1] - SPANS[which][0]
        if which % 2 == 1:
            tile = (index * rows) // CH
            columns = pl.ds(pl.multiple_of(tile * CH, CH), CH)
            turned[0:CH, 0:width] = master[layer, :, columns].T
            parts.append(own_rows(turned, index - tile * (CH // rows), rows)[:, 0:width])
        else:
            parts.append(own_rows(master.at[layer], index, rows))
    return parts


def new_rows(which, old, step):
    size = matrix_rate * match_scale * math.sqrt((3 * CH, WIDTH, HALF, HALF)[which])
    return old * (1.0 - matrix_rate * weight_decay) - size * step


def last_rows(works, picks, index, rows, scratch):
    def spot(n, which):
        return scratch.at[2 * n + which]

    def rows_of(n, which, value):
        ref, width = spot(n, which), value.shape[1]
        ref[:, 0:width] = value
        return own_rows(ref, index, rows)[:, 0:width]

    if rows % SLOT:
        ended = newton(works, 1)
        return [rows_of(n, 0, work.T if which == 1 else work) for n, (which, work) in enumerate(zip(picks, ended))]
    grams = [square_dot(work, ((1,), (1,))) for work in works]
    left = [
        (gram, work) if which == 1 else (rows_of(n, 0, gram), rows_of(n, 1, work))
        for n, (which, work, gram) in enumerate(zip(picks, works, grams))
    ]
    blends = [
        coeff_second * own + coeff_third * split_dot(own, gram, ((1,), (0,))) for (own, _), gram in zip(left, grams)
    ]
    ended = [
        coeff_first * own + split_dot(blend, work, ((1,), (0,))) for (_, own), blend, work in zip(left, blends, works)
    ]
    return [rows_of(n, 0, own.T) if which == 1 else own for n, (which, own) in enumerate(zip(picks, ended))]


SHARES = ((0, 2), (1, 3))
SHARE_WIDTH = 3 * CH + HALF


EARLY_STEPS = 2


def share_spots(picks):
    start, spots = 0, []
    for which in picks:
        width = SPANS[which][1] - SPANS[which][0]
        spots.append((which, CH if which == 1 else WIDTH, start, start + (WIDTH if which == 1 else width)))
        start += max(width, WIDTH)
    return spots


def newton_begin_kernel(stage, n_given, n_after, place, *refs):
    given, masters = refs[:n_given], refs[n_given : n_given + 4]
    old0, old1, works_o, turned_s, *scratch = refs[n_given + 4 + n_after :]
    index, rows = place[INDEX], old0.shape[0]
    whole = joined(stage, place, given, scratch[0] if scratch else None)
    for core, picks in enumerate(SHARES):
        @pl.when(place[CORE] == core)
        def _(picks=picks):
            for layer, old in enumerate((old0, old1)):
                for (start, stop), part in zip(SPANS, old_rows(layer, index, rows, masters, turned_s)):
                    old[:, start:stop] = part
            for (_, height, start, stop), work in zip(share_spots(picks), newton_from(whole, picks, EARLY_STEPS)):
                works_o[0:height, start:stop] = work


def newton_end_kernel(place, works, *refs):
    mine, theirs, rows_s = refs[-3:]
    index, rows = place[INDEX], mine.shape[0]
    for core, picks in enumerate(SHARES):
        @pl.when(place[CORE] == core)
        def _(picks=picks, core=core):
            spots = share_spots(picks)
            begun = [works[0:height, start:stop] for _, height, start, stop in spots]
            mine[...] = jnp.zeros_like(mine)
            theirs[...] = jnp.zeros_like(theirs)
            nearly = newton(begun, NS_STEPS - EARLY_STEPS - 1)
            if (2 * rows) % SLOT == 0:
                both = last_rows(nearly, picks, index // 2, 2 * rows, rows_s)
                pairs = [(block[0:rows], block[rows:]) for block in both]
            else:
                pairs = list(
                    zip(*[last_rows(nearly, picks, 2 * (index // 2) + n, rows, rows_s) for n in range(2)])
                )
            for (_, _, start, _), pair in zip(spots, pairs):
                width = pair[0].shape[1]
                mine[:, start : start + width] = pair[core]
                theirs[:, start : start + width] = pair[1 - core]


def run_newton_begin(stage, place, rows, given, masters, after):
    return pl.pallas_call(
        functools.partial(newton_begin_kernel, stage, len(given), len(after)),
        out_shape=[hbm((rows, 3 * HALF), f32)] * 2 + [sds((WIDTH, SHARE_WIDTH), f32)],
        in_specs=[smem_spec()] + [vmem_spec()] * (len(given) + 4) + waits(after),
        out_specs=[vmem_spec()] * 3,
        scratch_shapes=[pltpu.VMEM((WIDTH, HALF), f32)]
        + ([pltpu.VMEM((WIDTH // rows, rows, 3 * HALF), bf16)] if len(given) > 1 else []),
        compiler_params=params(SMALL),
        cost_estimate=cost(3),
        name="layer1_newton_begin",
    )(place, *given, *masters, *after)


def run_newton_end(place, rows, works, after):
    return pl.pallas_call(
        newton_end_kernel,
        out_shape=[sds((rows, SHARE_WIDTH), f32)] * 2,
        in_specs=[smem_spec(), vmem_spec()] + waits(after),
        out_specs=[vmem_spec()] * 2,
        scratch_shapes=[pltpu.VMEM((4, WIDTH, HALF), f32)],
        compiler_params=params(SMALL),
        cost_estimate=cost(4),
        name="layer1_newton_end",
    )(place, works, *after)


def finish_kernel(stage, n_given, place, *refs):
    given, refs = refs[:n_given], refs[n_given:]
    old0, old1, fresh0, fresh1, mine, theirs, vectors0, vectors1, shared_m, group_m, shared_w, group_w = refs[:12]
    outs, (rows_s, *scratch) = refs[12:24], refs[24:]
    whole = joined(stage, place, given, scratch[0] if scratch else None)
    for layer, fresh in enumerate((fresh0, fresh1)):
        for which, (start, stop) in enumerate(SPANS):
            outs[2 * which][layer] = fresh[:, start:stop]
    for core, picks in enumerate(SHARES):
        share = jnp.where(place[CORE] == core, mine[...], theirs[...])
        for which, _, first, _ in share_spots(picks):
            start, stop = SPANS[which]
            outs[2 * which + 1][1] = new_rows(which, old1[:, start:stop], share[:, first : first + stop - start])
    wide, own = shared_m.shape[1], group_m.shape[2]
    late = jnp.concatenate([read_sums(whole, fresh0.shape[0]), jnp.zeros((1, 4 * WIDTH), f32)], axis=1)
    late = jnp.broadcast_to(late, (SLOT, 6 * WIDTH))
    late = pltpu.roll(late, lax.rem(6 * WIDTH - place[INDEX] * wide, 6 * WIDTH), 1)[0:1, 0:wide]
    for layer, vectors in enumerate((vectors0, vectors1)):
        grad = vectors[:, 0:wide]
        if layer == 0:
            grad = grad + late
        new = momentum_decay * shared_m[layer : layer + 1, :] + grad
        outs[8][layer : layer + 1, :] = new
        outs[9][layer : layer + 1, :] = shared_w[layer : layer + 1, :] - vector_rate * new
        new = momentum_decay * group_m[layer] + vectors[:, CH : CH + own]
        outs[10][layer] = new
        outs[11][layer] = group_w[layer] - vector_rate * new
    works = newton_from(whole, range(4), NS_STEPS - 1)
    for which, step in enumerate(last_rows(works, range(4), place[INDEX], fresh0.shape[0], rows_s)):
        start, stop = SPANS[which]
        outs[2 * which + 1][0] = new_rows(which, old0[:, start:stop], step)


def run_finish(stage, rows, place, given, *args):
    shapes = []
    for start, stop in SPANS:
        shapes += [sds((LAYERS, rows, stop - start), f32)] * 2
    shapes += [sds(args[8].shape, f32)] * 2 + [sds(args[9].shape, f32)] * 2
    return pl.pallas_call(
        functools.partial(finish_kernel, stage, len(given)),
        out_shape=shapes,
        in_specs=[smem_spec()] + [vmem_spec()] * (len(given) + len(args)),
        out_specs=[vmem_spec()] * len(shapes),
        scratch_shapes=[pltpu.VMEM((8, WIDTH, HALF), f32)]
        + ([pltpu.VMEM((WIDTH // rows, rows, given[0].shape[2]), bf16)] if len(given) > 1 else []),
        compiler_params=params(SMALL),
        cost_estimate=cost(10),
        name="layer0_newton_finish",
    )(place, *given, *args)


def stages_of(devices):
    bits = [1 << n for n in range(devices.bit_length() - 1)]
    stages = [(bit,) for bit in bits[:2]]
    return stages + [tuple(bits[n : n + 2]) for n in range(2, len(bits), 2)]


def peers(stage):
    return [x * stage[0] for x in range((1 << len(stage)) - 1, 0, -1)]


def swap(x, axis, mask):
    n = lax.axis_size(axis)
    return lax.ppermute(x, axis, [(i, i ^ mask) for i in range(n)])


def send_parts(parts, stage):
    return [swap(part, "dp", mask) for part, mask in zip(parts, peers(stage))]


def send_all(held, stage):
    return [swap(held, "dp", mask) for mask in peers(stage)]


def part_chunks(stage, index, total, outs):
    radix = 1 << len(stage)
    own = (index // stage[0]) % radix
    for m in range(outs[0].shape[0]):
        for x in range(radix):
            outs[radix - 1 - x][m] = total(radix * m + (own ^ x)).astype(bf16)


def join_chunks(stage, index, held, gots, out):
    radix = 1 << len(stage)
    own = (index // stage[0]) % radix
    for m in range(held.shape[0]):
        for x, ref in enumerate((held, *gots[::-1])):
            out[radix * m + (own ^ x)] = ref[m]
    rows = held.shape[1]
    if held.shape[2] > 3 * HALF:
        sums = read_sums(held.at[0], rows)
        for ref in gots:
            sums = sums + read_sums(ref.at[0], rows)
        out[0] = with_sums(out[0, :, 0 : 3 * HALF], sums)


def sum_of(refs, n):
    total = refs[0][n].astype(f32)
    for ref in refs[1:]:
        total = total + ref[n].astype(f32)
    return total


def hop_kernel(joined, parted, place, *refs):
    index = place[INDEX]
    n_parts = 0 if parted is None else 1 << len(parted[1])
    outs = refs[len(refs) - len(joined) - n_parts :]
    for stage, out in zip(joined, outs):
        given, refs = refs[: 1 << len(stage)], refs[1 << len(stage) :]
        join_chunks(stage, index, given[0], given[1:], out)
    if parted is not None:
        given = refs[: 1 << len(parted[0])]
        part_chunks(parted[1], index, lambda n: sum_of(given, n), outs[len(joined) :])


def run_hop(place, joins=(), part=None, after=()):
    shapes, inputs = [], []
    for stage, held, gots in joins:
        shapes.append(sds((held.shape[0] << len(stage),) + held.shape[1:], bf16))
        inputs += [held, *gots]
    if part is not None:
        _, stage, keep, gots = part
        shapes += [sds((keep.shape[0] >> len(stage),) + keep.shape[1:], bf16)] * (1 << len(stage))
        inputs += [keep, *gots]
    outs = pl.pallas_call(
        functools.partial(hop_kernel, [join[0] for join in joins], part and part[:2]),
        out_shape=shapes,
        in_specs=[smem_spec()] + [vmem_spec()] * len(inputs) + waits(after),
        out_specs=[vmem_spec()] * len(shapes),
        compiler_params=params(SMALL),
        cost_estimate=cost(1),
        name="hop",
    )(place, *inputs, *after)
    return outs if part is None else (outs[:-1], outs[-1])


def local(
    tokens, cotangent, image_ids, qkv_weight, proj_weight, up_weight, down_weight, shared_vectors, group_vectors,
    qkv_moment, proj_moment, up_moment, down_moment, shared_moment, group_moment,
):
    devices = lax.axis_size("dp")
    index = lax.axis_index("dp")
    place = jnp.stack([index % 2, lax.axis_index("group"), index]).astype(jnp.int32)
    masters = (qkv_weight, proj_weight, up_weight, down_weight)
    moments = (qkv_moment, jnp.swapaxes(proj_moment, 1, 2), up_moment, jnp.swapaxes(down_moment, 1, 2))
    rows = WIDTH // devices
    stages = stages_of(devices)

    att0, mlp0, att1, mlp1, send = run_prepare(place, *masters)
    att0_o = swap(att0, "group", 1)
    gv, gvo = group_vectors, swap(group_vectors, "group", 1)
    mlp0_o = swap(mlp0, "group", 1)
    near = swap(send, "group", 1)
    far = swap(near, "dp", 1)
    sv = shared_vectors

    columns = jnp.swapaxes(image_ids[0].astype(f32), 0, 1).reshape(NS, STRIPE, SIDE)
    ids_t = jnp.pad(columns, ((0, 0), (0, 1), (0, 0)), constant_values=-1.0).reshape(NS * SLOT, SIDE)

    part_own, *rest_own, stream = run_attention(0, True, place, tokens, att0, sv, gv, ids_t)
    saved_own, own_kept = rest_own[:4], rest_own[4:]
    part_other, *saved_other = run_attention(0, False, place, stream, att0_o, sv, gvo, ids_t)
    middle, mid, active, slopes = run_feed(0, place, stream, part_own, part_other, mlp0, mlp0_o, sv, gv, gvo)
    outputs, grad, send1, keep1 = run_last_layer(
        1, devices, place, (middle, cotangent, att1, mlp1, near, far, sv, gv, gvo, ids_t)
    )

    def reduce_late(keep, gots, first):
        for stage, after in zip(stages[first:], stages[first + 1 :]):
            parts, keep = run_hop(place, part=(stage, after, keep, gots))
            gots = send_parts(parts, after)
        return keep, gots

    keep1 = pltpu.with_memory_space_constraint(keep1, pltpu.HBM)
    got1 = send_parts([send1], stages[0])
    parts, keep1 = run_hop(place, part=(stages[0], stages[1], keep1, got1))
    got1 = send_parts(parts, stages[1])
    gmid, gb, big_m, rows_m, bias_m = run_feed_back(
        0, place, grad, mid, slopes, active, mlp0, mlp0_o, sv, gv, gvo, (keep1,)
    )

    def back(mine, extra, after):
        saved, weights, vec = (saved_own, att0, gv) if mine else (saved_other, att0_o, gvo)
        return run_attention_back(0, mine, devices, place, gb, saved, weights, sv, vec, ids_t, extra, after)

    parts, keep1 = run_hop(place, part=(stages[1], stages[2], keep1, got1), after=(rows_m,))
    got1 = send_parts(parts, stages[2])
    da_own, big0 = back(True, (*own_kept, big_m, rows_m, bias_m), (keep1,))
    keep1, got1 = reduce_late(keep1, got1, 2)
    held1, fresh1, vectors1, send0, keep0 = run_momentum(1, devices, place, keep1, got1, moments, big0)
    got1 = send_all(held1, stages[-1])
    got0 = send_parts([send0], stages[0])
    parts, keep0 = run_hop(place, part=(stages[0], stages[1], keep0, got0))
    got0 = send_parts(parts, stages[1])
    (da_other,) = back(False, (), (keep0, held1))
    for stage in stages[-1:2:-1]:
        (held1,) = run_hop(place, joins=[(stage, held1, got1)])
        got1 = send_all(held1, stages[stages.index(stage) - 1])
    (held1, *parts), keep0 = run_hop(
        place, joins=[(stages[2], held1, got1)], part=(stages[1], stages[2], keep0, got0), after=(da_other,)
    )
    got1 = send_all(held1, stages[1])
    got0 = send_parts(parts, stages[2])
    input_grad, norm_sums = run_norm_back(0, place, stream, gmid, da_own, da_other, sv, (keep0, held1))
    keep0, got0 = reduce_late(keep0, got0, 2)
    held0, fresh0, vectors0 = run_momentum(0, devices, place, keep0, got0, moments, norm_sums)
    got0 = send_all(held0, stages[-1])
    def last_join(held, gots):
        if rows % 16 == 0:
            return (held, *gots)
        return (run_hop(place, joins=[(stages[0], held, gots)])[0].reshape(WIDTH, held.shape[2]),)

    (held1,) = run_hop(place, joins=[(stages[1], held1, got1)], after=(held0,))
    given1 = last_join(held1, send_all(held1, stages[0]))
    old0, old1, works = run_newton_begin(stages[0], place, rows, given1, masters, (held0,))
    for stage in stages[-1:2:-1]:
        (held0,) = run_hop(place, joins=[(stage, held0, got0)])
        got0 = send_all(held0, stages[stages.index(stage) - 1])
    (held0,) = run_hop(place, joins=[(stages[2], held0, got0)], after=(works,))
    got0 = send_all(held0, stages[1])
    mine, theirs = run_newton_end(place, rows, works, (held0,))
    theirs = swap(theirs, "dp", 1)
    (held0,) = run_hop(place, joins=[(stages[1], held0, got0)], after=(mine,))
    given0 = last_join(held0, send_all(held0, stages[0]))

    length = shared_moment.shape[1]
    shared_w = lax.dynamic_slice_in_dim(shared_vectors, index * length, length, 1)
    length = group_moment.shape[2]
    group_w = lax.dynamic_slice_in_dim(group_vectors, index * length, length, 2)
    out = run_finish(
        stages[0], rows, place, given0, old0, old1, fresh0, fresh1, mine, theirs, vectors0, vectors1,
        shared_moment, group_moment, shared_w, group_w,
    )
    out = [jnp.swapaxes(x, 1, 2) if n in (2, 3, 6, 7) else x for n, x in enumerate(out)]
    return (outputs, input_grad, *out)


def solution(mesh):
    return jax.shard_map(
        local,
        mesh=mesh,
        in_specs=(
            P("dp", None),
            P("dp", None),
            P("dp", None, None),
            P(None, None, "group"),
            P(None, "group", None),
            P(None, None, "group"),
            P(None, "group", None),
            P(),
            P(None, "group", None),
            P(None, "dp", "group"),
            P(None, "group", "dp"),
            P(None, "dp", "group"),
            P(None, "group", "dp"),
            P(None, "dp"),
            P(None, "group", "dp"),
        ),
        out_specs=(
            P("dp", None),
            P("dp", None),
            P(None, "dp", "group"),
            P(None, "dp", "group"),
            P(None, "group", "dp"),
            P(None, "group", "dp"),
            P(None, "dp", "group"),
            P(None, "dp", "group"),
            P(None, "group", "dp"),
            P(None, "group", "dp"),
            P(None, "dp"),
            P(None, "dp"),
            P(None, "group", "dp"),
            P(None, "group", "dp"),
        ),
        check_vma=False,
    )
```

```python
import functools
import math

import jax
import jax.numpy as jnp
from jax import lax
from jax.experimental import pallas as pl
from jax.experimental.pallas import tpu as pltpu
from jax.sharding import PartitionSpec as P

HEADS = 8
STRIPE = 7
LAYERS = 2
NS_STEPS = 5

epsilon = 1e-05
coeff_first = 3.4445
coeff_second = -4.775
coeff_third = 2.0315
momentum_decay = 0.95
matrix_rate = 0.25
weight_decay = 0.1
vector_rate = 0.001
match_scale = 0.2
masked_score = -1e30

f32 = jnp.float32
bf16 = jnp.bfloat16
LOG2E = 1.4426950408889634
MIB = 1024 * 1024
SMALL, LARGE = 26, 61

SIDE = 42
NS = 6
FA_GANG = 2
GANG = 3
SLOT = 8
ROWS = SIDE * SLOT
KEPT = 208
TOKENS = 320
KEYS = 5 * 256
WIDTH = 256
CH = 128
HALF = 512
HL = 4
HEAD = 32


def dot(a, b):
    return jnp.dot(a, b, preferred_element_type=f32)


def dot_t(a, b):
    return lax.dot_general(a, b, (((1,), (1,)), ((), ())), preferred_element_type=f32)


def dot_rows(a, b):
    return lax.dot_general(a, b, (((0,), (0,)), ((), ())), preferred_element_type=f32)


def lane_head():
    return lax.broadcasted_iota(jnp.int32, (1, CH), 1) // HEAD


def stripe_of(ref, g, s):
    if g == 0:
        block = ref[pl.ds(STRIPE * s, STRIPE)]
    else:
        block = ref[:, pl.ds(s, 1)]
    return block.reshape(ROWS, block.shape[-1])


def put_stripe(ref, g, s, value):
    if g == 0:
        ref[pl.ds(STRIPE * s, STRIPE)] = value.reshape(STRIPE, NS, SLOT, value.shape[-1])
    else:
        ref[:, pl.ds(s, 1)] = value.reshape(SIDE, 1, SLOT, value.shape[-1])


def normed(rows):
    mean = jnp.mean(rows, axis=-1, keepdims=True)
    centred = rows - mean
    spread = jnp.mean(centred * centred, axis=-1, keepdims=True)
    rstd = lax.rsqrt(spread + epsilon)
    return centred * rstd, rstd


def norm_back(grad, hat, rstd, gain):
    scaled = grad * gain
    first = jnp.mean(scaled, axis=-1, keepdims=True)
    second = jnp.mean(scaled * hat, axis=-1, keepdims=True)
    return rstd * (scaled - first - hat * second)


def tile_sum(rows):
    return jnp.sum(rows.reshape(-1, SLOT, rows.shape[-1]), axis=0)


def gelu_parts(x):
    phi = 0.5 + 0.5 * lax.erf(x * math.sqrt(0.5))
    bell = jnp.exp2(x * x * (-0.5 * LOG2E))
    return x * phi, phi + x * bell * (1.0 / math.sqrt(2.0 * math.pi))


def places(ndim):
    shape = (1,) * (ndim - 2) + (SLOT, 1)
    return lax.broadcasted_iota(jnp.int32, shape, ndim - 2)


def fine_shifts(x, g, edge):
    axis = x.ndim - 2
    place = places(x.ndim)
    up = pltpu.roll(x, SLOT - 1, axis)
    down = pltpu.roll(x, 1, axis)
    if g == 0:
        end = x[:, :1] if edge is None else jnp.full_like(x[:, :1], edge)
        after = jnp.concatenate([x[:, 1:], end], axis=1)
        before = jnp.concatenate([end, x[:, :-1]], axis=1)
        up = jnp.where(place == STRIPE - 1, pltpu.roll(after, STRIPE - 1, axis), up)
        down = jnp.where(place == 0, pltpu.roll(before, 2, axis), down)
        if edge is not None:
            up = jnp.where(place == STRIPE, edge, up)
            down = jnp.where(place == STRIPE, edge, down)
    elif edge is not None:
        up = jnp.where(place >= STRIPE - 1, edge, up)
        down = jnp.where((place == 0) | (place == STRIPE), edge, down)
    return up, down


def coarse(x, step, fill):
    if step == 0:
        return x
    end = jnp.full_like(x[:1], fill)
    if step > 0:
        return jnp.concatenate([x[1:], end], axis=0)
    return jnp.concatenate([end, x[:-1]], axis=0)


def masked_neighbours(x, ids, g):
    shape = (STRIPE, NS, SLOT, CH) if g == 0 else (SIDE, SLOT, CH)
    x = x.reshape(shape)
    centre = ids.reshape(shape)
    up, down = fine_shifts(x, g, None)
    up_ids, down_ids = fine_shifts(centre, g, -3.0)
    around = {0: (x, centre), 1: (up, up_ids), -1: (down, down_ids)}
    for row_step in (-1, 0, 1):
        for col_step in (-1, 0, 1):
            tap = 3 * (row_step + 1) + col_step + 1
            coarse_step, fine_step = (row_step, col_step) if g == 0 else (col_step, row_step)
            source, source_ids = around[fine_step]
            if coarse_step == 0 and fine_step == 0:
                yield tap, source.reshape(ROWS, CH)
                continue
            source = coarse(source, coarse_step, 0.0)
            source_ids = coarse(source_ids, coarse_step, -9.0)
            yield tap, jnp.where(source_ids == centre, source, 0.0).reshape(ROWS, CH)


def compact(x):
    width = x.shape[1]
    tiles = x[KEPT:].reshape(2, SLOT, SLOT, width)
    place = lax.broadcasted_iota(jnp.int32, (1, SLOT, 1), 1)
    parts = []
    for j in range(STRIPE):
        first, second = tiles[:, j], pltpu.roll(tiles[:, j + 1], STRIPE - j, 1)
        if j:
            first = pltpu.roll(first, SLOT - j, 1)
        parts.append(jnp.where(place < STRIPE - j, first, second))
    return jnp.concatenate([x[:KEPT], jnp.stack(parts, axis=1).reshape(TOKENS - KEPT, width)], axis=0)


def expand(x):
    width = x.shape[1]
    tiles = x[KEPT:].reshape(2, STRIPE, SLOT, width)
    place = lax.broadcasted_iota(jnp.int32, (1, SLOT, 1), 1)
    parts = [tiles[:, 0]]
    for t in range(1, STRIPE):
        both = pltpu.roll(tiles[:, t - 1], t, 1), pltpu.roll(tiles[:, t], t, 1)
        parts.append(jnp.where(place < t, *both))
    parts.append(pltpu.roll(tiles[:, STRIPE - 1], STRIPE, 1))
    parts = [jnp.where(place < STRIPE, part, 0.0) for part in parts]
    return jnp.concatenate([x[:KEPT], jnp.stack(parts, axis=1).reshape(ROWS - KEPT, width)], axis=0)


WIDE, TAIL = 256, 64


def by_heads(pieces):
    parts = [pieces(h) for h in range(HL)]
    return jnp.concatenate([part[0] for part in parts] + [part[1] for part in parts], axis=0)


def block_diagonal(x):
    head = lane_head()

    def pieces(h):
        own = x * jnp.where(head == h, 1.0, 0.0).astype(bf16)
        return own[:WIDE], own[WIDE:]

    return by_heads(pieces)


def lane_marks(pick):
    lane = lax.broadcasted_iota(jnp.int32, (1, CH), 1)

    def pieces(h):
        mark = jnp.where(pick(lane, h), 1.0, 0.0).astype(bf16)
        return jnp.broadcast_to(mark, (WIDE, CH)), jnp.broadcast_to(mark, (TAIL, CH))

    return by_heads(pieces)


def turned(x):
    return jnp.concatenate([x, jnp.zeros((3 * CH - TOKENS, CH), x.dtype)], axis=0).T[:, 0:TOKENS]


def head_rows(x, h):
    return x[h * HEAD : (h + 1) * HEAD]


def over_queries(left, weights):
    main = [dot(head_rows(left, h), weights[:, h * WIDE : (h + 1) * WIDE]) for h in range(HL)]
    tails = dot(left, weights[:, HL * WIDE :])
    last = []
    for h in range(HL):
        own = head_rows(tails, h)[:, (h // 2) * CH : (h // 2 + 1) * CH]
        last.append(pltpu.roll(own, TAIL, 1) if h % 2 else own)
    return jnp.concatenate([jnp.concatenate(main, axis=0), jnp.concatenate(last, axis=0)], axis=1)


def masked_softmax(q, keys, bias):
    tails = dot_t(q, keys[HL * WIDE :])
    left = lax.broadcasted_iota(jnp.int32, (1, CH), 1) < TAIL
    lowest = jnp.finfo(f32).min
    parts, last = [], []
    for h in range(0, HL, 2):
        scores = dot_t(q, keys[h * WIDE : (h + 2) * WIDE])
        own = [scores[:, n * CH : (n + 1) * CH] + bias[n % 2] for n in range(4)]
        tail = tails[:, (h // 2) * CH : (h // 2 + 1) * CH] + bias[2]
        top = jnp.maximum(jnp.maximum(own[0], own[1]), jnp.where(left, tail, lowest))
        other = jnp.maximum(jnp.maximum(own[2], own[3]), jnp.where(left, lowest, tail))
        top = jnp.max(top, axis=-1, keepdims=True)
        other = jnp.max(other, axis=-1, keepdims=True)
        parts += [jnp.exp2(x - y).astype(bf16) for x, y in zip(own, (top, top, other, other))]
        last.append(jnp.exp2(tail - jnp.where(left, top, other)).astype(bf16))
    return jnp.concatenate(parts + last, axis=1)


def spread_ids(ids_t, idc):
    for r in range(SIDE):
        column = jnp.broadcast_to(ids_t[:, r : r + 1], (NS * SLOT, CH))
        idc[r] = column.reshape(NS, SLOT, CH)


def spread_rows(source, target):
    place = lax.broadcasted_iota(jnp.int32, (SLOT, 1), 0)
    for r in range(SIDE):
        for column in range(NS):
            tile = source[pl.ds(SIDE * r + STRIPE * column, SLOT)]
            target[r, column] = jnp.where(place < STRIPE, tile, 0.0)


def pack_rows(source, target):
    for r in range(SIDE):
        for column in range(NS):
            start = SIDE * r + STRIPE * column
            if start + SLOT <= SIDE * SIDE:
                target[pl.ds(start, SLOT)] = source[r, column]
            else:
                target[pl.ds(start, STRIPE)] = source[r, column, 0:STRIPE]


def first_norm(rows, sv, layer):
    hat, _ = normed(rows)
    return (hat * shared_of(sv, layer, 0) + shared_of(sv, layer, 1)).astype(bf16)


def attend(g, a1, ids, weights, vec):
    mixed = dot(a1, weights)
    value = mixed[:, 2 * CH :] + vec[:, CH : 2 * CH]
    query = (mixed[:, :CH] + vec[:, :CH]) * (HEAD ** -0.5 * LOG2E)
    qkv = compact(jnp.concatenate([query, mixed[:, CH : 2 * CH], value], axis=1)).astype(bf16)
    q, k, v = qkv[:, :CH], qkv[:, CH : 2 * CH], qkv[:, 2 * CH :]
    ids_c = compact(ids)
    key_ids = jnp.concatenate([ids_c, jnp.full((3 * CH - TOKENS, CH), -5.0, f32)], axis=0).T[0:1]
    left = lax.broadcasted_iota(jnp.int32, (1, CH), 1) < TAIL
    last = key_ids[:, 2 * CH :]
    last = jnp.where(left, last, pltpu.roll(last, TAIL, 1))
    bias = [
        jnp.where(ids_c == part, 0.0, masked_score) for part in (key_ids[:, :CH], key_ids[:, CH : 2 * CH], last)
    ]
    e = masked_softmax(q, block_diagonal(k), bias)
    ones = lane_marks(lambda lane, h: lane // HEAD == h)
    both = dot(e, jnp.concatenate([block_diagonal(v), ones], axis=1))
    rl = 1.0 / both[:, CH:]
    att = both[:, :CH] * rl
    total = expand(att) + vec[:, 2 * CH : 3 * CH]
    for tap, near in masked_neighbours(value.astype(bf16).astype(f32), ids, g):
        total = total + near * vec[:, (3 + tap) * CH : (4 + tap) * CH]
    return qkv, e, rl, att.astype(bf16), total.astype(bf16)


def attend_back(g, gbs, ids, weights, proj, vec, qkv, e, rl, att, add):
    d_out = dot_t(gbs, proj).astype(bf16).astype(f32)
    q, k, v = qkv[:, 0:CH], qkv[:, CH : 2 * CH], qkv[:, 2 * CH :]
    scaled = (compact(d_out) * rl).astype(bf16)
    prod = scaled.astype(f32) * att.astype(f32)
    prod_high = prod.astype(bf16)
    prod_low = (prod - prod_high.astype(f32)).astype(bf16)
    lanes = lax.broadcasted_iota(jnp.int32, (CH, CH), 1)
    rows_of = lax.broadcasted_iota(jnp.int32, (CH, CH), 0)
    gather = jnp.where((lanes % HEAD == rows_of // HEAD) & (lanes < 3 * HEAD), 1.0, 0.0).astype(bf16)
    centre = dot(
        jnp.concatenate([prod_high, prod_low], axis=1), jnp.concatenate([gather, gather], axis=0)
    )
    first = centre.astype(bf16).astype(f32)
    rest = centre - first
    second = rest.astype(bf16).astype(f32)
    lane = lax.broadcasted_iota(jnp.int32, (1, CH), 1)
    pieces = jnp.where(lane < HEAD, first, jnp.where(lane < 2 * HEAD, second, rest - second))
    left = jnp.concatenate([scaled, (-pieces).astype(bf16)], axis=1)
    marks = lane_marks(lambda lane, h: (lane % HEAD == h) & (lane < 3 * HEAD))
    right = jnp.concatenate([block_diagonal(v), marks], axis=1)
    ds = (e.astype(f32) * dot_t(left, right)).astype(bf16)
    dq = dot(ds, block_diagonal(k)) * HEAD ** -0.5
    turned_grads = [over_queries(turned(q), ds) * (1.0 / LOG2E), over_queries(turned(scaled), e)]
    grads = jnp.concatenate([dq, jnp.concatenate(turned_grads, axis=0).T[0:TOKENS]], axis=1)
    grads = expand(grads)
    vf = expand(v.astype(f32))
    dv = grads[:, 2 * CH :]
    for tap, near in masked_neighbours(d_out, ids, g):
        mirror = 8 - tap
        dv = dv + near * vec[:, (3 + mirror) * CH : (4 + mirror) * CH]
        if add is not None:
            add(3 + mirror, tile_sum(near * vf))
    dq, dk, dv = grads[:, :CH].astype(bf16), grads[:, CH : 2 * CH].astype(bf16), dv.astype(bf16)
    if add is not None:
        add(0, tile_sum(dq.astype(f32)))
        add(1, tile_sum(dv.astype(f32)))
        add(2, tile_sum(d_out))
    dqkv = jnp.concatenate([dq, dk, dv], axis=1)
    return dqkv, dot_t(dqkv, weights).astype(bf16).astype(f32)


def qkv_of(buffer):
    return buffer[:, 0 : 3 * CH]


def proj_of(buffer):
    return jnp.concatenate([buffer[0:CH, 3 * CH : 4 * CH], buffer[CH : 2 * CH, 3 * CH : 4 * CH]], axis=1)


def up_of(buffer, start):
    return buffer[:, start : start + HALF]


def down_of(buffer, start):
    return jnp.concatenate(
        [buffer[:, start + HALF : start + HALF + WIDTH], buffer[:, start + HALF + WIDTH : start + 2 * HALF]], axis=0
    )


def assemble(whole, near, far, core):
    half = WIDTH // 2
    whole[pl.ds(core * half, half)] = near[...]
    whole[pl.ds((1 - core) * half, half)] = far[...]


def shared_of(sv, layer, index):
    return sv[layer : layer + 1, index * WIDTH : (index + 1) * WIDTH]


def mlp_forward(rows, sv, layer, pairs):
    hat, _ = normed(rows)
    a2 = (hat * shared_of(sv, layer, 3) + shared_of(sv, layer, 4)).astype(bf16)
    parts, kept, slopes = [], [], []
    for up, down, bias in pairs:
        active, slope = gelu_parts(dot(a2, up) + bias)
        active = active.astype(bf16)
        kept.append(active)
        slopes.append(slope.astype(bf16))
        parts.append(dot(active, down).astype(bf16).astype(f32))
    return rows + ((parts[0] + parts[1]) + shared_of(sv, layer, 5)), kept[0], slopes


def mlp_backward(rows, mid, slopes, sv, layer, pairs):
    gm = rows.astype(bf16)
    hat, rstd = normed(mid)
    a2 = (hat * shared_of(sv, layer, 3) + shared_of(sv, layer, 4)).astype(bf16)
    parts, hidden = [], []
    for (up, down, _), slope in zip(pairs, slopes):
        gh = (dot_t(gm, down) * slope.astype(f32)).astype(bf16)
        hidden.append(gh)
        parts.append(dot_t(gh, up).astype(bf16).astype(f32))
    da2 = parts[0] + parts[1]
    new = rows + norm_back(da2, hat, rstd, shared_of(sv, layer, 3))
    low = new.astype(bf16)
    sums = (
        tile_sum(low.astype(f32)), tile_sum(da2 * hat), tile_sum(da2), tile_sum(gm.astype(f32)),
        tile_sum(hidden[0].astype(f32)),
    )
    return new, low, gm, a2, hidden[0], sums


def one_row(tile):
    return jnp.sum(tile, axis=0, keepdims=True)


def pack_vectors(devices, shared_row, group_row):
    rows = WIDTH // devices
    wide = shared_row.shape[1] // devices
    own = group_row.shape[1] // devices
    lines = []
    for i in range(devices):
        pieces = []
        for piece in (shared_row[:, i * wide : (i + 1) * wide], group_row[:, i * own : (i + 1) * own]):
            pieces.append(piece)
            if piece.shape[1] < CH:
                pieces.append(jnp.zeros((1, CH - piece.shape[1]), f32))
        line = jnp.concatenate(pieces, axis=1)
        lines.append(jnp.concatenate([line, jnp.zeros((rows - 1, 2 * CH), f32)], axis=0))
    return jnp.concatenate(lines, axis=0)


def sds(shape, dtype):
    return jax.ShapeDtypeStruct(shape, dtype)


def hbm(shape, dtype):
    return pltpu.HBM(shape, dtype)


def chunk_shapes(devices):
    return [sds((devices // 2, WIDTH // devices, 3 * HALF + 2 * CH), bf16)] * 2


def put_chunks(send, keep, core, start, value):
    rows, width = send.shape[1], value.shape[1]
    for m in range(send.shape[0]):
        even = value[2 * m * rows : (2 * m + 1) * rows]
        odd = value[(2 * m + 1) * rows : (2 * m + 2) * rows]
        keep[m, :, start : start + width] = jnp.where(core == 0, even, odd).astype(bf16)
        send[m, :, start : start + width] = jnp.where(core == 0, odd, even).astype(bf16)


def vmem_spec():
    return pl.BlockSpec(memory_space=pltpu.VMEM)


def smem_spec():
    return pl.BlockSpec(memory_space=pltpu.SMEM)


def waits(arrays):
    return [pl.BlockSpec(memory_space=pl.ANY)] * len(arrays)


def kept(shape):
    return pl.BlockSpec(shape, lambda s: (0,) * len(shape))


def per_step(shape, first=0, count=1):
    return pl.BlockSpec((count,) + shape, lambda s: (s + first,) + (0,) * len(shape))


def cost(us):
    return pl.CostEstimate(flops=int(us * 1.1e9), bytes_accessed=10**6, transcendentals=0)


def params(mib):
    return pltpu.CompilerParams(vmem_limit_bytes=mib * MIB)


CANVAS = (SIDE, NS, SLOT, WIDTH)
CORE, GROUP, INDEX = 0, 1, 2


def prepare_first_kernel(qkv, proj, att):
    att[:, 0 : 3 * CH] = qkv[0].astype(bf16)
    att[0:CH, 3 * CH :] = proj[0, :, 0:CH].astype(bf16)
    att[CH:, 3 * CH :] = proj[0, :, CH:].astype(bf16)


def prepare_rest_kernel(place, qkv, proj, up, down, mlp0, att1, mlp1, send):
    half = WIDTH // 2
    att1[:, 0 : 3 * CH] = qkv[0].astype(bf16)
    att1[0:CH, 3 * CH :] = proj[0, :, 0:CH].astype(bf16)
    att1[CH:, 3 * CH :] = proj[0, :, CH:].astype(bf16)
    for layer, mlp in enumerate((mlp0, mlp1)):
        mlp[:, 0:HALF] = up[layer].astype(bf16)
        mlp[:, HALF : HALF + WIDTH] = down[layer, 0:WIDTH].astype(bf16)
        mlp[:, HALF + WIDTH :] = down[layer, WIDTH:].astype(bf16)
    mine = pl.ds(place[CORE] * half, half)
    send[:, 0:HALF] = att1[mine]
    send[:, HALF:] = mlp1[mine]


def layer_spec(shape, layer):
    return pl.BlockSpec((1,) + shape[1:], lambda s: (layer, 0, 0))


def run_prepare(place, qkv, proj, up, down):
    half = WIDTH // 2
    qkv, proj, up, down = (pltpu.with_memory_space_constraint(x, pltpu.HBM) for x in (qkv, proj, up, down))
    att0 = pl.pallas_call(
        prepare_first_kernel,
        grid=(1,),
        out_shape=sds((WIDTH, HALF), bf16),
        in_specs=[layer_spec(qkv.shape, 0), layer_spec(proj.shape, 0)],
        out_specs=kept((WIDTH, HALF)),
        compiler_params=params(SMALL),
        cost_estimate=cost(1),
        name="prepare_first",
    )(qkv, proj)
    rest = pl.pallas_call(
        prepare_rest_kernel,
        grid=(1,),
        out_shape=[
            hbm((WIDTH, 2 * HALF), bf16), hbm((WIDTH, HALF), bf16), hbm((WIDTH, 2 * HALF), bf16),
            sds((half, 3 * HALF), bf16),
        ],
        in_specs=[smem_spec(), layer_spec(qkv.shape, 1), layer_spec(proj.shape, 1), kept(up.shape), kept(down.shape)],
        out_specs=[
            kept((WIDTH, 2 * HALF)), kept((WIDTH, HALF)), kept((WIDTH, 2 * HALF)), kept((half, 3 * HALF)),
        ],
        compiler_params=params(SMALL),
        cost_estimate=cost(3),
        name="prepare_rest",
    )(place, qkv, proj, up, down)
    return att0, *rest


def attention_kernel(layer, mine, place, given, *refs):
    if mine:
        att_w, sv, gv, ids_t, part, qkv_o, e_o, rl_o, att_o, heads_o, a1_o, stream, idc, tall = refs
    else:
        stream = given
        att_w, sv, gv, ids_t, part, qkv_o, e_o, rl_o, att_o, idc = refs
    s = pl.program_id(0)

    @pl.when(s == 0)
    def _():
        spread_ids(ids_t, idc)
        if mine:
            tall[0 : SIDE * SIDE] = given[...].astype(f32)
            spread_rows(tall, stream)

    frame = place[GROUP] if mine else 1 - place[GROUP]
    for g in range(2):
        @pl.when(frame == g)
        def _(g=g):
            for n in range(FA_GANG):
                row = FA_GANG * s + n
                a1 = first_norm(stripe_of(stream, g, row), sv, layer)
                qkv, e, rl, att, heads = attend(g, a1, stripe_of(idc, g, row), qkv_of(att_w), gv[layer])
                qkv_o[n] = qkv
                e_o[n] = e
                rl_o[n] = rl
                att_o[n] = att
                part[n] = dot(heads, proj_of(att_w)).astype(bf16).astype(f32)
                if mine:
                    heads_o[n] = heads
                    a1_o[n] = a1


ATT_SAVED = [((TOKENS, 3 * CH), bf16), ((TOKENS, KEYS), bf16), ((TOKENS, CH), f32), ((TOKENS, CH), bf16)]


def run_attention(layer, mine, place, stream, weights, sv, gv, ids_t):
    outs = [((ROWS, WIDTH), f32)] + ATT_SAVED + ([((ROWS, CH), bf16), ((ROWS, WIDTH), bf16)] if mine else [])
    inputs = (stream, weights, sv, gv, ids_t)
    return pl.pallas_call(
        functools.partial(attention_kernel, layer, mine),
        grid=(NS // FA_GANG,),
        out_shape=[(sds if n == 0 else hbm)((NS,) + shape, dtype) for n, (shape, dtype) in enumerate(outs)]
        + ([sds(CANVAS, f32)] if mine else []),
        in_specs=[smem_spec(), kept(stream.shape) if mine else vmem_spec()] + [kept(x.shape) for x in inputs[1:]],
        out_specs=[per_step(shape, 0, FA_GANG) for shape, _ in outs] + ([kept(CANVAS)] if mine else []),
        scratch_shapes=[pltpu.VMEM((SIDE, NS, SLOT, CH), f32)]
        + ([pltpu.VMEM((SIDE * SIDE + 4, WIDTH), f32)] if mine else []),
        compiler_params=params(SMALL),
        cost_estimate=cost(11),
        name=f"layer{layer}_attention_{'own' if mine else 'other'}",
    )(place, *inputs)


def in_frames(own, mine, other, n):
    def across(ref):
        return ref[n].reshape(ROWS, WIDTH)

    def down(ref):
        columns = [ref[column, pl.ds(STRIPE * n, STRIPE)] for column in range(NS)]
        return jnp.stack(columns, axis=1).reshape(ROWS, WIDTH)

    return jnp.where(own == 0, across(mine), down(mine)) + jnp.where(own == 0, down(other), across(other))


def frame_views(mine, other):
    return [x.reshape(NS, SIDE, SLOT, WIDTH) for x in (mine, other)]


def canvas_block(count=1):
    return pl.BlockSpec((STRIPE * count, NS, SLOT, WIDTH), lambda s: (s, 0, 0, 0))


def feed_kernel(
    layer, place, stream, mine, other, mlp_w, mlp_o, sv, gv, gvo,
    out, mid, active, slopes,
):
    pairs = [
        (up_of(w, 0), down_of(w, 0), v[layer][:, 12 * CH :]) for w, v in ((mlp_w, gv), (mlp_o, gvo))
    ]
    for n in range(GANG):
        both = in_frames(place[GROUP], mine, other, GANG * pl.program_id(0) + n)
        rows = stripe_of(stream, 0, n) + (both + shared_of(sv, layer, 2))
        put_stripe(mid, 0, n, rows)
        new, held, slope = mlp_forward(rows, sv, layer, pairs)
        put_stripe(out, 0, n, new)
        active[n] = held
        slopes[n, 0] = slope[0]
        slopes[n, 1] = slope[1]


def run_feed(layer, place, stream, mine, other, mlp_w, mlp_o, sv, gv, gvo):
    rest = (mlp_w, mlp_o, sv, gv, gvo)
    return pl.pallas_call(
        functools.partial(feed_kernel, layer),
        grid=(NS // GANG,),
        out_shape=[
            hbm(CANVAS, f32), hbm(CANVAS, f32), hbm((NS, ROWS, HALF), bf16), hbm((NS, 2, ROWS, HALF), bf16)
        ],
        in_specs=[smem_spec(), canvas_block(GANG)] + [vmem_spec()] * 2 + [kept(x.shape) for x in rest],
        out_specs=[
            canvas_block(GANG), canvas_block(GANG), per_step((ROWS, HALF), 0, GANG), per_step((2, ROWS, HALF), 0, GANG)
        ],
        compiler_params=params(SMALL),
        cost_estimate=cost(10),
        name=f"layer{layer}_feed_forward",
    )(place, stream, *frame_views(mine, other), *rest)


def last_layer_kernel(
    layer, devices, place, stream, cot, att_w, mlp_w, near, far, sv, gv, gvo, ids_t,
    out, grad_in, send, keep,
    whole, att2, gv2, idc, mid, gmid, gb, qkv_s, e_s, rl_s, att_s, heads_s, active_s, a1_s, dqkv_s, gb_s,
    a2_s, gh_s, gm_s, acc_s, acc_b1, acc_g, tall,
):
    own = place[GROUP]
    assemble(whole, near, far, place[CORE])
    att2[own] = att_w[...]
    att2[1 - own] = whole[:, 0:HALF]
    gv2[own] = gv[layer]
    gv2[1 - own] = gvo[layer]
    spread_ids(ids_t, idc)
    acc_s[...] = jnp.zeros_like(acc_s)
    acc_b1[...] = jnp.zeros_like(acc_b1)
    acc_g[...] = jnp.zeros_like(acc_g)

    def norms(first, carry):
        for n in range(GANG):
            s = GANG * first + n
            put_stripe(gmid, 0, s, first_norm(stripe_of(stream, 0, s), sv, layer).astype(f32))
        return carry

    lax.fori_loop(0, NS // GANG, norms, 0)

    for g in range(2):
        def gang(first, carry, g=g):
            for n in range(GANG):
                s = GANG * first + n
                i = g * NS + s
                a1 = stripe_of(gmid, g, s).astype(bf16)
                qkv, e, rl, att, heads = attend(g, a1, stripe_of(idc, g, s), qkv_of(att2[g]), gv2[g])
                qkv_s[i] = qkv
                e_s[i] = e
                rl_s[i] = rl
                att_s[i] = att
                part = dot(heads, proj_of(att2[g])).astype(bf16).astype(f32)
                if g == 0:
                    put_stripe(mid, g, s, part)
                else:
                    rows = stripe_of(stream, g, s)
                    put_stripe(mid, g, s, rows + ((stripe_of(mid, g, s) + part) + shared_of(sv, layer, 2)))
                a1_s[g, s] = a1
                heads_s[g, s] = heads
            return carry

        lax.fori_loop(0, NS // GANG, gang, 0)

    def pairs():
        return [
            (up_of(mlp_w, 0), down_of(mlp_w, 0), gv[layer][:, 12 * CH :]),
            (up_of(whole, HALF), down_of(whole, HALF), gvo[layer][:, 12 * CH :]),
        ]

    tall[0 : SIDE * SIDE] = cot[...].astype(f32)
    spread_rows(tall, gmid)

    def block(s):
        rows = stripe_of(mid, 0, s)
        new, held, slope = mlp_forward(rows, sv, layer, pairs())
        put_stripe(grad_in, 0, s, new)
        active_s[s] = held
        grad = stripe_of(gmid, 0, s)
        new, low, gm, a2, gh, sums = mlp_backward(grad, rows, slope, sv, layer, pairs())
        put_stripe(gmid, 0, s, new)
        put_stripe(gb, 0, s, low.astype(f32))
        gm_s[s] = gm
        a2_s[s] = a2
        gh_s[s] = gh
        for index, value in zip((2, 3, 4, 5), sums):
            acc_s[index] += value
        acc_b1[...] += sums[4]

    def blocks(first, carry):
        for n in range(GANG):
            block(GANG * first + n)
        return carry

    lax.fori_loop(0, NS // GANG, blocks, 0)
    pack_rows(grad_in, tall)
    out[...] = tall[0 : SIDE * SIDE].astype(bf16)

    for g in range(2):
        def gang(first, carry, g=g):
            def add(index, value):
                acc_g[g, index] += value

            for n in range(GANG):
                s = GANG * first + n
                i = g * NS + s
                gbs = stripe_of(gb, g, s).astype(bf16)
                dqkv, part = attend_back(
                    g, gbs, stripe_of(idc, g, s), qkv_of(att2[g]), proj_of(att2[g]), gv2[g], qkv_s[i], e_s[i],
                    rl_s[i], att_s[i], add,
                )
                if g == 0:
                    put_stripe(mid, g, s, part)
                else:
                    put_stripe(mid, g, s, stripe_of(mid, g, s) + part)
                dqkv_s[g, s] = dqkv
                gb_s[g, s] = gbs
            return carry

        lax.fori_loop(0, NS // GANG, gang, 0)

    def final(first, carry):
        for n in range(GANG):
            s = GANG * first + n
            hat, rstd = normed(stripe_of(stream, 0, s))
            da = stripe_of(mid, 0, s)
            acc_s[0] += tile_sum(da * hat)
            acc_s[1] += tile_sum(da)
            put_stripe(
                grad_in, 0, s, stripe_of(gmid, 0, s) + norm_back(da, hat, rstd, shared_of(sv, layer, 0))
            )
        return carry

    lax.fori_loop(0, NS // GANG, final, 0)

    def flat(ref):
        return ref[...].reshape(NS * ROWS, ref.shape[-1])

    core = place[CORE]
    put_chunks(send, keep, core, 0, dot_rows(flat(a1_s.at[own]), flat(dqkv_s.at[own])))
    put_chunks(send, keep, core, 3 * CH, dot_rows(flat(gb_s.at[own]), flat(heads_s.at[own])))
    put_chunks(send, keep, core, HALF, dot_rows(flat(a2_s), flat(gh_s)))
    put_chunks(send, keep, core, 2 * HALF, dot_rows(flat(gm_s), flat(active_s)))
    shared_row = jnp.concatenate([one_row(acc_s[index]) for index in range(6)], axis=1)
    group_row = jnp.concatenate([one_row(acc_g[own, index]) for index in range(12)] + [one_row(acc_b1[...])], axis=1)
    put_chunks(send, keep, core, 3 * HALF, pack_vectors(devices, shared_row, group_row))


def run_last_layer(layer, devices, place, args):
    return pl.pallas_call(
        functools.partial(last_layer_kernel, layer, devices),
        out_shape=[sds((SIDE * SIDE, WIDTH), bf16), sds(CANVAS, f32)]
        + [pltpu.VMEM(x.shape, x.dtype) for x in chunk_shapes(devices)],
        in_specs=[smem_spec()] + [vmem_spec()] * len(args),
        out_specs=[vmem_spec()] * 4,
        scratch_shapes=[
            pltpu.VMEM((WIDTH, 3 * HALF), bf16),
            pltpu.VMEM((2, WIDTH, HALF), bf16),
            pltpu.VMEM((2, 1, 16 * CH), f32),
            pltpu.VMEM((SIDE, NS, SLOT, CH), f32),
            pltpu.VMEM(CANVAS, f32),
            pltpu.VMEM(CANVAS, f32),
            pltpu.VMEM(CANVAS, f32),
            pltpu.VMEM((2 * NS, TOKENS, 3 * CH), bf16),
            pltpu.VMEM((2 * NS, TOKENS, KEYS), bf16),
            pltpu.VMEM((2 * NS, TOKENS, CH), f32),
            pltpu.VMEM((2 * NS, TOKENS, CH), bf16),
            pltpu.VMEM((2, NS, ROWS, CH), bf16),
            pltpu.VMEM((NS, ROWS, HALF), bf16),
            pltpu.VMEM((2, NS, ROWS, WIDTH), bf16),
            pltpu.VMEM((2, NS, ROWS, 3 * CH), bf16),
            pltpu.VMEM((2, NS, ROWS, WIDTH), bf16),
            pltpu.VMEM((NS, ROWS, WIDTH), bf16),
            pltpu.VMEM((NS, ROWS, HALF), bf16),
            pltpu.VMEM((NS, ROWS, WIDTH), bf16),
            pltpu.VMEM((6, SLOT, WIDTH), f32),
            pltpu.VMEM((SLOT, HALF), f32),
            pltpu.VMEM((2, 12, SLOT, CH), f32),
            pltpu.VMEM((SIDE * SIDE + 4, WIDTH), f32),
        ],
        compiler_params=params(LARGE),
        cost_estimate=cost(65),
        name=f"layer{layer}_forward_backward",
    )(place, *args)


def feed_back_kernel(
    layer, place, grad, mid, slopes, active, mlp_w, mlp_o, sv, gv, gvo, *refs,
):
    gmid, gb, big, rows_out, bias_out, a2_s, gh_s, gm_s, act_s, acc_s, acc_b1 = refs[-11:]
    s = pl.program_id(0)

    @pl.when(s == 0)
    def _():
        acc_s[...] = jnp.zeros_like(acc_s)
        acc_b1[...] = jnp.zeros_like(acc_b1)

    pairs = [
        (up_of(w, 0), down_of(w, 0), v[layer][:, 12 * CH :]) for w, v in ((mlp_w, gv), (mlp_o, gvo))
    ]
    for n in range(GANG):
        new, low, gm, a2, gh, sums = mlp_backward(
            stripe_of(grad, 0, n), stripe_of(mid, 0, n), [slopes[n, 0], slopes[n, 1]], sv, layer, pairs
        )
        put_stripe(gmid, 0, n, new)
        put_stripe(gb, 0, n, low.astype(f32))
        gm_s[GANG * s + n] = gm
        a2_s[GANG * s + n] = a2
        gh_s[GANG * s + n] = gh
        act_s[GANG * s + n] = active[n]
        for index in range(4):
            acc_s[index] += sums[index]
        acc_b1[...] += sums[4]

    @pl.when(s == NS // GANG - 1)
    def _():
        def flat(ref):
            return ref[...].reshape(NS * ROWS, ref.shape[-1])

        big[:, 0:HALF] = dot_rows(flat(a2_s), flat(gh_s)).astype(bf16)
        big[:, HALF:] = dot_rows(flat(gm_s), flat(act_s)).astype(bf16)
        rows_out[...] = jnp.concatenate([one_row(acc_s[index]) for index in range(4)], axis=1)
        bias_out[...] = one_row(acc_b1[...])


def run_feed_back(layer, place, grad, mid, slopes, active, mlp_w, mlp_o, sv, gv, gvo, after):
    rest = (mlp_w, mlp_o, sv, gv, gvo)
    mid, slopes, active = (pltpu.with_memory_space_constraint(x, pltpu.HBM) for x in (mid, slopes, active))
    return pl.pallas_call(
        functools.partial(feed_back_kernel, layer),
        grid=(NS // GANG,),
        out_shape=[
            sds(CANVAS, f32), sds(CANVAS, f32), sds((WIDTH, 2 * HALF), bf16), sds((1, 4 * WIDTH), f32),
            sds((1, HALF), f32),
        ],
        in_specs=[smem_spec(), canvas_block(GANG), canvas_block(GANG), per_step((2, ROWS, HALF), 0, GANG), per_step((ROWS, HALF), 0, GANG)]
        + [kept(x.shape) for x in rest]
        + waits(after),
        out_specs=[canvas_block(GANG), canvas_block(GANG), kept((WIDTH, 2 * HALF)), kept((1, 4 * WIDTH)), kept((1, HALF))],
        scratch_shapes=[
            pltpu.VMEM((NS, ROWS, WIDTH), bf16),
            pltpu.VMEM((NS, ROWS, HALF), bf16),
            pltpu.VMEM((NS, ROWS, WIDTH), bf16),
            pltpu.VMEM((NS, ROWS, HALF), bf16),
            pltpu.VMEM((4, SLOT, WIDTH), f32),
            pltpu.VMEM((SLOT, HALF), f32),
        ],
        compiler_params=params(SMALL),
        cost_estimate=cost(11),
        name=f"layer{layer}_feed_backward",
    )(place, grad, mid, slopes, active, *rest, *after)


def attention_back_kernel(layer, mine, devices, place, gb, qkv, e, rl, att, *refs):
    if mine:
        att_w, sv, gv, ids_t, heads, a1, big_m, rows_m, bias_m = refs[:9]
        da, big, idc, dqkv_s, gb_s, acc_g = refs[-6:]
    else:
        att_w, sv, gv, ids_t = refs[:4]
        da, idc = refs[-2:]
    step = pl.program_id(0)

    @pl.when(step == 0)
    def _():
        spread_ids(ids_t, idc)
        if mine:
            acc_g[...] = jnp.zeros_like(acc_g)

    def add(index, value):
        acc_g[index] += value

    frame = place[GROUP] if mine else 1 - place[GROUP]
    for g in range(2):
        @pl.when(frame == g)
        def _(g=g):
            for n in range(GANG):
                s = GANG * step + n
                gbs = stripe_of(gb, g, s).astype(bf16)
                dqkv, part = attend_back(
                    g, gbs, stripe_of(idc, g, s), qkv_of(att_w), proj_of(att_w), gv[layer], qkv[n], e[n], rl[n], att[n],
                    add if mine else None,
                )
                da[n] = part
                if mine:
                    dqkv_s[s] = dqkv
                    gb_s[s] = gbs

    if mine:
        @pl.when(step == NS // GANG - 1)
        def _():
            def flat(ref):
                return ref[...].reshape(NS * ROWS, ref.shape[-1])

            big[:, 0 : 3 * CH] = dot_rows(flat(a1), flat(dqkv_s)).astype(bf16)
            big[:, 3 * CH : HALF] = dot_rows(flat(gb_s), flat(heads)).astype(bf16)
            big[:, HALF : 3 * HALF] = big_m[...]
            shared_row = jnp.concatenate([jnp.zeros((1, 2 * WIDTH), f32), rows_m[...]], axis=1)
            group_row = jnp.concatenate([one_row(acc_g[index]) for index in range(12)] + [bias_m[...]], axis=1)
            big[:, 3 * HALF :] = pack_vectors(devices, shared_row, group_row).astype(bf16)


def run_attention_back(layer, mine, devices, place, gb, saved, weights, sv, gv, ids_t, extra, after):
    rest = (weights, sv, gv, ids_t, *extra)
    outs = [sds((NS, ROWS, WIDTH), f32)]
    out_specs = [per_step((ROWS, WIDTH), 0, GANG)]
    scratch = [pltpu.VMEM((SIDE, NS, SLOT, CH), f32)]
    if mine:
        outs.append(sds((WIDTH, 3 * HALF + 2 * CH), bf16))
        out_specs.append(kept(outs[1].shape))
        scratch += [
            pltpu.VMEM((NS, ROWS, 3 * CH), bf16),
            pltpu.VMEM((NS, ROWS, WIDTH), bf16),
            pltpu.VMEM((12, SLOT, CH), f32),
        ]
    inputs = (place, gb, *saved, *rest, *after)
    return pl.pallas_call(
        functools.partial(attention_back_kernel, layer, mine, devices),
        grid=(NS // GANG,),
        out_shape=outs,
        in_specs=[smem_spec(), vmem_spec()]
        + [per_step(shape, 0, GANG) for shape, _ in ATT_SAVED]
        + [kept(x.shape) for x in rest]
        + waits(after),
        out_specs=out_specs,
        scratch_shapes=scratch,
        compiler_params=params(SMALL),
        cost_estimate=cost(10),
        name=f"layer{layer}_attention_back_{'own' if mine else 'other'}",
    )(*inputs)


def norm_back_kernel(layer, place, stream, gmid, mine, other, sv, *refs):
    out, sums, grad_in, acc = refs[-4:]
    s = pl.program_id(0)

    @pl.when(s == 0)
    def _():
        acc[...] = jnp.zeros_like(acc)

    for n in range(GANG):
        da = in_frames(place[GROUP], mine, other, GANG * s + n)
        hat, rstd = normed(stripe_of(stream, 0, n))
        acc[0] += tile_sum(da * hat)
        acc[1] += tile_sum(da)
        new = stripe_of(gmid, 0, n) + norm_back(da, hat, rstd, shared_of(sv, layer, 0))
        put_stripe(grad_in, 0, GANG * s + n, new)

    @pl.when(s == NS // GANG - 1)
    def _():
        pack_rows(grad_in, out)
        sums[...] = jnp.concatenate([one_row(acc[0]), one_row(acc[1])], axis=1)


def run_norm_back(layer, place, stream, gmid, mine, other, sv, after):
    return pl.pallas_call(
        functools.partial(norm_back_kernel, layer),
        grid=(NS // GANG,),
        out_shape=[sds((SIDE * SIDE, WIDTH), f32), sds((1, 2 * WIDTH), f32)],
        in_specs=[smem_spec(), canvas_block(GANG), canvas_block(GANG)] + [vmem_spec()] * 2 + [kept(sv.shape)] + waits(after),
        out_specs=[kept((SIDE * SIDE, WIDTH)), kept((1, 2 * WIDTH))],
        scratch_shapes=[pltpu.VMEM(CANVAS, f32), pltpu.VMEM((2, SLOT, WIDTH), f32)],
        compiler_params=params(SMALL),
        cost_estimate=cost(4),
        name=f"layer{layer}_norm_backward",
    )(place, stream, gmid, *frame_views(mine, other), sv, *after)


def halves_of(x):
    high = x.astype(bf16)
    return high, (x - high.astype(f32)).astype(bf16)


def split_dot(a, b, dims):
    (a_high, a_low), (b_high, b_low) = halves_of(a), halves_of(b)
    left = jnp.concatenate([a_high, a_high, a_low], axis=1)
    right = jnp.concatenate([b_high, b_low, b_high], axis=dims[1][0])
    return lax.dot_general(left, right, (dims, ((), ())), preferred_element_type=f32)


SPANS = ((0, 3 * CH), (3 * CH, HALF), (HALF, 2 * HALF), (2 * HALF, 3 * HALF))


def own_rows(ref, index, rows):
    if rows % SLOT == 0:
        return ref[pl.ds(pl.multiple_of(index * rows, SLOT), rows)]
    start = index * rows
    base = pl.multiple_of((start // SLOT) * SLOT, SLOT)
    return pltpu.roll(ref[pl.ds(base, SLOT)], SLOT - (start - base), 0)[0:rows]


def sums_width(rows):
    return max(CH, SLOT * CH // rows)


def sums_blocks(rows):
    per = sums_width(rows) // CH
    return [(b // per, 3 * HALF + (b % per) * CH) for b in range(SLOT)]


def read_sums(ref, rows):
    blocks = [ref[row : row + 1, lane : lane + CH].astype(f32) for row, lane in sums_blocks(rows)]
    return jnp.concatenate([blocks[n] + blocks[n + 4] for n in range(4)], axis=1)


def with_sums(matrix, sums):
    rows, width = matrix.shape[0], sums_width(matrix.shape[0])
    high, low = halves_of(sums)
    parts = [x[:, n * CH : (n + 1) * CH] for x in (high, low) for n in range(4)]
    per = width // CH
    lines = [jnp.concatenate(parts[n : n + per], axis=1) for n in range(0, SLOT, per)]
    if rows > len(lines):
        lines.append(jnp.zeros((rows - len(lines), width), bf16))
    beside = jnp.concatenate([x.astype(f32) for x in lines], axis=0).astype(bf16)
    return jnp.concatenate([matrix, beside], axis=1)


def momentum_kernel(layer, n_got, place, keep, *refs):
    gots, (qkv, proj, up, down, extra, whole, fresh, vectors), refs = refs[:n_got], refs[n_got : n_got + 8], refs[n_got + 8 :]
    total = keep[0].astype(f32)
    for got in gots:
        total = total + got[0].astype(f32)
    matrix = total[:, 0 : 3 * HALF]
    old = jnp.concatenate([qkv[layer], proj[layer], up[layer], down[layer]], axis=1)
    new = momentum_decay * old + matrix
    fresh[...] = new
    ahead = (matrix + momentum_decay * new).astype(bf16)
    vectors[...] = total[0:1, 3 * HALF :]
    if layer == 0:
        whole[0] = with_sums(ahead, extra[...])
    else:
        whole[0] = ahead
        put_chunks(*refs, place[CORE], 0, extra[...].astype(f32))


def run_momentum(layer, devices, place, keep, gots, moments, extra):
    rows = keep.shape[1]
    width = 3 * HALF + (0 if layer else sums_width(rows))
    outs = [sds((1, rows, width), bf16), hbm((rows, 3 * HALF), f32), sds((1, 2 * CH), f32)]
    if layer:
        outs += chunk_shapes(devices)
    return pl.pallas_call(
        functools.partial(momentum_kernel, layer, len(gots)),
        out_shape=outs,
        in_specs=[smem_spec()] + [vmem_spec()] * (6 + len(gots)),
        out_specs=[vmem_spec()] * len(outs),
        compiler_params=params(SMALL),
        cost_estimate=cost(1),
        name=f"layer{layer}_momentum",
    )(place, keep, *gots, *moments, extra)


def square_dot(x, dims):
    high, low = halves_of(x)
    mixed = lax.dot_general(high, low, (dims, ((), ())), preferred_element_type=f32)
    return lax.dot_general(high, high, (dims, ((), ())), preferred_element_type=f32) + (mixed + mixed.T)


def newton(works, steps):
    for _ in range(steps):
        grams = [square_dot(work, ((1,), (1,))) for work in works]
        blends = [coeff_second * gram + coeff_third * square_dot(gram, ((1,), (0,))) for gram in grams]
        works = [
            coeff_first * work + split_dot(blend, work, ((1,), (0,)))
            for work, blend in zip(works, blends)
        ]
    return works


def joined(stage, place, given, scratch):
    if len(given) == 1:
        return given[0][...]
    join_chunks(stage, place[INDEX], given[0], given[1:], scratch)
    return scratch[...].reshape(WIDTH, scratch.shape[2])


def newton_from(whole, picks, steps):
    works = [whole[:, SPANS[which][0] : SPANS[which][1]].astype(f32) for which in picks]
    works = [work.T if which == 1 else work for which, work in zip(picks, works)]
    lows = [work.astype(bf16) for work in works]
    factors = [1.0 / (jnp.sqrt(jnp.sum(work * work)) + 1e-07) for work in works]
    grams = [dot_t(low, low) * (factor * factor) for low, factor in zip(lows, factors)]
    blends = [coeff_second * gram + coeff_third * square_dot(gram, ((1,), (0,))) for gram in grams]
    works = [
        (coeff_first * work + dot(jnp.concatenate(halves_of(blend), axis=1), jnp.concatenate([low, low], axis=0))) * factor
        for work, low, blend, factor in zip(works, lows, blends, factors)
    ]
    return newton(works, steps - 1)


def old_rows(layer, index, rows, masters, turned):
    parts = []
    for which, master in enumerate(masters):
        width = SPANS[which][1] - SPANS[which][0]
        if which % 2 == 1:
            tile = (index * rows) // CH
            columns = pl.ds(pl.multiple_of(tile * CH, CH), CH)
            turned[0:CH, 0:width] = master[layer, :, columns].T
            parts.append(own_rows(turned, index - tile * (CH // rows), rows)[:, 0:width])
        else:
            parts.append(own_rows(master.at[layer], index, rows))
    return parts


def new_rows(which, old, step):
    size = matrix_rate * match_scale * math.sqrt((3 * CH, WIDTH, HALF, HALF)[which])
    return old * (1.0 - matrix_rate * weight_decay) - size * step


def last_rows(works, picks, index, rows, scratch):
    def spot(n, which):
        return scratch.at[2 * n + which]

    def rows_of(n, which, value):
        ref, width = spot(n, which), value.shape[1]
        ref[:, 0:width] = value
        return own_rows(ref, index, rows)[:, 0:width]

    if rows % SLOT:
        ended = newton(works, 1)
        return [rows_of(n, 0, work.T if which == 1 else work) for n, (which, work) in enumerate(zip(picks, ended))]
    grams = [square_dot(work, ((1,), (1,))) for work in works]
    left = [
        (gram, work) if which == 1 else (rows_of(n, 0, gram), rows_of(n, 1, work))
        for n, (which, work, gram) in enumerate(zip(picks, works, grams))
    ]
    blends = [
        coeff_second * own + coeff_third * split_dot(own, gram, ((1,), (0,))) for (own, _), gram in zip(left, grams)
    ]
    ended = [
        coeff_first * own + split_dot(blend, work, ((1,), (0,))) for (_, own), blend, work in zip(left, blends, works)
    ]
    return [rows_of(n, 0, own.T) if which == 1 else own for n, (which, own) in enumerate(zip(picks, ended))]


SHARES = ((0, 2), (1, 3))
SHARE_WIDTH = 3 * CH + HALF


EARLY_STEPS = 2


def share_spots(picks):
    start, spots = 0, []
    for which in picks:
        width = SPANS[which][1] - SPANS[which][0]
        spots.append((which, CH if which == 1 else WIDTH, start, start + (WIDTH if which == 1 else width)))
        start += max(width, WIDTH)
    return spots


def newton_begin_kernel(stage, n_given, n_after, place, *refs):
    given, masters = refs[:n_given], refs[n_given : n_given + 4]
    old0, old1, works_o, turned_s, *scratch = refs[n_given + 4 + n_after :]
    index, rows = place[INDEX], old0.shape[0]
    whole = joined(stage, place, given, scratch[0] if scratch else None)
    for core, picks in enumerate(SHARES):
        @pl.when(place[CORE] == core)
        def _(picks=picks):
            for layer, old in enumerate((old0, old1)):
                for (start, stop), part in zip(SPANS, old_rows(layer, index, rows, masters, turned_s)):
                    old[:, start:stop] = part
            for (_, height, start, stop), work in zip(share_spots(picks), newton_from(whole, picks, EARLY_STEPS)):
                works_o[0:height, start:stop] = work


def newton_end_kernel(place, works, *refs):
    mine, theirs, rows_s = refs[-3:]
    index, rows = place[INDEX], mine.shape[0]
    for core, picks in enumerate(SHARES):
        @pl.when(place[CORE] == core)
        def _(picks=picks, core=core):
            spots = share_spots(picks)
            begun = [works[0:height, start:stop] for _, height, start, stop in spots]
            mine[...] = jnp.zeros_like(mine)
            theirs[...] = jnp.zeros_like(theirs)
            nearly = newton(begun, NS_STEPS - EARLY_STEPS - 1)
            if (2 * rows) % SLOT == 0:
                both = last_rows(nearly, picks, index // 2, 2 * rows, rows_s)
                pairs = [(block[0:rows], block[rows:]) for block in both]
            else:
                pairs = list(
                    zip(*[last_rows(nearly, picks, 2 * (index // 2) + n, rows, rows_s) for n in range(2)])
                )
            for (_, _, start, _), pair in zip(spots, pairs):
                width = pair[0].shape[1]
                mine[:, start : start + width] = pair[core]
                theirs[:, start : start + width] = pair[1 - core]


def run_newton_begin(stage, place, rows, given, masters, after):
    return pl.pallas_call(
        functools.partial(newton_begin_kernel, stage, len(given), len(after)),
        out_shape=[hbm((rows, 3 * HALF), f32)] * 2 + [sds((WIDTH, SHARE_WIDTH), f32)],
        in_specs=[smem_spec()] + [vmem_spec()] * (len(given) + 4) + waits(after),
        out_specs=[vmem_spec()] * 3,
        scratch_shapes=[pltpu.VMEM((WIDTH, HALF), f32)]
        + ([pltpu.VMEM((WIDTH // rows, rows, 3 * HALF), bf16)] if len(given) > 1 else []),
        compiler_params=params(SMALL),
        cost_estimate=cost(3),
        name="layer1_newton_begin",
    )(place, *given, *masters, *after)


def run_newton_end(place, rows, works, after):
    return pl.pallas_call(
        newton_end_kernel,
        out_shape=[sds((rows, SHARE_WIDTH), f32)] * 2,
        in_specs=[smem_spec(), vmem_spec()] + waits(after),
        out_specs=[vmem_spec()] * 2,
        scratch_shapes=[pltpu.VMEM((4, WIDTH, HALF), f32)],
        compiler_params=params(SMALL),
        cost_estimate=cost(4),
        name="layer1_newton_end",
    )(place, works, *after)


def finish_kernel(stage, n_given, place, *refs):
    given, refs = refs[:n_given], refs[n_given:]
    old0, old1, fresh0, fresh1, mine, theirs, vectors0, vectors1, shared_m, group_m, shared_w, group_w = refs[:12]
    outs, (rows_s, *scratch) = refs[12:24], refs[24:]
    whole = joined(stage, place, given, scratch[0] if scratch else None)
    for layer, fresh in enumerate((fresh0, fresh1)):
        for which, (start, stop) in enumerate(SPANS):
            outs[2 * which][layer] = fresh[:, start:stop]
    for core, picks in enumerate(SHARES):
        share = jnp.where(place[CORE] == core, mine[...], theirs[...])
        for which, _, first, _ in share_spots(picks):
            start, stop = SPANS[which]
            outs[2 * which + 1][1] = new_rows(which, old1[:, start:stop], share[:, first : first + stop - start])
    wide, own = shared_m.shape[1], group_m.shape[2]
    late = jnp.concatenate([read_sums(whole, fresh0.shape[0]), jnp.zeros((1, 4 * WIDTH), f32)], axis=1)
    late = jnp.broadcast_to(late, (SLOT, 6 * WIDTH))
    late = pltpu.roll(late, lax.rem(6 * WIDTH - place[INDEX] * wide, 6 * WIDTH), 1)[0:1, 0:wide]
    for layer, vectors in enumerate((vectors0, vectors1)):
        grad = vectors[:, 0:wide]
        if layer == 0:
            grad = grad + late
        new = momentum_decay * shared_m[layer : layer + 1, :] + grad
        outs[8][layer : layer + 1, :] = new
        outs[9][layer : layer + 1, :] = shared_w[layer : layer + 1, :] - vector_rate * new
        new = momentum_decay * group_m[layer] + vectors[:, CH : CH + own]
        outs[10][layer] = new
        outs[11][layer] = group_w[layer] - vector_rate * new
    works = newton_from(whole, range(4), NS_STEPS - 1)
    for which, step in enumerate(last_rows(works, range(4), place[INDEX], fresh0.shape[0], rows_s)):
        start, stop = SPANS[which]
        outs[2 * which + 1][0] = new_rows(which, old0[:, start:stop], step)


def run_finish(stage, rows, place, given, *args):
    shapes = []
    for start, stop in SPANS:
        shapes += [sds((LAYERS, rows, stop - start), f32)] * 2
    shapes += [sds(args[8].shape, f32)] * 2 + [sds(args[9].shape, f32)] * 2
    return pl.pallas_call(
        functools.partial(finish_kernel, stage, len(given)),
        out_shape=shapes,
        in_specs=[smem_spec()] + [vmem_spec()] * (len(given) + len(args)),
        out_specs=[vmem_spec()] * len(shapes),
        scratch_shapes=[pltpu.VMEM((8, WIDTH, HALF), f32)]
        + ([pltpu.VMEM((WIDTH // rows, rows, given[0].shape[2]), bf16)] if len(given) > 1 else []),
        compiler_params=params(SMALL),
        cost_estimate=cost(10),
        name="layer0_newton_finish",
    )(place, *given, *args)


def stages_of(devices):
    bits = [1 << n for n in range(devices.bit_length() - 1)]
    stages = [(bit,) for bit in bits[:2]]
    return stages + [tuple(bits[n : n + 2]) for n in range(2, len(bits), 2)]


def peers(stage):
    return [x * stage[0] for x in range((1 << len(stage)) - 1, 0, -1)]


def swap(x, axis, mask):
    n = lax.axis_size(axis)
    return lax.ppermute(x, axis, [(i, i ^ mask) for i in range(n)])


def send_parts(parts, stage):
    return [swap(part, "dp", mask) for part, mask in zip(parts, peers(stage))]


def send_all(held, stage):
    return [swap(held, "dp", mask) for mask in peers(stage)]


def part_chunks(stage, index, total, outs):
    radix = 1 << len(stage)
    own = (index // stage[0]) % radix
    for m in range(outs[0].shape[0]):
        for x in range(radix):
            outs[radix - 1 - x][m] = total(radix * m + (own ^ x)).astype(bf16)


def join_chunks(stage, index, held, gots, out):
    radix = 1 << len(stage)
    own = (index // stage[0]) % radix
    for m in range(held.shape[0]):
        for x, ref in enumerate((held, *gots[::-1])):
            out[radix * m + (own ^ x)] = ref[m]
    rows = held.shape[1]
    if held.shape[2] > 3 * HALF:
        sums = read_sums(held.at[0], rows)
        for ref in gots:
            sums = sums + read_sums(ref.at[0], rows)
        out[0] = with_sums(out[0, :, 0 : 3 * HALF], sums)


def sum_of(refs, n):
    total = refs[0][n].astype(f32)
    for ref in refs[1:]:
        total = total + ref[n].astype(f32)
    return total


def hop_kernel(joined, parted, place, *refs):
    index = place[INDEX]
    n_parts = 0 if parted is None else 1 << len(parted[1])
    outs = refs[len(refs) - len(joined) - n_parts :]
    for stage, out in zip(joined, outs):
        given, refs = refs[: 1 << len(stage)], refs[1 << len(stage) :]
        join_chunks(stage, index, given[0], given[1:], out)
    if parted is not None:
        given = refs[: 1 << len(parted[0])]
        part_chunks(parted[1], index, lambda n: sum_of(given, n), outs[len(joined) :])


def run_hop(place, joins=(), part=None, after=()):
    shapes, inputs = [], []
    for stage, held, gots in joins:
        shapes.append(sds((held.shape[0] << len(stage),) + held.shape[1:], bf16))
        inputs += [held, *gots]
    if part is not None:
        _, stage, keep, gots = part
        shapes += [sds((keep.shape[0] >> len(stage),) + keep.shape[1:], bf16)] * (1 << len(stage))
        inputs += [keep, *gots]
    outs = pl.pallas_call(
        functools.partial(hop_kernel, [join[0] for join in joins], part and part[:2]),
        out_shape=shapes,
        in_specs=[smem_spec()] + [vmem_spec()] * len(inputs) + waits(after),
        out_specs=[vmem_spec()] * len(shapes),
        compiler_params=params(SMALL),
        cost_estimate=cost(1),
        name="hop",
    )(place, *inputs, *after)
    return outs if part is None else (outs[:-1], outs[-1])


def local(
    tokens, cotangent, image_ids, qkv_weight, proj_weight, up_weight, down_weight, shared_vectors, group_vectors,
    qkv_moment, proj_moment, up_moment, down_moment, shared_moment, group_moment,
):
    devices = lax.axis_size("dp")
    index = lax.axis_index("dp")
    place = jnp.stack([index % 2, lax.axis_index("group"), index]).astype(jnp.int32)
    masters = (qkv_weight, proj_weight, up_weight, down_weight)
    moments = (qkv_moment, jnp.swapaxes(proj_moment, 1, 2), up_moment, jnp.swapaxes(down_moment, 1, 2))
    rows = WIDTH // devices
    stages = stages_of(devices)

    att0, mlp0, att1, mlp1, send = run_prepare(place, *masters)
    att0_o = swap(att0, "group", 1)
    gv, gvo = group_vectors, swap(group_vectors, "group", 1)
    mlp0_o = swap(mlp0, "group", 1)
    near = swap(send, "group", 1)
    far = swap(near, "dp", 1)
    sv = shared_vectors

    columns = jnp.swapaxes(image_ids[0].astype(f32), 0, 1).reshape(NS, STRIPE, SIDE)
    ids_t = jnp.pad(columns, ((0, 0), (0, 1), (0, 0)), constant_values=-1.0).reshape(NS * SLOT, SIDE)

    part_own, *rest_own, stream = run_attention(0, True, place, tokens, att0, sv, gv, ids_t)
    saved_own, own_kept = rest_own[:4], rest_own[4:]
    part_other, *saved_other = run_attention(0, False, place, stream, att0_o, sv, gvo, ids_t)
    middle, mid, active, slopes = run_feed(0, place, stream, part_own, part_other, mlp0, mlp0_o, sv, gv, gvo)
    outputs, grad, send1, keep1 = run_last_layer(
        1, devices, place, (middle, cotangent, att1, mlp1, near, far, sv, gv, gvo, ids_t)
    )

    def reduce_late(keep, gots, first):
        for stage, after in zip(stages[first:], stages[first + 1 :]):
            parts, keep = run_hop(place, part=(stage, after, keep, gots))
            gots = send_parts(parts, after)
        return keep, gots

    got1 = send_parts([send1], stages[0])
    parts, keep1 = run_hop(place, part=(stages[0], stages[1], keep1, got1))
    got1 = send_parts(parts, stages[1])
    gmid, gb, big_m, rows_m, bias_m = run_feed_back(
        0, place, grad, mid, slopes, active, mlp0, mlp0_o, sv, gv, gvo, (keep1,)
    )

    def back(mine, extra, after):
        saved, weights, vec = (saved_own, att0, gv) if mine else (saved_other, att0_o, gvo)
        return run_attention_back(0, mine, devices, place, gb, saved, weights, sv, vec, ids_t, extra, after)

    parts, keep1 = run_hop(place, part=(stages[1], stages[2], keep1, got1), after=(rows_m,))
    got1 = send_parts(parts, stages[2])
    da_own, big0 = back(True, (*own_kept, big_m, rows_m, bias_m), (keep1,))
    keep1, got1 = reduce_late(keep1, got1, 2)
    held1, fresh1, vectors1, send0, keep0 = run_momentum(1, devices, place, keep1, got1, moments, big0)
    got1 = send_all(held1, stages[-1])
    got0 = send_parts([send0], stages[0])
    parts, keep0 = run_hop(place, part=(stages[0], stages[1], keep0, got0))
    got0 = send_parts(parts, stages[1])
    (da_other,) = back(False, (), (keep0, held1))
    for stage in stages[-1:2:-1]:
        (held1,) = run_hop(place, joins=[(stage, held1, got1)])
        got1 = send_all(held1, stages[stages.index(stage) - 1])
    (held1, *parts), keep0 = run_hop(
        place, joins=[(stages[2], held1, got1)], part=(stages[1], stages[2], keep0, got0), after=(da_other,)
    )
    got1 = send_all(held1, stages[1])
    got0 = send_parts(parts, stages[2])
    input_grad, norm_sums = run_norm_back(0, place, stream, gmid, da_own, da_other, sv, (keep0, held1))
    keep0, got0 = reduce_late(keep0, got0, 2)
    held0, fresh0, vectors0 = run_momentum(0, devices, place, keep0, got0, moments, norm_sums)
    got0 = send_all(held0, stages[-1])
    def last_join(held, gots):
        if rows % 16 == 0:
            return (held, *gots)
        return (run_hop(place, joins=[(stages[0], held, gots)])[0].reshape(WIDTH, held.shape[2]),)

    (held1,) = run_hop(place, joins=[(stages[1], held1, got1)], after=(held0,))
    given1 = last_join(held1, send_all(held1, stages[0]))
    old0, old1, works = run_newton_begin(stages[0], place, rows, given1, masters, (held0,))
    for stage in stages[-1:2:-1]:
        (held0,) = run_hop(place, joins=[(stage, held0, got0)])
        got0 = send_all(held0, stages[stages.index(stage) - 1])
    (held0,) = run_hop(place, joins=[(stages[2], held0, got0)], after=(works,))
    got0 = send_all(held0, stages[1])
    mine, theirs = run_newton_end(place, rows, works, (held0,))
    theirs = swap(theirs, "dp", 1)
    (held0,) = run_hop(place, joins=[(stages[1], held0, got0)], after=(mine,))
    given0 = last_join(held0, send_all(held0, stages[0]))

    length = shared_moment.shape[1]
    shared_w = lax.dynamic_slice_in_dim(shared_vectors, index * length, length, 1)
    length = group_moment.shape[2]
    group_w = lax.dynamic_slice_in_dim(group_vectors, index * length, length, 2)
    out = run_finish(
        stages[0], rows, place, given0, old0, old1, fresh0, fresh1, mine, theirs, vectors0, vectors1,
        shared_moment, group_moment, shared_w, group_w,
    )
    out = [jnp.swapaxes(x, 1, 2) if n in (2, 3, 6, 7) else x for n, x in enumerate(out)]
    return (outputs, input_grad, *out)


def solution(mesh):
    return jax.shard_map(
        local,
        mesh=mesh,
        in_specs=(
            P("dp", None),
            P("dp", None),
            P("dp", None, None),
            P(None, None, "group"),
            P(None, "group", None),
            P(None, None, "group"),
            P(None, "group", None),
            P(),
            P(None, "group", None),
            P(None, "dp", "group"),
            P(None, "group", "dp"),
            P(None, "dp", "group"),
            P(None, "group", "dp"),
            P(None, "dp"),
            P(None, "group", "dp"),
        ),
        out_specs=(
            P("dp", None),
            P("dp", None),
            P(None, "dp", "group"),
            P(None, "dp", "group"),
            P(None, "group", "dp"),
            P(None, "group", "dp"),
            P(None, "dp", "group"),
            P(None, "dp", "group"),
            P(None, "group", "dp"),
            P(None, "group", "dp"),
            P(None, "dp"),
            P(None, "dp"),
            P(None, "group", "dp"),
            P(None, "group", "dp"),
        ),
        check_vma=False,
    )
```
